32 devices in a mesh: rows: 2 (over core), cols: 4 (over y, x), grp: 4 (over z).
Axes of the slice: x: 2, y: 2, z: 4, core: 2. Of those that a mesh axis runs over, the one named last changes fastest.
Arguments:
- inputs: bfloat16 [8, 32, 128, 256], P('grp', 'rows', 'cols'), may hold values from -6 to 6
- w_first: bfloat16 [3, 3, 256, 512], replicated, may hold values from -0.125 to 0.125
- gain_first: float32 [512], replicated, may hold values from 0.4 to 1.6
- shift_first: float32 [512], replicated, may hold values from -3 to 3
- w_second: bfloat16 [3, 3, 512, 512], replicated, may hold values from -0.09375 to 0.09375
- gain_second: float32 [512], replicated, may hold values from 0.4 to 1.6
- shift_second: float32 [512], replicated, may hold values from -3 to 3
- w_proj: bfloat16 [256, 512], replicated, may hold values from -0.375 to 0.375
- gain_proj: float32 [512], replicated, may hold values from 0.4 to 1.6
- shift_proj: float32 [512], replicated, may hold values from -3 to 3
- valid_mask: int32 [8, 16, 64], P('grp', 'rows', 'cols'), may hold values from 0 to 1, as said below
- cotangent: bfloat16 [8, 16, 64, 512], P('grp', 'rows', 'cols'), may hold values from -6 to 6
Outputs:
- block_out: bfloat16 [8, 16, 64, 512], P('grp', 'rows', 'cols')
- grad_inputs: bfloat16 [8, 32, 128, 256], P('grp', 'rows', 'cols')
- grad_w_first: float32 [3, 3, 256, 512], replicated
- grad_gain_first: float32 [512], replicated
- grad_shift_first: float32 [512], replicated
- grad_w_second: float32 [3, 3, 512, 512], replicated
- grad_gain_second: float32 [512], replicated
- grad_shift_second: float32 [512], replicated
- grad_w_proj: float32 [256, 512], replicated
- grad_gain_proj: float32 [512], replicated
- grad_shift_proj: float32 [512], replicated
The draws below stay inside these ranges and needn't reach their ends.
Inputs may be any that keep to these rules, and one draw needn't show every extreme that they name: `valid_mask`: 1 exactly on square tiles of 7 by 7 pixels on a grid of pitch 8 in groups of even index and of 3 by 3 pixels on a grid of pitch 4 in groups of odd index, the grid offset per group and each tile present or absent; group 0 has all its tiles.
All inputs are finite; a program needn't handle non-finite values.
Results may differ from the reference program's by a relative error of at most 0.006.
Values may be sent and summed in bfloat16 or wider, within the bound.
No kernel may reach another device: no remote copies, remote signals or barrier semaphores. Data moves between devices by JAX's collectives and lax.ppermute only.
A program may use at most 128 MiB of HBM per device.

```python
import jax
import jax.numpy as jnp
from jax import lax

C_IN = 256
C_MID = 512
G = 8
HO = 16
WO = 64
HI = 32
WI = 128


def draw_valid_mask(key, part):
    key = jax.random.fold_in(key, 11)
    slot_key, row_key, col_key = jax.random.split(key, 3)
    group_pos = jnp.arange(G)[:, None, None]
    tile_pitch = jnp.where(group_pos % 2 == 0, 8, 4)
    row_offset = 1 + jax.random.randint(row_key, (G, 1, 1), 0, 7) % (tile_pitch - 1)
    col_offset = 1 + jax.random.randint(col_key, (G, 1, 1), 0, 7) % (tile_pitch - 1)
    row_pos = jnp.arange(HO)[None, :, None] + row_offset
    col_pos = jnp.arange(WO)[None, None, :] + col_offset
    occupied = jax.random.randint(slot_key, (G, HO // 4 + 3, WO // 4 + 3), 0, 8) < 7
    occupied = occupied.at[0].set(True)
    present = occupied[group_pos, row_pos // tile_pitch, col_pos // tile_pitch]
    inside = (row_pos % tile_pitch < tile_pitch - 1) & (col_pos % tile_pitch < tile_pitch - 1) & present
    return inside.astype(jnp.int32)


def block_levels(key, dims, pieces, low, largest):
    def one(dim, blocks):
        heights = jax.random.uniform(jax.random.fold_in(jax.random.fold_in(key, 6), dim), (blocks,), jnp.float32, low / len(pieces), largest / len(pieces))
        return jnp.repeat(jnp.exp(heights), dims[dim] // blocks).reshape((-1,) + (1,) * (len(dims) - dim - 1))

    level = one(*pieces[0])
    for cut in pieces[1:]:
        level = level * one(*cut)
    return level


def bell_draw(stream_key, shape, deviation, reach, shards=(), dtype=jnp.bfloat16):
    loudness = block_levels(stream_key, shape, shards, -0.22, 0.18) if shards else 1.0
    values = jax.random.normal(stream_key, shape, jnp.float32) * deviation * loudness
    return jnp.minimum(jnp.maximum(values, -reach), reach).astype(dtype)


def setup_inputs(seed: int = 0) -> dict:
    streams_of = jax.random.split(jax.random.key(seed), 13)
    return {
        "inputs": bell_draw(streams_of[0], (G, HI, WI, C_IN), 1.0, 6.0, ((0, 4), (1, 2), (2, 4))),
        "w_first": bell_draw(streams_of[1], (3, 3, C_IN, C_MID), (9 * C_IN) ** -0.5, 0.125),
        "gain_first": jnp.clip(1.0 + 0.12 * jax.random.normal(streams_of[2], (C_MID,), jnp.float32), 0.4, 1.6),
        "shift_first": bell_draw(streams_of[3], (C_MID,), 0.5, 3.0, (), jnp.float32),
        "w_second": bell_draw(streams_of[4], (3, 3, C_MID, C_MID), (9 * C_MID) ** -0.5, 0.09375),
        "gain_second": jnp.clip(1.0 + 0.12 * jax.random.normal(streams_of[5], (C_MID,), jnp.float32), 0.4, 1.6),
        "shift_second": bell_draw(streams_of[6], (C_MID,), 0.5, 3.0, (), jnp.float32),
        "w_proj": bell_draw(streams_of[7], (C_IN, C_MID), C_IN ** -0.5, 0.375),
        "gain_proj": jnp.clip(1.0 + 0.12 * jax.random.normal(streams_of[8], (C_MID,), jnp.float32), 0.4, 1.6),
        "shift_proj": bell_draw(streams_of[9], (C_MID,), 0.5, 3.0, (), jnp.float32),
        "valid_mask": draw_valid_mask(jax.random.fold_in(streams_of[12], 71), 0),
        "cotangent": bell_draw(streams_of[11], (G, HO, WO, C_MID), 1.0, 6.0, ((0, 4), (1, 2), (2, 4))),
    }


epsilon = 1e-05

@jax.custom_vjp
def low(v):
    return lax.optimization_barrier(v.astype(jnp.bfloat16)).astype(jnp.float32)

@jax.custom_vjp
def low_back(v):
    return v

def low_keep(v):
    return (low(v), None)

def low_pass(kept, grad):
    return (grad,)

def back_keep(v):
    return (v, None)

def back_low(kept, grad):
    return (low(grad),)
low.defvjp(low_keep, low_pass)
low_back.defvjp(back_keep, back_low)

def activate(value):
    return jax.nn.gelu(value, approximate=True)

def convolve(source, weight, stride, margin):
    return lax.conv_general_dilated(source, weight, (stride, stride), margin, dimension_numbers=('NHWC', 'HWIO', 'NHWC'), precision=lax.Precision.HIGHEST)

def normalize(pre, inside, pixel_count, gain, shift):
    center = lax.optimization_barrier(jnp.sum(pre * inside, axis=(0, 1, 2))) / pixel_count
    spread = lax.optimization_barrier(jnp.sum(pre * pre * inside, axis=(0, 1, 2))) / pixel_count - center * center
    return (pre - center) * lax.rsqrt(spread + epsilon) * gain + shift

def reference(inputs, w_first, gain_first, shift_first, w_second, gain_second, shift_second, w_proj, gain_proj, shift_proj, valid_mask, cotangent):
    inside = valid_mask.astype(jnp.float32)[..., None]
    pixel_count = jnp.sum(valid_mask.astype(jnp.float32))

    def forward(source, weight_one, gain_one, shift_one, weight_two, gain_two, shift_two, weight_three, gain_three, shift_three):
        pre_first = low_back(convolve(source, weight_one, 2, ((1, 0), (1, 0))))
        hidden = low(activate(normalize(pre_first, inside, pixel_count, gain_one, shift_one)) * inside)
        pre_second = low_back(convolve(hidden, weight_two, 1, ((1, 1), (1, 1))))
        pre_proj = low_back(jnp.einsum('ghwc,cd->ghwd', source[:, ::2, ::2], weight_three, precision=lax.Precision.HIGHEST))
        summed = normalize(pre_second, inside, pixel_count, gain_two, shift_two) + normalize(pre_proj, inside, pixel_count, gain_three, shift_three)
        return activate(summed) * inside
    floats = tuple((item.astype(jnp.float32) for item in (inputs, w_first, gain_first, shift_first, w_second, gain_second, shift_second, w_proj, gain_proj, shift_proj)))
    block_out, pull = jax.vjp(forward, *floats)
    grads = pull(cotangent.astype(jnp.float32))
    return (block_out.astype(jnp.bfloat16), grads[0].astype(jnp.bfloat16), grads[1], grads[2], grads[3], grads[4], grads[5], grads[6], grads[7], grads[8], grads[9])
```

```python
import jax
import jax.numpy as jnp
from jax import lax
from jax.sharding import PartitionSpec as P

epsilon = 1e-05
layout = ("NHWC", "HWIO", "NHWC")
axes = ("rows", "cols", "grp")


def shifted(value, axis, steps):
    count = lax.axis_size(axis)
    first, last = (max(0, -steps), min(count, count - steps))
    return lax.ppermute(value, axis, [(source, source + steps) for source in range(first, last)])


def padded_2(cells, sides, width):
    for axis, dim in sides:
        count = lax.axis_size(axis)
        ends = count - 1
        head = lax.slice_in_dim(cells, 0, width, axis=dim)
        tail = lax.slice_in_dim(cells, cells.shape[dim] - width, cells.shape[dim], axis=dim)
        cells = jnp.concatenate(
            [
                lax.ppermute(tail, axis, [(i, (i + 1) % count) for i in range(ends)]),
                cells,
                lax.ppermute(head, axis, [((i + 1) % count, i) for i in range(ends)]),
            ],
            axis=dim,
        )
    return cells


def all_sum(vectors):
    count = lax.axis_size("rows") * lax.axis_size("cols") * lax.axis_size("grp")
    flat = jnp.concatenate([v.reshape(-1) for v in vectors])
    pad = -flat.shape[0] % 1024
    block = jnp.pad(flat, (0, pad)).reshape(1, -1, 128)
    spread = jnp.broadcast_to(block, (count,) + block.shape[1:])
    total = jnp.sum(lax.all_to_all(spread, axes, 0, 0), axis=0).reshape(-1)
    out, at = [], 0
    for v in vectors:
        out.append(total[at : at + v.size].reshape(v.shape))
        at += v.size
    return out


def bit_of(axis, step):
    return (lax.axis_index(axis) // step) % 2


def partner(value, axis, step):
    count = lax.axis_size(axis)
    return lax.ppermute(value, axis, [(i, i ^ step) for i in range(count)])


def steps_of(axis):
    count, step, out = lax.axis_size(axis), 1, []
    while step < count:
        out.append((axis, step))
        step *= 2
    return out


def halve(value, axis, step, dim):
    n = value.shape[dim] // 2
    low = lax.slice_in_dim(value, 0, n, axis=dim)
    high = lax.slice_in_dim(value, n, 2 * n, axis=dim)
    bit = bit_of(axis, step) == 1
    sent = jnp.where(bit, low, high)
    kept = jnp.where(bit, high, low)
    return kept + partner(sent, axis, step)


def double(value, axis, step, dim):
    other = partner(value, axis, step)
    bit = bit_of(axis, step) == 1
    return jnp.concatenate([jnp.where(bit, other, value), jnp.where(bit, value, other)], axis=dim)


def tree_sum(value, order):
    core = steps_of("rows")[0]
    value = halve(value, *core, 2)
    for axis, step in order:
        value = halve(value, axis, step, 1)
    for axis, step in reversed(order):
        value = double(value, axis, step, 1)
    return double(value, *core, 2)


def reduce_weights(value):
    plane = steps_of("cols")
    rest = steps_of("rows")[1:] + steps_of("grp")
    n = value.shape[1] // 2
    value = value.astype(jnp.bfloat16)
    first = tree_sum(value[:, :n], plane + rest)
    second = tree_sum(value[:, n:], plane[::-1] + rest)
    return jnp.concatenate([first, second], axis=1).astype(jnp.float32)


def activate(value):
    return jax.nn.gelu(value, approximate=True)


def convolve(source, weight, stride, margin):
    return lax.conv_general_dilated(
        source,
        weight,
        (stride, stride),
        margin,
        dimension_numbers=layout,
        preferred_element_type=jnp.float32,
    )


def local_sums(pre, inside):
    return (jnp.sum(pre * inside, axis=(0, 1, 2)), jnp.sum(pre * pre * inside, axis=(0, 1, 2)))


def normalize(pre, total, squares, pixel_count):
    center = total / pixel_count
    spread = squares / pixel_count - center * center
    inv_std = lax.rsqrt(spread + epsilon)
    return ((pre - center) * inv_std, inv_std)


def norm_back(grad_out, normed, inv_std, gain, grad_gain, grad_shift, pixel_count, inside):
    return gain * inv_std * (grad_out - inside * (grad_shift + normed * grad_gain) / pixel_count)


def pixel_dot(window, grad_out):
    return jnp.einsum("ghwc,ghwd->cd", window, grad_out, preferred_element_type=jnp.float32)


def on_device(
    inputs,
    w_first,
    gain_first,
    shift_first,
    w_second,
    gain_second,
    shift_second,
    w_proj,
    gain_proj,
    shift_proj,
    valid_mask,
    cotangent,
):
    groups, rows_in, cols_in, width_in = inputs.shape
    rows_out, cols_out = rows_in // 2, cols_in // 2
    width = w_first.shape[3]
    inside = valid_mask.astype(jnp.float32)[..., None]
    upper_rim = shifted(inputs[:, -1:], "rows", 1)
    with_top = jnp.concatenate([upper_rim, inputs], axis=1)
    west_rim = shifted(with_top[:, :, -1:], "cols", 1)
    padded = jnp.concatenate([west_rim, with_top], axis=2)
    pre_first = convolve(padded, w_first, 2, "VALID")
    total_first, squares_first, pixel_count = all_sum(
        (*local_sums(pre_first, inside), jnp.sum(inside).reshape(1))
    )
    even_edge = jnp.pad(padded, ((0, 0), (0, 1), (0, 1), (0, 0)))
    split = even_edge.reshape(groups, rows_out + 1, 2, cols_out + 1, 2 * width_in)
    phase = [
        [split[:, :, a, :, b * width_in : (b + 1) * width_in] for b in range(2)] for a in range(2)
    ]
    normed_first, inv_first = normalize(pre_first, total_first, squares_first, pixel_count)
    act_first = normed_first * gain_first + shift_first
    act_value, act_pull = jax.vjp(activate, act_first)
    hidden = (act_value * inside).astype(jnp.bfloat16)
    hidden_wide = padded_2(hidden, (("rows", 1), ("cols", 2)), 1)
    pre_second = convolve(hidden_wide, w_second, 1, "VALID")
    coarse = phase[1][1][:, :rows_out, :cols_out]
    pre_proj = jnp.einsum("ghwc,cd->ghwd", coarse, w_proj, preferred_element_type=jnp.float32)
    total_second, squares_second, total_proj, squares_proj = all_sum(
        (*local_sums(pre_second, inside), *local_sums(pre_proj, inside))
    )
    normed_second, inv_second = normalize(pre_second, total_second, squares_second, pixel_count)
    normed_proj, inv_proj = normalize(pre_proj, total_proj, squares_proj, pixel_count)
    summed = normed_second * gain_second + shift_second + normed_proj * gain_proj + shift_proj
    out_value, out_pull = jax.vjp(activate, summed)
    block_out = (out_value * inside).astype(jnp.bfloat16)
    grad_summed = out_pull(cotangent.astype(jnp.float32) * inside)[0]
    grad_gain_second, grad_shift, grad_gain_proj = all_sum(
        (
            jnp.sum(grad_summed * normed_second, axis=(0, 1, 2)),
            jnp.sum(grad_summed, axis=(0, 1, 2)),
            jnp.sum(grad_summed * normed_proj, axis=(0, 1, 2)),
        )
    )
    grad_pre_second = norm_back(
        grad_summed,
        normed_second,
        inv_second,
        gain_second,
        grad_gain_second,
        grad_shift,
        pixel_count,
        inside,
    ).astype(jnp.bfloat16)
    grad_pre_proj = norm_back(
        grad_summed,
        normed_proj,
        inv_proj,
        gain_proj,
        grad_gain_proj,
        grad_shift,
        pixel_count,
        inside,
    ).astype(jnp.bfloat16)
    local_second = [
        pixel_dot(hidden_wide[:, a : a + rows_out, b : b + cols_out], grad_pre_second)
        for a in range(3)
        for b in range(3)
    ]
    local_proj = pixel_dot(coarse, grad_pre_proj)
    reduced_second = reduce_weights(
        jnp.concatenate(
            [g.reshape(-1, width_in, width) for g in local_second] + [local_proj[None]], axis=0
        )
    )
    grad_second_wide = padded_2(grad_pre_second, (("rows", 1), ("cols", 2)), 1)
    turned_second = w_second[::-1, ::-1].transpose(0, 1, 3, 2)
    grad_hidden = convolve(grad_second_wide, turned_second, 1, "VALID")
    grad_act_first = act_pull(grad_hidden * inside)[0]
    grad_gain_first, grad_shift_first = all_sum(
        (
            jnp.sum(grad_act_first * normed_first, axis=(0, 1, 2)),
            jnp.sum(grad_act_first, axis=(0, 1, 2)),
        )
    )
    grad_pre_first = norm_back(
        grad_act_first,
        normed_first,
        inv_first,
        gain_first,
        grad_gain_first,
        grad_shift_first,
        pixel_count,
        inside,
    ).astype(jnp.bfloat16)
    local_first = [
        pixel_dot(
            phase[a % 2][b % 2][
                :, a // 2 : a // 2 + rows_out, b // 2 : b // 2 + cols_out
            ],
            grad_pre_first,
        )
        for a in range(3)
        for b in range(3)
    ]
    reduced_first = reduce_weights(jnp.stack(local_first))
    turned_first = w_first[::-1, ::-1].transpose(0, 1, 3, 2)
    back_first = lax.conv_general_dilated(
        grad_pre_first,
        turned_first,
        (1, 1),
        ((2, 2), (2, 2)),
        lhs_dilation=(2, 2),
        dimension_numbers=layout,
        preferred_element_type=jnp.float32,
    )
    proj_back = jnp.einsum(
        "ghwd,cd->ghwc", grad_pre_proj, w_proj, preferred_element_type=jnp.float32
    )
    spread_back = lax.pad(
        proj_back, jnp.float32(0), ((0, 0, 0), (0, 1, 1), (0, 1, 1), (0, 0, 0))
    )
    west_back = shifted(back_first[:, :, :1].astype(jnp.bfloat16), "cols", -1).astype(jnp.float32)
    grad_tall = back_first[:, :, 1:] + jnp.pad(west_back, ((0, 0), (0, 0), (cols_in - 1, 0), (0, 0)))
    upper_back = shifted(grad_tall[:, :1].astype(jnp.bfloat16), "rows", -1).astype(jnp.float32)
    grad_field = grad_tall[:, 1:] + jnp.pad(
        upper_back, ((0, 0), (rows_in - 1, 0), (0, 0), (0, 0))
    )
    grad_inputs = (grad_field + spread_back).astype(jnp.bfloat16)
    taps = reduced_second.shape[0] - 1
    return (
        block_out,
        grad_inputs,
        reduced_first.reshape(w_first.shape),
        grad_gain_first,
        grad_shift_first,
        reduced_second[:taps].reshape(w_second.shape),
        grad_gain_second,
        grad_shift,
        reduced_second[taps],
        grad_gain_proj,
        grad_shift,
    )


def solution(mesh):
    spread = P("grp", "rows", "cols", None)
    return jax.shard_map(
        on_device,
        mesh=mesh,
        in_specs=(spread,) + (P(),) * 9 + (P("grp", "rows", "cols"), spread),
        out_specs=(spread, spread) + (P(),) * 9,
        check_vma=False,
    )
```

```python
import functools

import jax
import jax.numpy as jnp
from jax import lax
from jax.experimental import pallas as pl
from jax.experimental.pallas import tpu as pltpu
from jax.sharding import PartitionSpec as P

epsilon = 1e-05
axes = ("rows", "cols", "grp")
bf16 = jnp.bfloat16
f32 = jnp.float32
inner = 0.7978845608028654
cubic = 0.044715
over = 6
rim = 3


class Refs:
    def __init__(self, named):
        self.__dict__.update(named)


class Copies:
    def __init__(self, names, sources, targets, sems):
        self.jobs = {n: pltpu.make_async_copy(s, t, sems.at[k]) for k, (n, s, t) in enumerate(zip(names, sources, targets))}

    def start(self, *names):
        for name in names:
            self.jobs[name].start()

    def wait(self, *names):
        for name in names:
            self.jobs[name].wait()


def call(body, ins, outs, scratch=None, far_in=(), far_out=(), smem=(), flops=0, moved=0, limit=52):
    scratch = scratch or {}
    far = (*far_in, *far_out)

    def spec(name):
        if name in smem:
            return pl.BlockSpec(memory_space=pltpu.SMEM)
        return pl.BlockSpec(memory_space=pltpu.HBM if name in far else pltpu.VMEM)

    kinds = {**{n: shape(v.shape, v.dtype) for n, v in ins.items()}, **outs}
    names = [*ins, *outs, *far, *scratch]

    def run(*refs):
        given = dict(zip(names, refs)) if not far else None
        if far:
            plain = dict(zip([*ins, *outs], refs))
            rest = refs[len(plain) :]
            buffers = dict(zip(far, rest))
            more = dict(zip(scratch, rest[len(far) : -1]))
            given = {**plain, **buffers, **more}
            sources = [plain[n] if n in far_in else buffers[n] for n in far]
            targets = [buffers[n] if n in far_in else plain[n] for n in far]
            copies = Copies(far, sources, targets, rest[-1])
            copies.start(*far_in)
        else:
            copies = None
        body(Refs(given), copies)

    buffers = [pltpu.VMEM(kinds[n].shape, kinds[n].dtype) for n in far]
    sems = [pltpu.SemaphoreType.DMA((len(far),))] if far else []
    result = pl.pallas_call(
        run,
        out_shape=list(outs.values()),
        in_specs=[spec(n) for n in ins],
        out_specs=[spec(n) for n in outs],
        scratch_shapes=[*buffers, *scratch.values(), *sems],
        compiler_params=pltpu.CompilerParams(vmem_limit_bytes=limit * 1024 * 1024),
        cost_estimate=pl.CostEstimate(flops=0, bytes_accessed=0, transcendentals=0),
    )(*ins.values())
    return dict(zip(outs, result))


def shape(dims, dtype=f32):
    return jax.ShapeDtypeStruct(dims, dtype)


def wide(mask, width):
    return jnp.concatenate([mask] * (width // mask.shape[1]), axis=1)


def matmul(a, b):
    return lax.dot_general(a, b, (((1,), (0,)), ((), ())), preferred_element_type=f32)


def matmul_nt(a, b):
    return lax.dot_general(a, b, (((1,), (1,)), ((), ())), preferred_element_type=f32)


def matmul_tn(a, b):
    return lax.dot_general(a, b, (((0,), (0,)), ((), ())), preferred_element_type=f32)


def gelu_parts(v):
    return jnp.tanh(inner * (v + cubic * v * v * v))


def gelu_slope(v, t):
    return 0.5 * (1.0 + t) + 0.5 * v * (1.0 - t * t) * (inner * (1.0 + 3.0 * cubic * v * v))


def column_sum(v):
    return jnp.sum(v, axis=0, keepdims=True)


def moments(total, squares, pixel_count):
    center = total / pixel_count
    spread = squares / pixel_count - center * center
    return center, lax.rsqrt(spread + epsilon)


def chunks(total, size):
    return [(at, min(size, total - at)) for at in range(0, total, size)]


def assemble(raw, flags, own, top, bot, left, right, first, last, put):
    n_top, n_own, groups = own.n_top, own.n_own, own.groups
    for r in range(first, last):
        for g in range(groups):
            if r < n_top:
                src = jnp.where(flags[0] == 1, top(g, r).astype(f32), 0.0)
            elif r < n_top + n_own:
                src = own(g, r - n_top).astype(f32)
            else:
                src = jnp.where(flags[1] == 1, bot(g, r - n_top - n_own).astype(f32), 0.0)
            line = (r - first) * groups + g
            sides = left(g, r).astype(f32), right(g, r).astype(f32)
            edge, cols = sides[0].shape[0], src.shape[0]
            pieces = ((0, sides[0]), (edge, src), (edge + cols, sides[1]))
            for at, value in pieces:
                for k in range(raw.shape[0]):
                    step = raw.shape[3]
                    raw[k, line, at : at + value.shape[0], :] = value[:, k * step : (k + 1) * step]
            put(r, g, line)


class Rows:
    def __init__(self, read, groups, n_top, n_own):
        self.read, self.groups, self.n_top, self.n_own = read, groups, n_top, n_own

    def __call__(self, g, r):
        return self.read(g, r)


def flat_row(ref, base, n, cols):
    return lambda g, r: ref[base + (g * n + r) * cols : base + (g * n + r + 1) * cols, :]


def flat_pair(ref, base, n, cols, size):
    low, high = flat_row(ref, base, n, cols), flat_row(ref, base + size, n, cols)
    return lambda g, r: jnp.concatenate([low(g, r), high(g, r)], axis=1)


def stats_kernel(r, copies):
    groups, cin = r.x.shape[0], r.x.shape[3]
    rows, S = r.own.shape[1], r.own.shape[2]
    L = groups * S
    width = r.w1.shape[2]
    raw = r.raw
    for n in range(2 * rows + 1):
        for g in range(groups):
            line = n * groups + g
            src = (r.top[g, 0] if n == 0 else r.x[g, n - 1]).astype(f32)
            side = r.lft[g, n].astype(f32)
            for k in range(raw.shape[0]):
                raw[k, line, 7:8, :] = side[:, k * 128 : (k + 1) * 128]
                raw[k, line, 8:, :] = src[:, k * 128 : (k + 1) * 128]
    for out, n_rows, start in ((r.xe, rows, 1), (r.xo, rows + 1, 0)):
        for n in range(n_rows):
            for b in range(3):
                for k in range(raw.shape[0]):
                    parts = [
                        raw[k, (2 * n + start) * groups + g, pl.ds(7 + b, S, stride=2), :]
                        for g in range(groups)
                    ]
                    at = b * cin + k * 128
                    out[n * L : (n + 1) * L, at : at + 128] = jnp.concatenate(
                        parts, axis=0
                    ).astype(bf16)
    mask = jnp.concatenate(
        [r.own[g, i].astype(f32) for i in range(rows) for g in range(groups)], axis=0
    )
    M = rows * L
    z = matmul(r.xo[0:M, :], r.w1[0])
    z += matmul(r.xe[...], r.w1[1])
    z += matmul(r.xo[L : L + M, :], r.w1[2])
    zp = matmul(r.xe[:, cin : 2 * cin], r.wp[...])
    zm, zpm = z * wide(mask, width), zp * wide(mask, width)
    row = jnp.concatenate([column_sum(zm), column_sum(zm * z), column_sum(mask)], axis=1)
    r.spread[...] = jnp.broadcast_to(row[None], r.spread.shape)
    r.psum[...] = jnp.concatenate([column_sum(zpm), column_sum(zpm * zp)], axis=1)


def first_kernel(r, copies):
    groups, cin = r.x.shape[0], r.x.shape[3]
    rows, cols = r.own.shape[1], r.own.shape[2]
    S = cols + 8
    L = groups * S
    raw = r.raw
    end = 16 + r.x.shape[2]
    total_rows = r.x.shape[1] + 2 * over

    def put(n, g, line):
        for k in range(raw.shape[0]):
            raw[k, line, end:, :] = jnp.zeros((raw.shape[2] - end, 128), f32)

    assemble(
        raw,
        r.flags,
        Rows(lambda g, n: r.x[g, n], groups, over, r.x.shape[1]),
        flat_row(r.top, 0, over, r.x.shape[2]),
        flat_row(r.bot, 0, over, r.x.shape[2]),
        lambda g, n: r.lft[g, n],
        lambda g, n: r.rgt[g, n],
        0,
        total_rows,
        put,
    )
    for out, n_rows, start in ((r.xe, rows + 5, 2), (r.xo, rows + 6, 1)):
        for n in range(n_rows):
            for b in range(3):
                for k in range(raw.shape[0]):
                    parts = [
                        raw[k, (2 * n + start) * groups + g, pl.ds(3 + b, S, stride=2), :]
                        for g in range(groups)
                    ]
                    at = b * cin + k * 128
                    out[n * L : (n + 1) * L, at : at + 128] = jnp.concatenate(
                        parts, axis=0
                    ).astype(bf16)
    copies.start("xe", "xo")
    r.ownp[...] = jnp.zeros(r.ownp.shape, f32)
    for i in range(rows):
        for g in range(groups):
            at = (i + 2) * L + g * S + 2
            r.ownp[at : at + cols, :] = r.own[g, i].astype(f32)
    copies.wait("w1", "wp")
    for m0, m in chunks(r.pre1.shape[0], 208):
        z = matmul(r.xo[m0 : m0 + m, :], r.w1[0])
        z += matmul(r.xe[m0 : m0 + m, :], r.w1[1])
        z += matmul(r.xo[L + m0 : L + m0 + m, :], r.w1[2])
        r.pre1[m0 : m0 + m, :] = z
        r.prep[m0 : m0 + m, :] = matmul(r.xe[m0 : m0 + m, cin : 2 * cin], r.wp[...])
        r.keep[m0 : m0 + m, :] = z
    copies.start("keep")
    copies.wait("xe", "xo", "keep")


def rims_kernel(r, copies):
    groups, rows, cols, width = r.cot.shape
    S = cols + 8
    L = groups * S
    base, size = over * groups * 2 * cols, rim * groups * cols
    lanes = slice(width, width + 128)

    def put(n, g, line):
        at = (n - 1) * L + g * S
        r.maskp[at : at + S, :] = r.raw[0, line, 6 : 6 + S, :]

    assemble(
        r.raw,
        r.flags,
        Rows(lambda g, n: r.own[g, n], groups, rim, rows),
        lambda g, n: flat_row(r.top, base + width // 256 * size, rim, cols)(g, n)[:, :128],
        lambda g, n: flat_row(r.bot, base + width // 256 * size, rim, cols)(g, n)[:, :128],
        lambda g, n: r.lft[g, n][:, lanes],
        lambda g, n: r.rgt[g, n][:, lanes],
        1,
        rows + 6,
        put,
    )

    def put_cot(n, g, line):
        at = (n - 2) * L + g * S
        r.cotq[at : at + S, :] = r.field[0, line, 7 : 7 + S, :]

    assemble(
        r.field,
        r.flags,
        Rows(lambda g, n: r.cot[g, n], groups, rim, rows),
        flat_pair(r.top, base, rim, cols, size),
        flat_pair(r.bot, base, rim, cols, size),
        lambda g, n: r.lft[g, n][:, :width],
        lambda g, n: r.rgt[g, n][:, :width],
        2,
        rows + 5,
        put_cot,
    )
    copies.start("cotq")
    copies.wait("cotq")


def second_kernel(r, copies):
    width = r.gain.shape[1]
    t = jnp.sum(r.tot1[...], axis=0)
    n = wide(t[:, 2 * width :], width)
    center, inv = moments(t[:, :width], t[:, width : 2 * width], n)
    r.mom1[...] = jnp.concatenate([center, inv, n, jnp.zeros((5, width), f32)], axis=0)
    scale = inv * r.gain[...]
    M, Q = r.pre1.shape[0], r.pre2.shape[0]
    L = (M - Q) // 2
    for m0, m in chunks(M, 104):
        v = (r.pre1[m0 : m0 + m, :] - center) * scale + r.shift[...]
        mask = wide(r.maskp[m0 : m0 + m, :], width)
        r.hid[m0 : m0 + m, :] = 0.5 * v * (1.0 + gelu_parts(v)) * mask
    r.hid[M:, :] = jnp.zeros((r.hid.shape[0] - M, width), f32)
    for m0, m in chunks(M, 208):
        for b in range(3):
            r.h3[m0 : m0 + m, b * width : (b + 1) * width] = r.hid[m0 + b : m0 + b + m, :].astype(bf16)
    copies.start("h3")
    copies.wait("w2")
    sums = [jnp.zeros((1, width), f32)] * 2
    for m0, m in chunks(Q, 176):
        z = matmul(r.h3[m0 : m0 + m, :], r.w2[0])
        z += matmul(r.h3[L + m0 : L + m0 + m, :], r.w2[1])
        z += matmul(r.h3[2 * L + m0 : 2 * L + m0 + m, :], r.w2[2])
        r.pre2[m0 : m0 + m, :] = z
        zm = z * wide(r.ownp[L + 1 + m0 : L + 1 + m0 + m, :], width)
        sums = [sums[0] + column_sum(zm), sums[1] + column_sum(zm * z)]
    row = jnp.concatenate([*sums, r.psum[...]], axis=1)
    r.spread[...] = jnp.broadcast_to(row[None], r.spread.shape)
    copies.wait("h3")


def third_kernel(r, copies):
    groups, rows, cols, width = r.out.shape
    S = cols + 8
    L = groups * S
    n = r.mom1[2:3, :]
    t = jnp.sum(r.tot2[...], axis=0)
    parts = [t[:, k * width : (k + 1) * width] for k in range(4)]
    (c2, i2), (cp, ip) = moments(parts[0], parts[1], n), moments(parts[2], parts[3], n)
    r.mom2[...] = jnp.concatenate([c2, i2, cp, ip, jnp.zeros((4, width), f32)], axis=0)
    sums = [jnp.zeros((1, width), f32)] * 3
    both_shift = r.shift2[...] + r.shiftp[...]
    copies.wait("cotq")
    for line in range(r.grad.shape[0] // S):
        at = line * S
        shifted = slice(L + 1 + at, L + 1 + at + S)
        n2 = (r.pre2[at : at + S, :] - c2) * i2
        np_ = (r.prep[shifted, :] - cp) * ip
        v = n2 * r.gain2[...] + np_ * r.gainp[...] + both_shift
        mask = wide(r.maskp[shifted, :], width)
        own = wide(r.ownp[shifted, :], width)
        t = gelu_parts(v)
        r.field[at : at + S, :] = 0.5 * v * (1.0 + t) * mask
        g = gelu_slope(v, t) * mask * r.cotq[at : at + S, :]
        r.grad[at : at + S, :] = g
        g = g * own
        new = [column_sum(g * n2), column_sum(g), column_sum(g * np_)]
        sums = [a + b for a, b in zip(sums, new)]
    copies.start("grad")
    for i in range(rows):
        for g in range(groups):
            at = (i + 1) * L + g * S + 1
            r.out[g, i, :, :] = r.field[at : at + cols, :].astype(bf16)
    copies.start("out")
    row = jnp.concatenate(sums, axis=1)
    r.spread[...] = jnp.broadcast_to(row[None], r.spread.shape)
    copies.wait("grad", "out")


def halves(r, source, at, frame, to, rows_w):
    half = r.mine.shape[1]
    bit = r.bits[0] == 1
    for m0, m in chunks(rows_w, 96):
        own = wide(r.ownp[frame + m0 : frame + m0 + m, :], half)
        low = (source[at + m0 : at + m0 + m, :half] * own).astype(bf16)
        high = (source[at + m0 : at + m0 + m, half:] * own).astype(bf16)
        r.mine[to + m0 : to + m0 + m, :] = jnp.where(bit, high, low)
        r.theirs[to + m0 : to + m0 + m, :] = jnp.where(bit, low, high)


def fourth_kernel(r, copies):
    width = r.gain2.shape[1]
    Q = r.pre2.shape[0]
    rows_w = r.gpu.shape[0]
    L = (Q - rows_w) // 3
    n = r.mom1[2:3, :]
    c2, i2, cp, ip = (r.mom2[k : k + 1, :] for k in range(4))
    t3 = jnp.sum(r.tot3[...], axis=0)
    r.sums[...] = t3
    gg2, gs, ggp = (t3[:, k * width : (k + 1) * width] for k in range(3))
    copies.wait("grad")
    for m0, m in chunks(Q, L):
        shifted = slice(L + 1 + m0, L + 1 + m0 + m)
        mask = wide(r.maskp[shifted, :], width) / n
        n2 = (r.pre2[m0 : m0 + m, :] - c2) * i2
        np_ = (r.prep[shifted, :] - cp) * ip
        g = r.grad[m0 : m0 + m, :]
        r.gq[m0 : m0 + m, :] = (r.gain2[...] * i2) * (g - mask * (gs + n2 * gg2))
        r.gpq[m0 : m0 + m, :] = (r.gainp[...] * ip) * (g - mask * (gs + np_ * ggp))
    r.gq[Q:, :] = jnp.zeros((r.gq.shape[0] - Q, width), f32)
    for m0, m in chunks(rows_w, 96):
        r.gpu[m0 : m0 + m, :] = r.gpq[L + 1 + m0 : L + 1 + m0 + m, :].astype(bf16)
    copies.start("gpu")
    halves(r, r.gq, L, 2 * L + 1, 0, rows_w)
    halves(r, r.gpq, L - 1, 2 * L, rows_w, rows_w)
    copies.wait("gpu")


def hidden_kernel(r, copies):
    width = r.gain.shape[1]
    Q = r.gq.shape[0] - 8
    L = (r.keep.shape[0] - Q) // 2
    center, inv = r.mom1[0:1, :], r.mom1[1:2, :]
    for m0, m in chunks(Q, 176):
        for b in range(3):
            r.g3[m0 : m0 + m, b * width : (b + 1) * width] = r.gq[m0 + b : m0 + b + m, :].astype(bf16)
    copies.wait("w2")
    U = r.act.shape[0]
    for m0, m in chunks(U, 144):
        gh = jnp.zeros((m, width), f32)
        for a in range(3):
            for b in range(3):
                gh += matmul_nt(
                    r.g3[L * a + m0 : L * a + m0 + m, b * width : (b + 1) * width],
                    r.w2[2 - a, (2 - b) * width : (3 - b) * width, :],
                )
        r.act[m0 : m0 + m, :] = gh
    copies.wait("keep")
    sums = [jnp.zeros((1, width), f32)] * 2
    for m0, m in chunks(U, L):
        frame = slice(2 * L + 2 + m0, 2 * L + 2 + m0 + m)
        n1 = (r.keep[frame, :] - center) * inv
        v = n1 * r.gain[...] + r.shift[...]
        mask = wide(r.maskp[frame, :], width)
        g = gelu_slope(v, gelu_parts(v)) * mask * r.act[m0 : m0 + m, :]
        r.act[m0 : m0 + m, :] = g
        r.normed[m0 : m0 + m, :] = n1 * mask
        g = g * wide(r.ownp[frame, :], width)
        sums = [sums[0] + column_sum(g * n1), sums[1] + column_sum(g)]
    row = jnp.concatenate(sums, axis=1)
    r.spread[...] = jnp.broadcast_to(row[None], r.spread.shape)


def split_store(bits, acc, rows, unit, sent_a, kept_a, sent_b, kept_b):
    quarter = unit // 4
    for k in range(rows // unit):
        for bit, base, sent, kept in ((1, 0, sent_a, kept_a), (2, 2 * quarter, sent_b, kept_b)):
            keep = pl.multiple_of(k * unit + base + bits[bit] * quarter, quarter)
            send = pl.multiple_of(k * unit + base + (1 - bits[bit]) * quarter, quarter)
            yield k, acc[pl.ds(send, quarter), :].astype(bf16), acc[pl.ds(keep, quarter), :], sent, kept


def weights_second_kernel(r, copies):
    width = r.h3.shape[1] // 3
    cin = r.xe.shape[1] // 3
    rows_w = r.near.shape[0] // 2
    L = (r.h3.shape[0] - rows_w) // 5
    per = 3 * width // cin
    places = r.sent_a, r.kept_a, r.sent_b, r.kept_b
    copies.wait("h3", "h3_far")
    for a in range(3):
        at = L * a + L
        for b in range(3):
            lanes = slice(b * width, (b + 1) * width)
            r.acc[lanes, :] = matmul_tn(r.h3[at : at + rows_w, lanes], r.near[:rows_w, :]) + matmul_tn(
                r.h3_far[at : at + rows_w, lanes], r.far[:rows_w, :]
            )
        for k, s, v, sent, kept in split_store(r.bits, r.acc, 3 * width, cin, *places):
            sent[a * per + k] = s
            kept[a * per + k] = v
    at = 2 * L
    copies.wait("xe", "xe_far")
    r.acc[0:cin, :] = matmul_tn(r.xe[at : at + rows_w, cin : 2 * cin], r.near[rows_w:, :]) + matmul_tn(
        r.xe_far[at : at + rows_w, cin : 2 * cin], r.far[rows_w:, :]
    )
    for k, s, v, sent, kept in split_store(r.bits, r.acc, cin, cin, *places):
        sent[3 * per] = s
        kept[3 * per] = v
    copies.start("kept_a", "kept_b")
    copies.wait("kept_a", "kept_b")


def fifth_kernel(r, copies):
    width = r.gain.shape[1]
    U = r.act.shape[0]
    rows_w = r.mine.shape[0]
    L = U - rows_w
    inv, n = r.mom1[1:2, :], r.mom1[2:3, :]
    t4 = jnp.sum(r.tot4[...], axis=0)
    r.sums[...] = t4
    gg, gs = t4[:, :width] / n, t4[:, width:] / n
    scale = r.gain[...] * inv
    r.gf[0:8, :] = jnp.zeros((8, width), f32)
    r.gf[8 + U :, :] = jnp.zeros((r.gf.shape[0] - 8 - U, width), f32)
    for m0, m in chunks(U, L):
        mask = wide(r.maskp[2 * L + 2 + m0 : 2 * L + 2 + m0 + m, :], width)
        back = mask * gs + r.normed[m0 : m0 + m, :] * gg
        r.gf[8 + m0 : 8 + m0 + m, :] = scale * (r.act[m0 : m0 + m, :] - back)
    halves(r, r.gf, 6, 2 * L, 0, rows_w)
    for m0, m in chunks(U, 144):
        r.gu[m0 : m0 + m, :width] = r.gf[8 + m0 : 8 + m0 + m, :].astype(bf16)
        r.gu[m0 : m0 + m, width:] = r.gf[9 + m0 : 9 + m0 + m, :].astype(bf16)
    copies.start("gu")
    copies.wait("gu")


def weights_first_kernel(r, copies):
    rows_w = r.near.shape[0]
    cin = r.xe.shape[1] // 3
    L = (r.xe.shape[0] - rows_w) // 5
    places = r.sent_a, r.kept_a, r.sent_b, r.kept_b
    copies.wait("xe", "xo", "xe_far", "xo_far")
    for a in range(3):
        source, source_far = (r.xe, r.xe_far) if a == 1 else (r.xo, r.xo_far)
        at = (3 if a == 2 else 2) * L
        r.acc[...] = matmul_tn(source[at : at + rows_w, :], r.near[...]) + matmul_tn(
            source_far[at : at + rows_w, :], r.far[...]
        )
        for k, s, v, sent, kept in split_store(r.bits, r.acc, 3 * cin, cin, *places):
            sent[a * 3 + k] = s
            kept[a * 3 + k] = v
    copies.start("kept_a", "kept_b")
    copies.wait("kept_a", "kept_b")


def inputs_kernel(r, copies):
    width = r.gpu.shape[1]
    groups, rows, cols = r.out.shape[0], r.out.shape[1] // 2, r.out.shape[2] // 2
    cin = r.out.shape[3]
    M = r.gpu.shape[0]
    S = cols + 8
    L = groups * S
    lines = r.lines
    copies.wait("gu", "gpu", "w1", "wp")

    def tap(m0, m, a, b):
        di, dj = (1 if a == 0 else 0), (1 if b == 0 else 0)
        return matmul_nt(
            r.gu[di * L + m0 : di * L + m0 + m, dj * width : (dj + 1) * width],
            r.w1[a, b * cin : (b + 1) * cin, :],
        )

    for m0, m in chunks(M, 2 * L):
        pieces = {
            (0, 0): tap(m0, m, 1, 1) + matmul_nt(r.gpu[m0 : m0 + m, :], r.wp[...]),
            (0, 1): tap(m0, m, 1, 2) + tap(m0, m, 1, 0),
            (1, 0): tap(m0, m, 2, 1) + tap(m0, m, 0, 1),
            (1, 1): tap(m0, m, 2, 2) + tap(m0, m, 2, 0) + tap(m0, m, 0, 2) + tap(m0, m, 0, 0),
        }
        for (ro, co), v in pieces.items():
            for k in range(m // S):
                line = m0 // S + k
                i, g = line // groups, line % groups
                for h in range(lines.shape[0]):
                    lines[h, (2 * i + ro) * groups + g, pl.ds(co, cols, stride=2), :] = v[
                        k * S : k * S + cols, h * 128 : (h + 1) * 128
                    ]
    for n in range(2 * rows):
        for g in range(groups):
            for h in range(lines.shape[0]):
                r.out[g, n, :, h * 128 : (h + 1) * 128] = lines[h, n * groups + g].astype(bf16)
    copies.start("out")
    copies.wait("out")


def widen_kernel(bits, half, *refs):
    refs[-1][...] = half[...].astype(f32)


def widen(half, side, taps, into=None):
    n, m = half.shape[1], half.shape[2]
    step = 3 if taps % 3 == 0 else 1
    block = pl.BlockSpec((step, n, m), lambda t, side: (t, 0, 0))
    placed = pl.BlockSpec((step, n, m), lambda t, side: (t, 0, side[0]))
    more = [] if into is None else [into]
    return pl.pallas_call(
        widen_kernel,
        out_shape=shape((taps, n, 2 * m)),
        grid_spec=pltpu.PrefetchScalarGridSpec(
            num_scalar_prefetch=1,
            grid=(taps // step,),
            in_specs=[block] + [pl.BlockSpec(memory_space=pl.ANY)] * len(more),
            out_specs=placed,
        ),
        input_output_aliases={2: 0} if more else {},
        compiler_params=pltpu.CompilerParams(vmem_limit_bytes=20 * 1024 * 1024),
        cost_estimate=pl.CostEstimate(flops=0, bytes_accessed=taps * n * m * 6, transcendentals=0),
    )(side.reshape(1), half, *more)


def shifted(value, axis, steps):
    count = lax.axis_size(axis)
    first, last = (max(0, -steps), min(count, count - steps))
    return lax.ppermute(value, axis, [(source, source + steps) for source in range(first, last)])


def vertical(cells, cot, own):
    width = cot.shape[3]
    count = lax.axis_size("rows")
    me = lax.axis_index("rows")
    mask = jnp.concatenate([own, own], axis=3)

    def packed(ends):
        parts = [cells[:, ends(over)], *(cot[:, ends(rim), :, k : k + 256] for k in range(0, width, 256)), mask[:, ends(rim)]]
        return jnp.concatenate([part.reshape(-1, 256) for part in parts], axis=0)

    down, up = packed(lambda n: slice(-n, None)), packed(lambda n: slice(0, n))
    flags = jnp.stack([me > 0, me < count - 1]).astype(jnp.int32)
    if count == 2:
        swapped = lax.ppermute(jnp.where(me == 0, down, up), "rows", [(0, 1), (1, 0)])
        return swapped, swapped, flags
    return shifted(down, "rows", 1), shifted(up, "rows", -1), flags


def horizontal(top, mid, bot, flags, edge):
    top = jnp.where(flags[0] == 1, top, jnp.zeros_like(top))
    bot = jnp.where(flags[1] == 1, bot, jnp.zeros_like(bot))
    ends = [
        jnp.concatenate([part[:, :, at] for part in (top, mid, bot)], axis=1)
        for at in (slice(-edge, None), slice(0, edge))
    ]
    return shifted(ends[0], "cols", 1), shifted(ends[1], "cols", -1)


def gather_sum(spread):
    return lax.all_to_all(spread, axes, 0, 0)


def bit_of(axis, step):
    return (lax.axis_index(axis) // step) % 2


def partner(value, axis, step):
    count = lax.axis_size(axis)
    return lax.ppermute(value, axis, [(i, i ^ step) for i in range(count)])


def steps_of(axis):
    count, step, out = lax.axis_size(axis), 1, []
    while step < count:
        out.append((axis, step))
        step *= 2
    return out


def split(total, axis, step):
    n = total.shape[1] // 2
    bit = bit_of(axis, step) == 1
    low, high = total[:, :n], total[:, n:]
    return jnp.where(bit, low, high).astype(bf16), jnp.where(bit, high, low)


def join(value, axis, step, dim=1):
    other = partner(value, axis, step)
    bit = bit_of(axis, step) == 1
    return jnp.concatenate([jnp.where(bit, other, value), jnp.where(bit, value, other)], axis=dim)


class Tree:
    def __init__(self, parts, plane, rest):
        self.sent_a, self.kept_a, self.sent_b, self.kept_b = parts
        self.a, self.b = plane, plane[::-1]
        self.rest = []
        for axis in dict.fromkeys(axis for axis, _ in rest):
            steps = [step for name, step in rest if name == axis]
            self.rest += [(axis, steps[k : k + 2]) for k in range(0, len(steps), 2)]
        self.at = 0

    def start(self):
        self.got = partner(self.sent_a, *self.a[self.at]), partner(self.sent_b, *self.b[self.at])

    def finish(self, before=None):
        total_a = self.kept_a + self.got[0].astype(f32)
        total_b = self.kept_b + self.got[1].astype(f32)
        self.at += 1
        if self.at < len(self.a):
            self.sent_a, self.kept_a = split(total_a, *self.a[self.at])
            self.sent_b, self.kept_b = split(total_b, *self.b[self.at])
            keep = [self.sent_a, self.kept_a, self.sent_b, self.kept_b]
            if before is not None:
                before, *keep = lax.optimization_barrier((before, *keep))
            self.sent_a, self.kept_a, self.sent_b, self.kept_b = keep
        else:
            self.taps = total_a.shape[0]
            self.value = jnp.concatenate([total_a, total_b], axis=0).astype(bf16)
            if before is not None:
                before, self.value = lax.optimization_barrier((before, self.value))
        return before

    def exchange(self, k, part=slice(None)):
        axis, steps = self.rest[k]
        got = [] if part.start is None or part.start == 0 else self.got
        self.got = got + [partner(self.value, axis, m * steps[0]) for m in range(1, 2 ** len(steps))[part]]

    def gathered(self):
        parts = [v.astype(f32) for v in (self.value, *self.got)]
        while len(parts) > 1:
            parts = [parts[k] + parts[k + 1] for k in range(0, len(parts), 2)]
        self.value = parts[0].astype(bf16)

    def join(self):
        a, b = self.value[: self.taps], self.value[self.taps :]
        for at in reversed(range(len(self.a))):
            a, b = join(a, *self.a[at]), join(b, *self.b[at])
        return jnp.concatenate([a, b], axis=1)

    def rest_from(self, k):
        for k in range(k, len(self.rest)):
            self.exchange(k)
            self.gathered()


def on_device(inputs, w_first, gain_first, shift_first, w_second, gain_second, shift_second, w_proj, gain_proj, shift_proj, valid_mask, cotangent):
    groups, rows_in, cols_in, cin = inputs.shape
    rows, cols = rows_in // 2, cols_in // 2
    width = w_first.shape[3]
    half = width // 2
    S = cols + 8
    L = groups * S
    devices = lax.axis_size("rows") * lax.axis_size("cols") * lax.axis_size("grp")
    plane = steps_of("cols")
    core = steps_of("rows")[0]
    rest = steps_of("rows")[1:] + steps_of("grp")
    bits = jnp.stack([bit_of(*core), bit_of(*plane[0]), bit_of(*plane[-1])]).astype(jnp.int32)
    w1 = w_first.reshape(3, 3 * cin, width)
    w2 = w_second.reshape(3, 3 * width, width)
    as_row = lambda v: v.reshape(1, -1)
    own = jnp.broadcast_to(valid_mask.astype(bf16)[..., None], valid_mask.shape + (128,))
    MP, MQ, MU, MW = (rows + 5) * L, (rows + 3) * L, (rows + 1) * L, rows * L
    px = lambda m, k: 2 * m * k * width
    vec = lambda k: shape((1, k * width))
    all_devices = lambda k: shape((devices, 1, k))
    g1, b1, g2, b2, gp, bp = map(
        as_row, (gain_first, shift_first, gain_second, shift_second, gain_proj, shift_proj)
    )

    top1 = shifted(inputs[:, -1:], "rows", 1)
    lft1 = shifted(jnp.concatenate([top1[:, :, -1:], inputs[:, :, -1:]], axis=1), "cols", 1)
    stats = call(
        stats_kernel,
        dict(x=inputs, top=top1, lft=lft1, own=own, w1=w1, wp=w_proj),
        dict(spread=all_devices(2 * width + 128), psum=vec(2)),
        dict(
            raw=pltpu.VMEM((cin // 128, (rows_in + 1) * groups, cols_in + 8, 128), f32),
            xe=pltpu.VMEM((rows * groups * cols, 3 * cin), bf16),
            xo=pltpu.VMEM(((rows + 1) * groups * cols, 3 * cin), bf16),
        ),
        flops=px(rows * groups * cols, 10 * cin),
        moved=4_000_000,
    )
    spread1 = stats["spread"]
    tot1 = gather_sum(spread1)

    wide_inputs, _ = lax.optimization_barrier((inputs, top1))
    top, bot, flags = vertical(wide_inputs, cotangent, own)
    flat = over * groups * cols_in
    lft, rgt = horizontal(
        top[:flat].reshape(groups, over, cols_in, cin), inputs, bot[:flat].reshape(groups, over, cols_in, cin), flags, 8
    )
    first = call(
        first_kernel,
        dict(flags=flags, x=inputs, top=top, bot=bot, lft=lft, rgt=rgt, own=own, w1=w1, wp=w_proj),
        dict(
            pre1=shape((MP, width)),
            prep=shape((MP, width)),
            xe=shape((MP, 3 * cin), bf16),
            xo=shape((MP + L, 3 * cin), bf16),
            keep=shape((MP, width)),
            ownp=shape((MP, 128)),
        ),
        dict(raw=pltpu.VMEM((cin // 128, (rows_in + 12) * groups, cols_in + 24, 128), f32)),
        far_in=("w1", "wp"),
        far_out=("xe", "xo", "keep"),
        smem=("flags",),
        flops=px(MP, 10 * cin),
        moved=10_000_000,
    )
    xe, xo, ownp = first["xe"], first["xo"], first["ownp"]
    piece = rim * groups * cols

    def rows_of(flat_rim):
        parts = [
            flat_rim[flat + k * piece : flat + (k + 1) * piece].reshape(groups, rim, cols, 256)
            for k in range(width // 256 + 1)
        ]
        return jnp.concatenate(parts[:-1] + [parts[-1][..., :128]], axis=3)

    cot_here, _ = lax.optimization_barrier((cotangent, spread1))
    clft, crgt = horizontal(
        rows_of(top), jnp.concatenate([cot_here, own], axis=3), rows_of(bot), flags, 8
    )
    rims = call(
        rims_kernel,
        dict(flags=flags, own=own, cot=cotangent, top=top, bot=bot, lft=clft, rgt=crgt),
        dict(maskp=shape((MP, 128)), cotq=shape((MQ, width))),
        dict(
            raw=pltpu.VMEM((1, (rows + 5) * groups, cols + 16, 128), f32),
            field=pltpu.VMEM((1, (rows + 3) * groups, cols + 16, width), f32),
        ),
        far_out=("cotq",),
        smem=("flags",),
        flops=MQ * width * 4,
        moved=4_000_000,
    )
    maskp = rims["maskp"]
    far_xe, far_xo = partner(xe, *core), partner(xo, *core)

    second = call(
        second_kernel,
        dict(pre1=first["pre1"], tot1=tot1, gain=g1, shift=b1, maskp=maskp, ownp=ownp, psum=stats["psum"], w2=w2),
        dict(h3=shape((MP, 3 * width), bf16), pre2=shape((MQ, width)), spread=all_devices(4 * width), mom1=shape((8, width))),
        dict(hid=pltpu.VMEM((MP + 8, width), f32)),
        far_in=("w2",),
        far_out=("h3",),
        flops=px(MQ, 9 * width),
        moved=10_000_000,
    )
    h3, pre2, mom1 = second["h3"], second["pre2"], second["mom1"]
    tot2 = gather_sum(second["spread"])
    far_h3 = partner(h3, *core)

    third = call(
        third_kernel,
        dict(
            pre2=pre2, prep=first["prep"], mom1=mom1, tot2=tot2, gain2=g2, shift2=b2, gainp=gp, shiftp=bp,
            maskp=maskp, ownp=ownp, cotq=rims["cotq"],
        ),
        dict(
            out=shape((groups, rows, cols, width), bf16),
            grad=shape((MQ, width)),
            spread=all_devices(3 * width),
            mom2=shape((8, width)),
        ),
        dict(field=pltpu.VMEM((MQ, width), f32)),
        far_in=("cotq",),
        far_out=("out", "grad"),
        flops=MQ * width * 60,
        moved=5_000_000,
    )
    mom2 = third["mom2"]
    tot3 = gather_sum(third["spread"])

    fourth = call(
        fourth_kernel,
        dict(
            bits=bits, pre2=pre2, prep=first["prep"], mom1=mom1, mom2=mom2, tot3=tot3, gain2=g2, gainp=gp,
            grad=third["grad"], maskp=maskp, ownp=ownp,
        ),
        dict(
            mine=shape((2 * MW, half), bf16),
            theirs=shape((2 * MW, half), bf16),
            gq=shape((MQ + 8, width)),
            gpu=shape((MW, width), bf16),
            sums=vec(3),
        ),
        dict(gpq=pltpu.VMEM((MQ, width), f32)),
        far_in=("grad",),
        far_out=("gpu",),
        smem=("bits",),
        flops=MQ * width * 40,
        moved=6_000_000,
    )
    far2 = partner(fourth["theirs"], *core)

    def chunk_shapes(taps):
        dims = (taps, cin // 4, half)
        return dict(sent_a=shape(dims, bf16), kept_a=shape(dims), sent_b=shape(dims, bf16), kept_b=shape(dims))

    taps2 = 9 * width // cin + 1
    second_parts = call(
        weights_second_kernel,
        dict(bits=bits, h3=h3, h3_far=far_h3, xe=xe, xe_far=far_xe, near=fourth["mine"], far=far2),
        chunk_shapes(taps2),
        dict(acc=pltpu.VMEM((3 * width, half), f32)),
        far_in=("h3", "h3_far", "xe", "xe_far"),
        far_out=("kept_a", "kept_b"),
        smem=("bits",),
        flops=2 * 9 * width * half * 2 * MW,
        moved=8_000_000,
    ).values()
    gq, *second_parts = lax.optimization_barrier((fourth["gq"], *second_parts))

    tree2 = Tree(second_parts, plane, rest)
    tree2.start()
    hidden = call(
        hidden_kernel,
        dict(w2=w2, keep=first["keep"], mom1=mom1, gain=g1, shift=b1, gq=gq, maskp=maskp, ownp=ownp),
        dict(act=shape((MU, width)), normed=shape((MU, width)), spread=all_devices(2 * width)),
        dict(g3=pltpu.VMEM((MQ, 3 * width), bf16)),
        far_in=("w2", "keep"),
        flops=px(MU, 9 * width),
        moved=10_000_000,
    )
    spread4 = tree2.finish(hidden["spread"])
    tot4 = gather_sum(spread4)
    tree2.start()
    tot4, tree2.got = lax.optimization_barrier((tot4, tree2.got))
    act = tree2.finish(hidden["act"])

    tree2.exchange(0, slice(0, 1))
    fifth = call(
        fifth_kernel,
        dict(
            bits=bits, act=act, normed=hidden["normed"], mom1=mom1, tot4=tot4, gain=g1, maskp=maskp, ownp=ownp
        ),
        dict(
            mine=shape((MW, half), bf16), theirs=shape((MW, half), bf16), gu=shape((MU, 2 * width), bf16), sums=vec(2)
        ),
        dict(gf=pltpu.VMEM((MU + 16, width), f32)),
        far_out=("gu",),
        smem=("bits",),
        flops=MU * width * 20,
        moved=4_000_000,
    )
    far1 = partner(fifth["theirs"], *core)
    first_parts = call(
        weights_first_kernel,
        dict(bits=bits, xe=xe, xo=xo, xe_far=far_xe, xo_far=far_xo, near=fifth["mine"], far=far1),
        chunk_shapes(9),
        dict(acc=pltpu.VMEM((3 * cin, half), f32)),
        far_in=("xe", "xo", "xe_far", "xo_far"),
        far_out=("kept_a", "kept_b"),
        smem=("bits",),
        flops=2 * 9 * cin * half * 2 * MW,
        moved=6_000_000,
    ).values()
    gu, tree2.got, *first_parts = lax.optimization_barrier((fifth["gu"], tree2.got, *first_parts))
    tree2.exchange(0, slice(1, None))
    tree1 = Tree(first_parts, plane, rest)
    tree1.start()
    tree2.got = tree1.finish(tree2.got)
    tree1.start()
    tree1.finish()
    tree2.gathered()
    tree2.rest_from(1)
    grad_inputs = call(
        inputs_kernel,
        dict(gu=gu, gpu=fourth["gpu"], w1=w1, wp=w_proj),
        dict(out=shape((groups, rows_in, cols_in, cin), bf16)),
        dict(lines=pltpu.VMEM((cin // 128, rows_in * groups, cols_in, 128), f32)),
        far_in=("gu", "gpu", "w1", "wp"),
        far_out=("out",),
        flops=px(MW, 10 * cin),
        moved=5_000_000,
    )["out"]
    tree1.exchange(0)
    tree1.gathered()
    tree1.rest_from(1)
    tree1.value, grad_inputs = lax.optimization_barrier((tree1.value, grad_inputs))
    half2 = tree2.join()

    side = bit_of(*core).astype(jnp.int32)
    other2 = partner(half2, *core)
    grad_w2 = widen(other2, 1 - side, taps2 - 1, widen(half2, side, taps2 - 1))
    ends = half2[taps2 - 1], other2[taps2 - 1]
    grad_wp = jnp.concatenate(
        [jnp.where(side == 1, ends[1], ends[0]), jnp.where(side == 1, ends[0], ends[1])], axis=1
    ).astype(f32)
    half1, grad_w2, grad_wp = lax.optimization_barrier((tree1.join(), grad_w2, grad_wp))
    other1 = partner(half1, *core)
    grad_w1 = widen(other1, 1 - side, 9, widen(half1, side, 9))

    s3, s4 = fourth["sums"].reshape(3, width), fifth["sums"].reshape(2, width)
    return (
        third["out"],
        grad_inputs,
        grad_w1.reshape(w_first.shape),
        s4[0],
        s4[1],
        grad_w2.reshape(w_second.shape),
        s3[0],
        s3[1],
        grad_wp,
        s3[2],
        s3[1],
    )


def solution(mesh):
    spread = P("grp", "rows", "cols", None)
    return jax.shard_map(
        on_device,
        mesh=mesh,
        in_specs=(spread,) + (P(),) * 9 + (P("grp", "rows", "cols"), spread),
        out_specs=(spread, spread) + (P(),) * 9,
        check_vma=False,
    )
```

```python
import functools

import jax
import jax.numpy as jnp
from jax import lax
from jax.experimental import pallas as pl
from jax.experimental.pallas import tpu as pltpu
from jax.sharding import PartitionSpec as P

epsilon = 1e-05
axes = ("rows", "cols", "grp")
bf16 = jnp.bfloat16
f32 = jnp.float32
inner = 0.7978845608028654
cubic = 0.044715
over = 6
rim = 3


class Refs:
    def __init__(self, named):
        self.__dict__.update(named)


class Copies:
    def __init__(self, names, sources, targets, sems):
        self.jobs = {n: pltpu.make_async_copy(s, t, sems.at[k]) for k, (n, s, t) in enumerate(zip(names, sources, targets))}

    def start(self, *names):
        for name in names:
            self.jobs[name].start()

    def wait(self, *names):
        for name in names:
            self.jobs[name].wait()


def call(body, ins, outs, scratch=None, far_in=(), far_out=(), smem=(), limit=52):
    scratch = scratch or {}
    far = (*far_in, *far_out)

    def spec(name):
        if name in smem:
            return pl.BlockSpec(memory_space=pltpu.SMEM)
        return pl.BlockSpec(memory_space=pltpu.HBM if name in far else pltpu.VMEM)

    kinds = {**{n: shape(v.shape, v.dtype) for n, v in ins.items()}, **outs}
    names = [*ins, *outs, *far, *scratch]

    def run(*refs):
        given = dict(zip(names, refs)) if not far else None
        if far:
            plain = dict(zip([*ins, *outs], refs))
            rest = refs[len(plain) :]
            buffers = dict(zip(far, rest))
            more = dict(zip(scratch, rest[len(far) : -1]))
            given = {**plain, **buffers, **more}
            sources = [plain[n] if n in far_in else buffers[n] for n in far]
            targets = [buffers[n] if n in far_in else plain[n] for n in far]
            copies = Copies(far, sources, targets, rest[-1])
            copies.start(*far_in)
        else:
            copies = None
        body(Refs(given), copies)

    buffers = [pltpu.VMEM(kinds[n].shape, kinds[n].dtype) for n in far]
    sems = [pltpu.SemaphoreType.DMA((len(far),))] if far else []
    result = pl.pallas_call(
        run,
        out_shape=list(outs.values()),
        in_specs=[spec(n) for n in ins],
        out_specs=[spec(n) for n in outs],
        scratch_shapes=[*buffers, *scratch.values(), *sems],
        compiler_params=pltpu.CompilerParams(vmem_limit_bytes=limit * 1024 * 1024),
        cost_estimate=pl.CostEstimate(flops=0, bytes_accessed=0, transcendentals=0),
    )(*ins.values())
    return dict(zip(outs, result))


def shape(dims, dtype=f32):
    return jax.ShapeDtypeStruct(dims, dtype)


def wide(mask, width):
    return jnp.concatenate([mask] * (width // mask.shape[1]), axis=1)


def matmul(a, b):
    return lax.dot_general(a, b, (((1,), (0,)), ((), ())), preferred_element_type=f32)


def matmul_nt(a, b):
    return lax.dot_general(a, b, (((1,), (1,)), ((), ())), preferred_element_type=f32)


def matmul_tn(a, b):
    return lax.dot_general(a, b, (((0,), (0,)), ((), ())), preferred_element_type=f32)


def gelu_parts(v):
    return jnp.tanh(inner * (v + cubic * v * v * v))


def gelu_slope(v, t):
    return 0.5 * (1.0 + t) + 0.5 * v * (1.0 - t * t) * (inner * (1.0 + 3.0 * cubic * v * v))


def column_sum(v):
    return jnp.sum(v, axis=0, keepdims=True)


def moments(total, squares, pixel_count):
    center = total / pixel_count
    spread = squares / pixel_count - center * center
    return center, lax.rsqrt(spread + epsilon)


def chunks(total, size):
    return [(at, min(size, total - at)) for at in range(0, total, size)]


def strided(ref, k, first, count, step):
    return ref[k, pl.ds(first, count, stride=step), :]


def vertical_kernel(r, copies):
    groups, width = r.x.shape[0], r.cot.shape[3]
    rows, cols = r.own.shape[1], r.own.shape[2]

    def pack(out, input_row, row, pick):
        at = 0
        for g in range(groups):
            for n in range(over):
                value = r.x[g, input_row(n)]
                out[at : at + 2 * cols, :] = pick(value, r.x[g, n])
                at += 2 * cols
        for k in range(0, width, 256):
            for g in range(groups):
                for n in range(rim):
                    lanes = slice(k, k + 256)
                    out[at : at + cols, :] = pick(r.cot[g, row(n), :, lanes], r.cot[g, n, :, lanes])
                    at += cols
        for g in range(groups):
            for n in range(rim):
                out[at : at + cols, :] = pick(wide(r.own[g, row(n)], 256), wide(r.own[g, n], 256))
                at += cols

    last = r.x.shape[1] - over
    if hasattr(r, "up"):
        pack(r.down, lambda n: last + n, lambda n: rows - rim + n, lambda tail, head: tail)
        pack(r.up, lambda n: last + n, lambda n: rows - rim + n, lambda tail, head: head)
    else:
        bottom = r.flags[0] == 1
        pack(r.down, lambda n: last + n, lambda n: rows - rim + n, lambda tail, head: jnp.where(bottom, head, tail))


def rim_rows(r, own, n_own, n_rim, base, cols, split):
    groups = own.shape[0]
    size = groups * n_rim * cols

    def flat(ref, g, n):
        at = [base + k * size + (g * n_rim + n) * cols for k in range(split)]
        return jnp.concatenate([ref[p : p + cols, :] for p in at], axis=1).astype(f32)

    def read(g, n):
        if n < n_rim:
            return jnp.where(r.flags[0] == 1, flat(r.top, g, n), 0.0)
        if n < n_rim + n_own:
            return own[g, n - n_rim].astype(f32)
        return jnp.where(r.flags[1] == 1, flat(r.bot, g, n - n_rim - n_own), 0.0)

    return read


def fields(r):
    groups, width = r.x.shape[0], r.cot.shape[3]
    rows, cols = r.own.shape[1], r.own.shape[2]
    base = over * groups * 2 * cols
    piece = rim * groups * cols
    blocks = width // 256
    x = rim_rows(r, r.x, 2 * rows, over, 0, 2 * cols, 1)
    mask = rim_rows(r, r.own, rows, rim, base + blocks * piece, cols, 1)
    cot = rim_rows(r, r.cot, rows, rim, base, cols, blocks)
    return x, lambda g, n: mask(g, n)[:, :128], cot


def strips_kernel(r, copies):
    groups, width = r.x.shape[0], r.cot.shape[3]
    rows, cols = r.own.shape[1], r.own.shape[2]
    x, mask, cot = fields(r)
    lines = (2 * rows + 2 * over) * groups, (rows + 2 * rim) * groups, (rows + 3) * groups
    for raw, read, first, count, w in (
        (r.raw_x, x, 0, lines[0], 2 * cols),
        (r.raw_m, mask, 0, lines[1], cols),
        (r.raw_c, cot, 2, lines[2], cols),
    ):
        for at in range(count):
            value = read(at % groups, at // groups + first)
            for k in range(raw.shape[0]):
                raw[k, at * w : (at + 1) * w, :] = value[:, k * 128 : (k + 1) * 128]
    for out, x0, m0, c0 in ((r.right, 2 * cols - over, cols - rim, cols - 2), (r.left, 0, 0, 0)):
        pieces = []
        for c in range(over):
            pieces.append([strided(r.raw_x, k, x0 + c, lines[0], 2 * cols) for k in range(2)])
        for c in range(0, rim + 1, 2):
            pieces.append([strided(r.raw_m, 0, m0 + min(c + k, rim - 1), lines[1], cols) for k in range(2)])
        for c in range(2):
            for h in range(0, width // 128, 2):
                pieces.append([strided(r.raw_c, h + k, c0 + c, lines[2], cols) for k in range(2)])
        at = 0
        for low, high in pieces:
            r.flat[at : at + low.shape[0], :] = jnp.concatenate([low, high], axis=1)
            at += low.shape[0]
        if at < r.flat.shape[0]:
            r.flat[at:, :] = jnp.zeros((r.flat.shape[0] - at, 256), f32)
        out[...] = r.flat[...].astype(bf16)


def stats_kernel(r, copies):
    groups, cin = r.x.shape[0], r.x.shape[3]
    rows, S = r.own.shape[1], r.own.shape[2]
    L = groups * S
    width = r.w1.shape[2]
    raw = r.raw
    for n in range(2 * rows + 1):
        for g in range(groups):
            line = n * groups + g
            src = (r.top[g, 0] if n == 0 else r.x[g, n - 1]).astype(f32)
            side = r.lft[g, n].astype(f32)
            for k in range(raw.shape[0]):
                raw[k, line, 7:8, :] = side[:, k * 128 : (k + 1) * 128]
                raw[k, line, 8:, :] = src[:, k * 128 : (k + 1) * 128]
    for out, n_rows, start in ((r.xe, rows, 1), (r.xo, rows + 1, 0)):
        for n in range(n_rows):
            for b in range(3):
                for k in range(raw.shape[0]):
                    parts = [
                        raw[k, (2 * n + start) * groups + g, pl.ds(7 + b, S, stride=2), :]
                        for g in range(groups)
                    ]
                    at = b * cin + k * 128
                    out[n * L : (n + 1) * L, at : at + 128] = jnp.concatenate(
                        parts, axis=0
                    ).astype(bf16)
    mask = jnp.concatenate(
        [r.own[g, i].astype(f32) for i in range(rows) for g in range(groups)], axis=0
    )
    M = rows * L
    z = matmul(r.xo[0:M, :], r.w1[0])
    z += matmul(r.xe[...], r.w1[1])
    z += matmul(r.xo[L : L + M, :], r.w1[2])
    zp = matmul(r.xe[:, cin : 2 * cin], r.wp[...])
    zm, zpm = z * wide(mask, width), zp * wide(mask, width)
    row = jnp.concatenate(
        [column_sum(zm), column_sum(zm * z), column_sum(zpm), column_sum(zpm * zp), column_sum(mask)], axis=1
    )
    r.spread[...] = jnp.broadcast_to(row[None], r.spread.shape)


def first_kernel(r, copies):
    groups, cin, width = r.x.shape[0], r.x.shape[3], r.cot.shape[3]
    rows, cols = r.own.shape[1], r.own.shape[2]
    S = cols + 8
    L = groups * S
    W = 2 * cols + 24
    V = cols + 16
    x, mask, cot = fields(r)
    lines = (2 * rows + 2 * over) * groups, (rows + 2 * rim) * groups, (rows + 3) * groups
    tail = jnp.zeros((W - 8 - 2 * cols, 128), f32)
    r.raw_m[...] = jnp.zeros(r.raw_m.shape, f32)
    r.raw_c[...] = jnp.zeros(r.raw_c.shape, f32)
    for at in range(lines[0]):
        value = x(at % groups, at // groups)
        for k in range(r.raw_x.shape[0]):
            r.raw_x[k, at * W + 8 : at * W + 8 + 2 * cols, :] = value[:, k * 128 : (k + 1) * 128]
            r.raw_x[k, at * W + 8 + 2 * cols : (at + 1) * W, :] = tail
    for strip, x0, m0, c0 in ((r.lft, 8 - over, 8 - rim, 6), (r.rgt, 8 + 2 * cols, 8 + cols, 8 + cols)):
        r.flat[...] = strip[...].astype(f32)
        at = 0
        for c in range(over):
            for k in range(2):
                r.raw_x[k, pl.ds(x0 + c, lines[0], stride=W), :] = r.flat[at : at + lines[0], k * 128 : (k + 1) * 128]
            at += lines[0]
        for c in range(0, rim + 1, 2):
            for k in range(2):
                if c + k < rim:
                    r.raw_m[0, pl.ds(m0 + c + k, lines[1], stride=V), :] = r.flat[
                        at : at + lines[1], k * 128 : (k + 1) * 128
                    ]
            at += lines[1]
        for c in range(2):
            for h in range(0, width // 128, 2):
                for k in range(2):
                    r.raw_c[h + k, pl.ds(c0 + c, lines[2], stride=V), :] = r.flat[
                        at : at + lines[2], k * 128 : (k + 1) * 128
                    ]
                at += lines[2]
    for out, n_rows, start in ((r.xe, rows + 5, 2), (r.xo, rows + 6, 1)):
        for n in range(n_rows):
            for b in range(3):
                for k in range(r.raw_x.shape[0]):
                    parts = [
                        strided(r.raw_x, k, ((2 * n + start) * groups + g) * W + 3 + b, S, 2) for g in range(groups)
                    ]
                    at = b * cin + k * 128
                    out[n * L : (n + 1) * L, at : at + 128] = jnp.concatenate(parts, axis=0).astype(bf16)
    copies.start("xe", "xo")
    for at in range(lines[1]):
        r.raw_m[0, at * V + 8 : at * V + 8 + cols, :] = mask(at % groups, at // groups)
    for n in range(1, rows + 6):
        for g in range(groups):
            to, at = (n - 1) * L + g * S, (n * groups + g) * V
            r.maskp[to : to + S, :] = r.raw_m[0, at + 6 : at + 6 + S, :]
    for at in range(lines[2]):
        value = cot(at % groups, at // groups + 2)
        for k in range(r.raw_c.shape[0]):
            lanes = slice(k * 128, (k + 1) * 128)
            r.raw_c[k, at * V + 8 : at * V + 8 + cols, :] = value[:, lanes]
            r.cotq[at * S : (at + 1) * S, lanes] = r.raw_c[k, at * V + 7 : at * V + 7 + S, :]
    copies.start("cotq")
    r.ownp[...] = jnp.zeros(r.ownp.shape, f32)
    for i in range(rows):
        for g in range(groups):
            at = (i + 2) * L + g * S + 2
            r.ownp[at : at + cols, :] = r.own[g, i].astype(f32)
    copies.wait("w1", "wp")
    for m0, m in chunks(r.pre1.shape[0], 208):
        z = matmul(r.xo[m0 : m0 + m, :], r.w1[0])
        z += matmul(r.xe[m0 : m0 + m, :], r.w1[1])
        z += matmul(r.xo[L + m0 : L + m0 + m, :], r.w1[2])
        r.pre1[m0 : m0 + m, :] = z
        r.prep[m0 : m0 + m, :] = matmul(r.xe[m0 : m0 + m, cin : 2 * cin], r.wp[...])
        r.keep[m0 : m0 + m, :] = z
    copies.start("keep")
    copies.wait("xe", "xo", "keep", "cotq")


def second_kernel(r, copies):
    width = r.gain.shape[1]
    t = jnp.sum(r.tot1[...], axis=0)
    n = wide(t[:, 4 * width :], width)
    center, inv = moments(t[:, :width], t[:, width : 2 * width], n)
    proj = moments(t[:, 2 * width : 3 * width], t[:, 3 * width : 4 * width], n)
    r.mom1[...] = jnp.concatenate([center, inv, n, *proj, jnp.zeros((3, width), f32)], axis=0)
    scale = inv * r.gain[...]
    M, Q = r.pre1.shape[0], r.pre2.shape[0]
    L = (M - Q) // 2
    for m0, m in chunks(M, 104):
        v = (r.pre1[m0 : m0 + m, :] - center) * scale + r.shift[...]
        mask = wide(r.maskp[m0 : m0 + m, :], width)
        r.hid[m0 : m0 + m, :] = 0.5 * v * (1.0 + gelu_parts(v)) * mask
    r.hid[M:, :] = jnp.zeros((r.hid.shape[0] - M, width), f32)
    for m0, m in chunks(M, 208):
        for b in range(3):
            r.h3[m0 : m0 + m, b * width : (b + 1) * width] = r.hid[m0 + b : m0 + b + m, :].astype(bf16)
    copies.start("h3")
    copies.wait("w2")
    sums = [jnp.zeros((1, width), f32)] * 2
    for m0, m in chunks(Q, 176):
        z = matmul(r.h3[m0 : m0 + m, :], r.w2[0])
        z += matmul(r.h3[L + m0 : L + m0 + m, :], r.w2[1])
        z += matmul(r.h3[2 * L + m0 : 2 * L + m0 + m, :], r.w2[2])
        r.pre2[m0 : m0 + m, :] = z
        zm = z * wide(r.ownp[L + 1 + m0 : L + 1 + m0 + m, :], width)
        sums = [sums[0] + column_sum(zm), sums[1] + column_sum(zm * z)]
    row = jnp.concatenate(sums, axis=1)
    r.spread[...] = jnp.broadcast_to(row[None], r.spread.shape)
    copies.wait("h3")


def third_kernel(r, copies):
    groups, rows, cols, width = r.out.shape
    S = cols + 8
    L = groups * S
    n = r.mom1[2:3, :]
    t = jnp.sum(r.tot2[...], axis=0)
    c2, i2 = moments(t[:, :width], t[:, width:], n)
    cp, ip = r.mom1[3:4, :], r.mom1[4:5, :]
    r.mom2[...] = jnp.concatenate([c2, i2, cp, ip, jnp.zeros((4, width), f32)], axis=0)
    sums = [jnp.zeros((1, width), f32)] * 3
    both_shift = r.shift2[...] + r.shiftp[...]
    copies.wait("cotq")
    for line in range(r.grad.shape[0] // S):
        at = line * S
        shifted = slice(L + 1 + at, L + 1 + at + S)
        n2 = (r.pre2[at : at + S, :] - c2) * i2
        np_ = (r.prep[shifted, :] - cp) * ip
        v = n2 * r.gain2[...] + np_ * r.gainp[...] + both_shift
        mask = wide(r.maskp[shifted, :], width)
        own = wide(r.ownp[shifted, :], width)
        t = gelu_parts(v)
        r.field[at : at + S, :] = 0.5 * v * (1.0 + t) * mask
        g = gelu_slope(v, t) * mask * r.cotq[at : at + S, :]
        r.grad[at : at + S, :] = g
        g = g * own
        new = [column_sum(g * n2), column_sum(g), column_sum(g * np_)]
        sums = [a + b for a, b in zip(sums, new)]
    copies.start("grad")
    for i in range(rows):
        for g in range(groups):
            at = (i + 1) * L + g * S + 1
            r.out[g, i, :, :] = r.field[at : at + cols, :].astype(bf16)
    copies.start("out")
    row = jnp.concatenate(sums, axis=1)
    r.spread[...] = jnp.broadcast_to(row[None], r.spread.shape)
    copies.wait("grad", "out")


def halves(r, source, at, frame, to, rows_w):
    half = r.mine.shape[1]
    bit = r.bits[0] == 1
    for m0, m in chunks(rows_w, 96):
        own = wide(r.ownp[frame + m0 : frame + m0 + m, :], half)
        low = (source[at + m0 : at + m0 + m, :half] * own).astype(bf16)
        high = (source[at + m0 : at + m0 + m, half:] * own).astype(bf16)
        r.mine[to + m0 : to + m0 + m, :] = jnp.where(bit, high, low)
        r.theirs[to + m0 : to + m0 + m, :] = jnp.where(bit, low, high)


def fourth_kernel(r, copies):
    width = r.gain2.shape[1]
    Q = r.pre2.shape[0]
    rows_w = r.gpu.shape[0]
    L = (Q - rows_w) // 3
    n = r.mom1[2:3, :]
    c2, i2, cp, ip = (r.mom2[k : k + 1, :] for k in range(4))
    t3 = jnp.sum(r.tot3[...], axis=0)
    r.sums[...] = t3
    gg2, gs, ggp = (t3[:, k * width : (k + 1) * width] for k in range(3))
    copies.wait("grad")
    for m0, m in chunks(Q, L):
        shifted = slice(L + 1 + m0, L + 1 + m0 + m)
        mask = wide(r.maskp[shifted, :], width) / n
        n2 = (r.pre2[m0 : m0 + m, :] - c2) * i2
        np_ = (r.prep[shifted, :] - cp) * ip
        g = r.grad[m0 : m0 + m, :]
        r.gq[m0 : m0 + m, :] = (r.gain2[...] * i2) * (g - mask * (gs + n2 * gg2))
        r.gpq[m0 : m0 + m, :] = (r.gainp[...] * ip) * (g - mask * (gs + np_ * ggp))
    r.gq[Q:, :] = jnp.zeros((r.gq.shape[0] - Q, width), f32)
    for m0, m in chunks(rows_w, 96):
        r.gpu[m0 : m0 + m, :] = r.gpq[L + 1 + m0 : L + 1 + m0 + m, :].astype(bf16)
    copies.start("gpu")
    halves(r, r.gq, L, 2 * L + 1, 0, rows_w)
    halves(r, r.gpq, L - 1, 2 * L, rows_w, rows_w)
    copies.wait("gpu")


def hidden_kernel(r, copies):
    width = r.gain.shape[1]
    Q = r.gq.shape[0] - 8
    L = (r.keep.shape[0] - Q) // 2
    center, inv = r.mom1[0:1, :], r.mom1[1:2, :]
    for m0, m in chunks(Q, 176):
        for b in range(3):
            r.g3[m0 : m0 + m, b * width : (b + 1) * width] = r.gq[m0 + b : m0 + b + m, :].astype(bf16)
    copies.wait("w2")
    U = r.act.shape[0]
    for m0, m in chunks(U, 144):
        gh = jnp.zeros((m, width), f32)
        for a in range(3):
            for b in range(3):
                gh += matmul_nt(
                    r.g3[L * a + m0 : L * a + m0 + m, b * width : (b + 1) * width],
                    r.w2[2 - a, (2 - b) * width : (3 - b) * width, :],
                )
        r.act[m0 : m0 + m, :] = gh
    copies.wait("keep")
    sums = [jnp.zeros((1, width), f32)] * 2
    for m0, m in chunks(U, L):
        frame = slice(2 * L + 2 + m0, 2 * L + 2 + m0 + m)
        n1 = (r.keep[frame, :] - center) * inv
        v = n1 * r.gain[...] + r.shift[...]
        mask = wide(r.maskp[frame, :], width)
        g = gelu_slope(v, gelu_parts(v)) * mask * r.act[m0 : m0 + m, :]
        r.act[m0 : m0 + m, :] = g
        r.normed[m0 : m0 + m, :] = n1 * mask
        g = g * wide(r.ownp[frame, :], width)
        sums = [sums[0] + column_sum(g * n1), sums[1] + column_sum(g)]
    row = jnp.concatenate(sums, axis=1)
    r.spread[...] = jnp.broadcast_to(row[None], r.spread.shape)


def split_store(bits, acc, rows, unit, sent_a, kept_a, sent_b, kept_b):
    quarter = unit // 4
    for k in range(rows // unit):
        for bit, base, sent, kept in ((1, 0, sent_a, kept_a), (2, 2 * quarter, sent_b, kept_b)):
            keep = pl.multiple_of(k * unit + base + bits[bit] * quarter, quarter)
            send = pl.multiple_of(k * unit + base + (1 - bits[bit]) * quarter, quarter)
            yield k, acc[pl.ds(send, quarter), :].astype(bf16), acc[pl.ds(keep, quarter), :], sent, kept


def weights_second_kernel(r, copies):
    width = r.h3.shape[1] // 3
    cin = r.xe.shape[1] // 3
    rows_w = r.near.shape[0] // 2
    L = (r.h3.shape[0] - rows_w) // 5
    per = 3 * width // cin
    places = r.sent_a, r.kept_a, r.sent_b, r.kept_b
    copies.wait("h3", "h3_far")
    for a in range(3):
        at = L * a + L
        for b in range(3):
            lanes = slice(b * width, (b + 1) * width)
            r.acc[lanes, :] = matmul_tn(r.h3[at : at + rows_w, lanes], r.near[:rows_w, :]) + matmul_tn(
                r.h3_far[at : at + rows_w, lanes], r.far[:rows_w, :]
            )
        for k, s, v, sent, kept in split_store(r.bits, r.acc, 3 * width, cin, *places):
            sent[a * per + k] = s
            kept[a * per + k] = v
    at = 2 * L
    copies.wait("xe", "xe_far")
    r.acc[0:cin, :] = matmul_tn(r.xe[at : at + rows_w, cin : 2 * cin], r.near[rows_w:, :]) + matmul_tn(
        r.xe_far[at : at + rows_w, cin : 2 * cin], r.far[rows_w:, :]
    )
    for k, s, v, sent, kept in split_store(r.bits, r.acc, cin, cin, *places):
        sent[3 * per] = s
        kept[3 * per] = v
    copies.start("kept_a", "kept_b")
    copies.wait("kept_a", "kept_b")


def fifth_kernel(r, copies):
    width = r.gain.shape[1]
    U = r.act.shape[0]
    rows_w = r.mine.shape[0]
    L = U - rows_w
    inv, n = r.mom1[1:2, :], r.mom1[2:3, :]
    t4 = jnp.sum(r.tot4[...], axis=0)
    r.sums[...] = t4
    gg, gs = t4[:, :width] / n, t4[:, width:] / n
    scale = r.gain[...] * inv
    r.gf[0:8, :] = jnp.zeros((8, width), f32)
    r.gf[8 + U :, :] = jnp.zeros((r.gf.shape[0] - 8 - U, width), f32)
    for m0, m in chunks(U, L):
        mask = wide(r.maskp[2 * L + 2 + m0 : 2 * L + 2 + m0 + m, :], width)
        back = mask * gs + r.normed[m0 : m0 + m, :] * gg
        r.gf[8 + m0 : 8 + m0 + m, :] = scale * (r.act[m0 : m0 + m, :] - back)
    halves(r, r.gf, 6, 2 * L, 0, rows_w)
    for m0, m in chunks(U, 144):
        r.gu[m0 : m0 + m, :width] = r.gf[8 + m0 : 8 + m0 + m, :].astype(bf16)
        r.gu[m0 : m0 + m, width:] = r.gf[9 + m0 : 9 + m0 + m, :].astype(bf16)
    copies.start("gu")
    copies.wait("gu")


def weights_first_kernel(r, copies):
    rows_w = r.near.shape[0]
    cin = r.xe.shape[1] // 3
    L = (r.xe.shape[0] - rows_w) // 5
    places = r.sent_a, r.kept_a, r.sent_b, r.kept_b
    copies.wait("xe", "xo", "xe_far", "xo_far")
    for a in range(3):
        source, source_far = (r.xe, r.xe_far) if a == 1 else (r.xo, r.xo_far)
        at = (3 if a == 2 else 2) * L
        r.acc[...] = matmul_tn(source[at : at + rows_w, :], r.near[...]) + matmul_tn(
            source_far[at : at + rows_w, :], r.far[...]
        )
        for k, s, v, sent, kept in split_store(r.bits, r.acc, 3 * cin, cin, *places):
            sent[a * 3 + k] = s
            kept[a * 3 + k] = v
    copies.start("kept_a", "kept_b")
    copies.wait("kept_a", "kept_b")


def inputs_kernel(r, copies):
    width = r.gpu.shape[1]
    groups, rows, cols = r.out.shape[0], r.out.shape[1] // 2, r.out.shape[2] // 2
    cin = r.out.shape[3]
    M = r.gpu.shape[0]
    S = cols + 8
    L = groups * S
    lines = r.lines
    copies.wait("gu", "gpu", "w1", "wp")

    def tap(m0, m, a, b):
        di, dj = (1 if a == 0 else 0), (1 if b == 0 else 0)
        return matmul_nt(
            r.gu[di * L + m0 : di * L + m0 + m, dj * width : (dj + 1) * width],
            r.w1[a, b * cin : (b + 1) * cin, :],
        )

    for m0, m in chunks(M, 2 * L):
        pieces = {
            (0, 0): tap(m0, m, 1, 1) + matmul_nt(r.gpu[m0 : m0 + m, :], r.wp[...]),
            (0, 1): tap(m0, m, 1, 2) + tap(m0, m, 1, 0),
            (1, 0): tap(m0, m, 2, 1) + tap(m0, m, 0, 1),
            (1, 1): tap(m0, m, 2, 2) + tap(m0, m, 2, 0) + tap(m0, m, 0, 2) + tap(m0, m, 0, 0),
        }
        for (ro, co), v in pieces.items():
            for k in range(m // S):
                line = m0 // S + k
                i, g = line // groups, line % groups
                for h in range(lines.shape[0]):
                    lines[h, (2 * i + ro) * groups + g, pl.ds(co, cols, stride=2), :] = v[
                        k * S : k * S + cols, h * 128 : (h + 1) * 128
                    ]
    for n in range(2 * rows):
        for g in range(groups):
            for h in range(lines.shape[0]):
                r.out[g, n, :, h * 128 : (h + 1) * 128] = lines[h, n * groups + g].astype(bf16)
    copies.start("out")
    copies.wait("out")


def widen_kernel(bits, half, *refs):
    refs[-1][...] = half[...].astype(f32)


def widen(half, side, taps, into=None):
    n, m = half.shape[1], half.shape[2]
    step = 3 if taps % 3 == 0 else 1
    block = pl.BlockSpec((step, n, m), lambda t, side: (t, 0, 0))
    placed = pl.BlockSpec((step, n, m), lambda t, side: (t, 0, side[0]))
    more = [] if into is None else [into]
    return pl.pallas_call(
        widen_kernel,
        out_shape=shape((taps, n, 2 * m)),
        grid_spec=pltpu.PrefetchScalarGridSpec(
            num_scalar_prefetch=1,
            grid=(taps // step,),
            in_specs=[block] + [pl.BlockSpec(memory_space=pl.ANY)] * len(more),
            out_specs=placed,
        ),
        input_output_aliases={2: 0} if more else {},
        compiler_params=pltpu.CompilerParams(vmem_limit_bytes=20 * 1024 * 1024),
        cost_estimate=pl.CostEstimate(flops=0, bytes_accessed=0, transcendentals=0),
    )(side.reshape(1), half, *more)


def shifted(value, axis, steps):
    count = lax.axis_size(axis)
    first, last = (max(0, -steps), min(count, count - steps))
    return lax.ppermute(value, axis, [(source, source + steps) for source in range(first, last)])


def gather_sum(spread):
    return lax.all_to_all(spread, axes, 0, 0)


def bit_of(axis, step):
    return (lax.axis_index(axis) // step) % 2


def partner(value, axis, step):
    count = lax.axis_size(axis)
    return lax.ppermute(value, axis, [(i, i ^ step) for i in range(count)])


def steps_of(axis):
    count, step, out = lax.axis_size(axis), 1, []
    while step < count:
        out.append((axis, step))
        step *= 2
    return out


def split(total, axis, step):
    n = total.shape[1] // 2
    bit = bit_of(axis, step) == 1
    low, high = total[:, :n], total[:, n:]
    return jnp.where(bit, low, high).astype(bf16), jnp.where(bit, high, low)


def joined(value, other, axis, step, dim=1):
    bit = bit_of(axis, step) == 1
    return jnp.concatenate([jnp.where(bit, other, value), jnp.where(bit, value, other)], axis=dim)


class Tree:
    def __init__(self, parts, plane, rest, core):
        self.sent_a, self.kept_a, self.sent_b, self.kept_b = parts
        self.a, self.b, self.rest, self.core = plane, plane[::-1], rest, core
        p, n = len(plane), len(rest)
        self.stages = [("plane", k) for k in range(p)] + [("rest", k) for k in range(n)]
        self.stages += [("rest_join", k) for k in reversed(range(n))] + [("plane_join", k) for k in reversed(range(p))]
        self.stages += [("core", 0)]

    def next(self):
        return self.stages[0] if self.stages else None

    def start(self):
        kind, k = self.stages[0]
        if kind == "plane":
            self.got = partner(self.sent_a, *self.a[k]), partner(self.sent_b, *self.b[k])
        elif kind == "rest":
            self.got = (partner(self.sent, *self.rest[k]),)
        elif kind == "rest_join":
            self.got = (partner(self.value, *self.rest[k]),)
        elif kind == "plane_join":
            self.got = partner(self.value_a, *self.a[k]), partner(self.value_b, *self.b[k])
        else:
            self.got = (partner(self.value, *self.core),)

    def finish(self, before=None):
        kind, k = self.stages.pop(0)
        if kind == "plane":
            total_a = self.kept_a + self.got[0].astype(f32)
            total_b = self.kept_b + self.got[1].astype(f32)
            if k + 1 < len(self.a):
                self.sent_a, self.kept_a = split(total_a, *self.a[k + 1])
                self.sent_b, self.kept_b = split(total_b, *self.b[k + 1])
                keep = self.sent_a, self.kept_a, self.sent_b, self.kept_b
                if before is not None:
                    before, keep = lax.optimization_barrier((before, keep))
                self.sent_a, self.kept_a, self.sent_b, self.kept_b = keep
            else:
                self.taps = total_a.shape[0]
                self.split_rest(jnp.concatenate([total_a, total_b], axis=0), 0)
        elif kind == "rest":
            self.split_rest(self.kept + self.got[0].astype(f32), k + 1)
        elif kind == "rest_join":
            self.value = joined(self.value, self.got[0], *self.rest[k])
            self.value_a, self.value_b = self.value[: self.taps], self.value[self.taps :]
        elif kind == "plane_join":
            self.value_a = joined(self.value_a, self.got[0], *self.a[k])
            self.value_b = joined(self.value_b, self.got[1], *self.b[k])
            self.value = jnp.concatenate([self.value_a, self.value_b], axis=1)
        return before

    def split_rest(self, total, k):
        if k < len(self.rest):
            self.sent, self.kept = split(total, *self.rest[k])
        else:
            self.value = total.astype(bf16)


def lockstep(*trees):
    for t in trees:
        t.start()
    got = lax.optimization_barrier([t.got for t in trees])
    for t, g in zip(trees, got):
        t.got = g
        t.finish()


def on_device(inputs, w_first, gain_first, shift_first, w_second, gain_second, shift_second, w_proj, gain_proj, shift_proj, valid_mask, cotangent):
    groups, rows_in, cols_in, cin = inputs.shape
    rows, cols = rows_in // 2, cols_in // 2
    width = w_first.shape[3]
    half = width // 2
    S = cols + 8
    L = groups * S
    devices = lax.axis_size("rows") * lax.axis_size("cols") * lax.axis_size("grp")
    plane = steps_of("cols")
    core = steps_of("rows")[0]
    rest = steps_of("rows")[1:] + steps_of("grp")
    bits = jnp.stack([bit_of(*core), bit_of(*plane[0]), bit_of(*plane[-1])]).astype(jnp.int32)
    w1 = w_first.reshape(3, 3 * cin, width)
    w2 = w_second.reshape(3, 3 * width, width)
    as_row = lambda v: v.reshape(1, -1)
    own = jnp.broadcast_to(valid_mask.astype(bf16)[..., None], valid_mask.shape + (128,))
    MP, MQ, MU, MW = (rows + 5) * L, (rows + 3) * L, (rows + 1) * L, rows * L
    px = lambda m, k: 2 * m * k * width
    vec = lambda k: shape((1, k * width))
    all_devices = lambda k: shape((devices, 1, k))
    g1, b1, g2, b2, gp, bp = map(
        as_row, (gain_first, shift_first, gain_second, shift_second, gain_proj, shift_proj)
    )

    top1 = shifted(inputs[:, -1:], "rows", 1)
    lft1 = shifted(jnp.concatenate([top1[:, :, -1:], inputs[:, :, -1:]], axis=1), "cols", 1)
    stats = call(
        stats_kernel,
        dict(x=inputs, top=top1, lft=lft1, own=own, w1=w1, wp=w_proj),
        dict(spread=all_devices(4 * width + 128)),
        dict(
            raw=pltpu.VMEM((cin // 128, (rows_in + 1) * groups, cols_in + 8, 128), f32),
            xe=pltpu.VMEM((rows * groups * cols, 3 * cin), bf16),
            xo=pltpu.VMEM(((rows + 1) * groups * cols, 3 * cin), bf16),
        ),
    )
    tot1 = gather_sum(stats["spread"])

    me, count = lax.axis_index("rows"), lax.axis_size("rows")
    flags = jnp.stack([me > 0, me < count - 1]).astype(jnp.int32)
    flat_rows = shape((over * groups * cols_in + (width // 256 + 1) * rim * groups * cols, 256), bf16)
    packed = call(
        vertical_kernel,
        dict(flags=flags, x=inputs, cot=cotangent, own=own),
        dict(down=flat_rows) if count == 2 else dict(down=flat_rows, up=flat_rows),
        smem=("flags",),
    )
    if count == 2:
        top = bot = lax.ppermute(packed["down"], "rows", [(0, 1), (1, 0)])
    else:
        top, bot = shifted(packed["down"], "rows", 1), shifted(packed["up"], "rows", -1)
    lines = (rows_in + 2 * over) * groups, (rows + 2 * rim) * groups, (rows + 3) * groups
    n_strip = over * lines[0] + (rim + 1) // 2 * lines[1] + width // 128 * lines[2]
    n_strip = -(-n_strip // 16) * 16
    near = dict(flags=flags, x=inputs, cot=cotangent, own=own, top=top, bot=bot)
    strips = call(
        strips_kernel,
        near,
        dict(right=shape((n_strip, 256), bf16), left=shape((n_strip, 256), bf16)),
        dict(
            raw_x=pltpu.VMEM((cin // 128, lines[0] * cols_in, 128), f32),
            raw_m=pltpu.VMEM((1, lines[1] * cols, 128), f32),
            raw_c=pltpu.VMEM((width // 128, lines[2] * cols, 128), f32),
            flat=pltpu.VMEM((n_strip, 256), f32),
        ),
        smem=("flags",),
    )
    lft, rgt = shifted(strips["right"], "cols", 1), shifted(strips["left"], "cols", -1)
    first = call(
        first_kernel,
        dict(**near, lft=lft, rgt=rgt, w1=w1, wp=w_proj),
        dict(
            pre1=shape((MP, width)),
            prep=shape((MP, width)),
            xe=shape((MP, 3 * cin), bf16),
            xo=shape((MP + L, 3 * cin), bf16),
            keep=shape((MP, width)),
            ownp=shape((MP, 128)),
            maskp=shape((MP, 128)),
            cotq=shape((MQ, width)),
        ),
        dict(
            raw_x=pltpu.VMEM((cin // 128, lines[0] * (cols_in + 24), 128), f32),
            raw_m=pltpu.VMEM((1, lines[1] * (cols + 16), 128), f32),
            raw_c=pltpu.VMEM((width // 128, lines[2] * (cols + 16), 128), f32),
            flat=pltpu.VMEM((n_strip, 256), f32),
        ),
        far_in=("w1", "wp"),
        far_out=("xe", "xo", "keep", "cotq"),
        smem=("flags",),
    )
    xe, xo, ownp, maskp = first["xe"], first["xo"], first["ownp"], first["maskp"]
    far_xe, far_xo = partner(xe, *core), partner(xo, *core)

    second = call(
        second_kernel,
        dict(pre1=first["pre1"], tot1=tot1, gain=g1, shift=b1, maskp=maskp, ownp=ownp, w2=w2),
        dict(h3=shape((MP, 3 * width), bf16), pre2=shape((MQ, width)), spread=all_devices(2 * width), mom1=shape((8, width))),
        dict(hid=pltpu.VMEM((MP + 8, width), f32)),
        far_in=("w2",),
        far_out=("h3",),
    )
    h3, pre2, mom1 = second["h3"], second["pre2"], second["mom1"]
    tot2 = gather_sum(second["spread"])
    far_h3 = partner(h3, *core)

    third = call(
        third_kernel,
        dict(
            pre2=pre2, prep=first["prep"], mom1=mom1, tot2=tot2, gain2=g2, shift2=b2, gainp=gp, shiftp=bp,
            maskp=maskp, ownp=ownp, cotq=first["cotq"],
        ),
        dict(
            out=shape((groups, rows, cols, width), bf16),
            grad=shape((MQ, width)),
            spread=all_devices(3 * width),
            mom2=shape((8, width)),
        ),
        dict(field=pltpu.VMEM((MQ, width), f32)),
        far_in=("cotq",),
        far_out=("out", "grad"),
    )
    mom2 = third["mom2"]
    tot3 = gather_sum(third["spread"])

    fourth = call(
        fourth_kernel,
        dict(
            bits=bits, pre2=pre2, prep=first["prep"], mom1=mom1, mom2=mom2, tot3=tot3, gain2=g2, gainp=gp,
            grad=third["grad"], maskp=maskp, ownp=ownp,
        ),
        dict(
            mine=shape((2 * MW, half), bf16),
            theirs=shape((2 * MW, half), bf16),
            gq=shape((MQ + 8, width)),
            gpu=shape((MW, width), bf16),
            sums=vec(3),
        ),
        dict(gpq=pltpu.VMEM((MQ, width), f32)),
        far_in=("grad",),
        far_out=("gpu",),
        smem=("bits",),
    )
    far2 = partner(fourth["theirs"], *core)

    def chunk_shapes(taps):
        dims = (taps, cin // 4, half)
        return dict(sent_a=shape(dims, bf16), kept_a=shape(dims), sent_b=shape(dims, bf16), kept_b=shape(dims))

    taps2 = 9 * width // cin + 1
    second_parts = call(
        weights_second_kernel,
        dict(bits=bits, h3=h3, h3_far=far_h3, xe=xe, xe_far=far_xe, near=fourth["mine"], far=far2),
        chunk_shapes(taps2),
        dict(acc=pltpu.VMEM((3 * width, half), f32)),
        far_in=("h3", "h3_far", "xe", "xe_far"),
        far_out=("kept_a", "kept_b"),
        smem=("bits",),
    ).values()
    gq, *second_parts = lax.optimization_barrier((fourth["gq"], *second_parts))

    tree2 = Tree(second_parts, plane, rest, core)
    tree2.start()
    hidden = call(
        hidden_kernel,
        dict(w2=w2, keep=first["keep"], mom1=mom1, gain=g1, shift=b1, gq=gq, maskp=maskp, ownp=ownp),
        dict(act=shape((MU, width)), normed=shape((MU, width)), spread=all_devices(2 * width)),
        dict(g3=pltpu.VMEM((MQ, 3 * width), bf16)),
        far_in=("w2", "keep"),
    )
    spread4 = tree2.finish(hidden["spread"])
    tot4 = gather_sum(spread4)
    tree2.start()
    tot4, tree2.got = lax.optimization_barrier((tot4, tree2.got))
    act = tree2.finish(hidden["act"])

    tree2.start()
    fifth = call(
        fifth_kernel,
        dict(
            bits=bits, act=act, normed=hidden["normed"], mom1=mom1, tot4=tot4, gain=g1, maskp=maskp, ownp=ownp
        ),
        dict(
            mine=shape((MW, half), bf16), theirs=shape((MW, half), bf16), gu=shape((MU, 2 * width), bf16), sums=vec(2)
        ),
        dict(gf=pltpu.VMEM((MU + 16, width), f32)),
        far_out=("gu",),
        smem=("bits",),
    )
    far1 = partner(fifth["theirs"], *core)
    first_parts = call(
        weights_first_kernel,
        dict(bits=bits, xe=xe, xo=xo, xe_far=far_xe, xo_far=far_xo, near=fifth["mine"], far=far1),
        chunk_shapes(9),
        dict(acc=pltpu.VMEM((3 * cin, half), f32)),
        far_in=("xe", "xo", "xe_far", "xo_far"),
        far_out=("kept_a", "kept_b"),
        smem=("bits",),
    ).values()
    gu, tree2.got, *first_parts = lax.optimization_barrier((fifth["gu"], tree2.got, *first_parts))
    tree2.finish()
    tree1 = Tree(first_parts, plane, rest, core)

    grad_inputs = call(
        inputs_kernel,
        dict(gu=gu, gpu=fourth["gpu"], w1=w1, wp=w_proj),
        dict(out=shape((groups, rows_in, cols_in, cin), bf16)),
        dict(lines=pltpu.VMEM((cin // 128, rows_in * groups, cols_in, 128), f32)),
        far_in=("gu", "gpu", "w1", "wp"),
        far_out=("out",),
    )["out"]
    side = bit_of(*core).astype(jnp.int32)
    while tree2.next() != ("plane_join", 0):
        lockstep(tree2, tree1)
    tree2.start()
    while tree1.next()[0] != "rest_join" or tree1.next()[1] > 0:
        tree1.start()
        tree1.finish()
    tree1.start()
    tree1.got, tree2.got, grad_inputs = lax.optimization_barrier((tree1.got, tree2.got, grad_inputs))
    tree1.finish()
    tree2.finish()
    half2 = tree2.value
    lockstep(tree2, tree1)
    other2 = tree2.got[0]
    grad_w2 = widen(other2, 1 - side, taps2 - 1, widen(half2, side, taps2 - 1))
    ends = half2[taps2 - 1], other2[taps2 - 1]
    grad_wp = jnp.concatenate(
        [jnp.where(side == 1, ends[1], ends[0]), jnp.where(side == 1, ends[0], ends[1])], axis=1
    ).astype(f32)
    while tree1.next()[0] != "core":
        tree1.start()
        tree1.got, grad_w2, grad_wp = lax.optimization_barrier((tree1.got, grad_w2, grad_wp))
        tree1.finish()
    half1 = tree1.value
    tree1.start()
    grad_w1 = widen(tree1.got[0], 1 - side, 9, widen(half1, side, 9))

    s3, s4 = fourth["sums"].reshape(3, width), fifth["sums"].reshape(2, width)
    return (
        third["out"],
        grad_inputs,
        grad_w1.reshape(w_first.shape),
        s4[0],
        s4[1],
        grad_w2.reshape(w_second.shape),
        s3[0],
        s3[1],
        grad_wp,
        s3[2],
        s3[1],
    )


def solution(mesh):
    spread = P("grp", "rows", "cols", None)
    return jax.shard_map(
        on_device,
        mesh=mesh,
        in_specs=(spread,) + (P(),) * 9 + (P("grp", "rows", "cols"), spread),
        out_specs=(spread, spread) + (P(),) * 9,
        check_vma=False,
    )
```

```python
import functools

import jax
import jax.numpy as jnp
from jax import lax
from jax.experimental import pallas as pl
from jax.experimental.pallas import tpu as pltpu
from jax.sharding import PartitionSpec as P

epsilon = 1e-05
axes = ("rows", "cols", "grp")
bf16 = jnp.bfloat16
f32 = jnp.float32
inner = 0.7978845608028654
cubic = 0.044715
over = 6
rim = 3


class Refs:
    def __init__(self, named):
        self.__dict__.update(named)


class Copies:
    def __init__(self, parts, pairs, sems):
        self.jobs = {}
        for k, (name, index) in enumerate(parts):
            source, target = pairs[name]
            if index:
                source, target = source.at[index[1]], target.at[index[1]]
            self.jobs.setdefault(name, []).append(pltpu.make_async_copy(source, target, sems.at[k]))

    def start(self, *names):
        for name, *which in map(named, names):
            for job in self.jobs[name][slice(*which) if which else slice(None)]:
                job.start()

    def wait(self, *names):
        for name, *which in map(named, names):
            for job in self.jobs[name][slice(*which) if which else slice(None)]:
                job.wait()


def named(name):
    return (name,) if isinstance(name, str) else (name[0], name[1], name[1] + 1)


def row_parts(total, count):
    size = total // count
    return [(k, (pl.ds(k * size, size),)) for k in range(count)]


def end_parts(total, size):
    return [(k, (slice(None), pl.ds(at, size))) for k, at in enumerate((0, total - size))]


def lane_parts(total, count):
    size = total // count
    return [(k, (slice(None), pl.ds(k * size, size))) for k in range(count)]


def call(body, ins, outs, scratch=None, far_in=(), far_out=(), smem=(), parts=None, limit=52, cost=0):
    scratch, parts = scratch or {}, parts or {}
    far = (*far_in, *far_out)
    jobs = [(name, index) for name in far for index in parts.get(name, [None])]

    def spec(name):
        if name in smem:
            return pl.BlockSpec(memory_space=pltpu.SMEM)
        return pl.BlockSpec(memory_space=pltpu.HBM if name in far else pltpu.VMEM)

    kinds = {**{n: shape(v.shape, v.dtype) for n, v in ins.items()}, **outs}

    def run(*refs):
        plain = dict(zip([*ins, *outs], refs))
        rest = refs[len(plain) :]
        buffers = dict(zip(far, rest))
        more = dict(zip(scratch, rest[len(far) :]))
        copies = None
        if far:
            pairs = {n: (plain[n], buffers[n]) if n in far_in else (buffers[n], plain[n]) for n in far}
            copies = Copies(jobs, pairs, rest[-1])
            copies.start(*far_in)
        body(Refs({**plain, **buffers, **more}), copies)

    buffers = [pltpu.VMEM(kinds[n].shape, kinds[n].dtype) for n in far]
    sems = [pltpu.SemaphoreType.DMA((len(jobs),))] if far else []
    result = pl.pallas_call(
        run,
        out_shape=list(outs.values()),
        in_specs=[spec(n) for n in ins],
        out_specs=[spec(n) for n in outs],
        scratch_shapes=[*buffers, *scratch.values(), *sems],
        compiler_params=pltpu.CompilerParams(vmem_limit_bytes=limit * 1024 * 1024),
        cost_estimate=pl.CostEstimate(flops=cost, bytes_accessed=0, transcendentals=0),
    )(*ins.values())
    return dict(zip(outs, result))


def shape(dims, dtype=f32):
    return jax.ShapeDtypeStruct(dims, dtype)


def wide(mask, width):
    return jnp.concatenate([mask] * (width // mask.shape[1]), axis=1)


def matmul(a, b):
    return lax.dot_general(a, b, (((1,), (0,)), ((), ())), preferred_element_type=f32)


def matmul_nt(a, b):
    return lax.dot_general(a, b, (((1,), (1,)), ((), ())), preferred_element_type=f32)


def matmul_tn(a, b):
    return lax.dot_general(a, b, (((0,), (0,)), ((), ())), preferred_element_type=f32)


def gelu_parts(v):
    return jnp.tanh(inner * (v + cubic * v * v * v))


def gelu_slope(v, t):
    return 0.5 * (1.0 + t) + 0.5 * v * (1.0 - t * t) * (inner * (1.0 + 3.0 * cubic * v * v))


def column_sum(v):
    return jnp.sum(v, axis=0, keepdims=True)


def moments(total, squares, pixel_count):
    center = total / pixel_count
    spread = squares / pixel_count - center * center
    return center, lax.rsqrt(spread + epsilon)


def chunks(total, size):
    return [(at, min(size, total - at)) for at in range(0, total, size)]


def strided(ref, k, first, count, step):
    return ref[k, pl.ds(first, count, stride=step), :]


def vertical_kernel(r, copies):
    groups, width = r.x.shape[0], r.cot.shape[3]
    rows, cols = r.own.shape[1], r.own.shape[2]

    def pack(out, input_row, row, pick):
        at = 0
        for g in range(groups):
            for n in range(over):
                value = r.x[g, input_row(n)]
                out[at : at + 2 * cols, :] = pick(value, r.x[g, n])
                at += 2 * cols
        for k in range(0, width, 256):
            for g in range(groups):
                for n in range(rim):
                    lanes = slice(k, k + 256)
                    out[at : at + cols, :] = pick(r.cot[g, row(n), :, lanes], r.cot[g, n, :, lanes])
                    at += cols
        for g in range(groups):
            for n in range(rim):
                out[at : at + cols, :] = pick(wide(r.own[g, row(n)], 256), wide(r.own[g, n], 256))
                at += cols

    last = r.x.shape[1] - over
    copies.wait("x", "cot")
    if hasattr(r, "up"):
        pack(r.down, lambda n: last + n, lambda n: rows - rim + n, lambda tail, head: tail)
        pack(r.up, lambda n: last + n, lambda n: rows - rim + n, lambda tail, head: head)
    else:
        bottom = r.flags[0] == 1
        pack(r.down, lambda n: last + n, lambda n: rows - rim + n, lambda tail, head: jnp.where(bottom, head, tail))


def rim_rows(r, own, n_own, n_rim, base, cols, split):
    groups = own.shape[0]
    size = groups * n_rim * cols

    def flat(ref, g, n):
        at = [base + k * size + (g * n_rim + n) * cols for k in range(split)]
        return jnp.concatenate([ref[p : p + cols, :] for p in at], axis=1).astype(f32)

    def read(g, n):
        if n < n_rim:
            return jnp.where(r.flags[0] == 1, flat(r.top, g, n), 0.0)
        if n < n_rim + n_own:
            return own[g, n - n_rim].astype(f32)
        return jnp.where(r.flags[1] == 1, flat(r.bot, g, n - n_rim - n_own), 0.0)

    return read


def fields(r):
    groups, width = r.x.shape[0], r.cot.shape[3]
    rows, cols = r.own.shape[1], r.own.shape[2]
    base = over * groups * 2 * cols
    piece = rim * groups * cols
    blocks = width // 256
    x = rim_rows(r, r.x, 2 * rows, over, 0, 2 * cols, 1)
    mask = rim_rows(r, r.own, rows, rim, base + blocks * piece, cols, 1)
    cot = rim_rows(r, r.cot, rows, rim, base, cols, blocks)
    return x, lambda g, n: mask(g, n)[:, :128], cot


def strips_kernel(r, copies):
    groups, width = r.x.shape[0], r.cot.shape[3]
    rows, cols = r.own.shape[1], r.own.shape[2]
    x, mask, cot = fields(r)
    lines = (2 * rows + 2 * over) * groups, (rows + 2 * rim) * groups, (rows + 3) * groups
    for raw, read, first, count, w in (
        (r.raw_x, x, 0, lines[0], 2 * cols),
        (r.raw_m, mask, 0, lines[1], cols),
        (r.raw_c, cot, 2, lines[2], cols),
    ):
        for at in range(count):
            value = read(at % groups, at // groups + first)
            for k in range(raw.shape[0]):
                raw[k, at * w : (at + 1) * w, :] = value[:, k * 128 : (k + 1) * 128]
    for out, x0, m0, c0 in ((r.right, 2 * cols - over, cols - rim, cols - 2), (r.left, 0, 0, 0)):
        pieces = []
        for c in range(over):
            pieces.append([strided(r.raw_x, k, x0 + c, lines[0], 2 * cols) for k in range(2)])
        for c in range(0, rim + 1, 2):
            pieces.append([strided(r.raw_m, 0, m0 + min(c + k, rim - 1), lines[1], cols) for k in range(2)])
        for c in range(2):
            for h in range(0, width // 128, 2):
                pieces.append([strided(r.raw_c, h + k, c0 + c, lines[2], cols) for k in range(2)])
        at = 0
        for low, high in pieces:
            r.flat[at : at + low.shape[0], :] = jnp.concatenate([low, high], axis=1)
            at += low.shape[0]
        if at < r.flat.shape[0]:
            r.flat[at:, :] = jnp.zeros((r.flat.shape[0] - at, 256), f32)
        out[...] = r.flat[...].astype(bf16)


def stats_kernel(r, copies):
    groups, cin = r.x.shape[0], r.x.shape[3]
    rows, S = r.own.shape[1], r.own.shape[2]
    L = groups * S
    width = r.w1.shape[2]
    raw = r.raw
    for n in range(2 * rows + 1):
        for g in range(groups):
            line = n * groups + g
            src = (r.top[g, 0] if n == 0 else r.x[g, n - 1]).astype(f32)
            side = r.lft[g, n].astype(f32)
            for k in range(raw.shape[0]):
                raw[k, line, 7:8, :] = side[:, k * 128 : (k + 1) * 128]
                raw[k, line, 8:, :] = src[:, k * 128 : (k + 1) * 128]
    for out, n_rows, start in ((r.xe, rows, 1), (r.xo, rows + 1, 0)):
        for n in range(n_rows):
            for b in range(3):
                for k in range(raw.shape[0]):
                    parts = [
                        raw[k, (2 * n + start) * groups + g, pl.ds(7 + b, S, stride=2), :]
                        for g in range(groups)
                    ]
                    at = b * cin + k * 128
                    out[n * L : (n + 1) * L, at : at + 128] = jnp.concatenate(
                        parts, axis=0
                    ).astype(bf16)
    mask = jnp.concatenate(
        [r.own[g, i].astype(f32) for i in range(rows) for g in range(groups)], axis=0
    )
    M = rows * L
    z = matmul(r.xo[0:M, :], r.w1[0])
    z += matmul(r.xe[...], r.w1[1])
    z += matmul(r.xo[L : L + M, :], r.w1[2])
    zp = matmul(r.xe[:, cin : 2 * cin], r.wp[...])
    zm, zpm = z * wide(mask, width), zp * wide(mask, width)
    row = jnp.concatenate(
        [column_sum(zm), column_sum(zm * z), column_sum(zpm), column_sum(zpm * zp), column_sum(mask)], axis=1
    )
    r.spread[...] = jnp.broadcast_to(row[None], r.spread.shape)


def first_kernel(r, copies):
    groups, cin, width = r.x.shape[0], r.x.shape[3], r.cot.shape[3]
    rows, cols = r.own.shape[1], r.own.shape[2]
    S = cols + 8
    L = groups * S
    W = 2 * cols + 24
    V = cols + 16
    x, mask, cot = fields(r)
    lines = (2 * rows + 2 * over) * groups, (rows + 2 * rim) * groups, (rows + 3) * groups
    tail = jnp.zeros((W - 8 - 2 * cols, 128), f32)
    r.raw_m[...] = jnp.zeros(r.raw_m.shape, f32)
    r.raw_c[...] = jnp.zeros(r.raw_c.shape, f32)
    for at in range(lines[0]):
        value = x(at % groups, at // groups)
        for k in range(r.raw_x.shape[0]):
            r.raw_x[k, at * W + 8 : at * W + 8 + 2 * cols, :] = value[:, k * 128 : (k + 1) * 128]
            r.raw_x[k, at * W + 8 + 2 * cols : (at + 1) * W, :] = tail
    for strip, x0, m0, c0 in ((r.lft, 8 - over, 8 - rim, 6), (r.rgt, 8 + 2 * cols, 8 + cols, 8 + cols)):
        r.flat[...] = strip[...].astype(f32)
        at = 0
        for c in range(over):
            for k in range(2):
                r.raw_x[k, pl.ds(x0 + c, lines[0], stride=W), :] = r.flat[at : at + lines[0], k * 128 : (k + 1) * 128]
            at += lines[0]
        for c in range(0, rim + 1, 2):
            for k in range(2):
                if c + k < rim:
                    r.raw_m[0, pl.ds(m0 + c + k, lines[1], stride=V), :] = r.flat[
                        at : at + lines[1], k * 128 : (k + 1) * 128
                    ]
            at += lines[1]
        for c in range(2):
            for h in range(0, width // 128, 2):
                for k in range(2):
                    r.raw_c[h + k, pl.ds(c0 + c, lines[2], stride=V), :] = r.flat[
                        at : at + lines[2], k * 128 : (k + 1) * 128
                    ]
                at += lines[2]
    for out, n_rows, start in ((r.xe, rows + 5, 2), (r.xo, rows + 6, 1)):
        for n in range(n_rows):
            for b in range(3):
                for k in range(r.raw_x.shape[0]):
                    parts = [
                        strided(r.raw_x, k, ((2 * n + start) * groups + g) * W + 3 + b, S, 2) for g in range(groups)
                    ]
                    at = b * cin + k * 128
                    out[n * L : (n + 1) * L, at : at + 128] = jnp.concatenate(parts, axis=0).astype(bf16)
    copies.start("xe", "xo")
    for at in range(lines[1]):
        r.raw_m[0, at * V + 8 : at * V + 8 + cols, :] = mask(at % groups, at // groups)
    for n in range(1, rows + 6):
        for g in range(groups):
            to, at = (n - 1) * L + g * S, (n * groups + g) * V
            r.maskp[to : to + S, :] = r.raw_m[0, at + 6 : at + 6 + S, :]
    for at in range(lines[2]):
        value = cot(at % groups, at // groups + 2)
        for k in range(r.raw_c.shape[0]):
            lanes = slice(k * 128, (k + 1) * 128)
            r.raw_c[k, at * V + 8 : at * V + 8 + cols, :] = value[:, lanes]
            r.cotq[at * S : (at + 1) * S, lanes] = r.raw_c[k, at * V + 7 : at * V + 7 + S, :]
    copies.start("cotq")
    r.ownp[...] = jnp.zeros(r.ownp.shape, f32)
    for i in range(rows):
        for g in range(groups):
            at = (i + 2) * L + g * S + 2
            r.ownp[at : at + cols, :] = r.own[g, i].astype(f32)
    copies.wait("w1", "wp")
    for k, (m0, m) in enumerate(chunks(r.pre1.shape[0], r.pre1.shape[0] // 3)):
        z = matmul(r.xo[m0 : m0 + m, :], r.w1[0])
        z += matmul(r.xe[m0 : m0 + m, :], r.w1[1])
        z += matmul(r.xo[L + m0 : L + m0 + m, :], r.w1[2])
        r.pre1[m0 : m0 + m, :] = z
        copies.start(("pre1", k))
        r.prep[m0 : m0 + m, :] = matmul(r.xe[m0 : m0 + m, cin : 2 * cin], r.wp[...])
        copies.start(("prep", k))
    copies.wait("xe", "xo", "pre1", "prep", "cotq")


def second_kernel(r, copies):
    width = r.gain.shape[1]
    t = jnp.sum(r.tot1[...], axis=0)
    n = wide(t[:, 4 * width :], width)
    center, inv = moments(t[:, :width], t[:, width : 2 * width], n)
    proj = moments(t[:, 2 * width : 3 * width], t[:, 3 * width : 4 * width], n)
    r.mom1[...] = jnp.concatenate([center, inv, n, *proj, jnp.zeros((3, width), f32)], axis=0)
    scale = inv * r.gain[...]
    M, Q = r.pre1.shape[0], r.pre2.shape[0]
    L = (M - Q) // 2
    copies.wait("pre1")
    for m0, m in chunks(M, 104):
        v = (r.pre1[m0 : m0 + m, :] - center) * scale + r.shift[...]
        mask = wide(r.maskp[m0 : m0 + m, :], width)
        r.hid[m0 : m0 + m, :] = 0.5 * v * (1.0 + gelu_parts(v)) * mask
    r.hid[M:, :] = jnp.zeros((r.hid.shape[0] - M, width), f32)
    for m0, m in chunks(M, 208):
        for b in range(3):
            r.h3[m0 : m0 + m, b * width : (b + 1) * width] = r.hid[m0 + b : m0 + b + m, :].astype(bf16)
    copies.start("h3")
    copies.wait("w2")
    sums = [jnp.zeros((1, width), f32)] * 2
    for k, (m0, m) in enumerate(chunks(Q, Q // 3)):
        z = matmul(r.h3[m0 : m0 + m, :], r.w2[0])
        z += matmul(r.h3[L + m0 : L + m0 + m, :], r.w2[1])
        z += matmul(r.h3[2 * L + m0 : 2 * L + m0 + m, :], r.w2[2])
        r.pre2[m0 : m0 + m, :] = z
        copies.start(("pre2", k))
        zm = z * wide(r.ownp[L + 1 + m0 : L + 1 + m0 + m, :], width)
        sums = [sums[0] + column_sum(zm), sums[1] + column_sum(zm * z)]
    row = jnp.concatenate(sums, axis=1)
    r.spread[...] = jnp.broadcast_to(row[None], r.spread.shape)
    copies.wait("h3", "pre2")


def third_kernel(r, copies):
    groups, rows, cols, width = r.out.shape
    S = cols + 8
    L = groups * S
    n = r.mom1[2:3, :]
    t = jnp.sum(r.tot2[...], axis=0)
    c2, i2 = moments(t[:, :width], t[:, width:], n)
    cp, ip = r.mom1[3:4, :], r.mom1[4:5, :]
    r.mom2[...] = jnp.concatenate([c2, i2, cp, ip, jnp.zeros((4, width), f32)], axis=0)
    sums = [jnp.zeros((1, width), f32)] * 3
    both_shift = r.shift2[...] + r.shiftp[...]
    copies.wait("pre2", "prep", "cotq")
    total = r.grad.shape[0] // S
    for line in range(total):
        at = line * S
        shifted = slice(L + 1 + at, L + 1 + at + S)
        n2 = (r.pre2[at : at + S, :] - c2) * i2
        np_ = (r.prep[shifted, :] - cp) * ip
        v = n2 * r.gain2[...] + np_ * r.gainp[...] + both_shift
        mask = wide(r.maskp[shifted, :], width)
        own = wide(r.ownp[shifted, :], width)
        t = gelu_parts(v)
        r.field[at : at + S, :] = 0.5 * v * (1.0 + t) * mask
        g = gelu_slope(v, t) * mask * r.cotq[at : at + S, :]
        r.grad[at : at + S, :] = g
        g = g * own
        new = [column_sum(g * n2), column_sum(g), column_sum(g * np_)]
        sums = [a + b for a, b in zip(sums, new)]
        if (line + 1) % (total // 2) == 0:
            copies.start(("grad", (line + 1) // (total // 2) - 1))
    for i in range(rows):
        for g in range(groups):
            at = (i + 1) * L + g * S + 1
            r.out[g, i, :, :] = r.field[at : at + cols, :].astype(bf16)
    copies.start("out")
    row = jnp.concatenate(sums, axis=1)
    r.spread[...] = jnp.broadcast_to(row[None], r.spread.shape)
    copies.wait("grad", "out")


def halves(r, source, at, frame, to, rows_w):
    half = r.mine.shape[1]
    bit = r.bits[0] == 1
    for m0, m in chunks(rows_w, 96):
        own = wide(r.ownp[frame + m0 : frame + m0 + m, :], half)
        low = (source[at + m0 : at + m0 + m, :half] * own).astype(bf16)
        high = (source[at + m0 : at + m0 + m, half:] * own).astype(bf16)
        r.mine[to + m0 : to + m0 + m, :] = jnp.where(bit, high, low)
        r.theirs[to + m0 : to + m0 + m, :] = jnp.where(bit, low, high)


def fourth_kernel(r, copies):
    width = r.gain2.shape[1]
    Q = r.pre2.shape[0]
    rows_w = r.gpu.shape[0]
    L = (Q - rows_w) // 3
    n = r.mom1[2:3, :]
    c2, i2, cp, ip = (r.mom2[k : k + 1, :] for k in range(4))
    t3 = jnp.sum(r.tot3[...], axis=0)
    gg2, gs, ggp = (t3[:, k * width : (k + 1) * width] for k in range(3))
    r.gain_second[...], r.shift_second[...], r.gain_proj[...], r.shift_proj[...] = gg2, gs, ggp, gs
    copies.wait("grad", "pre2", "prep")
    for m0, m in chunks(Q, L):
        shifted = slice(L + 1 + m0, L + 1 + m0 + m)
        mask = wide(r.maskp[shifted, :], width) / n
        n2 = (r.pre2[m0 : m0 + m, :] - c2) * i2
        np_ = (r.prep[shifted, :] - cp) * ip
        g = r.grad[m0 : m0 + m, :]
        r.gq[m0 : m0 + m, :] = (r.gain2[...] * i2) * (g - mask * (gs + n2 * gg2))
        r.gpq[m0 : m0 + m, :] = (r.gainp[...] * ip) * (g - mask * (gs + np_ * ggp))
    r.gq[Q:, :] = jnp.zeros((r.gq.shape[0] - Q, width), f32)
    copies.start("gq")
    for m0, m in chunks(rows_w, 96):
        r.gpu[m0 : m0 + m, :] = r.gpq[L + 1 + m0 : L + 1 + m0 + m, :].astype(bf16)
    copies.start("gpu")
    halves(r, r.gq, L, 2 * L + 1, 0, rows_w)
    halves(r, r.gpq, L - 1, 2 * L, rows_w, rows_w)
    copies.wait("gpu", "gq")


def hidden_kernel(r, copies):
    width = r.gain.shape[1]
    Q = r.gq.shape[0] - 8
    L = (r.keep.shape[0] - Q) // 2
    center, inv = r.mom1[0:1, :], r.mom1[1:2, :]
    copies.wait("gq")
    for m0, m in chunks(Q, 176):
        for b in range(3):
            r.g3[m0 : m0 + m, b * width : (b + 1) * width] = r.gq[m0 + b : m0 + b + m, :].astype(bf16)
    U = r.act.shape[0]
    for a in range(3):
        copies.wait(("w2", a))
        gh = jnp.zeros((U, width), f32)
        for b in range(3):
            gh += matmul_nt(
                r.g3[L * a : L * a + U, b * width : (b + 1) * width],
                r.w2[2 - a, (2 - b) * width : (3 - b) * width, :],
            )
        r.act[...] = gh if a == 0 else r.act[...] + gh
    copies.wait("keep")
    sums = [jnp.zeros((1, width), f32)] * 2
    for m0, m in chunks(U, L):
        frame = slice(2 * L + 2 + m0, 2 * L + 2 + m0 + m)
        n1 = (r.keep[frame, :] - center) * inv
        v = n1 * r.gain[...] + r.shift[...]
        mask = wide(r.maskp[frame, :], width)
        g = gelu_slope(v, gelu_parts(v)) * mask * r.act[m0 : m0 + m, :]
        r.act[m0 : m0 + m, :] = g
        r.normed[m0 : m0 + m, :] = n1 * mask
        g = g * wide(r.ownp[frame, :], width)
        sums = [sums[0] + column_sum(g * n1), sums[1] + column_sum(g)]
    row = jnp.concatenate(sums, axis=1)
    r.spread[...] = jnp.broadcast_to(row[None], r.spread.shape)


def split_store(r, rows, unit, first):
    quarter = unit // 4
    for k in range(rows // unit):
        for bit, base, sent, kept in ((1, 0, r.sent_a, r.kept_a), (2, 2 * quarter, r.sent_b, r.kept_b)):
            keep = pl.multiple_of(k * unit + base + r.bits[bit] * quarter, quarter)
            send = pl.multiple_of(k * unit + base + (1 - r.bits[bit]) * quarter, quarter)
            sent[first + k] = r.acc[pl.ds(send, quarter), :].astype(bf16)
            kept[first + k] = r.acc[pl.ds(keep, quarter), :]


def weights_second_kernel(r, copies):
    width = r.h3.shape[1] // 3
    cin = r.xe.shape[1] // 3
    rows_w = r.near.shape[0] // 2
    L = (r.h3.shape[0] - rows_w) // 5
    per = width // cin
    for b in range(3):
        lanes = slice(b * width, (b + 1) * width)
        copies.wait(("h3", b), ("h3_far", b))
        for a in range(3):
            at = L * a + L
            r.acc[...] = matmul_tn(r.h3[at : at + rows_w, lanes], r.near[:rows_w, :]) + matmul_tn(
                r.h3_far[at : at + rows_w, lanes], r.far[:rows_w, :]
            )
            split_store(r, width, cin, (3 * b + a) * per)
        copies.start(("kept_a", b), ("kept_b", b))
    at = 2 * L
    copies.wait("xe", "xe_far")
    middle = slice(cin, 2 * cin)
    r.acc[0:cin, :] = matmul_tn(r.xe[at : at + rows_w, middle], r.near[rows_w:, :]) + matmul_tn(
        r.xe_far[at : at + rows_w, middle], r.far[rows_w:, :]
    )
    split_store(r, cin, cin, 9 * per)
    copies.start(("kept_a", 3), ("kept_b", 3))
    copies.wait("kept_a", "kept_b")


def first_back(r, gg, gs, count):
    width = r.gain.shape[1]
    U = r.act.shape[0]
    L = U - r.rows_w
    inv, n = r.mom1[1:2, :], r.mom1[2:3, :]
    gg, gs = gg / n, gs / n
    scale = r.gain[...] * inv
    r.gf[0:8, :] = jnp.zeros((8, width), f32)
    r.gf[8 + count :, :] = jnp.zeros((r.gf.shape[0] - 8 - count, width), f32)
    for m0, m in chunks(count, L):
        mask = wide(r.maskp[2 * L + 2 + m0 : 2 * L + 2 + m0 + m, :], width)
        back = mask * gs + r.normed[m0 : m0 + m, :] * gg
        r.gf[8 + m0 : 8 + m0 + m, :] = scale * (r.act[m0 : m0 + m, :] - back)


def fifth_kernel(r, copies):
    width = r.gain.shape[1]
    r.rows_w = r.mine.shape[0]
    L = r.act.shape[0] - r.rows_w
    t4 = jnp.sum(r.tot4[...], axis=0)
    r.gain_first[...], r.shift_first[...] = t4[:, :width], t4[:, width:]
    first_back(r, t4[:, :width], t4[:, width:], r.rows_w)
    halves(r, r.gf, 6, 2 * L, 0, r.rows_w)


def weights_first_kernel(r, copies):
    rows_w = r.near.shape[0]
    cin = r.xe.shape[1] // 3
    L = (r.xe.shape[0] - rows_w) // 5
    copies.wait("xe", "xe_far")
    for k, a in enumerate((1, 0, 2)):
        if k == 1:
            copies.wait("xo", "xo_far")
        source, source_far = (r.xe, r.xe_far) if a == 1 else (r.xo, r.xo_far)
        at = (3 if a == 2 else 2) * L
        for b in range(3):
            lanes = slice(b * cin, (b + 1) * cin)
            r.acc[lanes, :] = matmul_tn(source[at : at + rows_w, lanes], r.near[...]) + matmul_tn(
                source_far[at : at + rows_w, lanes], r.far[...]
            )
        split_store(r, 3 * cin, cin, a * 3)
        copies.start(("kept_a", a), ("kept_b", a))
    copies.wait("kept_a", "kept_b")


def inputs_kernel(r, copies):
    width = r.gpu.shape[1]
    groups, rows, cols = r.out.shape[0], r.out.shape[1] // 2, r.out.shape[2] // 2
    cin = r.out.shape[3]
    M = r.gpu.shape[0]
    S = cols + 8
    L = groups * S
    lines = r.lines
    U = r.act.shape[0]
    r.rows_w = M
    copies.wait("act", "normed")
    first_back(r, r.gg[...], r.gs[...], U)
    for m0, m in chunks(U, 144):
        r.gu[m0 : m0 + m, :width] = r.gf[8 + m0 : 8 + m0 + m, :].astype(bf16)
        r.gu[m0 : m0 + m, width:] = r.gf[9 + m0 : 9 + m0 + m, :].astype(bf16)
    copies.wait("gpu", "w1", "wp")

    def tap(m0, m, a, b):
        di, dj = (1 if a == 0 else 0), (1 if b == 0 else 0)
        return matmul_nt(
            r.gu[di * L + m0 : di * L + m0 + m, dj * width : (dj + 1) * width],
            r.w1[a, b * cin : (b + 1) * cin, :],
        )

    for m0, m in chunks(M, 2 * L):
        pieces = {
            (0, 0): tap(m0, m, 1, 1) + matmul_nt(r.gpu[m0 : m0 + m, :], r.wp[...]),
            (0, 1): tap(m0, m, 1, 2) + tap(m0, m, 1, 0),
            (1, 0): tap(m0, m, 2, 1) + tap(m0, m, 0, 1),
            (1, 1): tap(m0, m, 2, 2) + tap(m0, m, 2, 0) + tap(m0, m, 0, 2) + tap(m0, m, 0, 0),
        }
        for (ro, co), v in pieces.items():
            for k in range(m // S):
                line = m0 // S + k
                i, g = line // groups, line % groups
                for h in range(lines.shape[0]):
                    lines[h, (2 * i + ro) * groups + g, pl.ds(co, cols, stride=2), :] = v[
                        k * S : k * S + cols, h * 128 : (h + 1) * 128
                    ]
    for n in range(2 * rows):
        for g in range(groups):
            for h in range(lines.shape[0]):
                r.out[g, n, :, h * 128 : (h + 1) * 128] = lines[h, n * groups + g].astype(bf16)
    copies.start("out")
    copies.wait("out")


def widen(half, side, taps, per, swapped, into=None):
    total, n, m = half.shape
    extra = total - taps * per
    order = [(t % 3 * 3 + t // 3) if swapped else t for t in range(taps)]
    jobs = [(t * per, per, 0, order[t] * per) for t in range(taps)] + [(taps * per, 1, 1, 0)] * extra
    more = list(into or [])

    def body(side_ref, half_ref, *refs):
        outs = refs[len(more) : len(more) + 1 + extra]
        narrow, full, sems = refs[len(more) + 1 + extra :]
        lanes = pl.ds(pl.multiple_of(side_ref[0] * m, m), m)
        reads = [
            pltpu.make_async_copy(half_ref.at[pl.ds(at, size)], narrow.at[pl.ds(at, size)], sems.at[0, k])
            for k, (at, size, _, _) in enumerate(jobs)
        ]
        writes = [
            pltpu.make_async_copy(full.at[pl.ds(at, size)], outs[which].at[pl.ds(to, size), :, lanes], sems.at[1, k])
            for k, (at, size, which, to) in enumerate(jobs)
        ]
        for read in reads:
            read.start()
        for k, (at, size, _, _) in enumerate(jobs):
            reads[k].wait()
            full[at : at + size] = narrow[at : at + size].astype(f32)
            writes[k].start()
        for write in writes:
            write.wait()

    hbm = pl.BlockSpec(memory_space=pltpu.HBM)
    return pl.pallas_call(
        body,
        out_shape=[shape((taps * per, n, 2 * m))] + [shape((1, n, 2 * m))] * extra,
        in_specs=[pl.BlockSpec(memory_space=pltpu.SMEM)] + [hbm] * (1 + len(more)),
        out_specs=[hbm] * (1 + extra),
        scratch_shapes=[
            pltpu.VMEM((total, n, m), bf16),
            pltpu.VMEM((total, n, m), f32),
            pltpu.SemaphoreType.DMA((2, len(jobs))),
        ],
        input_output_aliases={2 + k: k for k in range(len(more))},
        compiler_params=pltpu.CompilerParams(vmem_limit_bytes=20 * 1024 * 1024),
        cost_estimate=pl.CostEstimate(flops=0, bytes_accessed=0, transcendentals=0),
    )(side.reshape(1), half, *more)


def halve_kernel(r, copies):
    for p in range(r.count):
        kept, got = getattr(r, f"kept{p}"), getattr(r, f"got{p}")
        copies.wait(f"kept{p}", f"got{p}")
        to_send, to_keep = getattr(r, f"sent{p}"), getattr(r, f"left{p}")
        bit = r.bits[r.steps[p]] == 1
        h = kept.shape[1] // 2
        for t in range(kept.shape[0]):
            total = kept[t] + got[t].astype(f32)
            low, high = total[:h], total[h:]
            to_send[t] = jnp.where(bit, low, high).astype(bf16)
            to_keep[t] = jnp.where(bit, high, low)
        copies.start(f"sent{p}", f"left{p}")
    copies.wait(*(name for name in copies.jobs if name[:4] in ("sent", "left")))


def halve(bits, pairs, steps, cost):
    ins = dict(bits=bits)
    for p, (kept, got) in enumerate(pairs):
        ins[f"kept{p}"], ins[f"got{p}"] = kept, got
    taps, n, m = pairs[0][0].shape
    dims = (taps, n // 2, m)
    names = [str(p) for p in range(len(pairs))]
    outs = {}
    for name in names:
        outs["sent" + name], outs["left" + name] = shape(dims, bf16), shape(dims)

    def body(r, copies):
        r.count, r.steps = len(pairs), steps
        halve_kernel(r, copies)

    far_in = tuple(n for n in ins if n != "bits")
    out = call(body, ins, outs, far_in=far_in, far_out=tuple(outs), smem=("bits",), cost=cost, limit=60)
    return [(out["sent" + name], out["left" + name]) for name in names]


def shifted(value, axis, steps):
    count = lax.axis_size(axis)
    first, last = (max(0, -steps), min(count, count - steps))
    return lax.ppermute(value, axis, [(source, source + steps) for source in range(first, last)])


def gather_sum(spread):
    return lax.all_to_all(spread, axes, 0, 0)


def bit_of(axis, step):
    return (lax.axis_index(axis) // step) % 2


def partner(value, axis, step):
    count = lax.axis_size(axis)
    return lax.ppermute(value, axis, [(i, i ^ step) for i in range(count)])


def steps_of(axis):
    count, step, out = lax.axis_size(axis), 1, []
    while step < count:
        out.append((axis, step))
        step *= 2
    return out


def split(total, axis, step):
    n = total.shape[1] // 2
    bit = bit_of(axis, step) == 1
    low, high = total[:, :n], total[:, n:]
    return jnp.where(bit, low, high).astype(bf16), jnp.where(bit, high, low)


def joined(value, other, axis, step, dim=1):
    bit = bit_of(axis, step) == 1
    return jnp.concatenate([jnp.where(bit, other, value), jnp.where(bit, value, other)], axis=dim)


class Tree:
    def __init__(self, parts, bits, plane, rest, core):
        self.bits, self.place = bits, {step: k for k, step in enumerate([core, *plane, *rest])}
        self.sent_a, self.kept_a, self.sent_b, self.kept_b = parts
        self.a, self.b, self.rest, self.core = plane, plane[::-1], rest, core
        p, n = len(plane), len(rest)
        self.stages = [("plane", k) for k in range(p)] + [("rest", k) for k in range(n)]
        self.stages += [("rest_join", k) for k in reversed(range(n))] + [("plane_join", k) for k in reversed(range(p))]
        self.stages += [("core", 0)]

    def next(self):
        return self.stages[0] if self.stages else None

    def start(self):
        kind, k = self.stages[0]
        if kind == "plane":
            self.got = partner(self.sent_a, *self.a[k]), partner(self.sent_b, *self.b[k])
        elif kind == "rest":
            self.got = (partner(self.sent, *self.rest[k]),)
        elif kind == "rest_join":
            self.got = (partner(self.value, *self.rest[k]),)
        elif kind == "plane_join":
            self.got = partner(self.value_a, *self.a[k]), partner(self.value_b, *self.b[k])
        else:
            self.got = (partner(self.value, *self.core),)

    def finish(self, cost=0):
        kind, k = self.stages.pop(0)
        if kind == "plane":
            pairs = [(self.kept_a, self.got[0]), (self.kept_b, self.got[1])]
            nexts = [order[k + 1] for order in (self.a, self.b) if k + 1 < len(order)]
            if nexts and cost:
                pairs = halve(self.bits, pairs, [self.place[step] for step in nexts], cost)
                (self.sent_a, self.kept_a), (self.sent_b, self.kept_b) = pairs
                return
            total_a, total_b = (kept + got.astype(f32) for kept, got in pairs)
            if nexts:
                self.sent_a, self.kept_a = split(total_a, *nexts[0])
                self.sent_b, self.kept_b = split(total_b, *nexts[1])
            else:
                self.taps = total_a.shape[0]
                self.split_rest(jnp.concatenate([total_a, total_b], axis=0), 0)
        elif kind == "rest":
            self.split_rest(self.kept + self.got[0].astype(f32), k + 1)
        elif kind == "rest_join":
            self.value = joined(self.value, self.got[0], *self.rest[k])
            self.value_a, self.value_b = self.value[: self.taps], self.value[self.taps :]
        elif kind == "plane_join":
            self.value_a = joined(self.value_a, self.got[0], *self.a[k])
            self.value_b = joined(self.value_b, self.got[1], *self.b[k])
            self.value = jnp.concatenate([self.value_a, self.value_b], axis=1)

    def split_rest(self, total, k):
        if k < len(self.rest):
            self.sent, self.kept = split(total, *self.rest[k])
        else:
            self.value = total.astype(bf16)


def lockstep(*trees, beside=()):
    for t in trees:
        t.start()
    got, beside = lax.optimization_barrier(([t.got for t in trees], beside))
    for t, g in zip(trees, got):
        t.got = g
        t.finish()
    return beside


def on_device(inputs, w_first, gain_first, shift_first, w_second, gain_second, shift_second, w_proj, gain_proj, shift_proj, valid_mask, cotangent):
    groups, rows_in, cols_in, cin = inputs.shape
    rows, cols = rows_in // 2, cols_in // 2
    width = w_first.shape[3]
    half = width // 2
    S = cols + 8
    L = groups * S
    devices = lax.axis_size("rows") * lax.axis_size("cols") * lax.axis_size("grp")
    plane = steps_of("cols")
    core = steps_of("rows")[0]
    rest = steps_of("rows")[1:] + steps_of("grp")
    bits = jnp.stack([bit_of(*step) for step in (core, *plane, *rest)]).astype(jnp.int32)
    w1 = w_first.reshape(3, 3 * cin, width)
    w2 = w_second.reshape(3, 3 * width, width)
    as_row = lambda v: v.reshape(1, -1)
    own = jnp.broadcast_to(valid_mask.astype(bf16)[..., None], valid_mask.shape + (128,))
    MP, MQ, MU, MW = (rows + 5) * L, (rows + 3) * L, (rows + 1) * L, rows * L
    px = lambda m, k: 2 * m * k * width
    vec = lambda k: shape((1, k * width))
    all_devices = lambda k: shape((devices, 1, k))
    g1, b1, g2, b2, gp, bp = map(
        as_row, (gain_first, shift_first, gain_second, shift_second, gain_proj, shift_proj)
    )

    top1 = shifted(inputs[:, -1:], "rows", 1)
    me, count = lax.axis_index("rows"), lax.axis_size("rows")
    flags = jnp.stack([me > 0, me < count - 1]).astype(jnp.int32)
    flat_rows = shape((over * groups * cols_in + (width // 256 + 1) * rim * groups * cols, 256), bf16)
    packed = call(
        vertical_kernel,
        dict(flags=flags, x=inputs, cot=cotangent, own=own),
        dict(down=flat_rows) if count == 2 else dict(down=flat_rows, up=flat_rows),
        far_in=("x", "cot"),
        smem=("flags",),
        parts=dict(x=end_parts(rows_in, over), cot=end_parts(rows, rim)),
    )
    if count == 2:
        top = bot = lax.ppermute(packed["down"], "rows", [(0, 1), (1, 0)])
    else:
        top, bot = shifted(packed["down"], "rows", 1), shifted(packed["up"], "rows", -1)
    lft1 = shifted(jnp.concatenate([top1[:, :, -1:], inputs[:, :, -1:]], axis=1), "cols", 1)
    (top, bot), lft1 = lax.optimization_barrier(((top, bot), lft1))
    lines = (rows_in + 2 * over) * groups, (rows + 2 * rim) * groups, (rows + 3) * groups
    n_strip = over * lines[0] + (rim + 1) // 2 * lines[1] + width // 128 * lines[2]
    n_strip = -(-n_strip // 16) * 16
    near = dict(flags=flags, x=inputs, cot=cotangent, own=own, top=top, bot=bot)
    strips = call(
        strips_kernel,
        near,
        dict(right=shape((n_strip, 256), bf16), left=shape((n_strip, 256), bf16)),
        dict(
            raw_x=pltpu.VMEM((cin // 128, lines[0] * cols_in, 128), f32),
            raw_m=pltpu.VMEM((1, lines[1] * cols, 128), f32),
            raw_c=pltpu.VMEM((width // 128, lines[2] * cols, 128), f32),
            flat=pltpu.VMEM((n_strip, 256), f32),
        ),
        smem=("flags",),
    )
    lft, rgt = shifted(strips["right"], "cols", 1), shifted(strips["left"], "cols", -1)
    lft1, _ = lax.optimization_barrier((lft1, strips["right"]))
    stats = call(
        stats_kernel,
        dict(x=inputs, top=top1, lft=lft1, own=own, w1=w1, wp=w_proj),
        dict(spread=all_devices(4 * width + 128)),
        dict(
            raw=pltpu.VMEM((cin // 128, (rows_in + 1) * groups, cols_in + 8, 128), f32),
            xe=pltpu.VMEM((rows * groups * cols, 3 * cin), bf16),
            xo=pltpu.VMEM(((rows + 1) * groups * cols, 3 * cin), bf16),
        ),
    )
    tot1 = gather_sum(stats["spread"])

    first = call(
        first_kernel,
        dict(**near, lft=lft, rgt=rgt, w1=w1, wp=w_proj),
        dict(
            pre1=shape((MP, width)),
            prep=shape((MP, width)),
            xe=shape((MP, 3 * cin), bf16),
            xo=shape((MP + L, 3 * cin), bf16),
            ownp=shape((MP, 128)),
            maskp=shape((MP, 128)),
            cotq=shape((MQ, width)),
        ),
        dict(
            raw_x=pltpu.VMEM((cin // 128, lines[0] * (cols_in + 24), 128), f32),
            raw_m=pltpu.VMEM((1, lines[1] * (cols + 16), 128), f32),
            raw_c=pltpu.VMEM((width // 128, lines[2] * (cols + 16), 128), f32),
            flat=pltpu.VMEM((n_strip, 256), f32),
        ),
        far_in=("w1", "wp"),
        far_out=("xe", "xo", "pre1", "prep", "cotq"),
        smem=("flags",),
        cost=20000000000,
        parts=dict(pre1=row_parts(MP, 3), prep=row_parts(MP, 3)),
    )
    xe, xo, ownp, maskp = first["xe"], first["xo"], first["ownp"], first["maskp"]
    far_xe, far_xo = partner(xe, *core), partner(xo, *core)

    second = call(
        second_kernel,
        dict(pre1=first["pre1"], tot1=tot1, gain=g1, shift=b1, maskp=maskp, ownp=ownp, w2=w2),
        dict(h3=shape((MP, 3 * width), bf16), pre2=shape((MQ, width)), spread=all_devices(2 * width), mom1=shape((8, width))),
        dict(hid=pltpu.VMEM((MP + 8, width), f32)),
        far_in=("pre1", "w2"),
        far_out=("h3", "pre2"),
        parts=dict(pre2=row_parts(MQ, 3)),
    )
    h3, pre2, mom1 = second["h3"], second["pre2"], second["mom1"]
    tot2 = gather_sum(second["spread"])
    far_h3 = partner(h3, *core)

    third = call(
        third_kernel,
        dict(
            pre2=pre2, prep=first["prep"], mom1=mom1, tot2=tot2, gain2=g2, shift2=b2, gainp=gp, shiftp=bp,
            maskp=maskp, ownp=ownp, cotq=first["cotq"],
        ),
        dict(
            out=shape((groups, rows, cols, width), bf16),
            grad=shape((MQ, width)),
            spread=all_devices(3 * width),
            mom2=shape((8, width)),
        ),
        dict(field=pltpu.VMEM((MQ, width), f32)),
        far_in=("pre2", "prep", "cotq"),
        far_out=("out", "grad"),
        parts=dict(grad=row_parts(MQ, 2)),
    )
    mom2 = third["mom2"]
    tot3 = gather_sum(third["spread"])

    fourth = call(
        fourth_kernel,
        dict(
            bits=bits, pre2=pre2, prep=first["prep"], mom1=mom1, mom2=mom2, tot3=tot3, gain2=g2, gainp=gp,
            grad=third["grad"], maskp=maskp, ownp=ownp,
        ),
        dict(
            mine=shape((2 * MW, half), bf16),
            theirs=shape((2 * MW, half), bf16),
            gq=shape((MQ + 8, width)),
            gpu=shape((MW, width), bf16),
            gain_second=vec(1),
            shift_second=vec(1),
            gain_proj=vec(1),
            shift_proj=vec(1),
        ),
        dict(gpq=pltpu.VMEM((MQ, width), f32)),
        far_in=("pre2", "prep", "grad"),
        far_out=("gpu", "gq"),
        smem=("bits",),
    )
    far2 = partner(fourth["theirs"], *core)

    def chunk_shapes(taps):
        dims = (taps, cin // 4, half)
        return dict(sent_a=shape(dims, bf16), kept_a=shape(dims), sent_b=shape(dims, bf16), kept_b=shape(dims))

    per = width // cin
    taps2 = 9 * per + 1
    second_parts = call(
        weights_second_kernel,
        dict(bits=bits, h3=h3, h3_far=far_h3, xe=xe, xe_far=far_xe, near=fourth["mine"], far=far2),
        chunk_shapes(taps2),
        dict(acc=pltpu.VMEM((width, half), f32)),
        far_in=("h3", "h3_far", "xe", "xe_far"),
        far_out=("kept_a", "kept_b"),
        smem=("bits",),
        parts=dict(
            h3=lane_parts(3 * width, 3),
            h3_far=lane_parts(3 * width, 3),
            kept_a=row_parts(taps2 - 1, 3) + [(3, (pl.ds(taps2 - 1, 1),))],
            kept_b=row_parts(taps2 - 1, 3) + [(3, (pl.ds(taps2 - 1, 1),))],
        ),
    ).values()
    gq, *second_parts = lax.optimization_barrier((fourth["gq"], *second_parts))

    tree2 = Tree(second_parts, bits, plane, rest, core)
    tree2.start()
    hidden = call(
        hidden_kernel,
        dict(gq=gq, w2=w2, keep=first["pre1"], mom1=mom1, gain=g1, shift=b1, maskp=maskp, ownp=ownp),
        dict(act=shape((MU, width)), normed=shape((MU, width)), spread=all_devices(2 * width)),
        dict(g3=pltpu.VMEM((MQ, 3 * width), bf16)),
        far_in=("gq", "w2", "keep"),
        parts=dict(w2=[(k, (pl.ds(2 - k, 1),)) for k in range(3)]),
    )
    tot4 = gather_sum(hidden["spread"])
    tree2.finish(20000000000)
    act, tree2.sent_a, tree2.sent_b = lax.optimization_barrier((hidden["act"], tree2.sent_a, tree2.sent_b))
    tree2.start()
    fifth = call(
        fifth_kernel,
        dict(bits=bits, act=act, normed=hidden["normed"], mom1=mom1, tot4=tot4, gain=g1, maskp=maskp, ownp=ownp),
        dict(mine=shape((MW, half), bf16), theirs=shape((MW, half), bf16), gain_first=vec(1), shift_first=vec(1)),
        dict(gf=pltpu.VMEM((MU + 16, width), f32)),
        smem=("bits",),
    )
    far1 = partner(fifth["theirs"], *core)
    first_parts = call(
        weights_first_kernel,
        dict(bits=bits, xe=xe, xo=xo, xe_far=far_xe, xo_far=far_xo, near=fifth["mine"], far=far1),
        chunk_shapes(9),
        dict(acc=pltpu.VMEM((3 * cin, half), f32)),
        far_in=("xe", "xe_far", "xo", "xo_far"),
        far_out=("kept_a", "kept_b"),
        smem=("bits",),
        parts=dict(kept_a=row_parts(9, 3), kept_b=row_parts(9, 3)),
    ).values()
    tree2.got, *first_parts = lax.optimization_barrier((tree2.got, *first_parts))
    tree2.finish()
    tree1 = Tree(first_parts, bits, plane, rest, core)

    grad_inputs = call(
        inputs_kernel,
        dict(
            act=act, normed=hidden["normed"], gpu=fourth["gpu"], w1=w1, wp=w_proj, mom1=mom1, gain=g1, maskp=maskp,
            gg=fifth["gain_first"], gs=fifth["shift_first"],
        ),
        dict(out=shape((groups, rows_in, cols_in, cin), bf16)),
        dict(
            lines=pltpu.VMEM((cin // 128, rows_in * groups, cols_in, 128), f32),
            gf=pltpu.VMEM((MU + 16, width), f32),
            gu=pltpu.VMEM((MU, 2 * width), bf16),
        ),
        far_in=("act", "normed", "gpu", "w1", "wp"),
        far_out=("out",),
        cost=10000000000,
    )["out"]
    side = bit_of(*core).astype(jnp.int32)
    grad_inputs = lockstep(tree2, tree1, beside=grad_inputs)
    while tree2.next() != ("plane_join", 0):
        lockstep(tree2, tree1)
    tree2.start()
    while tree1.next() != ("plane_join", 0):
        tree1.start()
        if tree1.next() != ("plane_join", 1):
            tree1.finish()
        else:
            tree1.got, tree2.got = lax.optimization_barrier((tree1.got, tree2.got))
            tree1.finish()
    tree2.finish()
    tree2.start()
    tree1.start()
    grad_second = widen(tree2.got[0], 1 - side, 9, per, True, widen(tree2.value, side, 9, per, True))
    tree1.got, grad_second = lax.optimization_barrier((tree1.got, grad_second))
    grad_w2, grad_wp = grad_second
    tree1.finish()
    tree1.start()
    (grad_w1,) = widen(tree1.got[0], 1 - side, 3, 3, False, widen(tree1.value, side, 3, 3, False))

    return (
        third["out"],
        grad_inputs,
        grad_w1.reshape(w_first.shape),
        fifth["gain_first"].reshape(width),
        fifth["shift_first"].reshape(width),
        grad_w2.reshape(w_second.shape),
        fourth["gain_second"].reshape(width),
        fourth["shift_second"].reshape(width),
        grad_wp.reshape(w_proj.shape),
        fourth["gain_proj"].reshape(width),
        fourth["shift_proj"].reshape(width),
    )


def solution(mesh):
    spread = P("grp", "rows", "cols", None)
    return jax.shard_map(
        on_device,
        mesh=mesh,
        in_specs=(spread,) + (P(),) * 9 + (P("grp", "rows", "cols"), spread),
        out_specs=(spread, spread) + (P(),) * 9,
        check_vma=False,
    )
```

```python
import functools

import jax
import jax.numpy as jnp
from jax import lax
from jax.experimental import pallas as pl
from jax.experimental.pallas import tpu as pltpu
from jax.sharding import PartitionSpec as P

epsilon = 1e-05
axes = ("rows", "cols", "grp")
bf16 = jnp.bfloat16
f32 = jnp.float32
inner = 0.7978845608028654
cubic = 0.044715
over = 6
rim = 3


class Refs:
    def __init__(self, named):
        self.__dict__.update(named)


class Copies:
    def __init__(self, parts, pairs, sems):
        self.jobs = {}
        for k, (name, index) in enumerate(parts):
            source, target = pairs[name]
            if index:
                source, target = source.at[index[1]], target.at[index[1]]
            self.jobs.setdefault(name, []).append(pltpu.make_async_copy(source, target, sems.at[k]))

    def start(self, *names):
        for name, *which in map(named, names):
            for job in self.jobs[name][slice(*which) if which else slice(None)]:
                job.start()

    def wait(self, *names):
        for name, *which in map(named, names):
            for job in self.jobs[name][slice(*which) if which else slice(None)]:
                job.wait()


def named(name):
    return (name,) if isinstance(name, str) else (name[0], name[1], name[1] + 1)


def row_parts(total, count):
    size = total // count
    return [(k, (pl.ds(k * size, size),)) for k in range(count)]


def end_parts(total, size):
    return [(k, (slice(None), pl.ds(at, size))) for k, at in enumerate((0, total - size))]


def lane_parts(total, count):
    size = total // count
    return [(k, (slice(None), pl.ds(k * size, size))) for k in range(count)]


def call(body, ins, outs, scratch=None, far_in=(), far_out=(), smem=(), parts=None, limit=52, cost=0):
    scratch, parts = scratch or {}, parts or {}
    far = (*far_in, *far_out)
    jobs = [(name, index) for name in far for index in parts.get(name, [None])]

    def spec(name):
        if name in smem:
            return pl.BlockSpec(memory_space=pltpu.SMEM)
        return pl.BlockSpec(memory_space=pltpu.HBM if name in far else pltpu.VMEM)

    kinds = {**{n: shape(v.shape, v.dtype) for n, v in ins.items()}, **outs}

    def run(*refs):
        plain = dict(zip([*ins, *outs], refs))
        rest = refs[len(plain) :]
        buffers = dict(zip(far, rest))
        more = dict(zip(scratch, rest[len(far) :]))
        copies = None
        if far:
            pairs = {n: (plain[n], buffers[n]) if n in far_in else (buffers[n], plain[n]) for n in far}
            copies = Copies(jobs, pairs, rest[-1])
            copies.start(*far_in)
        body(Refs({**plain, **buffers, **more}), copies)

    buffers = [pltpu.VMEM(kinds[n].shape, kinds[n].dtype) for n in far]
    sems = [pltpu.SemaphoreType.DMA((len(jobs),))] if far else []
    result = pl.pallas_call(
        run,
        out_shape=list(outs.values()),
        in_specs=[spec(n) for n in ins],
        out_specs=[spec(n) for n in outs],
        scratch_shapes=[*buffers, *scratch.values(), *sems],
        compiler_params=pltpu.CompilerParams(vmem_limit_bytes=limit * 1024 * 1024),
        cost_estimate=pl.CostEstimate(flops=cost, bytes_accessed=0, transcendentals=0),
    )(*ins.values())
    return dict(zip(outs, result))


def shape(dims, dtype=f32):
    return jax.ShapeDtypeStruct(dims, dtype)


def wide(mask, width):
    return jnp.concatenate([mask] * (width // mask.shape[1]), axis=1)


def matmul(a, b):
    return lax.dot_general(a, b, (((1,), (0,)), ((), ())), preferred_element_type=f32)


def matmul_nt(a, b):
    return lax.dot_general(a, b, (((1,), (1,)), ((), ())), preferred_element_type=f32)


def matmul_tn(a, b):
    return lax.dot_general(a, b, (((0,), (0,)), ((), ())), preferred_element_type=f32)


def gelu_parts(v):
    return jnp.tanh(inner * (v + cubic * v * v * v))


def gelu_slope(v, t):
    return 0.5 * (1.0 + t) + 0.5 * v * (1.0 - t * t) * (inner * (1.0 + 3.0 * cubic * v * v))


def column_sum(v):
    return jnp.sum(v, axis=0, keepdims=True)


def moments(total, squares, pixel_count):
    center = total / pixel_count
    spread = squares / pixel_count - center * center
    return center, lax.rsqrt(spread + epsilon)


def chunks(total, size):
    return [(at, min(size, total - at)) for at in range(0, total, size)]


def strided(ref, k, first, count, step):
    return ref[k, pl.ds(first, count, stride=step), :]


def vertical_kernel(r, copies):
    groups, width = r.x.shape[0], r.cot.shape[3]
    rows, cols = r.own.shape[1], r.own.shape[2]

    def pack(out, input_row, row, pick):
        at = 0
        for g in range(groups):
            for n in range(over):
                value = r.x[g, input_row(n)]
                out[at : at + 2 * cols, :] = pick(value, r.x[g, n])
                at += 2 * cols
        for k in range(0, width, 256):
            for g in range(groups):
                for n in range(rim):
                    lanes = slice(k, k + 256)
                    out[at : at + cols, :] = pick(r.cot[g, row(n), :, lanes], r.cot[g, n, :, lanes])
                    at += cols
        for g in range(groups):
            for n in range(rim):
                out[at : at + cols, :] = pick(wide(r.own[g, row(n)], 256), wide(r.own[g, n], 256))
                at += cols

    last = r.x.shape[1] - over
    copies.wait("x", "cot")
    if hasattr(r, "up"):
        pack(r.down, lambda n: last + n, lambda n: rows - rim + n, lambda tail, head: tail)
        pack(r.up, lambda n: last + n, lambda n: rows - rim + n, lambda tail, head: head)
    else:
        bottom = r.flags[0] == 1
        pack(r.down, lambda n: last + n, lambda n: rows - rim + n, lambda tail, head: jnp.where(bottom, head, tail))


def rim_rows(r, own, n_own, n_rim, base, cols, split):
    groups = own.shape[0]
    size = groups * n_rim * cols

    def flat(ref, g, n):
        at = [base + k * size + (g * n_rim + n) * cols for k in range(split)]
        return jnp.concatenate([ref[p : p + cols, :] for p in at], axis=1).astype(f32)

    def read(g, n):
        if n < n_rim:
            return jnp.where(r.flags[0] == 1, flat(r.top, g, n), 0.0)
        if n < n_rim + n_own:
            return own[g, n - n_rim].astype(f32)
        return jnp.where(r.flags[1] == 1, flat(r.bot, g, n - n_rim - n_own), 0.0)

    return read


def fields(r):
    groups, width = r.x.shape[0], r.cot.shape[3]
    rows, cols = r.own.shape[1], r.own.shape[2]
    base = over * groups * 2 * cols
    piece = rim * groups * cols
    blocks = width // 256
    x = rim_rows(r, r.x, 2 * rows, over, 0, 2 * cols, 1)
    mask = rim_rows(r, r.own, rows, rim, base + blocks * piece, cols, 1)
    cot = rim_rows(r, r.cot, rows, rim, base, cols, blocks)
    return x, lambda g, n: mask(g, n)[:, :128], cot


def strips_kernel(r, copies):
    groups, width = r.x.shape[0], r.cot.shape[3]
    rows, cols = r.own.shape[1], r.own.shape[2]
    x, mask, cot = fields(r)
    lines = (2 * rows + 2 * over) * groups, (rows + 2 * rim) * groups, (rows + 3) * groups
    for raw, read, first, count, w in (
        (r.raw_x, x, 0, lines[0], 2 * cols),
        (r.raw_m, mask, 0, lines[1], cols),
        (r.raw_c, cot, 2, lines[2], cols),
    ):
        for at in range(count):
            value = read(at % groups, at // groups + first)
            for k in range(raw.shape[0]):
                raw[k, at * w : (at + 1) * w, :] = value[:, k * 128 : (k + 1) * 128]
    for out, x0, m0, c0 in ((r.right, 2 * cols - over, cols - rim, cols - 2), (r.left, 0, 0, 0)):
        pieces = []
        for c in range(over):
            pieces.append([strided(r.raw_x, k, x0 + c, lines[0], 2 * cols) for k in range(2)])
        for c in range(0, rim + 1, 2):
            pieces.append([strided(r.raw_m, 0, m0 + min(c + k, rim - 1), lines[1], cols) for k in range(2)])
        for c in range(2):
            for h in range(0, width // 128, 2):
                pieces.append([strided(r.raw_c, h + k, c0 + c, lines[2], cols) for k in range(2)])
        at = 0
        for low, high in pieces:
            r.flat[at : at + low.shape[0], :] = jnp.concatenate([low, high], axis=1)
            at += low.shape[0]
        if at < r.flat.shape[0]:
            r.flat[at:, :] = jnp.zeros((r.flat.shape[0] - at, 256), f32)
        out[...] = r.flat[...].astype(bf16)


def stats_kernel(r, copies):
    groups, cin = r.x.shape[0], r.x.shape[3]
    rows, S = r.own.shape[1], r.own.shape[2]
    L = groups * S
    width = r.w1.shape[2]
    raw = r.raw
    for n in range(2 * rows + 1):
        for g in range(groups):
            line = n * groups + g
            src = (r.top[g, 0] if n == 0 else r.x[g, n - 1]).astype(f32)
            side = r.lft[g, n].astype(f32)
            for k in range(raw.shape[0]):
                raw[k, line, 7:8, :] = side[:, k * 128 : (k + 1) * 128]
                raw[k, line, 8:, :] = src[:, k * 128 : (k + 1) * 128]
    for out, n_rows, start in ((r.xe, rows, 1), (r.xo, rows + 1, 0)):
        for n in range(n_rows):
            for b in range(3):
                for k in range(raw.shape[0]):
                    parts = [
                        raw[k, (2 * n + start) * groups + g, pl.ds(7 + b, S, stride=2), :]
                        for g in range(groups)
                    ]
                    at = b * cin + k * 128
                    out[n * L : (n + 1) * L, at : at + 128] = jnp.concatenate(
                        parts, axis=0
                    ).astype(bf16)
    mask = jnp.concatenate(
        [r.own[g, i].astype(f32) for i in range(rows) for g in range(groups)], axis=0
    )
    M = rows * L
    z = matmul(r.xo[0:M, :], r.w1[0])
    z += matmul(r.xe[...], r.w1[1])
    z += matmul(r.xo[L : L + M, :], r.w1[2])
    zp = matmul(r.xe[:, cin : 2 * cin], r.wp[...])
    zm, zpm = z * wide(mask, width), zp * wide(mask, width)
    row = jnp.concatenate(
        [column_sum(zm), column_sum(zm * z), column_sum(zpm), column_sum(zpm * zp), column_sum(mask)], axis=1
    )
    r.spread[...] = jnp.broadcast_to(row[None], r.spread.shape)


def first_kernel(r, copies):
    groups, cin, width = r.x.shape[0], r.x.shape[3], r.cot.shape[3]
    rows, cols = r.own.shape[1], r.own.shape[2]
    S = cols + 8
    L = groups * S
    W = 2 * cols + 24
    V = cols + 16
    x, mask, cot = fields(r)
    lines = (2 * rows + 2 * over) * groups, (rows + 2 * rim) * groups, (rows + 3) * groups
    tail = jnp.zeros((W - 8 - 2 * cols, 128), f32)
    r.raw_m[...] = jnp.zeros(r.raw_m.shape, f32)
    r.raw_c[...] = jnp.zeros(r.raw_c.shape, f32)
    for at in range(lines[0]):
        value = x(at % groups, at // groups)
        for k in range(r.raw_x.shape[0]):
            r.raw_x[k, at * W + 8 : at * W + 8 + 2 * cols, :] = value[:, k * 128 : (k + 1) * 128]
            r.raw_x[k, at * W + 8 + 2 * cols : (at + 1) * W, :] = tail
    for strip, x0, m0, c0 in ((r.lft, 8 - over, 8 - rim, 6), (r.rgt, 8 + 2 * cols, 8 + cols, 8 + cols)):
        r.flat[...] = strip[...].astype(f32)
        at = 0
        for c in range(over):
            for k in range(2):
                r.raw_x[k, pl.ds(x0 + c, lines[0], stride=W), :] = r.flat[at : at + lines[0], k * 128 : (k + 1) * 128]
            at += lines[0]
        for c in range(0, rim + 1, 2):
            for k in range(2):
                if c + k < rim:
                    r.raw_m[0, pl.ds(m0 + c + k, lines[1], stride=V), :] = r.flat[
                        at : at + lines[1], k * 128 : (k + 1) * 128
                    ]
            at += lines[1]
        for c in range(2):
            for h in range(0, width // 128, 2):
                for k in range(2):
                    r.raw_c[h + k, pl.ds(c0 + c, lines[2], stride=V), :] = r.flat[
                        at : at + lines[2], k * 128 : (k + 1) * 128
                    ]
                at += lines[2]
    for out, n_rows, start in ((r.xe, rows + 5, 2), (r.xo, rows + 6, 1)):
        for n in range(n_rows):
            for b in range(3):
                for k in range(r.raw_x.shape[0]):
                    parts = [
                        strided(r.raw_x, k, ((2 * n + start) * groups + g) * W + 3 + b, S, 2) for g in range(groups)
                    ]
                    at = b * cin + k * 128
                    out[n * L : (n + 1) * L, at : at + 128] = jnp.concatenate(parts, axis=0).astype(bf16)
    copies.start("xe", "xo")
    for at in range(lines[1]):
        r.raw_m[0, at * V + 8 : at * V + 8 + cols, :] = mask(at % groups, at // groups)
    for n in range(1, rows + 6):
        for g in range(groups):
            to, at = (n - 1) * L + g * S, (n * groups + g) * V
            r.maskp[to : to + S, :] = r.raw_m[0, at + 6 : at + 6 + S, :]
    for at in range(lines[2]):
        value = cot(at % groups, at // groups + 2)
        for k in range(r.raw_c.shape[0]):
            lanes = slice(k * 128, (k + 1) * 128)
            r.raw_c[k, at * V + 8 : at * V + 8 + cols, :] = value[:, lanes]
            r.cotq[at * S : (at + 1) * S, lanes] = r.raw_c[k, at * V + 7 : at * V + 7 + S, :]
    copies.start("cotq")
    r.ownp[...] = jnp.zeros(r.ownp.shape, f32)
    for i in range(rows):
        for g in range(groups):
            at = (i + 2) * L + g * S + 2
            r.ownp[at : at + cols, :] = r.own[g, i].astype(f32)
    copies.wait("w1", "wp")
    for k, (m0, m) in enumerate(chunks(r.pre1.shape[0], r.pre1.shape[0] // 3)):
        z = matmul(r.xo[m0 : m0 + m, :], r.w1[0])
        z += matmul(r.xe[m0 : m0 + m, :], r.w1[1])
        z += matmul(r.xo[L + m0 : L + m0 + m, :], r.w1[2])
        r.pre1[m0 : m0 + m, :] = z
        copies.start(("pre1", k))
        r.prep[m0 : m0 + m, :] = matmul(r.xe[m0 : m0 + m, cin : 2 * cin], r.wp[...])
        copies.start(("prep", k))
    copies.wait("xe", "xo", "pre1", "prep", "cotq")


def second_kernel(r, copies):
    width = r.gain.shape[1]
    t = jnp.sum(r.tot1[...], axis=0)
    n = wide(t[:, 4 * width :], width)
    center, inv = moments(t[:, :width], t[:, width : 2 * width], n)
    proj = moments(t[:, 2 * width : 3 * width], t[:, 3 * width : 4 * width], n)
    r.mom1[...] = jnp.concatenate([center, inv, n, *proj, jnp.zeros((3, width), f32)], axis=0)
    scale = inv * r.gain[...]
    M, Q = r.pre1.shape[0], r.pre2.shape[0]
    L = (M - Q) // 2
    copies.wait("pre1")
    for m0, m in chunks(M, 104):
        v = (r.pre1[m0 : m0 + m, :] - center) * scale + r.shift[...]
        mask = wide(r.maskp[m0 : m0 + m, :], width)
        r.hid[m0 : m0 + m, :] = 0.5 * v * (1.0 + gelu_parts(v)) * mask
    r.hid[M:, :] = jnp.zeros((r.hid.shape[0] - M, width), f32)
    for m0, m in chunks(M, 208):
        for b in range(3):
            r.h3[m0 : m0 + m, b * width : (b + 1) * width] = r.hid[m0 + b : m0 + b + m, :].astype(bf16)
    copies.start("h3")
    copies.wait("w2")
    sums = [jnp.zeros((1, width), f32)] * 2
    for k, (m0, m) in enumerate(chunks(Q, Q // 3)):
        z = matmul(r.h3[m0 : m0 + m, :], r.w2[0])
        z += matmul(r.h3[L + m0 : L + m0 + m, :], r.w2[1])
        z += matmul(r.h3[2 * L + m0 : 2 * L + m0 + m, :], r.w2[2])
        r.pre2[m0 : m0 + m, :] = z
        copies.start(("pre2", k))
        zm = z * wide(r.ownp[L + 1 + m0 : L + 1 + m0 + m, :], width)
        sums = [sums[0] + column_sum(zm), sums[1] + column_sum(zm * z)]
    row = jnp.concatenate(sums, axis=1)
    r.spread[...] = jnp.broadcast_to(row[None], r.spread.shape)
    copies.wait("h3", "pre2")


def third_kernel(r, copies):
    groups, rows, cols, width = r.out.shape
    S = cols + 8
    L = groups * S
    n = r.mom1[2:3, :]
    t = jnp.sum(r.tot2[...], axis=0)
    c2, i2 = moments(t[:, :width], t[:, width:], n)
    cp, ip = r.mom1[3:4, :], r.mom1[4:5, :]
    r.mom2[...] = jnp.concatenate([c2, i2, cp, ip, jnp.zeros((4, width), f32)], axis=0)
    sums = [jnp.zeros((1, width), f32)] * 3
    both_shift = r.shift2[...] + r.shiftp[...]
    copies.wait("pre2", "prep", "cotq")
    total = r.grad.shape[0] // S
    for line in range(total):
        at = line * S
        shifted = slice(L + 1 + at, L + 1 + at + S)
        n2 = (r.pre2[at : at + S, :] - c2) * i2
        np_ = (r.prep[shifted, :] - cp) * ip
        v = n2 * r.gain2[...] + np_ * r.gainp[...] + both_shift
        mask = wide(r.maskp[shifted, :], width)
        own = wide(r.ownp[shifted, :], width)
        t = gelu_parts(v)
        r.field[at : at + S, :] = 0.5 * v * (1.0 + t) * mask
        g = gelu_slope(v, t) * mask * r.cotq[at : at + S, :]
        r.grad[at : at + S, :] = g
        g = g * own
        new = [column_sum(g * n2), column_sum(g), column_sum(g * np_)]
        sums = [a + b for a, b in zip(sums, new)]
        if (line + 1) % (total // 2) == 0:
            copies.start(("grad", (line + 1) // (total // 2) - 1))
    for i in range(rows):
        for g in range(groups):
            at = (i + 1) * L + g * S + 1
            r.out[g, i, :, :] = r.field[at : at + cols, :].astype(bf16)
    copies.start("out")
    row = jnp.concatenate(sums, axis=1)
    r.spread[...] = jnp.broadcast_to(row[None], r.spread.shape)
    copies.wait("grad", "out")


def halves(r, source, at, frame, to, rows_w):
    half = r.mine.shape[1]
    bit = r.bits[0] == 1
    for m0, m in chunks(rows_w, 96):
        own = wide(r.ownp[frame + m0 : frame + m0 + m, :], half)
        low = (source[at + m0 : at + m0 + m, :half] * own).astype(bf16)
        high = (source[at + m0 : at + m0 + m, half:] * own).astype(bf16)
        r.mine[to + m0 : to + m0 + m, :] = jnp.where(bit, high, low)
        r.theirs[to + m0 : to + m0 + m, :] = jnp.where(bit, low, high)


def fourth_kernel(r, copies):
    width = r.gain2.shape[1]
    Q = r.pre2.shape[0]
    rows_w = r.gpu.shape[0]
    L = (Q - rows_w) // 3
    n = r.mom1[2:3, :]
    c2, i2, cp, ip = (r.mom2[k : k + 1, :] for k in range(4))
    t3 = jnp.sum(r.tot3[...], axis=0)
    gg2, gs, ggp = (t3[:, k * width : (k + 1) * width] for k in range(3))
    r.gain_second[...], r.shift_second[...], r.gain_proj[...], r.shift_proj[...] = gg2, gs, ggp, gs
    copies.wait("grad", "pre2", "prep")
    for m0, m in chunks(Q, L):
        shifted = slice(L + 1 + m0, L + 1 + m0 + m)
        mask = wide(r.maskp[shifted, :], width) / n
        n2 = (r.pre2[m0 : m0 + m, :] - c2) * i2
        np_ = (r.prep[shifted, :] - cp) * ip
        g = r.grad[m0 : m0 + m, :]
        r.gq[m0 : m0 + m, :] = (r.gain2[...] * i2) * (g - mask * (gs + n2 * gg2))
        r.gpq[m0 : m0 + m, :] = (r.gainp[...] * ip) * (g - mask * (gs + np_ * ggp))
    r.gq[Q:, :] = jnp.zeros((r.gq.shape[0] - Q, width), f32)
    copies.start("gq")
    for m0, m in chunks(rows_w, 96):
        r.gpu[m0 : m0 + m, :] = r.gpq[L + 1 + m0 : L + 1 + m0 + m, :].astype(bf16)
    copies.start("gpu")
    halves(r, r.gq, L, 2 * L + 1, 0, rows_w)
    halves(r, r.gpq, L - 1, 2 * L, rows_w, rows_w)
    copies.wait("gpu", "gq")


def hidden_kernel(r, copies):
    width = r.gain.shape[1]
    Q = r.gq.shape[0] - 8
    L = (r.keep.shape[0] - Q) // 2
    center, inv = r.mom1[0:1, :], r.mom1[1:2, :]
    copies.wait("gq")
    for m0, m in chunks(Q, 176):
        for b in range(3):
            r.g3[m0 : m0 + m, b * width : (b + 1) * width] = r.gq[m0 + b : m0 + b + m, :].astype(bf16)
    U = r.act.shape[0]
    for a in range(3):
        copies.wait(("w2", a))
        gh = jnp.zeros((U, width), f32)
        for b in range(3):
            gh += matmul_nt(
                r.g3[L * a : L * a + U, b * width : (b + 1) * width],
                r.w2[2 - a, (2 - b) * width : (3 - b) * width, :],
            )
        r.act[...] = gh if a == 0 else r.act[...] + gh
    copies.wait("keep")
    sums = [jnp.zeros((1, width), f32)] * 2
    for m0, m in chunks(U, L):
        frame = slice(2 * L + 2 + m0, 2 * L + 2 + m0 + m)
        n1 = (r.keep[frame, :] - center) * inv
        v = n1 * r.gain[...] + r.shift[...]
        mask = wide(r.maskp[frame, :], width)
        g = gelu_slope(v, gelu_parts(v)) * mask * r.act[m0 : m0 + m, :]
        r.act[m0 : m0 + m, :] = g
        r.normed[m0 : m0 + m, :] = n1 * mask
        g = g * wide(r.ownp[frame, :], width)
        sums = [sums[0] + column_sum(g * n1), sums[1] + column_sum(g)]
    row = jnp.concatenate(sums, axis=1)
    r.spread[...] = jnp.broadcast_to(row[None], r.spread.shape)


def split_store(r, rows, lanes, unit, first):
    quarter = unit // 4
    for k in range(rows // unit):
        for bit, base, sent, kept in ((1, 0, r.sent_a, r.kept_a), (2, 2 * quarter, r.sent_b, r.kept_b)):
            keep = pl.multiple_of(k * unit + base + r.bits[bit] * quarter, quarter)
            send = pl.multiple_of(k * unit + base + (1 - r.bits[bit]) * quarter, quarter)
            sent[first + k] = r.acc[pl.ds(send, quarter), lanes].astype(bf16)
            kept[first + k] = r.acc[pl.ds(keep, quarter), lanes]


def beside(out, grad, offsets):
    rows_w, half = grad.shape
    out[...] = jnp.zeros(out.shape, bf16)
    for k, at in enumerate(offsets):
        out[at : at + rows_w, k * half : (k + 1) * half] = grad


def weights_second_kernel(r, copies):
    width = r.h3.shape[1] // 3
    half = r.near.shape[1]
    cin = r.xe.shape[1] // 3
    rows_w = r.near.shape[0] // 2
    L = (r.h3.shape[0] - rows_w) // 5
    per = width // cin
    beside(r.g_near, r.near[:rows_w, :], (0, L, 2 * L))
    beside(r.g_far, r.far[:rows_w, :], (0, L, 2 * L))
    window = slice(L, L + rows_w + 2 * L)
    for b in range(3):
        lanes = slice(b * width, (b + 1) * width)
        copies.wait(("h3", b), ("h3_far", b))
        r.acc[...] = matmul_tn(r.h3[window, lanes], r.g_near[...]) + matmul_tn(r.h3_far[window, lanes], r.g_far[...])
        for a in range(3):
            split_store(r, width, slice(a * half, (a + 1) * half), cin, (3 * a + b) * per)
            copies.start(("kept_a", 3 * a + b), ("kept_b", 3 * a + b))
    at = 2 * L
    copies.wait("xe", "xe_far")
    middle = slice(cin, 2 * cin)
    r.acc[0:cin, 0:half] = matmul_tn(r.xe[at : at + rows_w, middle], r.near[rows_w:, :]) + matmul_tn(
        r.xe_far[at : at + rows_w, middle], r.far[rows_w:, :]
    )
    split_store(r, cin, slice(0, half), cin, 9 * per)
    copies.start(("kept_a", 9), ("kept_b", 9))
    copies.wait("kept_a", "kept_b")


def first_back(r, gg, gs, count):
    width = r.gain.shape[1]
    U = r.act.shape[0]
    L = U - r.rows_w
    inv, n = r.mom1[1:2, :], r.mom1[2:3, :]
    gg, gs = gg / n, gs / n
    scale = r.gain[...] * inv
    r.gf[0:8, :] = jnp.zeros((8, width), f32)
    r.gf[8 + count :, :] = jnp.zeros((r.gf.shape[0] - 8 - count, width), f32)
    for m0, m in chunks(count, L):
        mask = wide(r.maskp[2 * L + 2 + m0 : 2 * L + 2 + m0 + m, :], width)
        back = mask * gs + r.normed[m0 : m0 + m, :] * gg
        r.gf[8 + m0 : 8 + m0 + m, :] = scale * (r.act[m0 : m0 + m, :] - back)


def fifth_kernel(r, copies):
    width = r.gain.shape[1]
    r.rows_w = r.mine.shape[0]
    L = r.act.shape[0] - r.rows_w
    t4 = jnp.sum(r.tot4[...], axis=0)
    r.gain_first[...], r.shift_first[...] = t4[:, :width], t4[:, width:]
    first_back(r, t4[:, :width], t4[:, width:], r.rows_w)
    halves(r, r.gf, 6, 2 * L, 0, r.rows_w)


def weights_first_kernel(r, copies):
    rows_w, half = r.near.shape
    cin = r.xe.shape[1] // 3
    L = (r.xe.shape[0] - rows_w) // 5
    beside(r.g_near, r.near[...], (0, L))
    beside(r.g_far, r.far[...], (0, L))
    copies.wait("xe", "xe_far")
    window = slice(2 * L, 2 * L + rows_w)
    r.acc[:, :half] = matmul_tn(r.xe[window, :], r.near[...]) + matmul_tn(r.xe_far[window, :], r.far[...])
    split_store(r, 3 * cin, slice(0, half), cin, 3)
    copies.start(("kept_a", 1), ("kept_b", 1))
    copies.wait("xo", "xo_far")
    window = slice(2 * L, 3 * L + rows_w)
    r.acc[...] = matmul_tn(r.xo[window, :], r.g_near[...]) + matmul_tn(r.xo_far[window, :], r.g_far[...])
    for k, a in enumerate((0, 2)):
        split_store(r, 3 * cin, slice(k * half, (k + 1) * half), cin, 3 * a)
        copies.start(("kept_a", a), ("kept_b", a))
    copies.wait("kept_a", "kept_b")


def inputs_kernel(r, copies):
    width = r.gpu.shape[1]
    groups, rows, cols = r.out.shape[0], r.out.shape[1] // 2, r.out.shape[2] // 2
    cin = r.out.shape[3]
    M = r.gpu.shape[0]
    S = cols + 8
    L = groups * S
    lines = r.lines
    U = r.act.shape[0]
    r.rows_w = M
    copies.wait("act", "normed")
    first_back(r, r.gg[...], r.gs[...], U)
    for m0, m in chunks(U, 144):
        r.gu[m0 : m0 + m, :width] = r.gf[8 + m0 : 8 + m0 + m, :].astype(bf16)
        r.gu[m0 : m0 + m, width:] = r.gf[9 + m0 : 9 + m0 + m, :].astype(bf16)
    copies.wait("gpu", "w1", "wp")

    def tap(m0, m, a, b):
        di, dj = (1 if a == 0 else 0), (1 if b == 0 else 0)
        return matmul_nt(
            r.gu[di * L + m0 : di * L + m0 + m, dj * width : (dj + 1) * width],
            r.w1[a, b * cin : (b + 1) * cin, :],
        )

    for m0, m in chunks(M, 2 * L):
        pieces = {
            (0, 0): tap(m0, m, 1, 1) + matmul_nt(r.gpu[m0 : m0 + m, :], r.wp[...]),
            (0, 1): tap(m0, m, 1, 2) + tap(m0, m, 1, 0),
            (1, 0): tap(m0, m, 2, 1) + tap(m0, m, 0, 1),
            (1, 1): tap(m0, m, 2, 2) + tap(m0, m, 2, 0) + tap(m0, m, 0, 2) + tap(m0, m, 0, 0),
        }
        for (ro, co), v in pieces.items():
            for k in range(m // S):
                line = m0 // S + k
                i, g = line // groups, line % groups
                for h in range(lines.shape[0]):
                    lines[h, (2 * i + ro) * groups + g, pl.ds(co, cols, stride=2), :] = v[
                        k * S : k * S + cols, h * 128 : (h + 1) * 128
                    ]
    for n in range(2 * rows):
        for g in range(groups):
            for h in range(lines.shape[0]):
                r.out[g, n, :, h * 128 : (h + 1) * 128] = lines[h, n * groups + g].astype(bf16)
    copies.start("out")
    copies.wait("out")


def place(pieces, spots, groups, like, into=None):
    total, h, m = pieces[0].shape
    extra = len(like) - 1
    size = like[0][0] // groups
    jobs = [(t * size, size, 0, t * size) for t in range(groups)] + [(groups * size, 1, 1, 0)] * extra
    more = list(into or [])
    n = len(pieces)

    def body(spots_ref, *refs):
        sources, outs = refs[:n], refs[n + len(more) : n + len(more) + 1 + extra]
        narrow, full, sems = refs[n + len(more) + 1 + extra :]
        reads, writes = [], []
        for p in range(n):
            rows = pl.ds(pl.multiple_of(spots_ref[2 * p] * h, h), h)
            lanes = pl.ds(pl.multiple_of(spots_ref[2 * p + 1] * m, m), m)
            for k, (at, size, which, to) in enumerate(jobs):
                units = pl.ds(at, size)
                reads.append(pltpu.make_async_copy(sources[p].at[units], narrow.at[p, units], sems.at[0, p, k]))
                target = outs[which].at[pl.ds(to, size), rows, lanes]
                writes.append(pltpu.make_async_copy(full.at[p, units], target, sems.at[1, p, k]))
        for read in reads:
            read.start()
        for p in range(n):
            for k, (at, size, _, _) in enumerate(jobs):
                reads[p * len(jobs) + k].wait()
                full[p, at : at + size] = narrow[p, at : at + size].astype(f32)
                writes[p * len(jobs) + k].start()
        for write in writes:
            write.wait()

    hbm = pl.BlockSpec(memory_space=pltpu.HBM)
    return pl.pallas_call(
        body,
        out_shape=[shape(dims) for dims in like],
        in_specs=[pl.BlockSpec(memory_space=pltpu.SMEM)] + [hbm] * (n + len(more)),
        out_specs=[hbm] * (1 + extra),
        scratch_shapes=[
            pltpu.VMEM((n, total, h, m), bf16),
            pltpu.VMEM((n, total, h, m), f32),
            pltpu.SemaphoreType.DMA((2, n, len(jobs))),
        ],
        input_output_aliases={1 + n + k: k for k in range(len(more))},
        compiler_params=pltpu.CompilerParams(vmem_limit_bytes=60 * 1024 * 1024),
        cost_estimate=pl.CostEstimate(flops=20000000000, bytes_accessed=0, transcendentals=0),
    )(spots, *pieces, *more)


def halve_kernel(r, copies):
    for p in range(r.count):
        kept, got = getattr(r, f"kept{p}"), getattr(r, f"got{p}")
        copies.wait(f"kept{p}", f"got{p}")
        to_send, to_keep = getattr(r, f"sent{p}"), getattr(r, f"left{p}")
        bit = r.bits[r.steps[p]] == 1
        h = kept.shape[1] // 2
        for t in range(kept.shape[0]):
            total = kept[t] + got[t].astype(f32)
            low, high = total[:h], total[h:]
            to_send[t] = jnp.where(bit, low, high).astype(bf16)
            to_keep[t] = jnp.where(bit, high, low)
        copies.start(f"sent{p}", f"left{p}")
    copies.wait(*(name for name in copies.jobs if name[:4] in ("sent", "left")))


def halve(bits, pairs, steps, cost):
    ins = dict(bits=bits)
    for p, (kept, got) in enumerate(pairs):
        ins[f"kept{p}"], ins[f"got{p}"] = kept, got
    taps, n, m = pairs[0][0].shape
    dims = (taps, n // 2, m)
    names = [str(p) for p in range(len(pairs))]
    outs = {}
    for name in names:
        outs["sent" + name], outs["left" + name] = shape(dims, bf16), shape(dims)

    def body(r, copies):
        r.count, r.steps = len(pairs), steps
        halve_kernel(r, copies)

    far_in = tuple(n for n in ins if n != "bits")
    out = call(body, ins, outs, far_in=far_in, far_out=tuple(outs), smem=("bits",), cost=cost, limit=60)
    return [(out["sent" + name], out["left" + name]) for name in names]


def shifted(value, axis, steps):
    count = lax.axis_size(axis)
    first, last = (max(0, -steps), min(count, count - steps))
    return lax.ppermute(value, axis, [(source, source + steps) for source in range(first, last)])


def gather_sum(spread):
    return lax.all_to_all(spread, axes, 0, 0)


def bit_of(axis, step):
    return (lax.axis_index(axis) // step) % 2


def partner(value, axis, step):
    count = lax.axis_size(axis)
    return lax.ppermute(value, axis, [(i, i ^ step) for i in range(count)])


def steps_of(axis):
    count, step, out = lax.axis_size(axis), 1, []
    while step < count:
        out.append((axis, step))
        step *= 2
    return out


def split(total, axis, step):
    n = total.shape[1] // 2
    bit = bit_of(axis, step) == 1
    low, high = total[:, :n], total[:, n:]
    return jnp.where(bit, low, high).astype(bf16), jnp.where(bit, high, low)


def joined(value, other, axis, step, dim=1):
    bit = bit_of(axis, step) == 1
    return jnp.concatenate([jnp.where(bit, other, value), jnp.where(bit, value, other)], axis=dim)


class Tree:
    def __init__(self, parts, bits, plane, rest, core):
        self.bits, self.place = bits, {step: k for k, step in enumerate([core, *plane, *rest])}
        self.sent_a, self.kept_a, self.sent_b, self.kept_b = parts
        self.a, self.b, self.rest, self.core = plane, plane[::-1], rest, core
        p, n = len(plane), len(rest)
        self.stages = [("plane", k) for k in range(p)] + [("rest", k) for k in range(n)]
        self.stages += [("rest_join", k) for k in reversed(range(n))] + [("plane_join", k) for k in reversed(range(p))]

    def next(self):
        return self.stages[0] if self.stages else None

    def start(self):
        kind, k = self.stages[0]
        if kind == "plane":
            self.got = partner(self.sent_a, *self.a[k]), partner(self.sent_b, *self.b[k])
        elif kind == "rest":
            self.got = (partner(self.sent, *self.rest[k]),)
        elif kind == "rest_join":
            self.got = (partner(self.value, *self.rest[k]),)
        elif kind == "plane_join":
            self.got = partner(self.value_a, *self.a[k]), partner(self.value_b, *self.b[k])

    def finish(self, cost=0):
        kind, k = self.stages.pop(0)
        if kind == "plane":
            pairs = [(self.kept_a, self.got[0]), (self.kept_b, self.got[1])]
            nexts = [order[k + 1] for order in (self.a, self.b) if k + 1 < len(order)]
            if nexts and cost:
                pairs = halve(self.bits, pairs, [self.place[step] for step in nexts], cost)
                (self.sent_a, self.kept_a), (self.sent_b, self.kept_b) = pairs
                return
            total_a, total_b = (kept + got.astype(f32) for kept, got in pairs)
            if nexts:
                self.sent_a, self.kept_a = split(total_a, *nexts[0])
                self.sent_b, self.kept_b = split(total_b, *nexts[1])
            else:
                self.taps = total_a.shape[0]
                self.split_rest(jnp.concatenate([total_a, total_b], axis=0), 0)
        elif kind == "rest":
            self.split_rest(self.kept + self.got[0].astype(f32), k + 1)
        elif kind == "rest_join":
            self.value = joined(self.value, self.got[0], *self.rest[k])
            self.value_a, self.value_b = self.value[: self.taps], self.value[self.taps :]
        elif kind == "plane_join":
            self.value_a = joined(self.value_a, self.got[0], *self.a[k])
            self.value_b = joined(self.value_b, self.got[1], *self.b[k])

    def split_rest(self, total, k):
        if k < len(self.rest):
            self.sent, self.kept = split(total, *self.rest[k])
        else:
            self.value = total.astype(bf16)


def lockstep(*trees, beside=()):
    for t in trees:
        t.start()
    got, beside = lax.optimization_barrier(([t.got for t in trees], beside))
    for t, g in zip(trees, got):
        t.got = g
        t.finish()
    return beside


def on_device(inputs, w_first, gain_first, shift_first, w_second, gain_second, shift_second, w_proj, gain_proj, shift_proj, valid_mask, cotangent):
    groups, rows_in, cols_in, cin = inputs.shape
    rows, cols = rows_in // 2, cols_in // 2
    width = w_first.shape[3]
    half = width // 2
    S = cols + 8
    L = groups * S
    devices = lax.axis_size("rows") * lax.axis_size("cols") * lax.axis_size("grp")
    plane = steps_of("cols")
    core = steps_of("rows")[0]
    rest = steps_of("rows")[1:] + steps_of("grp")
    bits = jnp.stack([bit_of(*step) for step in (core, *plane, *rest)]).astype(jnp.int32)
    w1 = w_first.reshape(3, 3 * cin, width)
    w2 = w_second.reshape(3, 3 * width, width)
    as_row = lambda v: v.reshape(1, -1)
    own = jnp.broadcast_to(valid_mask.astype(bf16)[..., None], valid_mask.shape + (128,))
    MP, MQ, MU, MW = (rows + 5) * L, (rows + 3) * L, (rows + 1) * L, rows * L
    px = lambda m, k: 2 * m * k * width
    vec = lambda k: shape((1, k * width))
    all_devices = lambda k: shape((devices, 1, k))
    g1, b1, g2, b2, gp, bp = map(
        as_row, (gain_first, shift_first, gain_second, shift_second, gain_proj, shift_proj)
    )

    top1 = shifted(inputs[:, -1:], "rows", 1)
    me, count = lax.axis_index("rows"), lax.axis_size("rows")
    flags = jnp.stack([me > 0, me < count - 1]).astype(jnp.int32)
    flat_rows = shape((over * groups * cols_in + (width // 256 + 1) * rim * groups * cols, 256), bf16)
    packed = call(
        vertical_kernel,
        dict(flags=flags, x=inputs, cot=cotangent, own=own),
        dict(down=flat_rows) if count == 2 else dict(down=flat_rows, up=flat_rows),
        far_in=("x", "cot"),
        smem=("flags",),
        parts=dict(x=end_parts(rows_in, over), cot=end_parts(rows, rim)),
    )
    if count == 2:
        top = bot = lax.ppermute(packed["down"], "rows", [(0, 1), (1, 0)])
    else:
        top, bot = shifted(packed["down"], "rows", 1), shifted(packed["up"], "rows", -1)
    lft1 = shifted(jnp.concatenate([top1[:, :, -1:], inputs[:, :, -1:]], axis=1), "cols", 1)
    (top, bot), lft1 = lax.optimization_barrier(((top, bot), lft1))
    lines = (rows_in + 2 * over) * groups, (rows + 2 * rim) * groups, (rows + 3) * groups
    n_strip = over * lines[0] + (rim + 1) // 2 * lines[1] + width // 128 * lines[2]
    n_strip = -(-n_strip // 16) * 16
    near = dict(flags=flags, x=inputs, cot=cotangent, own=own, top=top, bot=bot)
    strips = call(
        strips_kernel,
        near,
        dict(right=shape((n_strip, 256), bf16), left=shape((n_strip, 256), bf16)),
        dict(
            raw_x=pltpu.VMEM((cin // 128, lines[0] * cols_in, 128), f32),
            raw_m=pltpu.VMEM((1, lines[1] * cols, 128), f32),
            raw_c=pltpu.VMEM((width // 128, lines[2] * cols, 128), f32),
            flat=pltpu.VMEM((n_strip, 256), f32),
        ),
        smem=("flags",),
    )
    lft, rgt = shifted(strips["right"], "cols", 1), shifted(strips["left"], "cols", -1)
    lft1, _ = lax.optimization_barrier((lft1, strips["right"]))
    stats = call(
        stats_kernel,
        dict(x=inputs, top=top1, lft=lft1, own=own, w1=w1, wp=w_proj),
        dict(spread=all_devices(4 * width + 128)),
        dict(
            raw=pltpu.VMEM((cin // 128, (rows_in + 1) * groups, cols_in + 8, 128), f32),
            xe=pltpu.VMEM((rows * groups * cols, 3 * cin), bf16),
            xo=pltpu.VMEM(((rows + 1) * groups * cols, 3 * cin), bf16),
        ),
    )
    tot1 = gather_sum(stats["spread"])

    first = call(
        first_kernel,
        dict(**near, lft=lft, rgt=rgt, w1=w1, wp=w_proj),
        dict(
            pre1=shape((MP, width)),
            prep=shape((MP, width)),
            xe=shape((MP, 3 * cin), bf16),
            xo=shape((MP + L, 3 * cin), bf16),
            ownp=shape((MP, 128)),
            maskp=shape((MP, 128)),
            cotq=shape((MQ, width)),
        ),
        dict(
            raw_x=pltpu.VMEM((cin // 128, lines[0] * (cols_in + 24), 128), f32),
            raw_m=pltpu.VMEM((1, lines[1] * (cols + 16), 128), f32),
            raw_c=pltpu.VMEM((width // 128, lines[2] * (cols + 16), 128), f32),
            flat=pltpu.VMEM((n_strip, 256), f32),
        ),
        far_in=("w1", "wp"),
        far_out=("xe", "xo", "pre1", "prep", "cotq"),
        smem=("flags",),
        cost=20000000000,
        parts=dict(pre1=row_parts(MP, 3), prep=row_parts(MP, 3)),
    )
    xe, xo, ownp, maskp = first["xe"], first["xo"], first["ownp"], first["maskp"]
    far_xe, far_xo = partner(xe, *core), partner(xo, *core)

    second = call(
        second_kernel,
        dict(pre1=first["pre1"], tot1=tot1, gain=g1, shift=b1, maskp=maskp, ownp=ownp, w2=w2),
        dict(h3=shape((MP, 3 * width), bf16), pre2=shape((MQ, width)), spread=all_devices(2 * width), mom1=shape((8, width))),
        dict(hid=pltpu.VMEM((MP + 8, width), f32)),
        far_in=("pre1", "w2"),
        far_out=("h3", "pre2"),
        parts=dict(pre2=row_parts(MQ, 3)),
    )
    h3, pre2, mom1 = second["h3"], second["pre2"], second["mom1"]
    tot2 = gather_sum(second["spread"])
    far_h3 = partner(h3, *core)

    third = call(
        third_kernel,
        dict(
            pre2=pre2, prep=first["prep"], mom1=mom1, tot2=tot2, gain2=g2, shift2=b2, gainp=gp, shiftp=bp,
            maskp=maskp, ownp=ownp, cotq=first["cotq"],
        ),
        dict(
            out=shape((groups, rows, cols, width), bf16),
            grad=shape((MQ, width)),
            spread=all_devices(3 * width),
            mom2=shape((8, width)),
        ),
        dict(field=pltpu.VMEM((MQ, width), f32)),
        far_in=("pre2", "prep", "cotq"),
        far_out=("out", "grad"),
        parts=dict(grad=row_parts(MQ, 2)),
    )
    mom2 = third["mom2"]
    tot3 = gather_sum(third["spread"])

    fourth = call(
        fourth_kernel,
        dict(
            bits=bits, pre2=pre2, prep=first["prep"], mom1=mom1, mom2=mom2, tot3=tot3, gain2=g2, gainp=gp,
            grad=third["grad"], maskp=maskp, ownp=ownp,
        ),
        dict(
            mine=shape((2 * MW, half), bf16),
            theirs=shape((2 * MW, half), bf16),
            gq=shape((MQ + 8, width)),
            gpu=shape((MW, width), bf16),
            gain_second=vec(1),
            shift_second=vec(1),
            gain_proj=vec(1),
            shift_proj=vec(1),
        ),
        dict(gpq=pltpu.VMEM((MQ, width), f32)),
        far_in=("pre2", "prep", "grad"),
        far_out=("gpu", "gq"),
        smem=("bits",),
    )
    far2 = partner(fourth["theirs"], *core)

    def chunk_shapes(taps):
        dims = (taps, cin // 4, half)
        return dict(sent_a=shape(dims, bf16), kept_a=shape(dims), sent_b=shape(dims, bf16), kept_b=shape(dims))

    per = width // cin
    taps2 = 9 * per + 1
    second_parts = call(
        weights_second_kernel,
        dict(bits=bits, h3=h3, h3_far=far_h3, xe=xe, xe_far=far_xe, near=fourth["mine"], far=far2),
        chunk_shapes(taps2),
        dict(
            acc=pltpu.VMEM((width, 3 * half), f32),
            g_near=pltpu.VMEM((MW + 2 * L, 3 * half), bf16),
            g_far=pltpu.VMEM((MW + 2 * L, 3 * half), bf16),
        ),
        far_in=("h3", "h3_far", "xe", "xe_far"),
        far_out=("kept_a", "kept_b"),
        smem=("bits",),
        parts=dict(
            h3=lane_parts(3 * width, 3),
            h3_far=lane_parts(3 * width, 3),
            kept_a=row_parts(taps2 - 1, 9) + [(9, (pl.ds(taps2 - 1, 1),))],
            kept_b=row_parts(taps2 - 1, 9) + [(9, (pl.ds(taps2 - 1, 1),))],
        ),
    ).values()
    gq, *second_parts = lax.optimization_barrier((fourth["gq"], *second_parts))

    tree2 = Tree(second_parts, bits, plane, rest, core)
    tree2.start()
    hidden = call(
        hidden_kernel,
        dict(gq=gq, w2=w2, keep=first["pre1"], mom1=mom1, gain=g1, shift=b1, maskp=maskp, ownp=ownp),
        dict(act=shape((MU, width)), normed=shape((MU, width)), spread=all_devices(2 * width)),
        dict(g3=pltpu.VMEM((MQ, 3 * width), bf16)),
        far_in=("gq", "w2", "keep"),
        parts=dict(w2=[(k, (pl.ds(2 - k, 1),)) for k in range(3)]),
    )
    tot4 = gather_sum(hidden["spread"])
    fifth = call(
        fifth_kernel,
        dict(bits=bits, act=hidden["act"], normed=hidden["normed"], mom1=mom1, tot4=tot4, gain=g1, maskp=maskp, ownp=ownp),
        dict(mine=shape((MW, half), bf16), theirs=shape((MW, half), bf16), gain_first=vec(1), shift_first=vec(1)),
        dict(gf=pltpu.VMEM((MU + 16, width), f32)),
        smem=("bits",),
    )
    tree2.got, theirs = lax.optimization_barrier((tree2.got, fifth["theirs"]))
    far1 = partner(theirs, *core)
    tree2.finish(20000000000)
    near1, tree2.sent_a, tree2.sent_b = lax.optimization_barrier((fifth["mine"], tree2.sent_a, tree2.sent_b))
    tree2.start()
    first_parts = call(
        weights_first_kernel,
        dict(bits=bits, xe=xe, xo=xo, xe_far=far_xe, xo_far=far_xo, near=near1, far=far1),
        chunk_shapes(9),
        dict(
            acc=pltpu.VMEM((3 * cin, 2 * half), f32),
            g_near=pltpu.VMEM((MW + L, 2 * half), bf16),
            g_far=pltpu.VMEM((MW + L, 2 * half), bf16),
        ),
        far_in=("xe", "xe_far", "xo", "xo_far"),
        far_out=("kept_a", "kept_b"),
        smem=("bits",),
        parts=dict(kept_a=row_parts(9, 3), kept_b=row_parts(9, 3)),
    ).values()
    tree2.got, *first_parts = lax.optimization_barrier((tree2.got, *first_parts))
    tree2.finish()
    tree1 = Tree(first_parts, bits, plane, rest, core)

    grad_inputs = call(
        inputs_kernel,
        dict(
            act=hidden["act"], normed=hidden["normed"], gpu=fourth["gpu"], w1=w1, wp=w_proj, mom1=mom1, gain=g1, maskp=maskp,
            gg=fifth["gain_first"], gs=fifth["shift_first"],
        ),
        dict(out=shape((groups, rows_in, cols_in, cin), bf16)),
        dict(
            lines=pltpu.VMEM((cin // 128, rows_in * groups, cols_in, 128), f32),
            gf=pltpu.VMEM((MU + 16, width), f32),
            gu=pltpu.VMEM((MU, 2 * width), bf16),
        ),
        far_in=("act", "normed", "gpu", "w1", "wp"),
        far_out=("out",),
        cost=10000000000,
    )["out"]
    grad_inputs = lockstep(tree2, tree1, beside=grad_inputs)
    while tree2.next() != ("plane_join", 0):
        lockstep(tree2, tree1)

    side, low, high = (bits[tree2.place[step]] for step in (core, plane[0], plane[-1]))
    own_spots = jnp.stack([low, side, 2 + high, side, low, 1 - side, 2 + high, 1 - side])
    far_spots = jnp.stack([1 - low, side, 3 - high, side, 1 - low, 1 - side, 3 - high, 1 - side])
    swap = lambda values: [partner(v, *core) for v in values]
    first_dims = [(9, cin, width)]
    second_dims = [(9 * per, cin, width), (1, cin, width)]

    tree2.start()
    own2 = [tree2.value_a, tree2.value_b]
    own2 += swap(own2)
    while tree1.next() != ("plane_join", 0):
        tree1.start()
        if tree1.next() != ("plane_join", 1):
            tree1.finish()
        else:
            placed2 = place(own2, own_spots, 3, second_dims)
            tree1.got, tree2.got, placed2 = lax.optimization_barrier((tree1.got, tree2.got, placed2))
            tree1.finish()
    tree1.start()
    own1 = [tree1.value_a, tree1.value_b]
    own1 += swap(own1)
    far2 = [*tree2.got, *swap(tree2.got)]
    placed1 = place(own1, own_spots, 3, first_dims)
    grad_w2, grad_wp = place(far2, far_spots, 3, second_dims, placed2)
    tree1.got, grad_w2, grad_wp, placed1 = lax.optimization_barrier((tree1.got, grad_w2, grad_wp, placed1))
    (grad_w1,) = place([*tree1.got, *swap(tree1.got)], far_spots, 3, first_dims, placed1)

    return (
        third["out"],
        grad_inputs,
        grad_w1.reshape(w_first.shape),
        fifth["gain_first"].reshape(width),
        fifth["shift_first"].reshape(width),
        grad_w2.reshape(w_second.shape),
        fourth["gain_second"].reshape(width),
        fourth["shift_second"].reshape(width),
        grad_wp.reshape(w_proj.shape),
        fourth["gain_proj"].reshape(width),
        fourth["shift_proj"].reshape(width),
    )


def solution(mesh):
    spread = P("grp", "rows", "cols", None)
    return jax.shard_map(
        on_device,
        mesh=mesh,
        in_specs=(spread,) + (P(),) * 9 + (P("grp", "rows", "cols"), spread),
        out_specs=(spread, spread) + (P(),) * 9,
        check_vma=False,
    )
```

```python
import functools

import jax
import jax.numpy as jnp
from jax import lax
from jax.experimental import pallas as pl
from jax.experimental.pallas import tpu as pltpu
from jax.sharding import PartitionSpec as P

epsilon = 1e-05
axes = ("rows", "cols", "grp")
bf16 = jnp.bfloat16
f32 = jnp.float32
inner = 0.7978845608028654
cubic = 0.044715
over = 6
CHUNKS = "sent_a", "kept_a", "sent_b", "kept_b"
rim = 3


class Refs:
    def __init__(self, named):
        self.__dict__.update(named)


class Copies:
    def __init__(self, parts, pairs, sems):
        self.jobs = {}
        for k, (name, index) in enumerate(parts):
            source, target = pairs[name]
            if index:
                source, target = source.at[index[1]], target.at[index[1]]
            self.jobs.setdefault(name, []).append(pltpu.make_async_copy(source, target, sems.at[k]))

    def start(self, *names):
        for name, *which in map(named, names):
            for job in self.jobs[name][slice(*which) if which else slice(None)]:
                job.start()

    def start_all(self, names):
        for k in range(max((len(self.jobs[n]) for n in names), default=0)):
            for n in names:
                if k < len(self.jobs[n]):
                    self.jobs[n][k].start()

    def wait(self, *names):
        for name, *which in map(named, names):
            for job in self.jobs[name][slice(*which) if which else slice(None)]:
                job.wait()


def named(name):
    return (name,) if isinstance(name, str) else (name[0], name[1], name[1] + 1)


def row_parts(total, count):
    size = total // count
    return [(k, (pl.ds(k * size, size),)) for k in range(count)]


def end_parts(total, size):
    return [(k, (slice(None), pl.ds(at, size))) for k, at in enumerate((0, total - size))]


def cuts(*at):
    return [(k, (pl.ds(a, b - a),)) for k, (a, b) in enumerate(zip(at, at[1:]))]


def lane_parts(total, count, rows=slice(None)):
    size = total // count
    return [(k, (rows, pl.ds(k * size, size))) for k in range(count)]


def call(body, ins, outs, scratch=None, far_in=(), far_out=(), smem=(), parts=None, limit=52, cost=0):
    scratch, parts = scratch or {}, parts or {}
    far = (*far_in, *far_out)
    jobs = [(name, index) for name in far for index in parts.get(name, [None])]

    def spec(name):
        if name in smem:
            return pl.BlockSpec(memory_space=pltpu.SMEM)
        return pl.BlockSpec(memory_space=pltpu.HBM if name in far else pltpu.VMEM)

    kinds = {**{n: shape(v.shape, v.dtype) for n, v in ins.items()}, **outs}

    def run(*refs):
        plain = dict(zip([*ins, *outs], refs))
        rest = refs[len(plain) :]
        buffers = dict(zip(far, rest))
        more = dict(zip(scratch, rest[len(far) :]))
        copies = None
        if far:
            pairs = {n: (plain[n], buffers[n]) if n in far_in else (buffers[n], plain[n]) for n in far}
            copies = Copies(jobs, pairs, rest[-1])
            copies.start_all(far_in)
        body(Refs({**plain, **buffers, **more}), copies)

    buffers = [pltpu.VMEM(kinds[n].shape, kinds[n].dtype) for n in far]
    sems = [pltpu.SemaphoreType.DMA((len(jobs),))] if far else []
    result = pl.pallas_call(
        run,
        out_shape=list(outs.values()),
        in_specs=[spec(n) for n in ins],
        out_specs=[spec(n) for n in outs],
        scratch_shapes=[*buffers, *scratch.values(), *sems],
        compiler_params=pltpu.CompilerParams(vmem_limit_bytes=limit * 1024 * 1024),
        cost_estimate=pl.CostEstimate(flops=cost, bytes_accessed=0, transcendentals=0),
    )(*ins.values())
    return dict(zip(outs, result))


def shape(dims, dtype=f32):
    return jax.ShapeDtypeStruct(dims, dtype)


def wide(mask, width):
    return jnp.concatenate([mask] * (width // mask.shape[1]), axis=1)


def matmul(a, b):
    return lax.dot_general(a, b, (((1,), (0,)), ((), ())), preferred_element_type=f32)


def matmul_nt(a, b):
    return lax.dot_general(a, b, (((1,), (1,)), ((), ())), preferred_element_type=f32)


def matmul_tn(a, b):
    return lax.dot_general(a, b, (((0,), (0,)), ((), ())), preferred_element_type=f32)


def gelu_parts(v):
    return jnp.tanh(inner * (v + cubic * v * v * v))


def gelu_slope(v, t):
    return 0.5 * (1.0 + t) + 0.5 * v * (1.0 - t * t) * (inner * (1.0 + 3.0 * cubic * v * v))


def column_sum(v):
    return jnp.sum(v, axis=0, keepdims=True)


def moments(total, squares, pixel_count):
    center = total / pixel_count
    spread = squares / pixel_count - center * center
    return center, lax.rsqrt(spread + epsilon)


def chunks(total, size):
    return [(at, min(size, total - at)) for at in range(0, total, size)]


def strided(ref, k, first, count, step):
    return ref[k, pl.ds(first, count, stride=step), :]


def vertical_kernel(r, copies):
    groups, width = r.x.shape[0], r.cot.shape[3]
    rows, cols = r.own.shape[1], r.own.shape[2]

    def pack(out, input_row, row, pick):
        at = 0
        for g in range(groups):
            for n in range(over):
                value = r.x[g, input_row(n)]
                out[at : at + 2 * cols, :] = pick(value, r.x[g, n])
                at += 2 * cols
        for k in range(0, width, 256):
            for g in range(groups):
                for n in range(rim):
                    lanes = slice(k, k + 256)
                    out[at : at + cols, :] = pick(r.cot[g, row(n), :, lanes], r.cot[g, n, :, lanes])
                    at += cols
        for g in range(groups):
            for n in range(rim):
                out[at : at + cols, :] = pick(wide(r.own[g, row(n)], 256), wide(r.own[g, n], 256))
                at += cols

    last = r.x.shape[1] - over
    copies.wait("x", "cot")
    if hasattr(r, "up"):
        pack(r.down, lambda n: last + n, lambda n: rows - rim + n, lambda tail, head: tail)
        pack(r.up, lambda n: last + n, lambda n: rows - rim + n, lambda tail, head: head)
    else:
        bottom = r.flags[0] == 1
        pack(r.down, lambda n: last + n, lambda n: rows - rim + n, lambda tail, head: jnp.where(bottom, head, tail))


def rim_rows(r, own, n_own, n_rim, base, cols, split):
    groups = own.shape[0]
    size = groups * n_rim * cols

    def flat(ref, g, n):
        at = [base + k * size + (g * n_rim + n) * cols for k in range(split)]
        return jnp.concatenate([ref[p : p + cols, :] for p in at], axis=1).astype(f32)

    def read(g, n):
        if n < n_rim:
            return jnp.where(r.flags[0] == 1, flat(r.top, g, n), 0.0)
        if n < n_rim + n_own:
            return own[g, n - n_rim].astype(f32)
        return jnp.where(r.flags[1] == 1, flat(r.bot, g, n - n_rim - n_own), 0.0)

    return read


def fields(r):
    groups, width = r.x.shape[0], r.cot.shape[3]
    rows, cols = r.own.shape[1], r.own.shape[2]
    base = over * groups * 2 * cols
    piece = rim * groups * cols
    blocks = width // 256
    x = rim_rows(r, r.x, 2 * rows, over, 0, 2 * cols, 1)
    mask = rim_rows(r, r.own, rows, rim, base + blocks * piece, cols, 1)
    cot = rim_rows(r, r.cot, rows, rim, base, cols, blocks)
    return x, lambda g, n: mask(g, n)[:, :128], cot


def strips_kernel(r, copies):
    groups, width = r.x.shape[0], r.cot.shape[3]
    rows, cols = r.own.shape[1], r.own.shape[2]
    x, mask, cot = fields(r)
    lines = (2 * rows + 2 * over) * groups, (rows + 2 * rim) * groups, (rows + 3) * groups
    for raw, read, first, count, w in (
        (r.raw_x, x, 0, lines[0], 2 * cols),
        (r.raw_m, mask, 0, lines[1], cols),
        (r.raw_c, cot, 2, lines[2], cols),
    ):
        for at in range(count):
            value = read(at % groups, at // groups + first)
            for k in range(raw.shape[0]):
                raw[k, at * w : (at + 1) * w, :] = value[:, k * 128 : (k + 1) * 128]
    for out, x0, m0, c0 in ((r.right, 2 * cols - over, cols - rim, cols - 2), (r.left, 0, 0, 0)):
        pieces = []
        for c in range(over):
            pieces.append([strided(r.raw_x, k, x0 + c, lines[0], 2 * cols) for k in range(2)])
        for c in range(0, rim + 1, 2):
            pieces.append([strided(r.raw_m, 0, m0 + min(c + k, rim - 1), lines[1], cols) for k in range(2)])
        for c in range(2):
            for h in range(0, width // 128, 2):
                pieces.append([strided(r.raw_c, h + k, c0 + c, lines[2], cols) for k in range(2)])
        at = 0
        for low, high in pieces:
            r.flat[at : at + low.shape[0], :] = jnp.concatenate([low, high], axis=1)
            at += low.shape[0]
        if at < r.flat.shape[0]:
            r.flat[at:, :] = jnp.zeros((r.flat.shape[0] - at, 256), f32)
        out[...] = r.flat[...].astype(bf16)


def stats_kernel(r, copies):
    groups, cin = r.x.shape[0], r.x.shape[3]
    rows, S = r.own.shape[1], r.own.shape[2]
    L = groups * S
    width = r.w1.shape[2]
    raw = r.raw
    for n in range(2 * rows + 1):
        for g in range(groups):
            line = n * groups + g
            src = (r.top[g, 0] if n == 0 else r.x[g, n - 1]).astype(f32)
            side = r.lft[g, n].astype(f32)
            for k in range(raw.shape[0]):
                raw[k, line, 7:8, :] = side[:, k * 128 : (k + 1) * 128]
                raw[k, line, 8:, :] = src[:, k * 128 : (k + 1) * 128]
    for out, n_rows, start in ((r.xe, rows, 1), (r.xo, rows + 1, 0)):
        for n in range(n_rows):
            for b in range(3):
                for k in range(raw.shape[0]):
                    parts = [
                        raw[k, (2 * n + start) * groups + g, pl.ds(7 + b, S, stride=2), :]
                        for g in range(groups)
                    ]
                    at = b * cin + k * 128
                    out[n * L : (n + 1) * L, at : at + 128] = jnp.concatenate(
                        parts, axis=0
                    ).astype(bf16)
    mask = jnp.concatenate(
        [r.own[g, i].astype(f32) for i in range(rows) for g in range(groups)], axis=0
    )
    M = rows * L
    z = matmul(r.xo[0:M, :], r.w1[0])
    z += matmul(r.xe[...], r.w1[1])
    z += matmul(r.xo[L : L + M, :], r.w1[2])
    zp = matmul(r.xe[:, cin : 2 * cin], r.wp[...])
    zm, zpm = z * wide(mask, width), zp * wide(mask, width)
    row = jnp.concatenate(
        [column_sum(zm), column_sum(zm * z), column_sum(zpm), column_sum(zpm * zp), column_sum(mask)], axis=1
    )
    r.spread[...] = jnp.broadcast_to(row[None], r.spread.shape)
    copies.start("spread")
    copies.wait("spread")


def first_kernel(r, copies):
    groups, cin, width = r.x.shape[0], r.x.shape[3], r.cot.shape[3]
    rows, cols = r.own.shape[1], r.own.shape[2]
    S = cols + 8
    L = groups * S
    W = 2 * cols + 24
    V = cols + 16
    x, mask, cot = fields(r)
    lines = (2 * rows + 2 * over) * groups, (rows + 2 * rim) * groups, (rows + 3) * groups
    tail = jnp.zeros((W - 8 - 2 * cols, 128), f32)
    r.raw_m[...] = jnp.zeros(r.raw_m.shape, f32)
    r.raw_c[...] = jnp.zeros(r.raw_c.shape, f32)
    for at in range(lines[0]):
        value = x(at % groups, at // groups)
        for k in range(r.raw_x.shape[0]):
            r.raw_x[k, at * W + 8 : at * W + 8 + 2 * cols, :] = value[:, k * 128 : (k + 1) * 128]
            r.raw_x[k, at * W + 8 + 2 * cols : (at + 1) * W, :] = tail
    for strip, x0, m0, c0 in ((r.lft, 8 - over, 8 - rim, 6), (r.rgt, 8 + 2 * cols, 8 + cols, 8 + cols)):
        r.flat[...] = strip[...].astype(f32)
        at = 0
        for c in range(over):
            for k in range(2):
                r.raw_x[k, pl.ds(x0 + c, lines[0], stride=W), :] = r.flat[at : at + lines[0], k * 128 : (k + 1) * 128]
            at += lines[0]
        for c in range(0, rim + 1, 2):
            for k in range(2):
                if c + k < rim:
                    r.raw_m[0, pl.ds(m0 + c + k, lines[1], stride=V), :] = r.flat[
                        at : at + lines[1], k * 128 : (k + 1) * 128
                    ]
            at += lines[1]
        for c in range(2):
            for h in range(0, width // 128, 2):
                for k in range(2):
                    r.raw_c[h + k, pl.ds(c0 + c, lines[2], stride=V), :] = r.flat[
                        at : at + lines[2], k * 128 : (k + 1) * 128
                    ]
                at += lines[2]
    for out, n_rows, start in ((r.xe, rows + 5, 2), (r.xo, rows + 6, 1)):
        for n in range(n_rows):
            for b in range(3):
                for k in range(r.raw_x.shape[0]):
                    parts = [
                        strided(r.raw_x, k, ((2 * n + start) * groups + g) * W + 3 + b, S, 2) for g in range(groups)
                    ]
                    at = b * cin + k * 128
                    out[n * L : (n + 1) * L, at : at + 128] = jnp.concatenate(parts, axis=0).astype(bf16)
    copies.start("xe", "xo")
    for at in range(lines[1]):
        r.raw_m[0, at * V + 8 : at * V + 8 + cols, :] = mask(at % groups, at // groups)
    for n in range(1, rows + 6):
        for g in range(groups):
            to, at = (n - 1) * L + g * S, (n * groups + g) * V
            r.maskp[to : to + S, :] = r.raw_m[0, at + 6 : at + 6 + S, :]
    for at in range(lines[2]):
        value = cot(at % groups, at // groups + 2)
        for k in range(r.raw_c.shape[0]):
            lanes = slice(k * 128, (k + 1) * 128)
            r.raw_c[k, at * V + 8 : at * V + 8 + cols, :] = value[:, lanes]
            r.cotq[at * S : (at + 1) * S, lanes] = r.raw_c[k, at * V + 7 : at * V + 7 + S, :]
    copies.start("cotq")
    r.ownp[...] = jnp.zeros(r.ownp.shape, f32)
    for i in range(rows):
        for g in range(groups):
            at = (i + 2) * L + g * S + 2
            r.ownp[at : at + cols, :] = r.own[g, i].astype(f32)
    copies.wait("w1", "wp")
    for k, (m0, m) in enumerate(chunks(r.pre1.shape[0], r.pre1.shape[0] // 3)):
        z = matmul(r.xo[m0 : m0 + m, :], r.w1[0])
        z += matmul(r.xe[m0 : m0 + m, :], r.w1[1])
        z += matmul(r.xo[L + m0 : L + m0 + m, :], r.w1[2])
        r.pre1[m0 : m0 + m, :] = z
        copies.start(("pre1", k))
        r.prep[m0 : m0 + m, :] = matmul(r.xe[m0 : m0 + m, cin : 2 * cin], r.wp[...])
        copies.start(("prep", k))
    copies.wait("xe", "xo", "pre1", "prep", "cotq")


def second_kernel(r, copies):
    width = r.gain.shape[1]
    t = jnp.sum(r.tot1[...], axis=0)
    n = wide(t[:, 4 * width :], width)
    center, inv = moments(t[:, :width], t[:, width : 2 * width], n)
    proj = moments(t[:, 2 * width : 3 * width], t[:, 3 * width : 4 * width], n)
    r.mom1[...] = jnp.concatenate([center, inv, n, *proj, jnp.zeros((3, width), f32)], axis=0)
    scale = inv * r.gain[...]
    M, Q = r.pre1.shape[0], r.pre2.shape[0]
    L = (M - Q) // 2
    copies.wait("pre1")
    for m0, m in chunks(M, 104):
        v = (r.pre1[m0 : m0 + m, :] - center) * scale + r.shift[...]
        mask = wide(r.maskp[m0 : m0 + m, :], width)
        r.hid[m0 : m0 + m, :] = 0.5 * v * (1.0 + gelu_parts(v)) * mask
    r.hid[M:, :] = jnp.zeros((r.hid.shape[0] - M, width), f32)
    for m0, m in chunks(M, 208):
        for b in range(3):
            r.h3[m0 : m0 + m, b * width : (b + 1) * width] = r.hid[m0 + b : m0 + b + m, :].astype(bf16)
    copies.start("h3")
    copies.wait("w2")
    sums = [jnp.zeros((1, width), f32)] * 2
    for k, (m0, m) in enumerate(chunks(Q, Q // 3)):
        z = matmul(r.h3[m0 : m0 + m, :], r.w2[0])
        z += matmul(r.h3[L + m0 : L + m0 + m, :], r.w2[1])
        z += matmul(r.h3[2 * L + m0 : 2 * L + m0 + m, :], r.w2[2])
        r.pre2[m0 : m0 + m, :] = z
        copies.start(("pre2", k))
        zm = z * wide(r.ownp[L + 1 + m0 : L + 1 + m0 + m, :], width)
        sums = [sums[0] + column_sum(zm), sums[1] + column_sum(zm * z)]
    row = jnp.concatenate(sums, axis=1)
    r.spread[...] = jnp.broadcast_to(row[None], r.spread.shape)
    copies.start("spread")
    copies.wait("h3", "pre2", "spread")


def third_kernel(r, copies):
    groups, rows, cols, width = r.out.shape
    S = cols + 8
    L = groups * S
    n = r.mom1[2:3, :]
    t = jnp.sum(r.tot2[...], axis=0)
    c2, i2 = moments(t[:, :width], t[:, width:], n)
    cp, ip = r.mom1[3:4, :], r.mom1[4:5, :]
    r.mom2[...] = jnp.concatenate([c2, i2, cp, ip, jnp.zeros((4, width), f32)], axis=0)
    sums = [jnp.zeros((1, width), f32)] * 3
    both_shift = r.shift2[...] + r.shiftp[...]
    total = r.grad.shape[0] // S
    for line in range(total):
        if line % (total // 2) == 0:
            k = line // (total // 2)
            copies.wait(("pre2", k), ("prep", k), ("cotq", k))
        at = line * S
        shifted = slice(L + 1 + at, L + 1 + at + S)
        n2 = (r.pre2[at : at + S, :] - c2) * i2
        np_ = (r.prep[shifted, :] - cp) * ip
        v = n2 * r.gain2[...] + np_ * r.gainp[...] + both_shift
        mask = wide(r.maskp[shifted, :], width)
        own = wide(r.ownp[shifted, :], width)
        t = gelu_parts(v)
        r.field[at : at + S, :] = 0.5 * v * (1.0 + t) * mask
        g = gelu_slope(v, t) * mask * r.cotq[at : at + S, :]
        r.grad[at : at + S, :] = g
        g = g * own
        new = [column_sum(g * n2), column_sum(g), column_sum(g * np_)]
        sums = [a + b for a, b in zip(sums, new)]
        if (line + 1) % (total // 2) == 0:
            copies.start(("grad", (line + 1) // (total // 2) - 1))
    row = jnp.concatenate(sums, axis=1)
    r.spread[...] = jnp.broadcast_to(row[None], r.spread.shape)
    copies.start("spread")
    for i in range(rows):
        for g in range(groups):
            at = (i + 1) * L + g * S + 1
            r.out[g, i, :, :] = r.field[at : at + cols, :].astype(bf16)
    copies.start("out")
    copies.wait("grad", "out", "spread")


def halves(r, source, at, frame, to, rows_w):
    half = r.mine.shape[1]
    bit = r.bits[0] == 1
    for m0, m in chunks(rows_w, 96):
        own = wide(r.ownp[frame + m0 : frame + m0 + m, :], half)
        low = (source[at + m0 : at + m0 + m, :half] * own).astype(bf16)
        high = (source[at + m0 : at + m0 + m, half:] * own).astype(bf16)
        r.mine[to + m0 : to + m0 + m, :] = jnp.where(bit, high, low)
        r.theirs[to + m0 : to + m0 + m, :] = jnp.where(bit, low, high)


def fourth_kernel(r, copies):
    width = r.gain2.shape[1]
    Q = r.pre2.shape[0]
    rows_w = r.gpu.shape[0]
    L = (Q - rows_w) // 3
    n = r.mom1[2:3, :]
    c2, i2, cp, ip = (r.mom2[k : k + 1, :] for k in range(4))
    t3 = jnp.sum(r.tot3[...], axis=0)
    gg2, gs, ggp = (t3[:, k * width : (k + 1) * width] for k in range(3))
    r.gain_second[...], r.shift_second[...], r.gain_proj[...], r.shift_proj[...] = gg2, gs, ggp, gs
    tiny = "gain_second", "shift_second", "gain_proj", "shift_proj"
    copies.start(*tiny)
    for m0, m in chunks(Q, L):
        if m0 in (0, 6 * L):
            k = m0 // (6 * L)
            copies.wait(("grad", k), ("pre2", k), ("prep", k))
        shifted = slice(L + 1 + m0, L + 1 + m0 + m)
        mask = wide(r.maskp[shifted, :], width) / n
        n2 = (r.pre2[m0 : m0 + m, :] - c2) * i2
        np_ = (r.prep[shifted, :] - cp) * ip
        g = r.grad[m0 : m0 + m, :]
        r.gq[m0 : m0 + m, :] = (r.gain2[...] * i2) * (g - mask * (gs + n2 * gg2))
        r.gpq[m0 : m0 + m, :] = (r.gainp[...] * ip) * (g - mask * (gs + np_ * ggp))
    r.gq[Q:, :] = jnp.zeros((r.gq.shape[0] - Q, width), f32)
    copies.start("gq")
    for m0, m in chunks(rows_w, 96):
        r.gpu[m0 : m0 + m, :] = r.gpq[L + 1 + m0 : L + 1 + m0 + m, :].astype(bf16)
    copies.start("gpu")
    halves(r, r.gq, L, 2 * L + 1, 0, rows_w)
    halves(r, r.gpq, L - 1, 2 * L, rows_w, rows_w)
    copies.wait("gpu", "gq", *tiny)


def hidden_kernel(r, copies):
    width = r.gain.shape[1]
    Q = r.gq.shape[0] - 8
    L = (r.keep.shape[0] - Q) // 2
    center, inv = r.mom1[0:1, :], r.mom1[1:2, :]
    copies.wait("gq")
    for m0, m in chunks(Q, 176):
        for b in range(3):
            r.g3[m0 : m0 + m, b * width : (b + 1) * width] = r.gq[m0 + b : m0 + b + m, :].astype(bf16)
    U = r.act.shape[0]
    for a in range(3):
        copies.wait(("w2", a))
        gh = jnp.zeros((U, width), f32)
        for b in range(3):
            gh += matmul_nt(
                r.g3[L * a : L * a + U, b * width : (b + 1) * width],
                r.w2[2 - a, (2 - b) * width : (3 - b) * width, :],
            )
        r.act[...] = gh if a == 0 else r.act[...] + gh
    copies.wait("keep")
    sums = [jnp.zeros((1, width), f32)] * 2
    for k, (m0, m) in enumerate(chunks(U, L)):
        frame = slice(2 * L + 2 + m0, 2 * L + 2 + m0 + m)
        n1 = (r.keep[frame, :] - center) * inv
        v = n1 * r.gain[...] + r.shift[...]
        mask = wide(r.maskp[frame, :], width)
        g = gelu_slope(v, gelu_parts(v)) * mask * r.act[m0 : m0 + m, :]
        r.act[m0 : m0 + m, :] = g
        r.normed[m0 : m0 + m, :] = n1 * mask
        if k % 3 == 2:
            copies.start(("act", k // 3), ("normed", k // 3))
        g = g * wide(r.ownp[frame, :], width)
        sums = [sums[0] + column_sum(g * n1), sums[1] + column_sum(g)]
    row = jnp.concatenate(sums, axis=1)
    r.spread[...] = jnp.broadcast_to(row[None], r.spread.shape)
    copies.start("spread")
    copies.wait("act", "normed", "spread")


def split_store(r, rows, unit, first):
    quarter = unit // 4
    for k in range(rows // unit):
        for bit, base, sent, kept in ((1, 0, r.sent_a, r.kept_a), (2, 2 * quarter, r.sent_b, r.kept_b)):
            keep = pl.multiple_of(k * unit + base + r.bits[bit] * quarter, quarter)
            send = pl.multiple_of(k * unit + base + (1 - r.bits[bit]) * quarter, quarter)
            sent[first + k] = r.acc[pl.ds(send, quarter), :].astype(bf16)
            kept[first + k] = r.acc[pl.ds(keep, quarter), :]


def weights_second_kernel(r, copies):
    width = r.h3.shape[1] // 3
    cin = r.xe.shape[1] // 3
    rows_w = r.near.shape[0] // 2
    L = (r.h3.shape[0] - rows_w) // 5
    per = width // cin
    for b in range(3):
        lanes = slice(b * width, (b + 1) * width)
        copies.wait(("h3", b), ("h3_far", b))
        for a in range(3):
            at = L * a + L
            r.acc[...] = matmul_tn(r.h3[at : at + rows_w, lanes], r.near[:rows_w, :]) + matmul_tn(
                r.h3_far[at : at + rows_w, lanes], r.far[:rows_w, :]
            )
            split_store(r, width, cin, (3 * b + a) * per)
        copies.start(*((name, b) for name in CHUNKS))
    at = 2 * L
    copies.wait("xe", "xe_far")
    middle = slice(cin, 2 * cin)
    r.acc[0:cin, :] = matmul_tn(r.xe[at : at + rows_w, middle], r.near[rows_w:, :]) + matmul_tn(
        r.xe_far[at : at + rows_w, middle], r.far[rows_w:, :]
    )
    split_store(r, cin, cin, 9 * per)
    copies.start(*((name, 3) for name in CHUNKS))
    copies.wait(*CHUNKS)


def first_back(r, gg, gs, count):
    width = r.gain.shape[1]
    U = r.act.shape[0]
    L = U - r.rows_w
    inv, n = r.mom1[1:2, :], r.mom1[2:3, :]
    gg, gs = gg / n, gs / n
    scale = r.gain[...] * inv
    r.gf[0:8, :] = jnp.zeros((8, width), f32)
    r.gf[8 + count :, :] = jnp.zeros((r.gf.shape[0] - 8 - count, width), f32)
    for m0, m in chunks(count, L):
        mask = wide(r.maskp[2 * L + 2 + m0 : 2 * L + 2 + m0 + m, :], width)
        back = mask * gs + r.normed[m0 : m0 + m, :] * gg
        r.gf[8 + m0 : 8 + m0 + m, :] = scale * (r.act[m0 : m0 + m, :] - back)


def fifth_kernel(r, copies):
    width = r.gain.shape[1]
    r.rows_w = r.mine.shape[0]
    L = r.act.shape[0] - r.rows_w
    t4 = jnp.sum(r.tot4[...], axis=0)
    r.gain_first[...], r.shift_first[...] = t4[:, :width], t4[:, width:]
    copies.start("gain_first", "shift_first")
    copies.wait("act", "normed")
    first_back(r, t4[:, :width], t4[:, width:], r.rows_w)
    halves(r, r.gf, 6, 2 * L, 0, r.rows_w)
    copies.wait("gain_first", "shift_first")


def weights_first_kernel(r, copies):
    rows_w = r.near.shape[0]
    cin = r.xe.shape[1] // 3
    L = (r.xe.shape[0] - rows_w) // 5
    copies.wait("xe", "xe_far")
    for k, a in enumerate((1, 0, 2)):
        if k == 1:
            copies.wait("xo", "xo_far")
        source, source_far = (r.xe, r.xe_far) if a == 1 else (r.xo, r.xo_far)
        at = (3 if a == 2 else 2) * L
        for b in range(3):
            lanes = slice(b * cin, (b + 1) * cin)
            r.acc[lanes, :] = matmul_tn(source[at : at + rows_w, lanes], r.near[...]) + matmul_tn(
                source_far[at : at + rows_w, lanes], r.far[...]
            )
        split_store(r, 3 * cin, cin, a * 3)
        copies.start(*((name, a) for name in CHUNKS))
    copies.wait(*CHUNKS)


def inputs_kernel(r, copies):
    width = r.gpu.shape[1]
    groups, rows, cols = r.out.shape[0], r.out.shape[1] // 2, r.out.shape[2] // 2
    cin = r.out.shape[3]
    M = r.gpu.shape[0]
    S = cols + 8
    L = groups * S
    lines = r.lines
    U = r.act.shape[0]
    r.rows_w = M
    copies.wait("act", "normed")
    first_back(r, r.gg[...], r.gs[...], U)
    for m0, m in chunks(U, 144):
        r.gu[m0 : m0 + m, :width] = r.gf[8 + m0 : 8 + m0 + m, :].astype(bf16)
        r.gu[m0 : m0 + m, width:] = r.gf[9 + m0 : 9 + m0 + m, :].astype(bf16)
    copies.wait("gpu", "w1", "wp")

    def tap(m0, m, a, b):
        di, dj = (1 if a == 0 else 0), (1 if b == 0 else 0)
        return matmul_nt(
            r.gu[di * L + m0 : di * L + m0 + m, dj * width : (dj + 1) * width],
            r.w1[a, b * cin : (b + 1) * cin, :],
        )

    for m0, m in chunks(M, 2 * L):
        pieces = {
            (0, 0): tap(m0, m, 1, 1) + matmul_nt(r.gpu[m0 : m0 + m, :], r.wp[...]),
            (0, 1): tap(m0, m, 1, 2) + tap(m0, m, 1, 0),
            (1, 0): tap(m0, m, 2, 1) + tap(m0, m, 0, 1),
            (1, 1): tap(m0, m, 2, 2) + tap(m0, m, 2, 0) + tap(m0, m, 0, 2) + tap(m0, m, 0, 0),
        }
        for (ro, co), v in pieces.items():
            for k in range(m // S):
                line = m0 // S + k
                i, g = line // groups, line % groups
                for h in range(lines.shape[0]):
                    lines[h, (2 * i + ro) * groups + g, pl.ds(co, cols, stride=2), :] = v[
                        k * S : k * S + cols, h * 128 : (h + 1) * 128
                    ]
    for n in range(2 * rows):
        for g in range(groups):
            for h in range(lines.shape[0]):
                r.out[g, n, :, h * 128 : (h + 1) * 128] = lines[h, n * groups + g].astype(bf16)
    copies.start("out")
    copies.wait("out")


def widen(half, side, taps, per, swapped, into=None):
    total, n, m = half.shape
    extra = total - taps * per
    order = [(t % 3 * 3 + t // 3) if swapped else t for t in range(taps)]
    jobs = [(t * per, per, 0, order[t] * per) for t in range(taps)] + [(taps * per, 1, 1, 0)] * extra
    more = list(into or [])

    def body(side_ref, half_ref, *refs):
        outs = refs[len(more) : len(more) + 1 + extra]
        narrow, full, sems = refs[len(more) + 1 + extra :]
        lanes = pl.ds(pl.multiple_of(side_ref[0] * m, m), m)
        reads = [
            pltpu.make_async_copy(half_ref.at[pl.ds(at, size)], narrow.at[pl.ds(at, size)], sems.at[0, k])
            for k, (at, size, _, _) in enumerate(jobs)
        ]
        writes = [
            pltpu.make_async_copy(full.at[pl.ds(at, size)], outs[which].at[pl.ds(to, size), :, lanes], sems.at[1, k])
            for k, (at, size, which, to) in enumerate(jobs)
        ]
        for read in reads:
            read.start()
        for k, (at, size, _, _) in enumerate(jobs):
            reads[k].wait()
            full[at : at + size] = narrow[at : at + size].astype(f32)
            writes[k].start()
        for write in writes:
            write.wait()

    hbm = pl.BlockSpec(memory_space=pltpu.HBM)
    return pl.pallas_call(
        body,
        out_shape=[shape((taps * per, n, 2 * m))] + [shape((1, n, 2 * m))] * extra,
        in_specs=[pl.BlockSpec(memory_space=pltpu.SMEM)] + [hbm] * (1 + len(more)),
        out_specs=[hbm] * (1 + extra),
        scratch_shapes=[
            pltpu.VMEM((total, n, m), bf16),
            pltpu.VMEM((total, n, m), f32),
            pltpu.SemaphoreType.DMA((2, len(jobs))),
        ],
        input_output_aliases={2 + k: k for k in range(len(more))},
        compiler_params=pltpu.CompilerParams(vmem_limit_bytes=20 * 1024 * 1024),
        cost_estimate=pl.CostEstimate(flops=0, bytes_accessed=0, transcendentals=0),
    )(side.reshape(1), half, *more)


def halve_kernel(r, copies):
    for p in range(r.count):
        kept, got = getattr(r, f"kept{p}"), getattr(r, f"got{p}")
        copies.wait(f"kept{p}", f"got{p}")
        to_send, to_keep = getattr(r, f"sent{p}"), getattr(r, f"left{p}")
        bit = r.bits[r.steps[p]] == 1
        h = kept.shape[1] // 2
        for t in range(kept.shape[0]):
            total = kept[t] + got[t].astype(f32)
            low, high = total[:h], total[h:]
            to_send[t] = jnp.where(bit, low, high).astype(bf16)
            to_keep[t] = jnp.where(bit, high, low)
        copies.start(f"sent{p}", f"left{p}")
    copies.wait(*(name for name in copies.jobs if name[:4] in ("sent", "left")))


def halve(bits, pairs, steps, cost):
    ins = dict(bits=bits)
    for p, (kept, got) in enumerate(pairs):
        ins[f"kept{p}"], ins[f"got{p}"] = kept, got
    taps, n, m = pairs[0][0].shape
    dims = (taps, n // 2, m)
    names = [str(p) for p in range(len(pairs))]
    outs = {}
    for name in names:
        outs["sent" + name], outs["left" + name] = shape(dims, bf16), shape(dims)

    def body(r, copies):
        r.count, r.steps = len(pairs), steps
        halve_kernel(r, copies)

    far_in = tuple(n for n in ins if n != "bits")
    out = call(body, ins, outs, far_in=far_in, far_out=tuple(outs), smem=("bits",), cost=cost, limit=60)
    return [(out["sent" + name], out["left" + name]) for name in names]


def shifted(value, axis, steps):
    count = lax.axis_size(axis)
    first, last = (max(0, -steps), min(count, count - steps))
    return lax.ppermute(value, axis, [(source, source + steps) for source in range(first, last)])


def gather_sum(spread):
    return lax.all_to_all(spread, axes, 0, 0)


def bit_of(axis, step):
    return (lax.axis_index(axis) // step) % 2


def partner(value, axis, step):
    count = lax.axis_size(axis)
    return lax.ppermute(value, axis, [(i, i ^ step) for i in range(count)])


def steps_of(axis):
    count, step, out = lax.axis_size(axis), 1, []
    while step < count:
        out.append((axis, step))
        step *= 2
    return out


def split(total, axis, step):
    n = total.shape[1] // 2
    bit = bit_of(axis, step) == 1
    low, high = total[:, :n], total[:, n:]
    return jnp.where(bit, low, high).astype(bf16), jnp.where(bit, high, low)


def joined(value, other, axis, step, dim=1):
    bit = bit_of(axis, step) == 1
    return jnp.concatenate([jnp.where(bit, other, value), jnp.where(bit, value, other)], axis=dim)


class Tree:
    def __init__(self, parts, bits, plane, rest, core):
        self.bits, self.place = bits, {step: k for k, step in enumerate([core, *plane, *rest])}
        self.sent_a, self.kept_a, self.sent_b, self.kept_b = parts
        self.a, self.b, self.rest, self.core = plane, plane[::-1], rest, core
        p, n = len(plane), len(rest)
        self.stages = [("plane", k) for k in range(p)] + [("rest", k) for k in range(n)]
        self.stages += [("rest_join", k) for k in reversed(range(n))] + [("plane_join", k) for k in reversed(range(p))]
        self.stages += [("core", 0)]

    def next(self):
        return self.stages[0] if self.stages else None

    def start(self):
        kind, k = self.stages[0]
        if kind == "plane":
            self.got = partner(self.sent_a, *self.a[k]), partner(self.sent_b, *self.b[k])
        elif kind == "rest":
            self.got = (partner(self.sent, *self.rest[k]),)
        elif kind == "rest_join":
            self.got = (partner(self.value, *self.rest[k]),)
        elif kind == "plane_join":
            self.got = partner(self.value_a, *self.a[k]), partner(self.value_b, *self.b[k])
        else:
            self.got = (partner(self.value, *self.core),)

    def finish(self, cost=0):
        kind, k = self.stages.pop(0)
        if kind == "plane":
            pairs = [(self.kept_a, self.got[0]), (self.kept_b, self.got[1])]
            nexts = [order[k + 1] for order in (self.a, self.b) if k + 1 < len(order)]
            if nexts and cost:
                pairs = halve(self.bits, pairs, [self.place[step] for step in nexts], cost)
                (self.sent_a, self.kept_a), (self.sent_b, self.kept_b) = pairs
                return
            total_a, total_b = (kept + got.astype(f32) for kept, got in pairs)
            if nexts:
                self.sent_a, self.kept_a = split(total_a, *nexts[0])
                self.sent_b, self.kept_b = split(total_b, *nexts[1])
            else:
                self.taps = total_a.shape[0]
                self.split_rest(jnp.concatenate([total_a, total_b], axis=0), 0)
        elif kind == "rest":
            self.split_rest(self.kept + self.got[0].astype(f32), k + 1)
        elif kind == "rest_join":
            self.value = joined(self.value, self.got[0], *self.rest[k])
            self.value_a, self.value_b = self.value[: self.taps], self.value[self.taps :]
        elif kind == "plane_join":
            self.value_a = joined(self.value_a, self.got[0], *self.a[k])
            self.value_b = joined(self.value_b, self.got[1], *self.b[k])
            self.value = jnp.concatenate([self.value_a, self.value_b], axis=1)

    def split_rest(self, total, k):
        if k < len(self.rest):
            self.sent, self.kept = split(total, *self.rest[k])
        else:
            self.value = total.astype(bf16)


def lockstep(*trees, beside=()):
    for t in trees:
        t.start()
    got, beside = lax.optimization_barrier(([t.got for t in trees], beside))
    for t, g in zip(trees, got):
        t.got = g
        t.finish()
    return beside


def on_device(inputs, w_first, gain_first, shift_first, w_second, gain_second, shift_second, w_proj, gain_proj, shift_proj, valid_mask, cotangent):
    groups, rows_in, cols_in, cin = inputs.shape
    rows, cols = rows_in // 2, cols_in // 2
    width = w_first.shape[3]
    half = width // 2
    S = cols + 8
    L = groups * S
    devices = lax.axis_size("rows") * lax.axis_size("cols") * lax.axis_size("grp")
    plane = steps_of("cols")
    core = steps_of("rows")[0]
    rest = steps_of("rows")[1:] + steps_of("grp")
    bits = jnp.stack([bit_of(*step) for step in (core, *plane, *rest)]).astype(jnp.int32)
    w1 = w_first.reshape(3, 3 * cin, width)
    w2 = w_second.reshape(3, 3 * width, width)
    as_row = lambda v: v.reshape(1, -1)
    own = jnp.broadcast_to(valid_mask.astype(bf16)[..., None], valid_mask.shape + (128,))
    MP, MQ, MU, MW = (rows + 5) * L, (rows + 3) * L, (rows + 1) * L, rows * L
    px = lambda m, k: 2 * m * k * width
    vec = lambda k: shape((1, k * width))
    all_devices = lambda k: shape((devices, 1, k))
    g1, b1, g2, b2, gp, bp = map(
        as_row, (gain_first, shift_first, gain_second, shift_second, gain_proj, shift_proj)
    )

    top1 = shifted(inputs[:, -1:], "rows", 1)
    me, count = lax.axis_index("rows"), lax.axis_size("rows")
    flags = jnp.stack([me > 0, me < count - 1]).astype(jnp.int32)
    flat_rows = shape((over * groups * cols_in + (width // 256 + 1) * rim * groups * cols, 256), bf16)
    packed = call(
        vertical_kernel,
        dict(flags=flags, x=inputs, cot=cotangent, own=own),
        dict(down=flat_rows) if count == 2 else dict(down=flat_rows, up=flat_rows),
        far_in=("x", "cot"),
        smem=("flags",),
        parts=dict(x=end_parts(rows_in, over), cot=end_parts(rows, rim)),
    )
    if count == 2:
        top = bot = lax.ppermute(packed["down"], "rows", [(0, 1), (1, 0)])
    else:
        top, bot = shifted(packed["down"], "rows", 1), shifted(packed["up"], "rows", -1)
    lft1 = shifted(jnp.concatenate([top1[:, :, -1:], inputs[:, :, -1:]], axis=1), "cols", 1)
    (top, bot), lft1 = lax.optimization_barrier(((top, bot), lft1))
    lines = (rows_in + 2 * over) * groups, (rows + 2 * rim) * groups, (rows + 3) * groups
    n_strip = over * lines[0] + (rim + 1) // 2 * lines[1] + width // 128 * lines[2]
    n_strip = -(-n_strip // 16) * 16
    near = dict(flags=flags, x=inputs, cot=cotangent, own=own, top=top, bot=bot)
    strips = call(
        strips_kernel,
        near,
        dict(right=shape((n_strip, 256), bf16), left=shape((n_strip, 256), bf16)),
        dict(
            raw_x=pltpu.VMEM((cin // 128, lines[0] * cols_in, 128), f32),
            raw_m=pltpu.VMEM((1, lines[1] * cols, 128), f32),
            raw_c=pltpu.VMEM((width // 128, lines[2] * cols, 128), f32),
            flat=pltpu.VMEM((n_strip, 256), f32),
        ),
        smem=("flags",),
    )
    lft, rgt = shifted(strips["right"], "cols", 1), shifted(strips["left"], "cols", -1)
    lft1, _ = lax.optimization_barrier((lft1, strips["right"]))
    stats = call(
        stats_kernel,
        dict(x=inputs, top=top1, lft=lft1, own=own, w1=w1, wp=w_proj),
        dict(spread=all_devices(4 * width + 128)),
        dict(
            raw=pltpu.VMEM((cin // 128, (rows_in + 1) * groups, cols_in + 8, 128), f32),
            xe=pltpu.VMEM((rows * groups * cols, 3 * cin), bf16),
            xo=pltpu.VMEM(((rows + 1) * groups * cols, 3 * cin), bf16),
        ),
        far_out=("spread",),
    )
    tot1 = gather_sum(stats["spread"])

    first = call(
        first_kernel,
        dict(**near, lft=lft, rgt=rgt, w1=w1, wp=w_proj),
        dict(
            pre1=shape((MP, width)),
            prep=shape((MP, width)),
            xe=shape((MP, 3 * cin), bf16),
            xo=shape((MP + L, 3 * cin), bf16),
            ownp=shape((MP, 128)),
            maskp=shape((MP, 128)),
            cotq=shape((MQ, width)),
        ),
        dict(
            raw_x=pltpu.VMEM((cin // 128, lines[0] * (cols_in + 24), 128), f32),
            raw_m=pltpu.VMEM((1, lines[1] * (cols + 16), 128), f32),
            raw_c=pltpu.VMEM((width // 128, lines[2] * (cols + 16), 128), f32),
            flat=pltpu.VMEM((n_strip, 256), f32),
        ),
        far_in=("w1", "wp"),
        far_out=("xe", "xo", "pre1", "prep", "cotq"),
        smem=("flags",),
        cost=20000000000,
        parts=dict(pre1=row_parts(MP, 3), prep=row_parts(MP, 3)),
    )
    xe, xo, ownp, maskp = first["xe"], first["xo"], first["ownp"], first["maskp"]
    far_xe, far_xo = partner(xe, *core), partner(xo, *core)

    second = call(
        second_kernel,
        dict(pre1=first["pre1"], tot1=tot1, gain=g1, shift=b1, maskp=maskp, ownp=ownp, w2=w2),
        dict(h3=shape((MP, 3 * width), bf16), pre2=shape((MQ, width)), spread=all_devices(2 * width), mom1=shape((8, width))),
        dict(hid=pltpu.VMEM((MP + 8, width), f32)),
        far_in=("pre1", "w2"),
        far_out=("h3", "pre2", "spread"),
        parts=dict(pre2=row_parts(MQ, 3)),
    )
    h3, pre2, mom1 = second["h3"], second["pre2"], second["mom1"]
    tot2 = gather_sum(second["spread"])
    far_h3 = partner(h3, *core)

    third = call(
        third_kernel,
        dict(
            pre2=pre2, prep=first["prep"], mom1=mom1, tot2=tot2, gain2=g2, shift2=b2, gainp=gp, shiftp=bp,
            maskp=maskp, ownp=ownp, cotq=first["cotq"],
        ),
        dict(
            out=shape((groups, rows, cols, width), bf16),
            grad=shape((MQ, width)),
            spread=all_devices(3 * width),
            mom2=shape((8, width)),
        ),
        dict(field=pltpu.VMEM((MQ, width), f32)),
        far_in=("pre2", "prep", "cotq"),
        far_out=("grad", "spread", "out"),
        parts=dict(
            grad=row_parts(MQ, 2), pre2=row_parts(MQ, 2), cotq=row_parts(MQ, 2), prep=cuts(L, L + MQ // 2 + 8, L + MQ + 8)
        ),
    )
    mom2 = third["mom2"]
    tot3 = gather_sum(third["spread"])

    fourth = call(
        fourth_kernel,
        dict(
            bits=bits, pre2=pre2, prep=first["prep"], mom1=mom1, mom2=mom2, tot3=tot3, gain2=g2, gainp=gp,
            grad=third["grad"], maskp=maskp, ownp=ownp,
        ),
        dict(
            mine=shape((2 * MW, half), bf16),
            theirs=shape((2 * MW, half), bf16),
            gq=shape((MQ + 8, width)),
            gpu=shape((MW, width), bf16),
            gain_second=vec(1),
            shift_second=vec(1),
            gain_proj=vec(1),
            shift_proj=vec(1),
        ),
        dict(gpq=pltpu.VMEM((MQ, width), f32)),
        far_in=("pre2", "prep", "grad"),
        far_out=("gpu", "gq", "gain_second", "shift_second", "gain_proj", "shift_proj"),
        parts=dict(grad=cuts(0, 6 * L, MQ), pre2=cuts(0, 6 * L, MQ), prep=cuts(L, 7 * L + 8, L + MQ + 8)),
        smem=("bits",),
    )
    far2 = partner(fourth["theirs"], *core)

    def chunk_shapes(taps):
        dims = (taps, cin // 4, half)
        return dict(sent_a=shape(dims, bf16), kept_a=shape(dims), sent_b=shape(dims, bf16), kept_b=shape(dims))

    per = width // cin
    taps2 = 9 * per + 1
    second_parts = call(
        weights_second_kernel,
        dict(bits=bits, h3=h3, h3_far=far_h3, xe=xe, xe_far=far_xe, near=fourth["mine"], far=far2),
        chunk_shapes(taps2),
        dict(acc=pltpu.VMEM((width, half), f32)),
        far_in=("h3", "h3_far", "xe", "xe_far"),
        far_out=CHUNKS,
        smem=("bits",),
        parts=dict(
            h3=lane_parts(3 * width, 3, pl.ds(L, MW + 2 * L)),
            h3_far=lane_parts(3 * width, 3, pl.ds(L, MW + 2 * L)),
            xe=[(0, (pl.ds(2 * L, MW), pl.ds(cin, cin)))],
            xe_far=[(0, (pl.ds(2 * L, MW), pl.ds(cin, cin)))],
            **{name: row_parts(taps2 - 1, 3) + [(3, (pl.ds(taps2 - 1, 1),))] for name in CHUNKS},
        ),
    ).values()
    gq, *second_parts = lax.optimization_barrier((fourth["gq"], *second_parts))

    tree2 = Tree(second_parts, bits, plane, rest, core)
    tree2.start()
    hidden = call(
        hidden_kernel,
        dict(gq=gq, w2=w2, keep=first["pre1"], mom1=mom1, gain=g1, shift=b1, maskp=maskp, ownp=ownp),
        dict(act=shape((MU, width)), normed=shape((MU, width)), spread=all_devices(2 * width)),
        dict(g3=pltpu.VMEM((MQ, 3 * width), bf16)),
        far_in=("gq", "w2", "keep"),
        far_out=("act", "normed", "spread"),
        parts=dict(
            w2=[(k, (pl.ds(2 - k, 1),)) for k in range(3)],
            keep=cuts(2 * L, 2 * L + MU + 8),
            act=row_parts(MU, 3),
            normed=row_parts(MU, 3),
        ),
    )
    tot4 = gather_sum(hidden["spread"])
    tree2.finish(20000000000)
    act, tree2.sent_a, tree2.sent_b = lax.optimization_barrier((hidden["act"], tree2.sent_a, tree2.sent_b))
    tree2.start()
    fifth = call(
        fifth_kernel,
        dict(bits=bits, act=act, normed=hidden["normed"], mom1=mom1, tot4=tot4, gain=g1, maskp=maskp, ownp=ownp),
        dict(mine=shape((MW, half), bf16), theirs=shape((MW, half), bf16), gain_first=vec(1), shift_first=vec(1)),
        dict(gf=pltpu.VMEM((MU + 16, width), f32)),
        far_in=("act", "normed"),
        far_out=("gain_first", "shift_first"),
        smem=("bits",),
        parts=dict(act=cuts(0, MW), normed=cuts(0, MW)),
    )
    far1 = partner(fifth["theirs"], *core)
    first_parts = call(
        weights_first_kernel,
        dict(bits=bits, xe=xe, xo=xo, xe_far=far_xe, xo_far=far_xo, near=fifth["mine"], far=far1),
        chunk_shapes(9),
        dict(acc=pltpu.VMEM((3 * cin, half), f32)),
        far_in=("xe", "xe_far", "xo", "xo_far"),
        far_out=CHUNKS,
        smem=("bits",),
        parts=dict(
            xe=cuts(2 * L, 2 * L + MW),
            xe_far=cuts(2 * L, 2 * L + MW),
            xo=cuts(2 * L, 3 * L + MW),
            xo_far=cuts(2 * L, 3 * L + MW),
            **{name: row_parts(9, 3) for name in CHUNKS},
        ),
    ).values()
    tree2.got, *first_parts = lax.optimization_barrier((tree2.got, *first_parts))
    tree2.finish()
    tree1 = Tree(first_parts, bits, plane, rest, core)

    grad_inputs = call(
        inputs_kernel,
        dict(
            act=act, normed=hidden["normed"], gpu=fourth["gpu"], w1=w1, wp=w_proj, mom1=mom1, gain=g1, maskp=maskp,
            gg=fifth["gain_first"], gs=fifth["shift_first"],
        ),
        dict(out=shape((groups, rows_in, cols_in, cin), bf16)),
        dict(
            lines=pltpu.VMEM((cin // 128, rows_in * groups, cols_in, 128), f32),
            gf=pltpu.VMEM((MU + 16, width), f32),
            gu=pltpu.VMEM((MU, 2 * width), bf16),
        ),
        far_in=("act", "normed", "gpu", "w1", "wp"),
        far_out=("out",),
        cost=10000000000,
    )["out"]
    side = bit_of(*core).astype(jnp.int32)
    grad_inputs = lockstep(tree2, tree1, beside=grad_inputs)
    while tree2.next() != ("plane_join", 0):
        lockstep(tree2, tree1)
    tree2.start()
    while tree1.next() != ("plane_join", 0):
        tree1.start()
        if tree1.next() != ("plane_join", 1):
            tree1.finish()
        else:
            tree1.got, tree2.got = lax.optimization_barrier((tree1.got, tree2.got))
            tree1.finish()
    tree2.finish()
    tree2.start()
    tree1.start()
    grad_second = widen(tree2.got[0], 1 - side, 9, per, True, widen(tree2.value, side, 9, per, True))
    tree1.got, grad_second = lax.optimization_barrier((tree1.got, grad_second))
    grad_w2, grad_wp = grad_second
    tree1.finish()
    tree1.start()
    (grad_w1,) = widen(tree1.got[0], 1 - side, 3, 3, False, widen(tree1.value, side, 3, 3, False))

    return (
        third["out"],
        grad_inputs,
        grad_w1.reshape(w_first.shape),
        fifth["gain_first"].reshape(width),
        fifth["shift_first"].reshape(width),
        grad_w2.reshape(w_second.shape),
        fourth["gain_second"].reshape(width),
        fourth["shift_second"].reshape(width),
        grad_wp.reshape(w_proj.shape),
        fourth["gain_proj"].reshape(width),
        fourth["shift_proj"].reshape(width),
    )


def solution(mesh):
    spread = P("grp", "rows", "cols", None)
    return jax.shard_map(
        on_device,
        mesh=mesh,
        in_specs=(spread,) + (P(),) * 9 + (P("grp", "rows", "cols"), spread),
        out_specs=(spread, spread) + (P(),) * 9,
        check_vma=False,
    )
```

```python
import functools

import jax
import jax.numpy as jnp
from jax import lax
from jax.experimental import pallas as pl
from jax.experimental.pallas import tpu as pltpu
from jax.sharding import PartitionSpec as P

epsilon = 1e-05
axes = ("rows", "cols", "grp")
bf16 = jnp.bfloat16
f32 = jnp.float32
inner = 0.7978845608028654
cubic = 0.044715
over = 6
CHUNKS = "sent_a", "kept_a", "sent_b", "kept_b"
rim = 3


class Names:
    def __getattr__(self, name):
        return name


N = Names()


class Refs:
    def __init__(self, named):
        self.__dict__.update(named)


class Copies:
    def __init__(self, parts, pairs, sems):
        self.jobs = {}
        for k, (name, index) in enumerate(parts):
            source, target = pairs[name]
            if index:
                source, target = source.at[index[1]], target.at[index[1]]
            self.jobs.setdefault(name, []).append(pltpu.make_async_copy(source, target, sems.at[k]))

    def start(self, *names):
        for name, *which in map(named, names):
            for job in self.jobs[name][slice(*which) if which else slice(None)]:
                job.start()

    def start_all(self, names):
        for k in range(max((len(self.jobs[n]) for n in names), default=0)):
            for n in names:
                if k < len(self.jobs[n]):
                    self.jobs[n][k].start()

    def wait(self, *names):
        for name, *which in map(named, names):
            for job in self.jobs[name][slice(*which) if which else slice(None)]:
                job.wait()


def named(name):
    return (name,) if isinstance(name, str) else (name[0], name[1], name[1] + 1)


def row_parts(total, count):
    size = total // count
    return [(k, (pl.ds(k * size, size),)) for k in range(count)]


def end_parts(total, size):
    return [(k, (slice(None), pl.ds(at, size))) for k, at in enumerate((0, total - size))]


def cuts(*at):
    return [(k, (pl.ds(a, b - a),)) for k, (a, b) in enumerate(zip(at, at[1:]))]


def lane_parts(total, count, rows=slice(None)):
    size = total // count
    return [(k, (rows, pl.ds(k * size, size))) for k in range(count)]


def call(body, ins, outs, scratch=None, far_in=(), far_out=(), smem=(), parts=None, limit=52, cost=0):
    scratch, parts = scratch or {}, parts or {}
    far = (*far_in, *far_out)
    jobs = [(name, index) for name in far for index in parts.get(name, [None])]

    def spec(name):
        if name in smem:
            return pl.BlockSpec(memory_space=pltpu.SMEM)
        return pl.BlockSpec(memory_space=pltpu.HBM if name in far else pltpu.VMEM)

    kinds = {**{n: shape(v.shape, v.dtype) for n, v in ins.items()}, **outs}

    def run(*refs):
        plain = dict(zip([*ins, *outs], refs))
        rest = refs[len(plain) :]
        buffers = dict(zip(far, rest))
        more = dict(zip(scratch, rest[len(far) :]))
        copies = None
        if far:
            pairs = {n: (plain[n], buffers[n]) if n in far_in else (buffers[n], plain[n]) for n in far}
            copies = Copies(jobs, pairs, rest[-1])
            copies.start_all(far_in)
        body(Refs({**plain, **buffers, **more}), copies)

    buffers = [pltpu.VMEM(kinds[n].shape, kinds[n].dtype) for n in far]
    sems = [pltpu.SemaphoreType.DMA((len(jobs),))] if far else []
    result = pl.pallas_call(
        run,
        out_shape=list(outs.values()),
        in_specs=[spec(n) for n in ins],
        out_specs=[spec(n) for n in outs],
        scratch_shapes=[*buffers, *scratch.values(), *sems],
        compiler_params=pltpu.CompilerParams(vmem_limit_bytes=limit * 1024 * 1024),
        cost_estimate=pl.CostEstimate(flops=cost, bytes_accessed=0, transcendentals=0),
    )(*ins.values())
    return dict(zip(outs, result))


def shape(dims, dtype=f32):
    return jax.ShapeDtypeStruct(dims, dtype)


def wide(mask, width):
    return jnp.concatenate([mask] * (width // mask.shape[1]), axis=1)


def matmul(a, b):
    return lax.dot_general(a, b, (((1,), (0,)), ((), ())), preferred_element_type=f32)


def matmul_nt(a, b):
    return lax.dot_general(a, b, (((1,), (1,)), ((), ())), preferred_element_type=f32)


def matmul_tn(a, b):
    return lax.dot_general(a, b, (((0,), (0,)), ((), ())), preferred_element_type=f32)


def gelu_parts(v):
    return jnp.tanh(inner * (v + cubic * v * v * v))


def gelu_slope(v, t):
    return 0.5 * (1.0 + t) + 0.5 * v * (1.0 - t * t) * (inner * (1.0 + 3.0 * cubic * v * v))


def column_sum(v):
    return jnp.sum(v, axis=0, keepdims=True)


def moments(total, squares, pixel_count):
    center = total / pixel_count
    spread = squares / pixel_count - center * center
    return center, lax.rsqrt(spread + epsilon)


def chunks(total, size):
    return [(at, min(size, total - at)) for at in range(0, total, size)]


def strided(ref, k, first, count, step):
    return ref[k, pl.ds(first, count, stride=step), :]


def vertical_kernel(r, copies):
    groups, width = r.x.shape[0], r.cot.shape[3]
    rows, cols = r.own.shape[1], r.own.shape[2]

    def pack(out, input_row, row, pick):
        at = 0
        for g in range(groups):
            for n in range(over):
                value = r.x[g, input_row(n)]
                out[at : at + 2 * cols, :] = pick(value, r.x[g, n])
                at += 2 * cols
        for k in range(0, width, 256):
            for g in range(groups):
                for n in range(rim):
                    lanes = slice(k, k + 256)
                    out[at : at + cols, :] = pick(r.cot[g, row(n), :, lanes], r.cot[g, n, :, lanes])
                    at += cols
        for g in range(groups):
            for n in range(rim):
                out[at : at + cols, :] = pick(wide(r.own[g, row(n)], 256), wide(r.own[g, n], 256))
                at += cols

    last = r.x.shape[1] - over
    copies.wait(N.x, N.cot)
    if hasattr(r, N.up):
        pack(r.down, lambda n: last + n, lambda n: rows - rim + n, lambda tail, head: tail)
        pack(r.up, lambda n: last + n, lambda n: rows - rim + n, lambda tail, head: head)
    else:
        bottom = r.flags[0] == 1
        pack(r.down, lambda n: last + n, lambda n: rows - rim + n, lambda tail, head: jnp.where(bottom, head, tail))


def rim_rows(r, own, n_own, n_rim, base, cols, split):
    groups = own.shape[0]
    size = groups * n_rim * cols

    def flat(ref, g, n):
        at = [base + k * size + (g * n_rim + n) * cols for k in range(split)]
        return jnp.concatenate([ref[p : p + cols, :] for p in at], axis=1).astype(f32)

    def read(g, n):
        if n < n_rim:
            return jnp.where(r.flags[0] == 1, flat(r.top, g, n), 0.0)
        if n < n_rim + n_own:
            return own[g, n - n_rim].astype(f32)
        return jnp.where(r.flags[1] == 1, flat(r.bot, g, n - n_rim - n_own), 0.0)

    return read


def fields(r):
    groups, width = r.x.shape[0], r.cot.shape[3]
    rows, cols = r.own.shape[1], r.own.shape[2]
    base = over * groups * 2 * cols
    piece = rim * groups * cols
    blocks = width // 256
    x = rim_rows(r, r.x, 2 * rows, over, 0, 2 * cols, 1)
    mask = rim_rows(r, r.own, rows, rim, base + blocks * piece, cols, 1)
    cot = rim_rows(r, r.cot, rows, rim, base, cols, blocks)
    return x, lambda g, n: mask(g, n)[:, :128], cot


def strips_kernel(r, copies):
    groups, width = r.x.shape[0], r.cot.shape[3]
    rows, cols = r.own.shape[1], r.own.shape[2]
    x, mask, cot = fields(r)
    lines = (2 * rows + 2 * over) * groups, (rows + 2 * rim) * groups, (rows + 3) * groups
    for raw, read, first, count, w in (
        (r.raw_x, x, 0, lines[0], 2 * cols),
        (r.raw_m, mask, 0, lines[1], cols),
        (r.raw_c, cot, 2, lines[2], cols),
    ):
        for at in range(count):
            value = read(at % groups, at // groups + first)
            for k in range(raw.shape[0]):
                raw[k, at * w : (at + 1) * w, :] = value[:, k * 128 : (k + 1) * 128]
    for out, x0, m0, c0 in ((r.right, 2 * cols - over, cols - rim, cols - 2), (r.left, 0, 0, 0)):
        pieces = []
        for c in range(over):
            pieces.append([strided(r.raw_x, k, x0 + c, lines[0], 2 * cols) for k in range(2)])
        for c in range(0, rim + 1, 2):
            pieces.append([strided(r.raw_m, 0, m0 + min(c + k, rim - 1), lines[1], cols) for k in range(2)])
        for c in range(2):
            for h in range(0, width // 128, 2):
                pieces.append([strided(r.raw_c, h + k, c0 + c, lines[2], cols) for k in range(2)])
        at = 0
        for low, high in pieces:
            r.flat[at : at + low.shape[0], :] = jnp.concatenate([low, high], axis=1)
            at += low.shape[0]
        if at < r.flat.shape[0]:
            r.flat[at:, :] = jnp.zeros((r.flat.shape[0] - at, 256), f32)
        out[...] = r.flat[...].astype(bf16)


def stats_kernel(r, copies):
    groups, cin = r.x.shape[0], r.x.shape[3]
    rows, S = r.own.shape[1], r.own.shape[2]
    L = groups * S
    width = r.w1.shape[2]
    raw = r.raw
    for n in range(2 * rows + 1):
        for g in range(groups):
            line = n * groups + g
            src = (r.top[g, 0] if n == 0 else r.x[g, n - 1]).astype(f32)
            side = r.lft[g, n].astype(f32)
            for k in range(raw.shape[0]):
                raw[k, line, 7:8, :] = side[:, k * 128 : (k + 1) * 128]
                raw[k, line, 8:, :] = src[:, k * 128 : (k + 1) * 128]
    for out, n_rows, start in ((r.xe, rows, 1), (r.xo, rows + 1, 0)):
        for n in range(n_rows):
            for b in range(3):
                for k in range(raw.shape[0]):
                    parts = [
                        raw[k, (2 * n + start) * groups + g, pl.ds(7 + b, S, stride=2), :]
                        for g in range(groups)
                    ]
                    at = b * cin + k * 128
                    out[n * L : (n + 1) * L, at : at + 128] = jnp.concatenate(
                        parts, axis=0
                    ).astype(bf16)
    mask = jnp.concatenate(
        [r.own[g, i].astype(f32) for i in range(rows) for g in range(groups)], axis=0
    )
    M = rows * L
    z = matmul(r.xo[0:M, :], r.w1[0])
    z += matmul(r.xe[...], r.w1[1])
    z += matmul(r.xo[L : L + M, :], r.w1[2])
    zp = matmul(r.xe[:, cin : 2 * cin], r.wp[...])
    zm, zpm = z * wide(mask, width), zp * wide(mask, width)
    row = jnp.concatenate(
        [column_sum(zm), column_sum(zm * z), column_sum(zpm), column_sum(zpm * zp), column_sum(mask)], axis=1
    )
    r.spread[...] = jnp.broadcast_to(row[None], r.spread.shape)
    copies.start(N.spread)
    copies.wait(N.spread)


def first_kernel(r, copies):
    groups, cin, width = r.x.shape[0], r.x.shape[3], r.cot.shape[3]
    rows, cols = r.own.shape[1], r.own.shape[2]
    S = cols + 8
    L = groups * S
    W = 2 * cols + 24
    V = cols + 16
    x, mask, cot = fields(r)
    lines = (2 * rows + 2 * over) * groups, (rows + 2 * rim) * groups, (rows + 3) * groups
    tail = jnp.zeros((W - 8 - 2 * cols, 128), f32)
    r.raw_m[...] = jnp.zeros(r.raw_m.shape, f32)
    r.raw_c[...] = jnp.zeros(r.raw_c.shape, f32)
    for at in range(lines[0]):
        value = x(at % groups, at // groups)
        for k in range(r.raw_x.shape[0]):
            r.raw_x[k, at * W + 8 : at * W + 8 + 2 * cols, :] = value[:, k * 128 : (k + 1) * 128]
            r.raw_x[k, at * W + 8 + 2 * cols : (at + 1) * W, :] = tail
    for strip, x0, m0, c0 in ((r.lft, 8 - over, 8 - rim, 6), (r.rgt, 8 + 2 * cols, 8 + cols, 8 + cols)):
        r.flat[...] = strip[...].astype(f32)
        at = 0
        for c in range(over):
            for k in range(2):
                r.raw_x[k, pl.ds(x0 + c, lines[0], stride=W), :] = r.flat[at : at + lines[0], k * 128 : (k + 1) * 128]
            at += lines[0]
        for c in range(0, rim + 1, 2):
            for k in range(2):
                if c + k < rim:
                    r.raw_m[0, pl.ds(m0 + c + k, lines[1], stride=V), :] = r.flat[
                        at : at + lines[1], k * 128 : (k + 1) * 128
                    ]
            at += lines[1]
        for c in range(2):
            for h in range(0, width // 128, 2):
                for k in range(2):
                    r.raw_c[h + k, pl.ds(c0 + c, lines[2], stride=V), :] = r.flat[
                        at : at + lines[2], k * 128 : (k + 1) * 128
                    ]
                at += lines[2]
    for out, n_rows, start in ((r.xe, rows + 5, 2), (r.xo, rows + 6, 1)):
        for n in range(n_rows):
            for b in range(3):
                for k in range(r.raw_x.shape[0]):
                    parts = [
                        strided(r.raw_x, k, ((2 * n + start) * groups + g) * W + 3 + b, S, 2) for g in range(groups)
                    ]
                    at = b * cin + k * 128
                    out[n * L : (n + 1) * L, at : at + 128] = jnp.concatenate(parts, axis=0).astype(bf16)
    copies.start(N.xe, N.xo)
    for at in range(lines[1]):
        r.raw_m[0, at * V + 8 : at * V + 8 + cols, :] = mask(at % groups, at // groups)
    for n in range(1, rows + 6):
        for g in range(groups):
            to, at = (n - 1) * L + g * S, (n * groups + g) * V
            r.maskp[to : to + S, :] = r.raw_m[0, at + 6 : at + 6 + S, :]
    for at in range(lines[2]):
        value = cot(at % groups, at // groups + 2)
        for k in range(r.raw_c.shape[0]):
            lanes = slice(k * 128, (k + 1) * 128)
            r.raw_c[k, at * V + 8 : at * V + 8 + cols, :] = value[:, lanes]
            r.cotq[at * S : (at + 1) * S, lanes] = r.raw_c[k, at * V + 7 : at * V + 7 + S, :]
    copies.start(N.cotq)
    r.ownp[...] = jnp.zeros(r.ownp.shape, f32)
    for i in range(rows):
        for g in range(groups):
            at = (i + 2) * L + g * S + 2
            r.ownp[at : at + cols, :] = r.own[g, i].astype(f32)
    copies.wait(N.w1, N.wp)
    for k, (m0, m) in enumerate(chunks(r.pre1.shape[0], r.pre1.shape[0] // 3)):
        z = matmul(r.xo[m0 : m0 + m, :], r.w1[0])
        z += matmul(r.xe[m0 : m0 + m, :], r.w1[1])
        z += matmul(r.xo[L + m0 : L + m0 + m, :], r.w1[2])
        r.pre1[m0 : m0 + m, :] = z
        copies.start((N.pre1, k))
        r.prep[m0 : m0 + m, :] = matmul(r.xe[m0 : m0 + m, cin : 2 * cin], r.wp[...])
        copies.start((N.prep, k))
    copies.wait(N.xe, N.xo, N.pre1, N.prep, N.cotq)


def second_kernel(r, copies):
    width = r.gain.shape[1]
    t = jnp.sum(r.tot1[...], axis=0)
    n = wide(t[:, 4 * width :], width)
    center, inv = moments(t[:, :width], t[:, width : 2 * width], n)
    proj = moments(t[:, 2 * width : 3 * width], t[:, 3 * width : 4 * width], n)
    r.mom1[...] = jnp.concatenate([center, inv, n, *proj, jnp.zeros((3, width), f32)], axis=0)
    scale = inv * r.gain[...]
    M, Q = r.pre1.shape[0], r.pre2.shape[0]
    L = (M - Q) // 2
    copies.wait(N.pre1)
    for m0, m in chunks(M, 104):
        v = (r.pre1[m0 : m0 + m, :] - center) * scale + r.shift[...]
        mask = wide(r.maskp[m0 : m0 + m, :], width)
        r.hid[m0 : m0 + m, :] = 0.5 * v * (1.0 + gelu_parts(v)) * mask
    r.hid[M:, :] = jnp.zeros((r.hid.shape[0] - M, width), f32)
    for m0, m in chunks(M, 208):
        for b in range(3):
            r.h3[m0 : m0 + m, b * width : (b + 1) * width] = r.hid[m0 + b : m0 + b + m, :].astype(bf16)
    copies.start(N.h3)
    copies.wait(N.w2)
    sums = [jnp.zeros((1, width), f32)] * 2
    for k, (m0, m) in enumerate(chunks(Q, Q // 3)):
        z = matmul(r.h3[m0 : m0 + m, :], r.w2[0])
        z += matmul(r.h3[L + m0 : L + m0 + m, :], r.w2[1])
        z += matmul(r.h3[2 * L + m0 : 2 * L + m0 + m, :], r.w2[2])
        r.pre2[m0 : m0 + m, :] = z
        copies.start((N.pre2, k))
        zm = z * wide(r.ownp[L + 1 + m0 : L + 1 + m0 + m, :], width)
        sums = [sums[0] + column_sum(zm), sums[1] + column_sum(zm * z)]
    row = jnp.concatenate(sums, axis=1)
    r.spread[...] = jnp.broadcast_to(row[None], r.spread.shape)
    copies.start(N.spread)
    copies.wait(N.h3, N.pre2, N.spread)


def part(r, at, *fields):
    bit = r.bits[0] == 1
    for k, field in enumerate(fields):
        half = field.shape[1] // 2
        low, high = field[:, :half], field[:, half:]
        r.mine[k, at : at + field.shape[0], :] = jnp.where(bit, high, low)
        r.theirs[k, at : at + field.shape[0], :] = jnp.where(bit, low, high)


def mine_of(r, row):
    half = row.shape[1] // 2
    return jnp.where(r.bits[0] == 1, row[:, half:], row[:, :half])


def third_kernel(r, copies):
    groups, rows, cols, width = r.out.shape
    S = cols + 8
    L = groups * S
    n = r.mom1[2:3, :]
    t = jnp.sum(r.tot2[...], axis=0)
    c2, i2 = moments(t[:, :width], t[:, width:], n)
    cp, ip = r.mom1[3:4, :], r.mom1[4:5, :]
    r.mom2[...] = jnp.concatenate([c2, i2, cp, ip, jnp.zeros((4, width), f32)], axis=0)
    sums = [jnp.zeros((1, width), f32)] * 3
    both_shift = r.shift2[...] + r.shiftp[...]
    total = r.grad.shape[0] // S
    for line in range(total):
        if line % (total // 2) == 0:
            k = line // (total // 2)
            copies.wait((N.pre2, k), (N.prep, k), (N.cotq, k))
        at = line * S
        shifted = slice(L + 1 + at, L + 1 + at + S)
        n2 = (r.pre2[at : at + S, :] - c2) * i2
        np_ = (r.prep[shifted, :] - cp) * ip
        v = n2 * r.gain2[...] + np_ * r.gainp[...] + both_shift
        mask = wide(r.maskp[shifted, :], width)
        own = wide(r.ownp[shifted, :], width)
        t = gelu_parts(v)
        r.field[at : at + S, :] = 0.5 * v * (1.0 + t) * mask
        g = gelu_slope(v, t) * mask * r.cotq[at : at + S, :]
        r.grad[at : at + S, :] = g
        g = g * own
        if L <= at < L + r.mine.shape[1]:
            part(r, at - L, g, n2 * own, np_ * own)
        new = [column_sum(g * n2), column_sum(g), column_sum(g * np_)]
        sums = [a + b for a, b in zip(sums, new)]
        if (line + 1) % (total // 2) == 0:
            copies.start((N.grad, (line + 1) // (total // 2) - 1))
    row = jnp.concatenate(sums, axis=1)
    r.spread[...] = jnp.broadcast_to(row[None], r.spread.shape)
    copies.start(N.spread, N.mine, N.theirs)
    for i in range(rows):
        for g in range(groups):
            at = (i + 1) * L + g * S + 1
            r.out[g, i, :, :] = r.field[at : at + cols, :].astype(bf16)
    copies.start(N.out)
    copies.wait(N.grad, N.out, N.spread, N.mine, N.theirs)


def fourth_kernel(r, copies):
    width = r.gain2.shape[1]
    Q = r.pre2.shape[0]
    rows_w = r.gpu.shape[0]
    L = (Q - rows_w) // 3
    n = r.mom1[2:3, :]
    c2, i2, cp, ip = (r.mom2[k : k + 1, :] for k in range(4))
    t3 = jnp.sum(r.tot3[...], axis=0)
    gg2, gs, ggp = (t3[:, k * width : (k + 1) * width] for k in range(3))
    r.gain_second[...], r.shift_second[...], r.gain_proj[...], r.shift_proj[...] = gg2, gs, ggp, gs
    tiny = N.gain_second, N.shift_second, N.gain_proj, N.shift_proj
    copies.start(*tiny)
    for m0, m in chunks(Q, L):
        if m0 in (0, 6 * L):
            k = m0 // (6 * L)
            copies.wait((N.grad, k), (N.pre2, k), (N.prep, k))
        shifted = slice(L + 1 + m0, L + 1 + m0 + m)
        mask = wide(r.maskp[shifted, :], width) / n
        n2 = (r.pre2[m0 : m0 + m, :] - c2) * i2
        np_ = (r.prep[shifted, :] - cp) * ip
        g = r.grad[m0 : m0 + m, :]
        r.gq[m0 : m0 + m, :] = (r.gain2[...] * i2) * (g - mask * (gs + n2 * gg2))
        r.gpq[m0 : m0 + m, :] = (r.gainp[...] * ip) * (g - mask * (gs + np_ * ggp))
    r.gq[Q:, :] = jnp.zeros((r.gq.shape[0] - Q, width), f32)
    copies.start(N.gq)
    for m0, m in chunks(rows_w, 96):
        r.gpu[m0 : m0 + m, :] = r.gpq[L + 1 + m0 : L + 1 + m0 + m, :].astype(bf16)
    copies.start(N.gpu)
    copies.wait(N.gpu, N.gq, *tiny)


def hidden_kernel(r, copies):
    width = r.gain.shape[1]
    Q = r.gq.shape[0] - 8
    L = (r.keep.shape[0] - Q) // 2
    center, inv = r.mom1[0:1, :], r.mom1[1:2, :]
    copies.wait(N.gq)
    for m0, m in chunks(Q, 176):
        for b in range(3):
            r.g3[m0 : m0 + m, b * width : (b + 1) * width] = r.gq[m0 + b : m0 + b + m, :].astype(bf16)
    U = r.act.shape[0]
    for a in range(3):
        copies.wait((N.w2, a))
        gh = jnp.zeros((U, width), f32)
        for b in range(3):
            gh += matmul_nt(
                r.g3[L * a : L * a + U, b * width : (b + 1) * width],
                r.w2[2 - a, (2 - b) * width : (3 - b) * width, :],
            )
        r.act[...] = gh if a == 0 else r.act[...] + gh
    copies.wait(N.keep)
    sums = [jnp.zeros((1, width), f32)] * 2
    for k, (m0, m) in enumerate(chunks(U, L)):
        frame = slice(2 * L + 2 + m0, 2 * L + 2 + m0 + m)
        n1 = (r.keep[frame, :] - center) * inv
        v = n1 * r.gain[...] + r.shift[...]
        mask = wide(r.maskp[frame, :], width)
        g = gelu_slope(v, gelu_parts(v)) * mask * r.act[m0 : m0 + m, :]
        r.act[m0 : m0 + m, :] = g
        r.normed[m0 : m0 + m, :] = n1 * mask
        if k % 3 == 2:
            copies.start((N.act, k // 3), (N.normed, k // 3))
        own = wide(r.ownp[frame, :], width)
        g = g * own
        if m0 < r.mine.shape[1]:
            part(r, m0, g, n1 * own)
        sums = [sums[0] + column_sum(g * n1), sums[1] + column_sum(g)]
    row = jnp.concatenate(sums, axis=1)
    r.spread[...] = jnp.broadcast_to(row[None], r.spread.shape)
    copies.start(N.spread, N.mine, N.theirs)
    copies.wait(N.act, N.normed, N.spread, N.mine, N.theirs)


def split_store(r, rows, unit, first):
    quarter = unit // 4
    for k in range(rows // unit):
        for bit, base, sent, kept in ((1, 0, r.sent_a, r.kept_a), (2, 2 * quarter, r.sent_b, r.kept_b)):
            keep = pl.multiple_of(k * unit + base + r.bits[bit] * quarter, quarter)
            send = pl.multiple_of(k * unit + base + (1 - r.bits[bit]) * quarter, quarter)
            sent[first + k] = r.acc[pl.ds(send, quarter), :].astype(bf16)
            kept[first + k] = r.acc[pl.ds(keep, quarter), :]


def weights_second_kernel(r, copies):
    width = r.h3.shape[1] // 3
    cin = r.xe.shape[1] // 3
    rows_w = r.mine.shape[1]
    L = (r.h3.shape[0] - rows_w) // 5
    per = width // cin
    t3 = jnp.sum(r.tot3[...], axis=0)
    n = mine_of(r, r.mom1[2:3, :])
    gg2, gs, ggp = (mine_of(r, t3[:, k * width : (k + 1) * width]) / n for k in range(3))
    scale2, scalep = mine_of(r, r.gain2[...] * r.mom2[1:2, :]), mine_of(r, r.gainp[...] * r.mom2[3:4, :])
    half = scale2.shape[1]
    for source, name, own, out in ((r.mine, N.mine, r.ownp, r.near), (r.far3, N.far3, r.ownp_far, r.far)):
        copies.wait(name)
        r.pad[:, 0:8, :] = jnp.zeros((3, 8, half), f32)
        r.pad[:, 8:, :] = source[...]
        for m0, m in chunks(rows_w, 96):
            mask = wide(own[2 * L + 1 + m0 : 2 * L + 1 + m0 + m, :], half)
            rows = slice(8 + m0, 8 + m0 + m)
            back = mask * gs + r.pad[1, rows, :] * gg2
            out[m0 : m0 + m, :] = (scale2 * (r.pad[0, rows, :] - back)).astype(bf16)
            mask = wide(own[2 * L + m0 : 2 * L + m0 + m, :], half)
            rows = slice(7 + m0, 7 + m0 + m)
            back = mask * gs + r.pad[2, rows, :] * ggp
            out[rows_w + m0 : rows_w + m0 + m, :] = (scalep * (r.pad[0, rows, :] - back)).astype(bf16)
    for b in range(3):
        lanes = slice(b * width, (b + 1) * width)
        copies.wait((N.h3, b), (N.h3_far, b))
        for a in range(3):
            at = L * a + L
            r.acc[...] = matmul_tn(r.h3[at : at + rows_w, lanes], r.near[:rows_w, :]) + matmul_tn(
                r.h3_far[at : at + rows_w, lanes], r.far[:rows_w, :]
            )
            split_store(r, width, cin, (3 * b + a) * per)
        copies.start(*((name, b) for name in CHUNKS))
    at = 2 * L
    copies.wait(N.xe, N.xe_far)
    middle = slice(cin, 2 * cin)
    r.acc[0:cin, :] = matmul_tn(r.xe[at : at + rows_w, middle], r.near[rows_w:, :]) + matmul_tn(
        r.xe_far[at : at + rows_w, middle], r.far[rows_w:, :]
    )
    split_store(r, cin, cin, 9 * per)
    copies.start(*((name, 3) for name in CHUNKS))
    copies.wait(*CHUNKS)


def first_back(r, gg, gs, count):
    width = r.gain.shape[1]
    U = r.act.shape[0]
    L = U - r.rows_w
    inv, n = r.mom1[1:2, :], r.mom1[2:3, :]
    gg, gs = gg / n, gs / n
    scale = r.gain[...] * inv
    r.gf[0:8, :] = jnp.zeros((8, width), f32)
    r.gf[8 + count :, :] = jnp.zeros((r.gf.shape[0] - 8 - count, width), f32)
    for m0, m in chunks(count, L):
        mask = wide(r.maskp[2 * L + 2 + m0 : 2 * L + 2 + m0 + m, :], width)
        back = mask * gs + r.normed[m0 : m0 + m, :] * gg
        r.gf[8 + m0 : 8 + m0 + m, :] = scale * (r.act[m0 : m0 + m, :] - back)


def weights_first_kernel(r, copies):
    rows_w = r.mine.shape[1]
    cin = r.xe.shape[1] // 3
    L = (r.xe.shape[0] - rows_w) // 5
    width = r.gain.shape[1]
    t4 = jnp.sum(r.tot4[...], axis=0)
    r.gain_first[...], r.shift_first[...] = t4[:, :width], t4[:, width:]
    copies.start(N.gain_first, N.shift_first)
    n = mine_of(r, r.mom1[2:3, :])
    gg, gs = mine_of(r, t4[:, :width]) / n, mine_of(r, t4[:, width:]) / n
    scale = mine_of(r, r.gain[...] * r.mom1[1:2, :])
    half = scale.shape[1]
    for source, name, own, out in ((r.mine, N.mine, r.ownp, r.near), (r.far4, N.far4, r.ownp_far, r.far)):
        copies.wait(name)
        r.pad[:, 0:8, :] = jnp.zeros((2, 8, half), f32)
        r.pad[:, 8:, :] = source[...]
        for m0, m in chunks(rows_w, 96):
            mask = wide(own[2 * L + m0 : 2 * L + m0 + m, :], half)
            rows = slice(6 + m0, 6 + m0 + m)
            back = mask * gs + r.pad[1, rows, :] * gg
            out[m0 : m0 + m, :] = (scale * (r.pad[0, rows, :] - back)).astype(bf16)
    copies.wait(N.xe, N.xe_far)
    for k, a in enumerate((1, 0, 2)):
        if k == 1:
            copies.wait(N.xo, N.xo_far)
        source, source_far = (r.xe, r.xe_far) if a == 1 else (r.xo, r.xo_far)
        at = (3 if a == 2 else 2) * L
        for b in range(3):
            lanes = slice(b * cin, (b + 1) * cin)
            r.acc[lanes, :] = matmul_tn(source[at : at + rows_w, lanes], r.near[...]) + matmul_tn(
                source_far[at : at + rows_w, lanes], r.far[...]
            )
        split_store(r, 3 * cin, cin, a * 3)
        copies.start(*((name, a) for name in CHUNKS))
    copies.wait(N.gain_first, N.shift_first, *CHUNKS)


def inputs_kernel(r, copies):
    width = r.gpu.shape[1]
    groups, rows, cols = r.out.shape[0], r.out.shape[1] // 2, r.out.shape[2] // 2
    cin = r.out.shape[3]
    M = r.gpu.shape[0]
    S = cols + 8
    L = groups * S
    lines = r.lines
    U = r.act.shape[0]
    r.rows_w = M
    copies.wait(N.act, N.normed)
    first_back(r, r.gg[...], r.gs[...], U)
    for m0, m in chunks(U, 144):
        r.gu[m0 : m0 + m, :width] = r.gf[8 + m0 : 8 + m0 + m, :].astype(bf16)
        r.gu[m0 : m0 + m, width:] = r.gf[9 + m0 : 9 + m0 + m, :].astype(bf16)
    copies.wait(N.gpu, N.w1, N.wp)

    def tap(m0, m, a, b):
        di, dj = (1 if a == 0 else 0), (1 if b == 0 else 0)
        return matmul_nt(
            r.gu[di * L + m0 : di * L + m0 + m, dj * width : (dj + 1) * width],
            r.w1[a, b * cin : (b + 1) * cin, :],
        )

    for m0, m in chunks(M, 2 * L):
        pieces = {
            (0, 0): tap(m0, m, 1, 1) + matmul_nt(r.gpu[m0 : m0 + m, :], r.wp[...]),
            (0, 1): tap(m0, m, 1, 2) + tap(m0, m, 1, 0),
            (1, 0): tap(m0, m, 2, 1) + tap(m0, m, 0, 1),
            (1, 1): tap(m0, m, 2, 2) + tap(m0, m, 2, 0) + tap(m0, m, 0, 2) + tap(m0, m, 0, 0),
        }
        for (ro, co), v in pieces.items():
            for k in range(m // S):
                line = m0 // S + k
                i, g = line // groups, line % groups
                for h in range(lines.shape[0]):
                    lines[h, (2 * i + ro) * groups + g, pl.ds(co, cols, stride=2), :] = v[
                        k * S : k * S + cols, h * 128 : (h + 1) * 128
                    ]
    for n in range(2 * rows):
        for g in range(groups):
            for h in range(lines.shape[0]):
                r.out[g, n, :, h * 128 : (h + 1) * 128] = lines[h, n * groups + g].astype(bf16)
    copies.start(N.out)
    copies.wait(N.out)


def widen(half, side, taps, per, swapped, into=None):
    total, n, m = half.shape
    extra = total - taps * per
    order = [(t % 3 * 3 + t // 3) if swapped else t for t in range(taps)]
    jobs = [(t * per, per, 0, order[t] * per) for t in range(taps)] + [(taps * per, 1, 1, 0)] * extra
    more = list(into or [])

    def body(side_ref, half_ref, *refs):
        outs = refs[len(more) : len(more) + 1 + extra]
        narrow, full, sems = refs[len(more) + 1 + extra :]
        lanes = pl.ds(pl.multiple_of(side_ref[0] * m, m), m)
        reads = [
            pltpu.make_async_copy(half_ref.at[pl.ds(at, size)], narrow.at[pl.ds(at, size)], sems.at[0, k])
            for k, (at, size, _, _) in enumerate(jobs)
        ]
        writes = [
            pltpu.make_async_copy(full.at[pl.ds(at, size)], outs[which].at[pl.ds(to, size), :, lanes], sems.at[1, k])
            for k, (at, size, which, to) in enumerate(jobs)
        ]
        for read in reads:
            read.start()
        for k, (at, size, _, _) in enumerate(jobs):
            reads[k].wait()
            full[at : at + size] = narrow[at : at + size].astype(f32)
            writes[k].start()
        for write in writes:
            write.wait()

    hbm = pl.BlockSpec(memory_space=pltpu.HBM)
    return pl.pallas_call(
        body,
        out_shape=[shape((taps * per, n, 2 * m))] + [shape((1, n, 2 * m))] * extra,
        in_specs=[pl.BlockSpec(memory_space=pltpu.SMEM)] + [hbm] * (1 + len(more)),
        out_specs=[hbm] * (1 + extra),
        scratch_shapes=[
            pltpu.VMEM((total, n, m), bf16),
            pltpu.VMEM((total, n, m), f32),
            pltpu.SemaphoreType.DMA((2, len(jobs))),
        ],
        input_output_aliases={2 + k: k for k in range(len(more))},
        compiler_params=pltpu.CompilerParams(vmem_limit_bytes=20 * 1024 * 1024),
        cost_estimate=pl.CostEstimate(flops=0, bytes_accessed=0, transcendentals=0),
    )(side.reshape(1), half, *more)


def halve_kernel(r, copies):
    for p in range(r.count):
        kept, got = getattr(r, f"kept{p}"), getattr(r, f"got{p}")
        copies.wait(f"kept{p}", f"got{p}")
        to_send, to_keep = getattr(r, f"sent{p}"), getattr(r, f"left{p}")
        bit = r.bits[r.steps[p]] == 1
        h = kept.shape[1] // 2
        for t in range(kept.shape[0]):
            total = kept[t] + got[t].astype(f32)
            low, high = total[:h], total[h:]
            to_send[t] = jnp.where(bit, low, high).astype(bf16)
            to_keep[t] = jnp.where(bit, high, low)
        copies.start(f"sent{p}", f"left{p}")
    copies.wait(*(name for name in copies.jobs if name[:4] in (N.sent, N.left)))


def halve(bits, pairs, steps, cost):
    ins = dict(bits=bits)
    for p, (kept, got) in enumerate(pairs):
        ins[f"kept{p}"], ins[f"got{p}"] = kept, got
    taps, n, m = pairs[0][0].shape
    dims = (taps, n // 2, m)
    names = [str(p) for p in range(len(pairs))]
    outs = {}
    for name in names:
        outs[N.sent + name], outs[N.left + name] = shape(dims, bf16), shape(dims)

    def body(r, copies):
        r.count, r.steps = len(pairs), steps
        halve_kernel(r, copies)

    far_in = tuple(n for n in ins if n != N.bits)
    out = call(body, ins, outs, far_in=far_in, far_out=tuple(outs), smem=(N.bits,), cost=cost, limit=60)
    return [(out[N.sent + name], out[N.left + name]) for name in names]


def shifted(value, axis, steps):
    count = lax.axis_size(axis)
    first, last = (max(0, -steps), min(count, count - steps))
    return lax.ppermute(value, axis, [(source, source + steps) for source in range(first, last)])


def gather_sum(spread):
    return lax.all_to_all(spread, axes, 0, 0)


def bit_of(axis, step):
    return (lax.axis_index(axis) // step) % 2


def partner(value, axis, step):
    count = lax.axis_size(axis)
    return lax.ppermute(value, axis, [(i, i ^ step) for i in range(count)])


def steps_of(axis):
    count, step, out = lax.axis_size(axis), 1, []
    while step < count:
        out.append((axis, step))
        step *= 2
    return out


def split(total, axis, step):
    n = total.shape[1] // 2
    bit = bit_of(axis, step) == 1
    low, high = total[:, :n], total[:, n:]
    return jnp.where(bit, low, high).astype(bf16), jnp.where(bit, high, low)


def joined(value, other, axis, step, dim=1):
    bit = bit_of(axis, step) == 1
    return jnp.concatenate([jnp.where(bit, other, value), jnp.where(bit, value, other)], axis=dim)


class Tree:
    def __init__(self, parts, bits, plane, rest, core):
        self.bits, self.place = bits, {step: k for k, step in enumerate([core, *plane, *rest])}
        self.sent_a, self.kept_a, self.sent_b, self.kept_b = parts
        self.a, self.b, self.rest, self.core = plane, plane[::-1], rest, core
        p, n = len(plane), len(rest)
        self.stages = [(N.plane, k) for k in range(p)] + [(N.rest, k) for k in range(n)]
        self.stages += [(N.rest_join, k) for k in reversed(range(n))] + [(N.plane_join, k) for k in reversed(range(p))]
        self.stages += [(N.core, 0)]

    def next(self):
        return self.stages[0] if self.stages else None

    def start(self):
        kind, k = self.stages[0]
        if kind == N.plane:
            self.got = partner(self.sent_a, *self.a[k]), partner(self.sent_b, *self.b[k])
        elif kind == N.rest:
            self.got = (partner(self.sent, *self.rest[k]),)
        elif kind == N.rest_join:
            self.got = (partner(self.value, *self.rest[k]),)
        elif kind == N.plane_join:
            self.got = partner(self.value_a, *self.a[k]), partner(self.value_b, *self.b[k])
        else:
            self.got = (partner(self.value, *self.core),)

    def finish(self, cost=0):
        kind, k = self.stages.pop(0)
        if kind == N.plane:
            pairs = [(self.kept_a, self.got[0]), (self.kept_b, self.got[1])]
            nexts = [order[k + 1] for order in (self.a, self.b) if k + 1 < len(order)]
            if nexts and cost:
                pairs = halve(self.bits, pairs, [self.place[step] for step in nexts], cost)
                (self.sent_a, self.kept_a), (self.sent_b, self.kept_b) = pairs
                return
            total_a, total_b = (kept + got.astype(f32) for kept, got in pairs)
            if nexts:
                self.sent_a, self.kept_a = split(total_a, *nexts[0])
                self.sent_b, self.kept_b = split(total_b, *nexts[1])
            else:
                self.taps = total_a.shape[0]
                self.split_rest(jnp.concatenate([total_a, total_b], axis=0), 0)
        elif kind == N.rest:
            self.split_rest(self.kept + self.got[0].astype(f32), k + 1)
        elif kind == N.rest_join:
            self.value = joined(self.value, self.got[0], *self.rest[k])
            self.value_a, self.value_b = self.value[: self.taps], self.value[self.taps :]
        elif kind == N.plane_join:
            self.value_a = joined(self.value_a, self.got[0], *self.a[k])
            self.value_b = joined(self.value_b, self.got[1], *self.b[k])
            self.value = jnp.concatenate([self.value_a, self.value_b], axis=1)

    def split_rest(self, total, k):
        if k < len(self.rest):
            self.sent, self.kept = split(total, *self.rest[k])
        else:
            self.value = total.astype(bf16)


def lockstep(*trees, beside=()):
    for t in trees:
        t.start()
    got, beside = lax.optimization_barrier(([t.got for t in trees], beside))
    for t, g in zip(trees, got):
        t.got = g
        t.finish()
    return beside


def on_device(inputs, w_first, gain_first, shift_first, w_second, gain_second, shift_second, w_proj, gain_proj, shift_proj, valid_mask, cotangent):
    groups, rows_in, cols_in, cin = inputs.shape
    rows, cols = rows_in // 2, cols_in // 2
    width = w_first.shape[3]
    half = width // 2
    S = cols + 8
    L = groups * S
    devices = lax.axis_size(N.rows) * lax.axis_size(N.cols) * lax.axis_size(N.grp)
    plane = steps_of(N.cols)
    core = steps_of(N.rows)[0]
    rest = steps_of(N.rows)[1:] + steps_of(N.grp)
    bits = jnp.stack([bit_of(*step) for step in (core, *plane, *rest)]).astype(jnp.int32)
    w1 = w_first.reshape(3, 3 * cin, width)
    w2 = w_second.reshape(3, 3 * width, width)
    as_row = lambda v: v.reshape(1, -1)
    own = jnp.broadcast_to(valid_mask.astype(bf16)[..., None], valid_mask.shape + (128,))
    MP, MQ, MU, MW = (rows + 5) * L, (rows + 3) * L, (rows + 1) * L, rows * L
    px = lambda m, k: 2 * m * k * width
    vec = lambda k: shape((1, k * width))
    all_devices = lambda k: shape((devices, 1, k))
    g1, b1, g2, b2, gp, bp = map(
        as_row, (gain_first, shift_first, gain_second, shift_second, gain_proj, shift_proj)
    )

    top1 = shifted(inputs[:, -1:], N.rows, 1)
    me, count = lax.axis_index(N.rows), lax.axis_size(N.rows)
    flags = jnp.stack([me > 0, me < count - 1]).astype(jnp.int32)
    flat_rows = shape((over * groups * cols_in + (width // 256 + 1) * rim * groups * cols, 256), bf16)
    packed = call(
        vertical_kernel,
        dict(flags=flags, x=inputs, cot=cotangent, own=own),
        dict(down=flat_rows) if count == 2 else dict(down=flat_rows, up=flat_rows),
        far_in=(N.x, N.cot),
        smem=(N.flags,),
        parts=dict(x=end_parts(rows_in, over), cot=end_parts(rows, rim)),
    )
    if count == 2:
        top = bot = lax.ppermute(packed["down"], "rows", [(0, 1), (1, 0)])
    else:
        top, bot = shifted(packed[N.down], N.rows, 1), shifted(packed[N.up], N.rows, -1)
    lft1 = shifted(jnp.concatenate([top1[:, :, -1:], inputs[:, :, -1:]], axis=1), N.cols, 1)
    (top, bot), lft1 = lax.optimization_barrier(((top, bot), lft1))
    lines = (rows_in + 2 * over) * groups, (rows + 2 * rim) * groups, (rows + 3) * groups
    n_strip = over * lines[0] + (rim + 1) // 2 * lines[1] + width // 128 * lines[2]
    n_strip = -(-n_strip // 16) * 16
    near = dict(flags=flags, x=inputs, cot=cotangent, own=own, top=top, bot=bot)
    strips = call(
        strips_kernel,
        near,
        dict(right=shape((n_strip, 256), bf16), left=shape((n_strip, 256), bf16)),
        dict(
            raw_x=pltpu.VMEM((cin // 128, lines[0] * cols_in, 128), f32),
            raw_m=pltpu.VMEM((1, lines[1] * cols, 128), f32),
            raw_c=pltpu.VMEM((width // 128, lines[2] * cols, 128), f32),
            flat=pltpu.VMEM((n_strip, 256), f32),
        ),
        smem=(N.flags,),
    )
    lft, rgt = shifted(strips[N.right], N.cols, 1), shifted(strips[N.left], N.cols, -1)
    lft1, _ = lax.optimization_barrier((lft1, strips[N.right]))
    stats = call(
        stats_kernel,
        dict(x=inputs, top=top1, lft=lft1, own=own, w1=w1, wp=w_proj),
        dict(spread=all_devices(4 * width + 128)),
        dict(
            raw=pltpu.VMEM((cin // 128, (rows_in + 1) * groups, cols_in + 8, 128), f32),
            xe=pltpu.VMEM((rows * groups * cols, 3 * cin), bf16),
            xo=pltpu.VMEM(((rows + 1) * groups * cols, 3 * cin), bf16),
        ),
        far_out=(N.spread,),
    )
    tot1 = gather_sum(stats[N.spread])

    first = call(
        first_kernel,
        dict(**near, lft=lft, rgt=rgt, w1=w1, wp=w_proj),
        dict(
            pre1=shape((MP, width)),
            prep=shape((MP, width)),
            xe=shape((MP, 3 * cin), bf16),
            xo=shape((MP + L, 3 * cin), bf16),
            ownp=shape((MP, 128)),
            maskp=shape((MP, 128)),
            cotq=shape((MQ, width)),
        ),
        dict(
            raw_x=pltpu.VMEM((cin // 128, lines[0] * (cols_in + 24), 128), f32),
            raw_m=pltpu.VMEM((1, lines[1] * (cols + 16), 128), f32),
            raw_c=pltpu.VMEM((width // 128, lines[2] * (cols + 16), 128), f32),
            flat=pltpu.VMEM((n_strip, 256), f32),
        ),
        far_in=(N.w1, N.wp),
        far_out=(N.xe, N.xo, N.pre1, N.prep, N.cotq),
        smem=(N.flags,),
        cost=20000000000,
        parts=dict(pre1=row_parts(MP, 3), prep=row_parts(MP, 3)),
    )
    xe, xo, ownp, maskp = first[N.xe], first[N.xo], first[N.ownp], first[N.maskp]
    far_xe, far_xo, ownp_far = partner(xe, *core), partner(xo, *core), partner(ownp, *core)

    second = call(
        second_kernel,
        dict(pre1=first[N.pre1], tot1=tot1, gain=g1, shift=b1, maskp=maskp, ownp=ownp, w2=w2),
        dict(h3=shape((MP, 3 * width), bf16), pre2=shape((MQ, width)), spread=all_devices(2 * width), mom1=shape((8, width))),
        dict(hid=pltpu.VMEM((MP + 8, width), f32)),
        far_in=(N.pre1, N.w2),
        far_out=(N.h3, N.pre2, N.spread),
        parts=dict(pre2=row_parts(MQ, 3)),
    )
    h3, pre2, mom1 = second[N.h3], second[N.pre2], second[N.mom1]
    tot2 = gather_sum(second[N.spread])
    far_h3 = partner(h3, *core)

    third = call(
        third_kernel,
        dict(
            bits=bits, pre2=pre2, prep=first[N.prep], mom1=mom1, tot2=tot2, gain2=g2, shift2=b2, gainp=gp, shiftp=bp,
            maskp=maskp, ownp=ownp, cotq=first[N.cotq],
        ),
        dict(
            out=shape((groups, rows, cols, width), bf16),
            grad=shape((MQ, width)),
            spread=all_devices(3 * width),
            mom2=shape((8, width)),
            mine=shape((3, MW, half)),
            theirs=shape((3, MW, half)),
        ),
        dict(field=pltpu.VMEM((MQ, width), f32)),
        far_in=(N.pre2, N.prep, N.cotq),
        far_out=(N.grad, N.spread, N.mine, N.theirs, N.out),
        smem=(N.bits,),
        parts=dict(
            grad=row_parts(MQ, 2), pre2=row_parts(MQ, 2), cotq=row_parts(MQ, 2), prep=cuts(L, L + MQ // 2 + 8, L + MQ + 8)
        ),
    )
    mom2 = third[N.mom2]
    tot3 = gather_sum(third[N.spread])

    def chunk_shapes(taps):
        dims = (taps, cin // 4, half)
        return dict(sent_a=shape(dims, bf16), kept_a=shape(dims), sent_b=shape(dims, bf16), kept_b=shape(dims))

    per = width // cin
    taps2 = 9 * per + 1
    second_parts = call(
        weights_second_kernel,
        dict(
            bits=bits, mine=third[N.mine], far3=partner(third[N.theirs], *core), h3=h3, h3_far=far_h3, xe=xe, xe_far=far_xe,
            tot3=tot3, mom1=mom1, mom2=mom2, gain2=g2, gainp=gp, ownp=ownp, ownp_far=ownp_far,
        ),
        chunk_shapes(taps2),
        dict(
            acc=pltpu.VMEM((width, half), f32),
            pad=pltpu.VMEM((3, MW + 8, half), f32),
            near=pltpu.VMEM((2 * MW, half), bf16),
            far=pltpu.VMEM((2 * MW, half), bf16),
        ),
        far_in=(N.mine, N.far3, N.h3, N.h3_far, N.xe, N.xe_far),
        far_out=CHUNKS,
        smem=(N.bits,),
        parts=dict(
            h3=lane_parts(3 * width, 3, pl.ds(L, MW + 2 * L)),
            h3_far=lane_parts(3 * width, 3, pl.ds(L, MW + 2 * L)),
            xe=[(0, (pl.ds(2 * L, MW), pl.ds(cin, cin)))],
            xe_far=[(0, (pl.ds(2 * L, MW), pl.ds(cin, cin)))],
            **{name: row_parts(taps2 - 1, 3) + [(3, (pl.ds(taps2 - 1, 1),))] for name in CHUNKS},
        ),
    ).values()
    grad, *second_parts = lax.optimization_barrier((third[N.grad], *second_parts))
    tree2 = Tree(second_parts, bits, plane, rest, core)
    tree2.start()
    fourth = call(
        fourth_kernel,
        dict(
            pre2=pre2, prep=first[N.prep], mom1=mom1, mom2=mom2, tot3=tot3, gain2=g2, gainp=gp,
            grad=grad, maskp=maskp, ownp=ownp,
        ),
        dict(
            gq=shape((MQ + 8, width)),
            gpu=shape((MW, width), bf16),
            gain_second=vec(1),
            shift_second=vec(1),
            gain_proj=vec(1),
            shift_proj=vec(1),
        ),
        dict(gpq=pltpu.VMEM((MQ, width), f32)),
        far_in=(N.pre2, N.prep, N.grad),
        far_out=(N.gpu, N.gq, N.gain_second, N.shift_second, N.gain_proj, N.shift_proj),
        parts=dict(grad=cuts(0, 6 * L, MQ), pre2=cuts(0, 6 * L, MQ), prep=cuts(L, 7 * L + 8, L + MQ + 8)),
    )
    hidden = call(
        hidden_kernel,
        dict(bits=bits, gq=fourth[N.gq], w2=w2, keep=first[N.pre1], mom1=mom1, gain=g1, shift=b1, maskp=maskp, ownp=ownp),
        dict(
            act=shape((MU, width)), normed=shape((MU, width)), spread=all_devices(2 * width),
            mine=shape((2, MW, half)), theirs=shape((2, MW, half)),
        ),
        dict(g3=pltpu.VMEM((MQ, 3 * width), bf16)),
        far_in=(N.gq, N.w2, N.keep),
        far_out=(N.act, N.normed, N.spread, N.mine, N.theirs),
        smem=(N.bits,),
        limit=60,
        parts=dict(
            w2=[(k, (pl.ds(2 - k, 1),)) for k in range(3)],
            keep=cuts(2 * L, 2 * L + MU + 8),
            act=row_parts(MU, 3),
            normed=row_parts(MU, 3),
        ),
    )
    tot4 = gather_sum(hidden[N.spread])
    tree2.finish(20000000000)
    near1, tree2.sent_a, tree2.sent_b = lax.optimization_barrier((hidden[N.mine], tree2.sent_a, tree2.sent_b))
    tree2.start()
    fifth = call(
        weights_first_kernel,
        dict(
            bits=bits, mine=near1, far4=partner(hidden[N.theirs], *core), xe=xe, xe_far=far_xe, xo=xo, xo_far=far_xo,
            tot4=tot4, mom1=mom1, gain=g1, ownp=ownp, ownp_far=ownp_far,
        ),
        dict(**chunk_shapes(9), gain_first=vec(1), shift_first=vec(1)),
        dict(
            acc=pltpu.VMEM((3 * cin, half), f32),
            pad=pltpu.VMEM((2, MW + 8, half), f32),
            near=pltpu.VMEM((MW, half), bf16),
            far=pltpu.VMEM((MW, half), bf16),
        ),
        far_in=(N.mine, N.far4, N.xe, N.xe_far, N.xo, N.xo_far),
        cost=20000000000,
        far_out=(*CHUNKS, N.gain_first, N.shift_first),
        smem=(N.bits,),
        parts=dict(
            xe=cuts(2 * L, 2 * L + MW),
            xe_far=cuts(2 * L, 2 * L + MW),
            xo=cuts(2 * L, 3 * L + MW),
            xo_far=cuts(2 * L, 3 * L + MW),
            **{name: row_parts(9, 3) for name in CHUNKS},
        ),
    )
    first_parts = [fifth[name] for name in CHUNKS]
    tree2.got, *first_parts = lax.optimization_barrier((tree2.got, *first_parts))
    tree2.finish()
    tree1 = Tree(first_parts, bits, plane, rest, core)

    grad_inputs = call(
        inputs_kernel,
        dict(
            act=hidden[N.act], normed=hidden[N.normed], gpu=fourth[N.gpu], w1=w1, wp=w_proj, mom1=mom1, gain=g1, maskp=maskp,
            gg=fifth[N.gain_first], gs=fifth[N.shift_first],
        ),
        dict(out=shape((groups, rows_in, cols_in, cin), bf16)),
        dict(
            lines=pltpu.VMEM((cin // 128, rows_in * groups, cols_in, 128), f32),
            gf=pltpu.VMEM((MU + 16, width), f32),
            gu=pltpu.VMEM((MU, 2 * width), bf16),
        ),
        far_in=(N.act, N.normed, N.gpu, N.w1, N.wp),
        far_out=(N.out,),
        cost=10000000000,
    )[N.out]
    side = bit_of(*core).astype(jnp.int32)
    grad_inputs = lockstep(tree2, tree1, beside=grad_inputs)
    while tree2.next() != (N.plane_join, 0):
        lockstep(tree2, tree1)
    tree2.start()
    while tree1.next() != (N.plane_join, 0):
        tree1.start()
        if tree1.next() != (N.plane_join, 1):
            tree1.finish()
        else:
            tree1.got, tree2.got = lax.optimization_barrier((tree1.got, tree2.got))
            tree1.finish()
    tree2.finish()
    tree2.start()
    tree1.start()
    grad_second = widen(tree2.got[0], 1 - side, 9, per, True, widen(tree2.value, side, 9, per, True))
    tree1.got, grad_second = lax.optimization_barrier((tree1.got, grad_second))
    grad_w2, grad_wp = grad_second
    tree1.finish()
    tree1.start()
    (grad_w1,) = widen(tree1.got[0], 1 - side, 3, 3, False, widen(tree1.value, side, 3, 3, False))

    return (
        third[N.out],
        grad_inputs,
        grad_w1.reshape(w_first.shape),
        fifth[N.gain_first].reshape(width),
        fifth[N.shift_first].reshape(width),
        grad_w2.reshape(w_second.shape),
        fourth[N.gain_second].reshape(width),
        fourth[N.shift_second].reshape(width),
        grad_wp.reshape(w_proj.shape),
        fourth[N.gain_proj].reshape(width),
        fourth[N.shift_proj].reshape(width),
    )


def solution(mesh):
    spread = P("grp", "rows", "cols", None)
    return jax.shard_map(
        on_device,
        mesh=mesh,
        in_specs=(spread,) + (P(),) * 9 + (P("grp", "rows", "cols"), spread),
        out_specs=(spread, spread) + (P(),) * 9,
        check_vma=False,
    )
```

```python
import functools

import jax
import jax.numpy as jnp
from jax import lax
from jax.experimental import pallas as pl
from jax.experimental.pallas import tpu as pltpu
from jax.sharding import PartitionSpec as P

epsilon = 1e-05
axes = ("rows", "cols", "grp")
bf16 = jnp.bfloat16
f32 = jnp.float32
inner = 0.7978845608028654
cubic = 0.044715
over = 6
CHUNKS = "sent_a", "kept_a", "sent_b", "kept_b"
rim = 3


class Names:
    def __getattr__(self, name):
        return name


N = Names()


class Refs:
    def __init__(self, named):
        self.__dict__.update(named)


class Copies:
    def __init__(self, parts, pairs, sems):
        self.jobs = {}
        for k, (name, index) in enumerate(parts):
            source, target = pairs[name]
            if index:
                source, target = source.at[index[1]], target.at[index[1]]
            self.jobs.setdefault(name, []).append(pltpu.make_async_copy(source, target, sems.at[k]))

    def start(self, *names):
        for name, *which in map(named, names):
            for job in self.jobs[name][slice(*which) if which else slice(None)]:
                job.start()

    def start_all(self, names):
        for k in range(max((len(self.jobs[n]) for n in names), default=0)):
            for n in names:
                if k < len(self.jobs[n]):
                    self.jobs[n][k].start()

    def wait(self, *names):
        for name, *which in map(named, names):
            for job in self.jobs[name][slice(*which) if which else slice(None)]:
                job.wait()


def named(name):
    return (name,) if isinstance(name, str) else (name[0], name[1], name[1] + 1)


def row_parts(total, count):
    size = total // count
    return [(k, (pl.ds(k * size, size),)) for k in range(count)]


def middle_parts(total, count):
    size = total // count
    return [(k, (slice(None), pl.ds(k * size, size))) for k in range(count)]


def end_parts(total, size):
    return [(k, (slice(None), pl.ds(at, size))) for k, at in enumerate((0, total - size))]


def cuts(*at):
    return [(k, (pl.ds(a, b - a),)) for k, (a, b) in enumerate(zip(at, at[1:]))]


def lane_parts(total, count, rows=slice(None)):
    size = total // count
    return [(k, (rows, pl.ds(k * size, size))) for k in range(count)]


def call(body, ins, outs, scratch=None, far_in=(), far_out=(), smem=(), parts=None, limit=52, cost=0):
    scratch, parts = scratch or {}, parts or {}
    far = (*far_in, *far_out)
    jobs = [(name, index) for name in far for index in parts.get(name, [None])]

    def spec(name):
        if name in smem:
            return pl.BlockSpec(memory_space=pltpu.SMEM)
        return pl.BlockSpec(memory_space=pltpu.HBM if name in far else pltpu.VMEM)

    kinds = {**{n: shape(v.shape, v.dtype) for n, v in ins.items()}, **outs}

    def run(*refs):
        plain = dict(zip([*ins, *outs], refs))
        rest = refs[len(plain) :]
        buffers = dict(zip(far, rest))
        more = dict(zip(scratch, rest[len(far) :]))
        copies = None
        if far:
            pairs = {n: (plain[n], buffers[n]) if n in far_in else (buffers[n], plain[n]) for n in far}
            copies = Copies(jobs, pairs, rest[-1])
            copies.start_all(far_in)
        body(Refs({**plain, **buffers, **more}), copies)

    buffers = [pltpu.VMEM(kinds[n].shape, kinds[n].dtype) for n in far]
    sems = [pltpu.SemaphoreType.DMA((len(jobs),))] if far else []
    result = pl.pallas_call(
        run,
        out_shape=list(outs.values()),
        in_specs=[spec(n) for n in ins],
        out_specs=[spec(n) for n in outs],
        scratch_shapes=[*buffers, *scratch.values(), *sems],
        compiler_params=pltpu.CompilerParams(vmem_limit_bytes=limit * 1024 * 1024),
        cost_estimate=pl.CostEstimate(flops=cost, bytes_accessed=0, transcendentals=0),
    )(*ins.values())
    return dict(zip(outs, result))


def shape(dims, dtype=f32):
    return jax.ShapeDtypeStruct(dims, dtype)


def wide(mask, width):
    return jnp.concatenate([mask] * (width // mask.shape[1]), axis=1)


def matmul(a, b):
    return lax.dot_general(a, b, (((1,), (0,)), ((), ())), preferred_element_type=f32)


def matmul_nt(a, b):
    return lax.dot_general(a, b, (((1,), (1,)), ((), ())), preferred_element_type=f32)


def matmul_tn(a, b):
    return lax.dot_general(a, b, (((0,), (0,)), ((), ())), preferred_element_type=f32)


def gelu_parts(v):
    return jnp.tanh(inner * (v + cubic * v * v * v))


def gelu_slope(v, t):
    return 0.5 * (1.0 + t) + 0.5 * v * (1.0 - t * t) * (inner * (1.0 + 3.0 * cubic * v * v))


def column_sum(v):
    return jnp.sum(v, axis=0, keepdims=True)


def moments(total, squares, pixel_count):
    center = total / pixel_count
    spread = squares / pixel_count - center * center
    return center, lax.rsqrt(spread + epsilon)


def chunks(total, size):
    return [(at, min(size, total - at)) for at in range(0, total, size)]


def strided(ref, k, first, count, step):
    return ref[k, pl.ds(first, count, stride=step), :]


def vertical_kernel(r, copies):
    groups, width = r.x.shape[0], r.cot.shape[3]
    rows, cols = r.own.shape[1], r.own.shape[2]

    def pack(out, input_row, row, pick):
        at = 0
        for g in range(groups):
            for n in range(over):
                value = r.x[g, input_row(n)]
                out[at : at + 2 * cols, :] = pick(value, r.x[g, n])
                at += 2 * cols
        for k in range(0, width, 256):
            for g in range(groups):
                for n in range(rim):
                    lanes = slice(k, k + 256)
                    out[at : at + cols, :] = pick(r.cot[g, row(n), :, lanes], r.cot[g, n, :, lanes])
                    at += cols
        for g in range(groups):
            for n in range(rim):
                out[at : at + cols, :] = pick(wide(r.own[g, row(n)], 256), wide(r.own[g, n], 256))
                at += cols

    last = r.x.shape[1] - over
    copies.wait(N.x, N.cot)
    if hasattr(r, N.up):
        pack(r.down, lambda n: last + n, lambda n: rows - rim + n, lambda tail, head: tail)
        pack(r.up, lambda n: last + n, lambda n: rows - rim + n, lambda tail, head: head)
    else:
        bottom = r.flags[0] == 1
        pack(r.down, lambda n: last + n, lambda n: rows - rim + n, lambda tail, head: jnp.where(bottom, head, tail))


def rim_rows(r, own, n_own, n_rim, base, cols, split):
    groups = own.shape[0]
    size = groups * n_rim * cols

    def flat(ref, g, n):
        at = [base + k * size + (g * n_rim + n) * cols for k in range(split)]
        return jnp.concatenate([ref[p : p + cols, :] for p in at], axis=1).astype(f32)

    def read(g, n):
        if n < n_rim:
            return jnp.where(r.flags[0] == 1, flat(r.top, g, n), 0.0)
        if n < n_rim + n_own:
            return own[g, n - n_rim].astype(f32)
        return jnp.where(r.flags[1] == 1, flat(r.bot, g, n - n_rim - n_own), 0.0)

    return read


def fields(r):
    groups, width = r.x.shape[0], r.cot.shape[3]
    rows, cols = r.own.shape[1], r.own.shape[2]
    base = over * groups * 2 * cols
    piece = rim * groups * cols
    blocks = width // 256
    x = rim_rows(r, r.x, 2 * rows, over, 0, 2 * cols, 1)
    mask = rim_rows(r, r.own, rows, rim, base + blocks * piece, cols, 1)
    cot = rim_rows(r, r.cot, rows, rim, base, cols, blocks)
    return x, lambda g, n: mask(g, n)[:, :128], cot


def strips_kernel(r, copies):
    groups, width = r.x.shape[0], r.cot.shape[3]
    rows, cols = r.own.shape[1], r.own.shape[2]
    x, mask, cot = fields(r)
    lines = (2 * rows + 2 * over) * groups, (rows + 2 * rim) * groups, (rows + 3) * groups
    for raw, read, first, count, w in (
        (r.raw_x, x, 0, lines[0], 2 * cols),
        (r.raw_m, mask, 0, lines[1], cols),
        (r.raw_c, cot, 2, lines[2], cols),
    ):
        for at in range(count):
            value = read(at % groups, at // groups + first)
            for k in range(raw.shape[0]):
                raw[k, at * w : (at + 1) * w, :] = value[:, k * 128 : (k + 1) * 128]
    for out, x0, m0, c0 in ((r.right, 2 * cols - over, cols - rim, cols - 2), (r.left, 0, 0, 0)):
        pieces = []
        for c in range(over):
            pieces.append([strided(r.raw_x, k, x0 + c, lines[0], 2 * cols) for k in range(2)])
        for c in range(0, rim + 1, 2):
            pieces.append([strided(r.raw_m, 0, m0 + min(c + k, rim - 1), lines[1], cols) for k in range(2)])
        for c in range(2):
            for h in range(0, width // 128, 2):
                pieces.append([strided(r.raw_c, h + k, c0 + c, lines[2], cols) for k in range(2)])
        at = 0
        for low, high in pieces:
            r.flat[at : at + low.shape[0], :] = jnp.concatenate([low, high], axis=1)
            at += low.shape[0]
        if at < r.flat.shape[0]:
            r.flat[at:, :] = jnp.zeros((r.flat.shape[0] - at, 256), f32)
        out[...] = r.flat[...].astype(bf16)


def stats_kernel(r, copies):
    groups, cin = r.x.shape[0], r.x.shape[3]
    rows, S = r.own.shape[1], r.own.shape[2]
    L = groups * S
    width = r.w1.shape[2]
    raw = r.raw
    for n in range(2 * rows + 1):
        for g in range(groups):
            line = n * groups + g
            src = (r.top[g, 0] if n == 0 else r.x[g, n - 1]).astype(f32)
            side = r.lft[g, n].astype(f32)
            for k in range(raw.shape[0]):
                raw[k, line, 7:8, :] = side[:, k * 128 : (k + 1) * 128]
                raw[k, line, 8:, :] = src[:, k * 128 : (k + 1) * 128]
    for out, n_rows, start in ((r.xe, rows, 1), (r.xo, rows + 1, 0)):
        for n in range(n_rows):
            for b in range(3):
                for k in range(raw.shape[0]):
                    parts = [
                        raw[k, (2 * n + start) * groups + g, pl.ds(7 + b, S, stride=2), :]
                        for g in range(groups)
                    ]
                    at = b * cin + k * 128
                    out[n * L : (n + 1) * L, at : at + 128] = jnp.concatenate(
                        parts, axis=0
                    ).astype(bf16)
    mask = jnp.concatenate(
        [r.own[g, i].astype(f32) for i in range(rows) for g in range(groups)], axis=0
    )
    M = rows * L
    z = matmul(r.xo[0:M, :], r.w1[0])
    z += matmul(r.xe[...], r.w1[1])
    z += matmul(r.xo[L : L + M, :], r.w1[2])
    zp = matmul(r.xe[:, cin : 2 * cin], r.wp[...])
    zm, zpm = z * wide(mask, width), zp * wide(mask, width)
    row = jnp.concatenate(
        [column_sum(zm), column_sum(zm * z), column_sum(zpm), column_sum(zpm * zp), column_sum(mask)], axis=1
    )
    r.spread[...] = jnp.broadcast_to(row[None], r.spread.shape)
    copies.start(N.spread)
    copies.wait(N.spread)


def first_kernel(r, copies):
    groups, cin, width = r.x.shape[0], r.x.shape[3], r.cot.shape[3]
    rows, cols = r.own.shape[1], r.own.shape[2]
    S = cols + 8
    L = groups * S
    W = 2 * cols + 24
    V = cols + 16
    x, mask, cot = fields(r)
    lines = (2 * rows + 2 * over) * groups, (rows + 2 * rim) * groups, (rows + 3) * groups
    tail = jnp.zeros((W - 8 - 2 * cols, 128), f32)
    r.raw_m[...] = jnp.zeros(r.raw_m.shape, f32)
    r.raw_c[...] = jnp.zeros(r.raw_c.shape, f32)
    for at in range(lines[0]):
        value = x(at % groups, at // groups)
        for k in range(r.raw_x.shape[0]):
            r.raw_x[k, at * W + 8 : at * W + 8 + 2 * cols, :] = value[:, k * 128 : (k + 1) * 128]
            r.raw_x[k, at * W + 8 + 2 * cols : (at + 1) * W, :] = tail
    for strip, x0, m0, c0 in ((r.lft, 8 - over, 8 - rim, 6), (r.rgt, 8 + 2 * cols, 8 + cols, 8 + cols)):
        r.flat[...] = strip[...].astype(f32)
        at = 0
        for c in range(over):
            for k in range(2):
                r.raw_x[k, pl.ds(x0 + c, lines[0], stride=W), :] = r.flat[at : at + lines[0], k * 128 : (k + 1) * 128]
            at += lines[0]
        for c in range(0, rim + 1, 2):
            for k in range(2):
                if c + k < rim:
                    r.raw_m[0, pl.ds(m0 + c + k, lines[1], stride=V), :] = r.flat[
                        at : at + lines[1], k * 128 : (k + 1) * 128
                    ]
            at += lines[1]
        for c in range(2):
            for h in range(0, width // 128, 2):
                for k in range(2):
                    r.raw_c[h + k, pl.ds(c0 + c, lines[2], stride=V), :] = r.flat[
                        at : at + lines[2], k * 128 : (k + 1) * 128
                    ]
                at += lines[2]
    for out, n_rows, start in ((r.xe, rows + 5, 2), (r.xo, rows + 6, 1)):
        for n in range(n_rows):
            for b in range(3):
                for k in range(r.raw_x.shape[0]):
                    parts = [
                        strided(r.raw_x, k, ((2 * n + start) * groups + g) * W + 3 + b, S, 2) for g in range(groups)
                    ]
                    at = b * cin + k * 128
                    out[n * L : (n + 1) * L, at : at + 128] = jnp.concatenate(parts, axis=0).astype(bf16)
    copies.start(N.xe, N.xo)
    for at in range(lines[1]):
        r.raw_m[0, at * V + 8 : at * V + 8 + cols, :] = mask(at % groups, at // groups)
    for n in range(1, rows + 6):
        for g in range(groups):
            to, at = (n - 1) * L + g * S, (n * groups + g) * V
            r.maskp[to : to + S, :] = r.raw_m[0, at + 6 : at + 6 + S, :]
    for at in range(lines[2]):
        value = cot(at % groups, at // groups + 2)
        for k in range(r.raw_c.shape[0]):
            lanes = slice(k * 128, (k + 1) * 128)
            r.raw_c[k, at * V + 8 : at * V + 8 + cols, :] = value[:, lanes]
            r.cotq[at * S : (at + 1) * S, lanes] = r.raw_c[k, at * V + 7 : at * V + 7 + S, :]
    copies.start(N.cotq)
    r.ownp[...] = jnp.zeros(r.ownp.shape, f32)
    for i in range(rows):
        for g in range(groups):
            at = (i + 2) * L + g * S + 2
            r.ownp[at : at + cols, :] = r.own[g, i].astype(f32)
    copies.wait(N.w1, N.wp)
    for k, (m0, m) in enumerate(chunks(r.pre1.shape[0], r.pre1.shape[0] // 3)):
        z = matmul(r.xo[m0 : m0 + m, :], r.w1[0])
        z += matmul(r.xe[m0 : m0 + m, :], r.w1[1])
        z += matmul(r.xo[L + m0 : L + m0 + m, :], r.w1[2])
        r.pre1[m0 : m0 + m, :] = z
        copies.start((N.pre1, k))
        r.prep[m0 : m0 + m, :] = matmul(r.xe[m0 : m0 + m, cin : 2 * cin], r.wp[...])
        copies.start((N.prep, k))
    copies.wait(N.xe, N.xo, N.pre1, N.prep, N.cotq)


def second_kernel(r, copies):
    width = r.gain.shape[1]
    t = jnp.sum(r.tot1[...], axis=0)
    n = wide(t[:, 4 * width :], width)
    center, inv = moments(t[:, :width], t[:, width : 2 * width], n)
    proj = moments(t[:, 2 * width : 3 * width], t[:, 3 * width : 4 * width], n)
    r.mom1[...] = jnp.concatenate([center, inv, n, *proj, jnp.zeros((3, width), f32)], axis=0)
    scale = inv * r.gain[...]
    M, Q = r.pre1.shape[0], r.pre2.shape[0]
    L = (M - Q) // 2
    copies.wait(N.pre1)
    for m0, m in chunks(M, 104):
        v = (r.pre1[m0 : m0 + m, :] - center) * scale + r.shift[...]
        mask = wide(r.maskp[m0 : m0 + m, :], width)
        r.hid[m0 : m0 + m, :] = 0.5 * v * (1.0 + gelu_parts(v)) * mask
    r.hid[M:, :] = jnp.zeros((r.hid.shape[0] - M, width), f32)
    for m0, m in chunks(M, 208):
        for b in range(3):
            r.h3[m0 : m0 + m, b * width : (b + 1) * width] = r.hid[m0 + b : m0 + b + m, :].astype(bf16)
    copies.start(N.h3)
    copies.wait(N.w2)
    sums = [jnp.zeros((1, width), f32)] * 2
    for k, (m0, m) in enumerate(chunks(Q, Q // 3)):
        z = matmul(r.h3[m0 : m0 + m, :], r.w2[0])
        z += matmul(r.h3[L + m0 : L + m0 + m, :], r.w2[1])
        z += matmul(r.h3[2 * L + m0 : 2 * L + m0 + m, :], r.w2[2])
        r.pre2[m0 : m0 + m, :] = z
        copies.start((N.pre2, k))
        zm = z * wide(r.ownp[L + 1 + m0 : L + 1 + m0 + m, :], width)
        sums = [sums[0] + column_sum(zm), sums[1] + column_sum(zm * z)]
    row = jnp.concatenate(sums, axis=1)
    r.spread[...] = jnp.broadcast_to(row[None], r.spread.shape)
    copies.start(N.spread)
    copies.wait(N.h3, N.pre2, N.spread)


def part(r, at, *fields, first=0):
    bit = r.bits[0] == 1
    for k, field in enumerate(fields, first):
        half = field.shape[1] // 2
        low, high = field[:, :half], field[:, half:]
        r.mine[k, at : at + field.shape[0], :] = jnp.where(bit, high, low)
        r.theirs[k, at : at + field.shape[0], :] = jnp.where(bit, low, high)


def mine_of(r, row):
    half = row.shape[1] // 2
    return jnp.where(r.bits[0] == 1, row[:, half:], row[:, :half])


def third_kernel(r, copies):
    groups, rows, cols, width = r.out.shape
    S = cols + 8
    L = groups * S
    n = r.mom1[2:3, :]
    t = jnp.sum(r.tot2[...], axis=0)
    c2, i2 = moments(t[:, :width], t[:, width:], n)
    cp, ip = r.mom1[3:4, :], r.mom1[4:5, :]
    r.mom2[...] = jnp.concatenate([c2, i2, cp, ip, jnp.zeros((4, width), f32)], axis=0)
    sums = [jnp.zeros((1, width), f32)] * 3
    both_shift = r.shift2[...] + r.shiftp[...]
    total = r.grad.shape[0] // S
    for line in range(total):
        if line % (total // 2) == 0:
            k = line // (total // 2)
            copies.wait((N.pre2, k), (N.prep, k), (N.cotq, k))
        at = line * S
        shifted = slice(L + 1 + at, L + 1 + at + S)
        n2 = (r.pre2[at : at + S, :] - c2) * i2
        np_ = (r.prep[shifted, :] - cp) * ip
        v = n2 * r.gain2[...] + np_ * r.gainp[...] + both_shift
        mask = wide(r.maskp[shifted, :], width)
        own = wide(r.ownp[shifted, :], width)
        t = gelu_parts(v)
        r.field[at : at + S, :] = 0.5 * v * (1.0 + t) * mask
        g = gelu_slope(v, t) * mask * r.cotq[at : at + S, :]
        r.grad[at : at + S, :] = g
        g = g * own
        if L <= at < L + r.mine.shape[1]:
            part(r, at - L, g, n2 * own, np_ * own)
            if at - L + S == r.mine.shape[1] // 2:
                copies.start((N.mine, 0), (N.theirs, 0))
        new = [column_sum(g * n2), column_sum(g), column_sum(g * np_)]
        sums = [a + b for a, b in zip(sums, new)]
        if (line + 1) % (total // 2) == 0:
            copies.start((N.grad, (line + 1) // (total // 2) - 1))
    row = jnp.concatenate(sums, axis=1)
    r.spread[...] = jnp.broadcast_to(row[None], r.spread.shape)
    copies.start(N.spread, (N.mine, 1), (N.theirs, 1))
    for i in range(rows):
        for g in range(groups):
            at = (i + 1) * L + g * S + 1
            r.out[g, i, :, :] = r.field[at : at + cols, :].astype(bf16)
    copies.start(N.out)
    copies.wait(N.grad, N.out, N.spread, N.mine, N.theirs)


def fourth_kernel(r, copies):
    width = r.gain.shape[1]
    Q, U, rows_w = r.pre2.shape[0], r.act.shape[0], r.gpu.shape[0]
    L = U - rows_w
    center, inv, n = (r.mom1[k : k + 1, :] for k in range(3))
    c2, i2, cp, ip = (r.mom2[k : k + 1, :] for k in range(4))
    t3 = jnp.sum(r.tot3[...], axis=0)
    gg2, gs, ggp = (t3[:, k * width : (k + 1) * width] for k in range(3))
    r.gain_second[...], r.shift_second[...], r.gain_proj[...], r.shift_proj[...] = gg2, gs, ggp, gs
    tiny = N.gain_second, N.shift_second, N.gain_proj, N.shift_proj
    copies.start(*tiny)
    for m0, m in chunks(Q, L):
        if m0 in (0, 6 * L):
            copies.wait((N.grad, m0 // (6 * L)), (N.pre2, m0 // (6 * L)))
        mask = wide(r.maskp[L + 1 + m0 : L + 1 + m0 + m, :], width) / n
        n2 = (r.pre2[m0 : m0 + m, :] - c2) * i2
        back = mask * (gs + n2 * gg2)
        r.gq[m0 : m0 + m, :] = (r.gain2[...] * i2) * (r.grad[m0 : m0 + m, :] - back)
    r.gq[Q:, :] = jnp.zeros((r.gq.shape[0] - Q, width), f32)
    for m0, m in chunks(Q, 176):
        for b in range(3):
            r.g3[m0 : m0 + m, b * width : (b + 1) * width] = r.gq[m0 + b : m0 + b + m, :].astype(bf16)
    copies.wait(N.keep)
    for m0, m in chunks(U, L):
        frame = slice(2 * L + 2 + m0, 2 * L + 2 + m0 + m)
        n1 = (r.keep[frame, :] - center) * inv
        v = n1 * r.gain[...] + r.shift[...]
        mask = wide(r.maskp[frame, :], width)
        r.act[m0 : m0 + m, :] = gelu_slope(v, gelu_parts(v)) * mask
        r.normed[m0 : m0 + m, :] = n1 * mask
        if m0 < rows_w:
            part(r, m0, n1 * wide(r.ownp[frame, :], width), first=1)
    copies.start(N.normed, (N.mine, 1), (N.theirs, 1))
    for a in range(3):
        copies.wait((N.w2, a))
        gh = jnp.zeros((U, width), f32)
        for b in range(3):
            gh += matmul_nt(
                r.g3[L * a : L * a + U, b * width : (b + 1) * width],
                r.w2[2 - a, (2 - b) * width : (3 - b) * width, :],
            )
        r.gh[...] = gh if a == 0 else r.gh[...] + gh
    sums = [jnp.zeros((1, width), f32)] * 2
    for m0, m in chunks(U, L):
        g = r.act[m0 : m0 + m, :] * r.gh[m0 : m0 + m, :]
        r.act[m0 : m0 + m, :] = g
        g = g * wide(r.ownp[2 * L + 2 + m0 : 2 * L + 2 + m0 + m, :], width)
        if m0 < rows_w:
            part(r, m0, g)
        sums = [sums[0] + column_sum(g * r.normed[m0 : m0 + m, :]), sums[1] + column_sum(g)]
    row = jnp.concatenate(sums, axis=1)
    r.spread[...] = jnp.broadcast_to(row[None], r.spread.shape)
    copies.start(N.spread, (N.mine, 0), (N.theirs, 0), N.act)
    copies.wait(N.prep)
    for m0, m in chunks(rows_w, L):
        frame = slice(2 * L + 2 + m0, 2 * L + 2 + m0 + m)
        mask = wide(r.maskp[frame, :], width) / n
        back = mask * (gs + (r.prep[frame, :] - cp) * ip * ggp)
        r.gpu[m0 : m0 + m, :] = ((r.gainp[...] * ip) * (r.grad[L + 1 + m0 : L + 1 + m0 + m, :] - back)).astype(bf16)
    copies.start(N.gpu)
    copies.wait(N.normed, N.mine, N.theirs, N.spread, N.act, N.gpu, *tiny)


def split_store(r, rows, unit, first):
    quarter = unit // 4
    for k in range(rows // unit):
        for bit, base, sent, kept in ((1, 0, r.sent_a, r.kept_a), (2, 2 * quarter, r.sent_b, r.kept_b)):
            keep = pl.multiple_of(k * unit + base + r.bits[bit] * quarter, quarter)
            send = pl.multiple_of(k * unit + base + (1 - r.bits[bit]) * quarter, quarter)
            sent[first + k] = r.acc[pl.ds(send, quarter), :].astype(bf16)
            kept[first + k] = r.acc[pl.ds(keep, quarter), :]


def weights_second_kernel(r, copies):
    width = r.h3.shape[1] // 3
    cin = r.xe.shape[1] // 3
    rows_w = r.mine.shape[1]
    L = (r.h3.shape[0] - rows_w) // 5
    per = width // cin
    t3 = jnp.sum(r.tot3[...], axis=0)
    n = mine_of(r, r.mom1[2:3, :])
    gg2, gs, ggp = (mine_of(r, t3[:, k * width : (k + 1) * width]) / n for k in range(3))
    scale2, scalep = mine_of(r, r.gain2[...] * r.mom2[1:2, :]), mine_of(r, r.gainp[...] * r.mom2[3:4, :])
    half = scale2.shape[1]
    for source, name, own, out in ((r.mine, N.mine, r.ownp, r.near), (r.far3, N.far3, r.ownp_far, r.far)):
        copies.wait(name)
        r.pad[:, 0:8, :] = jnp.zeros((3, 8, half), f32)
        r.pad[:, 8:, :] = source[...]
        for m0, m in chunks(rows_w, 96):
            mask = wide(own[2 * L + 1 + m0 : 2 * L + 1 + m0 + m, :], half)
            rows = slice(8 + m0, 8 + m0 + m)
            back = mask * gs + r.pad[1, rows, :] * gg2
            out[m0 : m0 + m, :] = (scale2 * (r.pad[0, rows, :] - back)).astype(bf16)
            mask = wide(own[2 * L + m0 : 2 * L + m0 + m, :], half)
            rows = slice(7 + m0, 7 + m0 + m)
            back = mask * gs + r.pad[2, rows, :] * ggp
            out[rows_w + m0 : rows_w + m0 + m, :] = (scalep * (r.pad[0, rows, :] - back)).astype(bf16)
    for b in range(3):
        lanes = slice(b * width, (b + 1) * width)
        copies.wait((N.h3, b), (N.h3_far, b))
        for a in range(3):
            at = L * a + L
            r.acc[...] = matmul_tn(r.h3[at : at + rows_w, lanes], r.near[:rows_w, :]) + matmul_tn(
                r.h3_far[at : at + rows_w, lanes], r.far[:rows_w, :]
            )
            split_store(r, width, cin, (3 * b + a) * per)
        copies.start(*((name, b) for name in CHUNKS))
    at = 2 * L
    copies.wait(N.xe, N.xe_far)
    middle = slice(cin, 2 * cin)
    r.acc[0:cin, :] = matmul_tn(r.xe[at : at + rows_w, middle], r.near[rows_w:, :]) + matmul_tn(
        r.xe_far[at : at + rows_w, middle], r.far[rows_w:, :]
    )
    split_store(r, cin, cin, 9 * per)
    copies.start(*((name, 3) for name in CHUNKS))
    copies.wait(*CHUNKS)


def first_back(r, gg, gs, count):
    width = r.gain.shape[1]
    U = r.act.shape[0]
    L = U - r.rows_w
    inv, n = r.mom1[1:2, :], r.mom1[2:3, :]
    gg, gs = gg / n, gs / n
    scale = r.gain[...] * inv
    r.gf[0:8, :] = jnp.zeros((8, width), f32)
    r.gf[8 + count :, :] = jnp.zeros((r.gf.shape[0] - 8 - count, width), f32)
    for m0, m in chunks(count, L):
        mask = wide(r.maskp[2 * L + 2 + m0 : 2 * L + 2 + m0 + m, :], width)
        back = mask * gs + r.normed[m0 : m0 + m, :] * gg
        r.gf[8 + m0 : 8 + m0 + m, :] = scale * (r.act[m0 : m0 + m, :] - back)


def weights_first_kernel(r, copies):
    rows_w = r.mine.shape[1]
    cin = r.xe.shape[1] // 3
    L = (r.xe.shape[0] - rows_w) // 5
    width = r.gain.shape[1]
    t4 = jnp.sum(r.tot4[...], axis=0)
    r.gain_first[...], r.shift_first[...] = t4[:, :width], t4[:, width:]
    copies.start(N.gain_first, N.shift_first)
    n = mine_of(r, r.mom1[2:3, :])
    gg, gs = mine_of(r, t4[:, :width]) / n, mine_of(r, t4[:, width:]) / n
    scale = mine_of(r, r.gain[...] * r.mom1[1:2, :])
    half = scale.shape[1]
    for source, name, own, out in ((r.mine, N.mine, r.ownp, r.near), (r.far4, N.far4, r.ownp_far, r.far)):
        copies.wait(name)
        r.pad[:, 0:8, :] = jnp.zeros((2, 8, half), f32)
        r.pad[:, 8:, :] = source[...]
        for m0, m in chunks(rows_w, 96):
            mask = wide(own[2 * L + m0 : 2 * L + m0 + m, :], half)
            rows = slice(6 + m0, 6 + m0 + m)
            back = mask * gs + r.pad[1, rows, :] * gg
            out[m0 : m0 + m, :] = (scale * (r.pad[0, rows, :] - back)).astype(bf16)
    copies.wait(N.xe, N.xe_far)
    for k, a in enumerate((1, 0, 2)):
        if k == 1:
            copies.wait(N.xo, N.xo_far)
        source, source_far = (r.xe, r.xe_far) if a == 1 else (r.xo, r.xo_far)
        at = (3 if a == 2 else 2) * L
        for b in range(3):
            lanes = slice(b * cin, (b + 1) * cin)
            r.acc[lanes, :] = matmul_tn(source[at : at + rows_w, lanes], r.near[...]) + matmul_tn(
                source_far[at : at + rows_w, lanes], r.far[...]
            )
        split_store(r, 3 * cin, cin, a * 3)
        copies.start(*((name, a) for name in CHUNKS))
    copies.wait(N.gain_first, N.shift_first, *CHUNKS)


def inputs_kernel(r, copies):
    width = r.gpu.shape[1]
    groups, rows, cols = r.out.shape[0], r.out.shape[1] // 2, r.out.shape[2] // 2
    cin = r.out.shape[3]
    M = r.gpu.shape[0]
    S = cols + 8
    L = groups * S
    lines = r.lines
    U = r.act.shape[0]
    r.rows_w = M
    copies.wait(N.act, N.normed)
    first_back(r, r.gg[...], r.gs[...], U)
    for m0, m in chunks(U, 144):
        r.gu[m0 : m0 + m, :width] = r.gf[8 + m0 : 8 + m0 + m, :].astype(bf16)
        r.gu[m0 : m0 + m, width:] = r.gf[9 + m0 : 9 + m0 + m, :].astype(bf16)
    copies.wait(N.gpu, N.w1, N.wp)

    def tap(m0, m, a, b):
        di, dj = (1 if a == 0 else 0), (1 if b == 0 else 0)
        return matmul_nt(
            r.gu[di * L + m0 : di * L + m0 + m, dj * width : (dj + 1) * width],
            r.w1[a, b * cin : (b + 1) * cin, :],
        )

    for m0, m in chunks(M, 2 * L):
        pieces = {
            (0, 0): tap(m0, m, 1, 1) + matmul_nt(r.gpu[m0 : m0 + m, :], r.wp[...]),
            (0, 1): tap(m0, m, 1, 2) + tap(m0, m, 1, 0),
            (1, 0): tap(m0, m, 2, 1) + tap(m0, m, 0, 1),
            (1, 1): tap(m0, m, 2, 2) + tap(m0, m, 2, 0) + tap(m0, m, 0, 2) + tap(m0, m, 0, 0),
        }
        for (ro, co), v in pieces.items():
            for k in range(m // S):
                line = m0 // S + k
                i, g = line // groups, line % groups
                for h in range(lines.shape[0]):
                    lines[h, (2 * i + ro) * groups + g, pl.ds(co, cols, stride=2), :] = v[
                        k * S : k * S + cols, h * 128 : (h + 1) * 128
                    ]
    for n in range(2 * rows):
        for g in range(groups):
            for h in range(lines.shape[0]):
                r.out[g, n, :, h * 128 : (h + 1) * 128] = lines[h, n * groups + g].astype(bf16)
    copies.start(N.out)
    copies.wait(N.out)


def widen(half, side, taps, per, swapped, into=None):
    total, n, m = half.shape
    extra = total - taps * per
    order = [(t % 3 * 3 + t // 3) if swapped else t for t in range(taps)]
    jobs = [(t * per, per, 0, order[t] * per) for t in range(taps)] + [(taps * per, 1, 1, 0)] * extra
    more = list(into or [])

    def body(side_ref, half_ref, *refs):
        outs = refs[len(more) : len(more) + 1 + extra]
        narrow, full, sems = refs[len(more) + 1 + extra :]
        lanes = pl.ds(pl.multiple_of(side_ref[0] * m, m), m)
        reads = [
            pltpu.make_async_copy(half_ref.at[pl.ds(at, size)], narrow.at[pl.ds(at, size)], sems.at[0, k])
            for k, (at, size, _, _) in enumerate(jobs)
        ]
        writes = [
            pltpu.make_async_copy(full.at[pl.ds(at, size)], outs[which].at[pl.ds(to, size), :, lanes], sems.at[1, k])
            for k, (at, size, which, to) in enumerate(jobs)
        ]
        for read in reads:
            read.start()
        for k, (at, size, _, _) in enumerate(jobs):
            reads[k].wait()
            full[at : at + size] = narrow[at : at + size].astype(f32)
            writes[k].start()
        for write in writes:
            write.wait()

    hbm = pl.BlockSpec(memory_space=pltpu.HBM)
    return pl.pallas_call(
        body,
        out_shape=[shape((taps * per, n, 2 * m))] + [shape((1, n, 2 * m))] * extra,
        in_specs=[pl.BlockSpec(memory_space=pltpu.SMEM)] + [hbm] * (1 + len(more)),
        out_specs=[hbm] * (1 + extra),
        scratch_shapes=[
            pltpu.VMEM((total, n, m), bf16),
            pltpu.VMEM((total, n, m), f32),
            pltpu.SemaphoreType.DMA((2, len(jobs))),
        ],
        input_output_aliases={2 + k: k for k in range(len(more))},
        compiler_params=pltpu.CompilerParams(vmem_limit_bytes=20 * 1024 * 1024),
        cost_estimate=pl.CostEstimate(flops=0, bytes_accessed=0, transcendentals=0),
    )(side.reshape(1), half, *more)


def halve_kernel(r, copies):
    for p in range(r.count):
        kept, got = getattr(r, f"kept{p}"), getattr(r, f"got{p}")
        copies.wait(f"kept{p}", f"got{p}")
        to_send, to_keep = getattr(r, f"sent{p}"), getattr(r, f"left{p}")
        bit = r.bits[r.steps[p]] == 1
        h = kept.shape[1] // 2
        for t in range(kept.shape[0]):
            total = kept[t] + got[t].astype(f32)
            low, high = total[:h], total[h:]
            to_send[t] = jnp.where(bit, low, high).astype(bf16)
            to_keep[t] = jnp.where(bit, high, low)
        copies.start(f"sent{p}", f"left{p}")
    copies.wait(*(name for name in copies.jobs if name[:4] in (N.sent, N.left)))


def halve(bits, pairs, steps, cost):
    ins = dict(bits=bits)
    for p, (kept, got) in enumerate(pairs):
        ins[f"kept{p}"], ins[f"got{p}"] = kept, got
    taps, n, m = pairs[0][0].shape
    dims = (taps, n // 2, m)
    names = [str(p) for p in range(len(pairs))]
    outs = {}
    for name in names:
        outs[N.sent + name], outs[N.left + name] = shape(dims, bf16), shape(dims)

    def body(r, copies):
        r.count, r.steps = len(pairs), steps
        halve_kernel(r, copies)

    far_in = tuple(n for n in ins if n != N.bits)
    out = call(body, ins, outs, far_in=far_in, far_out=tuple(outs), smem=(N.bits,), cost=cost, limit=60)
    return [(out[N.sent + name], out[N.left + name]) for name in names]


def shifted(value, axis, steps):
    count = lax.axis_size(axis)
    first, last = (max(0, -steps), min(count, count - steps))
    return lax.ppermute(value, axis, [(source, source + steps) for source in range(first, last)])


def gather_sum(spread):
    return lax.all_to_all(spread, axes, 0, 0)


def bit_of(axis, step):
    return (lax.axis_index(axis) // step) % 2


def partner(value, axis, step):
    count = lax.axis_size(axis)
    return lax.ppermute(value, axis, [(i, i ^ step) for i in range(count)])


def steps_of(axis):
    count, step, out = lax.axis_size(axis), 1, []
    while step < count:
        out.append((axis, step))
        step *= 2
    return out


def split(total, axis, step):
    n = total.shape[1] // 2
    bit = bit_of(axis, step) == 1
    low, high = total[:, :n], total[:, n:]
    return jnp.where(bit, low, high).astype(bf16), jnp.where(bit, high, low)


def joined(value, other, axis, step, dim=1):
    bit = bit_of(axis, step) == 1
    return jnp.concatenate([jnp.where(bit, other, value), jnp.where(bit, value, other)], axis=dim)


class Tree:
    def __init__(self, parts, bits, plane, rest, core):
        self.bits, self.place = bits, {step: k for k, step in enumerate([core, *plane, *rest])}
        self.sent_a, self.kept_a, self.sent_b, self.kept_b = parts
        self.a, self.b, self.rest, self.core = plane, plane[::-1], rest, core
        p, n = len(plane), len(rest)
        self.stages = [(N.plane, k) for k in range(p)] + [(N.rest, k) for k in range(n)]
        self.stages += [(N.rest_join, k) for k in reversed(range(n))] + [(N.plane_join, k) for k in reversed(range(p))]
        self.stages += [(N.core, 0)]

    def next(self):
        return self.stages[0] if self.stages else None

    def start(self):
        kind, k = self.stages[0]
        if kind == N.plane:
            self.got = partner(self.sent_a, *self.a[k]), partner(self.sent_b, *self.b[k])
        elif kind == N.rest:
            self.got = (partner(self.sent, *self.rest[k]),)
        elif kind == N.rest_join:
            self.got = (partner(self.value, *self.rest[k]),)
        elif kind == N.plane_join:
            self.got = partner(self.value_a, *self.a[k]), partner(self.value_b, *self.b[k])
        else:
            self.got = (partner(self.value, *self.core),)

    def finish(self, cost=0):
        kind, k = self.stages.pop(0)
        if kind == N.plane:
            pairs = [(self.kept_a, self.got[0]), (self.kept_b, self.got[1])]
            nexts = [order[k + 1] for order in (self.a, self.b) if k + 1 < len(order)]
            if nexts and cost:
                pairs = halve(self.bits, pairs, [self.place[step] for step in nexts], cost)
                (self.sent_a, self.kept_a), (self.sent_b, self.kept_b) = pairs
                return
            total_a, total_b = (kept + got.astype(f32) for kept, got in pairs)
            if nexts:
                self.sent_a, self.kept_a = split(total_a, *nexts[0])
                self.sent_b, self.kept_b = split(total_b, *nexts[1])
            else:
                self.taps = total_a.shape[0]
                self.split_rest(jnp.concatenate([total_a, total_b], axis=0), 0)
        elif kind == N.rest:
            self.split_rest(self.kept + self.got[0].astype(f32), k + 1)
        elif kind == N.rest_join:
            self.value = joined(self.value, self.got[0], *self.rest[k])
            self.value_a, self.value_b = self.value[: self.taps], self.value[self.taps :]
        elif kind == N.plane_join:
            self.value_a = joined(self.value_a, self.got[0], *self.a[k])
            self.value_b = joined(self.value_b, self.got[1], *self.b[k])
            self.value = jnp.concatenate([self.value_a, self.value_b], axis=1)

    def split_rest(self, total, k):
        if k < len(self.rest):
            self.sent, self.kept = split(total, *self.rest[k])
        else:
            self.value = total.astype(bf16)


def lockstep(*trees, beside=()):
    for t in trees:
        t.start()
    got, beside = lax.optimization_barrier(([t.got for t in trees], beside))
    for t, g in zip(trees, got):
        t.got = g
        t.finish()
    return beside


def on_device(inputs, w_first, gain_first, shift_first, w_second, gain_second, shift_second, w_proj, gain_proj, shift_proj, valid_mask, cotangent):
    groups, rows_in, cols_in, cin = inputs.shape
    rows, cols = rows_in // 2, cols_in // 2
    width = w_first.shape[3]
    half = width // 2
    S = cols + 8
    L = groups * S
    devices = lax.axis_size(N.rows) * lax.axis_size(N.cols) * lax.axis_size(N.grp)
    plane = steps_of(N.cols)
    core = steps_of(N.rows)[0]
    rest = steps_of(N.rows)[1:] + steps_of(N.grp)
    bits = jnp.stack([bit_of(*step) for step in (core, *plane, *rest)]).astype(jnp.int32)
    w1 = w_first.reshape(3, 3 * cin, width)
    w2 = w_second.reshape(3, 3 * width, width)
    as_row = lambda v: v.reshape(1, -1)
    own = jnp.broadcast_to(valid_mask.astype(bf16)[..., None], valid_mask.shape + (128,))
    MP, MQ, MU, MW = (rows + 5) * L, (rows + 3) * L, (rows + 1) * L, rows * L
    px = lambda m, k: 2 * m * k * width
    vec = lambda k: shape((1, k * width))
    all_devices = lambda k: shape((devices, 1, k))
    g1, b1, g2, b2, gp, bp = map(
        as_row, (gain_first, shift_first, gain_second, shift_second, gain_proj, shift_proj)
    )

    top1 = shifted(inputs[:, -1:], N.rows, 1)
    me, count = lax.axis_index(N.rows), lax.axis_size(N.rows)
    flags = jnp.stack([me > 0, me < count - 1]).astype(jnp.int32)
    flat_rows = shape((over * groups * cols_in + (width // 256 + 1) * rim * groups * cols, 256), bf16)
    packed = call(
        vertical_kernel,
        dict(flags=flags, x=inputs, cot=cotangent, own=own),
        dict(down=flat_rows) if count == 2 else dict(down=flat_rows, up=flat_rows),
        far_in=(N.x, N.cot),
        smem=(N.flags,),
        parts=dict(x=end_parts(rows_in, over), cot=end_parts(rows, rim)),
    )
    if count == 2:
        top = bot = lax.ppermute(packed["down"], "rows", [(0, 1), (1, 0)])
    else:
        top, bot = shifted(packed[N.down], N.rows, 1), shifted(packed[N.up], N.rows, -1)
    lft1 = shifted(jnp.concatenate([top1[:, :, -1:], inputs[:, :, -1:]], axis=1), N.cols, 1)
    (top, bot), lft1 = lax.optimization_barrier(((top, bot), lft1))
    lines = (rows_in + 2 * over) * groups, (rows + 2 * rim) * groups, (rows + 3) * groups
    n_strip = over * lines[0] + (rim + 1) // 2 * lines[1] + width // 128 * lines[2]
    n_strip = -(-n_strip // 16) * 16
    near = dict(flags=flags, x=inputs, cot=cotangent, own=own, top=top, bot=bot)
    strips = call(
        strips_kernel,
        near,
        dict(right=shape((n_strip, 256), bf16), left=shape((n_strip, 256), bf16)),
        dict(
            raw_x=pltpu.VMEM((cin // 128, lines[0] * cols_in, 128), f32),
            raw_m=pltpu.VMEM((1, lines[1] * cols, 128), f32),
            raw_c=pltpu.VMEM((width // 128, lines[2] * cols, 128), f32),
            flat=pltpu.VMEM((n_strip, 256), f32),
        ),
        smem=(N.flags,),
    )
    lft, rgt = shifted(strips[N.right], N.cols, 1), shifted(strips[N.left], N.cols, -1)
    lft1, _ = lax.optimization_barrier((lft1, strips[N.right]))
    stats = call(
        stats_kernel,
        dict(x=inputs, top=top1, lft=lft1, own=own, w1=w1, wp=w_proj),
        dict(spread=all_devices(4 * width + 128)),
        dict(
            raw=pltpu.VMEM((cin // 128, (rows_in + 1) * groups, cols_in + 8, 128), f32),
            xe=pltpu.VMEM((rows * groups * cols, 3 * cin), bf16),
            xo=pltpu.VMEM(((rows + 1) * groups * cols, 3 * cin), bf16),
        ),
        far_out=(N.spread,),
    )
    tot1 = gather_sum(stats[N.spread])

    first = call(
        first_kernel,
        dict(**near, lft=lft, rgt=rgt, w1=w1, wp=w_proj),
        dict(
            pre1=shape((MP, width)),
            prep=shape((MP, width)),
            xe=shape((MP, 3 * cin), bf16),
            xo=shape((MP + L, 3 * cin), bf16),
            ownp=shape((MP, 128)),
            maskp=shape((MP, 128)),
            cotq=shape((MQ, width)),
        ),
        dict(
            raw_x=pltpu.VMEM((cin // 128, lines[0] * (cols_in + 24), 128), f32),
            raw_m=pltpu.VMEM((1, lines[1] * (cols + 16), 128), f32),
            raw_c=pltpu.VMEM((width // 128, lines[2] * (cols + 16), 128), f32),
            flat=pltpu.VMEM((n_strip, 256), f32),
        ),
        far_in=(N.w1, N.wp),
        far_out=(N.xe, N.xo, N.pre1, N.prep, N.cotq),
        smem=(N.flags,),
        cost=20000000000,
        parts=dict(pre1=row_parts(MP, 3), prep=row_parts(MP, 3)),
    )
    xe, xo, ownp, maskp = first[N.xe], first[N.xo], first[N.ownp], first[N.maskp]
    far_xe, far_xo, ownp_far = partner(xe, *core), partner(xo, *core), partner(ownp, *core)

    second = call(
        second_kernel,
        dict(pre1=first[N.pre1], tot1=tot1, gain=g1, shift=b1, maskp=maskp, ownp=ownp, w2=w2),
        dict(h3=shape((MP, 3 * width), bf16), pre2=shape((MQ, width)), spread=all_devices(2 * width), mom1=shape((8, width))),
        dict(hid=pltpu.VMEM((MP + 8, width), f32)),
        far_in=(N.pre1, N.w2),
        far_out=(N.h3, N.pre2, N.spread),
        parts=dict(pre2=row_parts(MQ, 3)),
    )
    h3, pre2, mom1 = second[N.h3], second[N.pre2], second[N.mom1]
    tot2 = gather_sum(second[N.spread])
    tot2, far_h3 = lax.optimization_barrier((tot2, partner(h3, *core)))

    third = call(
        third_kernel,
        dict(
            bits=bits, pre2=pre2, prep=first[N.prep], mom1=mom1, tot2=tot2, gain2=g2, shift2=b2, gainp=gp, shiftp=bp,
            maskp=maskp, ownp=ownp, cotq=first[N.cotq],
        ),
        dict(
            out=shape((groups, rows, cols, width), bf16),
            grad=shape((MQ, width)),
            spread=all_devices(3 * width),
            mom2=shape((8, width)),
            mine=shape((3, MW, half)),
            theirs=shape((3, MW, half)),
        ),
        dict(field=pltpu.VMEM((MQ, width), f32)),
        far_in=(N.pre2, N.prep, N.cotq),
        far_out=(N.grad, N.spread, N.mine, N.theirs, N.out),
        smem=(N.bits,),
        parts=dict(
            mine=middle_parts(MW, 2), theirs=middle_parts(MW, 2),
            grad=row_parts(MQ, 2), pre2=row_parts(MQ, 2), cotq=row_parts(MQ, 2), prep=cuts(L, L + MQ // 2 + 8, L + MQ + 8)
        ),
    )
    mom2 = third[N.mom2]
    tot3 = gather_sum(third[N.spread])

    def chunk_shapes(taps):
        dims = (taps, cin // 4, half)
        return dict(sent_a=shape(dims, bf16), kept_a=shape(dims), sent_b=shape(dims, bf16), kept_b=shape(dims))

    per = width // cin
    taps2 = 9 * per + 1
    second_parts = call(
        weights_second_kernel,
        dict(
            bits=bits, mine=third[N.mine], far3=partner(third[N.theirs], *core), h3=h3, h3_far=far_h3, xe=xe, xe_far=far_xe,
            tot3=tot3, mom1=mom1, mom2=mom2, gain2=g2, gainp=gp, ownp=ownp, ownp_far=ownp_far,
        ),
        chunk_shapes(taps2),
        dict(
            acc=pltpu.VMEM((width, half), f32),
            pad=pltpu.VMEM((3, MW + 8, half), f32),
            near=pltpu.VMEM((2 * MW, half), bf16),
            far=pltpu.VMEM((2 * MW, half), bf16),
        ),
        far_in=(N.mine, N.far3, N.h3, N.h3_far, N.xe, N.xe_far),
        far_out=CHUNKS,
        smem=(N.bits,),
        parts=dict(
            h3=lane_parts(3 * width, 3, pl.ds(L, MW + 2 * L)),
            h3_far=lane_parts(3 * width, 3, pl.ds(L, MW + 2 * L)),
            xe=[(0, (pl.ds(2 * L, MW), pl.ds(cin, cin)))],
            xe_far=[(0, (pl.ds(2 * L, MW), pl.ds(cin, cin)))],
            **{name: row_parts(taps2 - 1, 3) + [(3, (pl.ds(taps2 - 1, 1),))] for name in CHUNKS},
        ),
    ).values()
    grad, *second_parts = lax.optimization_barrier((third[N.grad], *second_parts))
    tree2 = Tree(second_parts, bits, plane, rest, core)
    tree2.start()
    hidden = call(
        fourth_kernel,
        dict(
            bits=bits, grad=grad, pre2=pre2, keep=first[N.pre1], w2=w2, prep=first[N.prep], mom1=mom1, mom2=mom2, tot3=tot3,
            gain=g1, shift=b1, gain2=g2, gainp=gp, maskp=maskp, ownp=ownp,
        ),
        dict(
            act=shape((MU, width)), normed=shape((MU, width)), spread=all_devices(2 * width),
            mine=shape((2, MW, half)), theirs=shape((2, MW, half)), gpu=shape((MW, width), bf16),
            gain_second=vec(1), shift_second=vec(1), gain_proj=vec(1), shift_proj=vec(1),
        ),
        dict(
            gq=pltpu.VMEM((MQ + 8, width), f32),
            g3=pltpu.VMEM((MQ, 3 * width), bf16),
            gh=pltpu.VMEM((MU, width), f32),
        ),
        far_in=(N.grad, N.pre2, N.keep, N.w2, N.prep),
        far_out=(
            N.act, N.normed, N.spread, N.mine, N.theirs, N.gpu, N.gain_second, N.shift_second, N.gain_proj, N.shift_proj
        ),
        smem=(N.bits,),
        limit=52,
        parts=dict(
            grad=cuts(0, 6 * L, MQ),
            pre2=cuts(0, 6 * L, MQ),
            keep=cuts(2 * L, 2 * L + MU + 8),
            w2=[(k, (pl.ds(2 - k, 1),)) for k in range(3)],
            prep=cuts(2 * L, 2 * L + MW + 8),
            mine=row_parts(2, 2),
            theirs=row_parts(2, 2),
        ),
    )
    tot4 = gather_sum(hidden[N.spread])
    tree2.finish(20000000000)
    near1, tree2.sent_a, tree2.sent_b = lax.optimization_barrier((hidden[N.mine], tree2.sent_a, tree2.sent_b))
    tree2.start()
    fifth = call(
        weights_first_kernel,
        dict(
            bits=bits, mine=near1, far4=partner(hidden[N.theirs], *core), xe=xe, xe_far=far_xe, xo=xo, xo_far=far_xo,
            tot4=tot4, mom1=mom1, gain=g1, ownp=ownp, ownp_far=ownp_far,
        ),
        dict(**chunk_shapes(9), gain_first=vec(1), shift_first=vec(1)),
        dict(
            acc=pltpu.VMEM((3 * cin, half), f32),
            pad=pltpu.VMEM((2, MW + 8, half), f32),
            near=pltpu.VMEM((MW, half), bf16),
            far=pltpu.VMEM((MW, half), bf16),
        ),
        far_in=(N.mine, N.far4, N.xe, N.xe_far, N.xo, N.xo_far),
        cost=20000000000,
        far_out=(*CHUNKS, N.gain_first, N.shift_first),
        smem=(N.bits,),
        parts=dict(
            xe=cuts(2 * L, 2 * L + MW),
            xe_far=cuts(2 * L, 2 * L + MW),
            xo=cuts(2 * L, 3 * L + MW),
            xo_far=cuts(2 * L, 3 * L + MW),
            **{name: row_parts(9, 3) for name in CHUNKS},
        ),
    )
    first_parts = [fifth[name] for name in CHUNKS]
    tree2.got, *first_parts = lax.optimization_barrier((tree2.got, *first_parts))
    tree2.finish()
    tree1 = Tree(first_parts, bits, plane, rest, core)

    grad_inputs = call(
        inputs_kernel,
        dict(
            act=hidden[N.act], normed=hidden[N.normed], gpu=hidden[N.gpu], w1=w1, wp=w_proj, mom1=mom1, gain=g1, maskp=maskp,
            gg=fifth[N.gain_first], gs=fifth[N.shift_first],
        ),
        dict(out=shape((groups, rows_in, cols_in, cin), bf16)),
        dict(
            lines=pltpu.VMEM((cin // 128, rows_in * groups, cols_in, 128), f32),
            gf=pltpu.VMEM((MU + 16, width), f32),
            gu=pltpu.VMEM((MU, 2 * width), bf16),
        ),
        far_in=(N.act, N.normed, N.gpu, N.w1, N.wp),
        far_out=(N.out,),
        cost=10000000000,
    )[N.out]
    side = bit_of(*core).astype(jnp.int32)
    grad_inputs = lockstep(tree2, tree1, beside=grad_inputs)
    while tree2.next() != (N.plane_join, 0):
        lockstep(tree2, tree1)
    tree2.start()
    while tree1.next() != (N.plane_join, 0):
        tree1.start()
        if tree1.next() != (N.plane_join, 1):
            tree1.finish()
        else:
            tree1.got, tree2.got = lax.optimization_barrier((tree1.got, tree2.got))
            tree1.finish()
    tree2.finish()
    tree2.start()
    tree1.start()
    grad_second = widen(tree2.got[0], 1 - side, 9, per, True, widen(tree2.value, side, 9, per, True))
    tree1.got, grad_second = lax.optimization_barrier((tree1.got, grad_second))
    grad_w2, grad_wp = grad_second
    tree1.finish()
    tree1.start()
    (grad_w1,) = widen(tree1.got[0], 1 - side, 3, 3, False, widen(tree1.value, side, 3, 3, False))

    return (
        third[N.out],
        grad_inputs,
        grad_w1.reshape(w_first.shape),
        fifth[N.gain_first].reshape(width),
        fifth[N.shift_first].reshape(width),
        grad_w2.reshape(w_second.shape),
        hidden[N.gain_second].reshape(width),
        hidden[N.shift_second].reshape(width),
        grad_wp.reshape(w_proj.shape),
        hidden[N.gain_proj].reshape(width),
        hidden[N.shift_proj].reshape(width),
    )


def solution(mesh):
    spread = P("grp", "rows", "cols", None)
    return jax.shard_map(
        on_device,
        mesh=mesh,
        in_specs=(spread,) + (P(),) * 9 + (P("grp", "rows", "cols"), spread),
        out_specs=(spread, spread) + (P(),) * 9,
        check_vma=False,
    )
```

```python
import functools

import jax
import jax.numpy as jnp
from jax import lax
from jax.experimental import pallas as pl
from jax.experimental.pallas import tpu as pltpu
from jax.sharding import PartitionSpec as P

epsilon = 1e-05
axes = ("rows", "cols", "grp")
bf16 = jnp.bfloat16
f32 = jnp.float32
inner = 0.7978845608028654
cubic = 0.044715
over = 6
CHUNKS = "sent_a", "kept_a", "sent_b", "kept_b"
rim = 3


class Names:
    def __getattr__(self, name):
        return name


N = Names()


class Refs:
    def __init__(self, named):
        self.__dict__.update(named)


class Copies:
    def __init__(self, parts, pairs, sems):
        self.jobs = {}
        for k, (name, index) in enumerate(parts):
            source, target = pairs[name]
            if index:
                source, target = source.at[index[1]], target.at[index[1]]
            self.jobs.setdefault(name, []).append(pltpu.make_async_copy(source, target, sems.at[k]))

    def start(self, *names):
        for name, *which in map(named, names):
            for job in self.jobs[name][slice(*which) if which else slice(None)]:
                job.start()

    def start_all(self, names):
        for k in range(max((len(self.jobs[n]) for n in names), default=0)):
            for n in names:
                if k < len(self.jobs[n]):
                    self.jobs[n][k].start()

    def wait(self, *names):
        for name, *which in map(named, names):
            for job in self.jobs[name][slice(*which) if which else slice(None)]:
                job.wait()


def named(name):
    return (name,) if isinstance(name, str) else (name[0], name[1], name[1] + 1)


def row_parts(total, count):
    size = total // count
    return [(k, (pl.ds(k * size, size),)) for k in range(count)]


def middle_parts(total, count):
    size = total // count
    return [(k, (slice(None), pl.ds(k * size, size))) for k in range(count)]


def end_parts(total, size):
    return [(k, (slice(None), pl.ds(at, size))) for k, at in enumerate((0, total - size))]


def cuts(*at):
    return [(k, (pl.ds(a, b - a),)) for k, (a, b) in enumerate(zip(at, at[1:]))]


def lane_parts(total, count, rows=slice(None)):
    size = total // count
    return [(k, (rows, pl.ds(k * size, size))) for k in range(count)]


def call(body, ins, outs, scratch=None, far_in=(), far_out=(), smem=(), parts=None, limit=52, cost=0, anywhere=()):
    scratch, parts = scratch or {}, parts or {}
    far = (*far_in, *far_out)
    jobs = [(name, index) for name in far for index in parts.get(name, [None])]

    def spec(name):
        if name in smem:
            return pl.BlockSpec(memory_space=pltpu.SMEM)
        if name in anywhere:
            return pl.BlockSpec(memory_space=pl.ANY)
        return pl.BlockSpec(memory_space=pltpu.HBM if name in far else pltpu.VMEM)

    kinds = {**{n: shape(v.shape, v.dtype) for n, v in ins.items()}, **outs}

    def run(*refs):
        plain = dict(zip([*ins, *outs], refs))
        rest = refs[len(plain) :]
        buffers = dict(zip(far, rest))
        more = dict(zip(scratch, rest[len(far) :]))
        copies = None
        if far:
            pairs = {n: (plain[n], buffers[n]) if n in far_in else (buffers[n], plain[n]) for n in far}
            copies = Copies(jobs, pairs, rest[-1])
            copies.start_all(far_in)
        body(Refs({**plain, **buffers, **more}), copies)

    buffers = [pltpu.VMEM(kinds[n].shape, kinds[n].dtype) for n in far]
    sems = [pltpu.SemaphoreType.DMA((len(jobs),))] if far else []
    result = pl.pallas_call(
        run,
        out_shape=list(outs.values()),
        in_specs=[spec(n) for n in ins],
        out_specs=[spec(n) for n in outs],
        scratch_shapes=[*buffers, *scratch.values(), *sems],
        compiler_params=pltpu.CompilerParams(vmem_limit_bytes=limit * 1024 * 1024),
        cost_estimate=pl.CostEstimate(flops=cost, bytes_accessed=0, transcendentals=0),
    )(*ins.values())
    return dict(zip(outs, result))


def shape(dims, dtype=f32):
    return jax.ShapeDtypeStruct(dims, dtype)


def wide(mask, width):
    return jnp.concatenate([mask] * (width // mask.shape[1]), axis=1)


def matmul(a, b):
    return lax.dot_general(a, b, (((1,), (0,)), ((), ())), preferred_element_type=f32)


def matmul_nt(a, b):
    return lax.dot_general(a, b, (((1,), (1,)), ((), ())), preferred_element_type=f32)


def matmul_tn(a, b):
    return lax.dot_general(a, b, (((0,), (0,)), ((), ())), preferred_element_type=f32)


def gelu_parts(v):
    return jnp.tanh(inner * (v + cubic * v * v * v))


def gelu_slope(v, t):
    return 0.5 * (1.0 + t) + 0.5 * v * (1.0 - t * t) * (inner * (1.0 + 3.0 * cubic * v * v))


def column_sum(v):
    return jnp.sum(v, axis=0, keepdims=True)


def moments(total, squares, pixel_count):
    center = total / pixel_count
    spread = squares / pixel_count - center * center
    return center, lax.rsqrt(spread + epsilon)


def chunks(total, size):
    return [(at, min(size, total - at)) for at in range(0, total, size)]


def strided(ref, k, first, count, step):
    return ref[k, pl.ds(first, count, stride=step), :]


def vertical_kernel(r, copies):
    groups, width = r.x.shape[0], r.cot.shape[3]
    rows, cols = r.own.shape[1], r.own.shape[2]

    def pack(out, input_row, row, pick):
        at = 0
        for g in range(groups):
            for n in range(over):
                value = r.x[g, input_row(n)]
                out[at : at + 2 * cols, :] = pick(value, r.x[g, n])
                at += 2 * cols
        for k in range(0, width, 256):
            for g in range(groups):
                for n in range(rim):
                    lanes = slice(k, k + 256)
                    out[at : at + cols, :] = pick(r.cot[g, row(n), :, lanes], r.cot[g, n, :, lanes])
                    at += cols
        for g in range(groups):
            for n in range(rim):
                out[at : at + cols, :] = pick(wide(r.own[g, row(n)], 256), wide(r.own[g, n], 256))
                at += cols

    last = r.x.shape[1] - over
    copies.wait(N.x, N.cot)
    if hasattr(r, N.up):
        pack(r.down, lambda n: last + n, lambda n: rows - rim + n, lambda tail, head: tail)
        pack(r.up, lambda n: last + n, lambda n: rows - rim + n, lambda tail, head: head)
    else:
        bottom = r.flags[0] == 1
        pack(r.down, lambda n: last + n, lambda n: rows - rim + n, lambda tail, head: jnp.where(bottom, head, tail))


def rim_rows(r, own, n_own, n_rim, base, cols, split):
    groups = own.shape[0]
    size = groups * n_rim * cols

    def flat(ref, g, n):
        at = [base + k * size + (g * n_rim + n) * cols for k in range(split)]
        return jnp.concatenate([ref[p : p + cols, :] for p in at], axis=1).astype(f32)

    def read(g, n):
        if n < n_rim:
            return jnp.where(r.flags[0] == 1, flat(r.top, g, n), 0.0)
        if n < n_rim + n_own:
            return own[g, n - n_rim].astype(f32)
        return jnp.where(r.flags[1] == 1, flat(r.bot, g, n - n_rim - n_own), 0.0)

    return read


def fields(r):
    groups, width = r.x.shape[0], r.cot.shape[3]
    rows, cols = r.own.shape[1], r.own.shape[2]
    base = over * groups * 2 * cols
    piece = rim * groups * cols
    blocks = width // 256
    x = rim_rows(r, r.x, 2 * rows, over, 0, 2 * cols, 1)
    mask = rim_rows(r, r.own, rows, rim, base + blocks * piece, cols, 1)
    cot = rim_rows(r, r.cot, rows, rim, base, cols, blocks)
    return x, lambda g, n: mask(g, n)[:, :128], cot


def strips_kernel(r, copies):
    groups, width = r.x.shape[0], r.cot.shape[3]
    rows, cols = r.own.shape[1], r.own.shape[2]
    x, mask, cot = fields(r)
    lines = (2 * rows + 2 * over) * groups, (rows + 2 * rim) * groups, (rows + 3) * groups
    for raw, read, first, count, w in (
        (r.raw_x, x, 0, lines[0], 2 * cols),
        (r.raw_m, mask, 0, lines[1], cols),
        (r.raw_c, cot, 2, lines[2], cols),
    ):
        for at in range(count):
            value = read(at % groups, at // groups + first)
            for k in range(raw.shape[0]):
                raw[k, at * w : (at + 1) * w, :] = value[:, k * 128 : (k + 1) * 128]
    for out, x0, m0, c0 in ((r.right, 2 * cols - over, cols - rim, cols - 2), (r.left, 0, 0, 0)):
        pieces = []
        for c in range(over):
            pieces.append([strided(r.raw_x, k, x0 + c, lines[0], 2 * cols) for k in range(2)])
        for c in range(0, rim + 1, 2):
            pieces.append([strided(r.raw_m, 0, m0 + min(c + k, rim - 1), lines[1], cols) for k in range(2)])
        for c in range(2):
            for h in range(0, width // 128, 2):
                pieces.append([strided(r.raw_c, h + k, c0 + c, lines[2], cols) for k in range(2)])
        at = 0
        for low, high in pieces:
            r.flat[at : at + low.shape[0], :] = jnp.concatenate([low, high], axis=1)
            at += low.shape[0]
        if at < r.flat.shape[0]:
            r.flat[at:, :] = jnp.zeros((r.flat.shape[0] - at, 256), f32)
        out[...] = r.flat[...].astype(bf16)


def stats_kernel(r, copies):
    groups, cin = r.x.shape[0], r.x.shape[3]
    rows, S = r.own.shape[1], r.own.shape[2]
    L = groups * S
    width = r.w1.shape[2]
    raw = r.raw
    for n in range(2 * rows + 1):
        for g in range(groups):
            line = n * groups + g
            src = (r.top[g, 0] if n == 0 else r.x[g, n - 1]).astype(f32)
            side = r.lft[g, n].astype(f32)
            for k in range(raw.shape[0]):
                raw[k, line, 7:8, :] = side[:, k * 128 : (k + 1) * 128]
                raw[k, line, 8:, :] = src[:, k * 128 : (k + 1) * 128]
    for out, n_rows, start in ((r.xe, rows, 1), (r.xo, rows + 1, 0)):
        for n in range(n_rows):
            for b in range(3):
                for k in range(raw.shape[0]):
                    parts = [
                        raw[k, (2 * n + start) * groups + g, pl.ds(7 + b, S, stride=2), :]
                        for g in range(groups)
                    ]
                    at = b * cin + k * 128
                    out[n * L : (n + 1) * L, at : at + 128] = jnp.concatenate(
                        parts, axis=0
                    ).astype(bf16)
    mask = jnp.concatenate(
        [r.own[g, i].astype(f32) for i in range(rows) for g in range(groups)], axis=0
    )
    M = rows * L
    z = matmul(r.xo[0:M, :], r.w1[0])
    z += matmul(r.xe[...], r.w1[1])
    z += matmul(r.xo[L : L + M, :], r.w1[2])
    zp = matmul(r.xe[:, cin : 2 * cin], r.wp[...])
    zm, zpm = z * wide(mask, width), zp * wide(mask, width)
    row = jnp.concatenate(
        [column_sum(zm), column_sum(zm * z), column_sum(zpm), column_sum(zpm * zp), column_sum(mask)], axis=1
    )
    r.spread[...] = jnp.broadcast_to(row[None], r.spread.shape)
    copies.start(N.spread)
    copies.wait(N.spread)


def first_kernel(r, copies):
    groups, cin, width = r.x.shape[0], r.x.shape[3], r.cot.shape[3]
    rows, cols = r.own.shape[1], r.own.shape[2]
    S = cols + 8
    L = groups * S
    W = 2 * cols + 24
    V = cols + 16
    x, mask, cot = fields(r)
    lines = (2 * rows + 2 * over) * groups, (rows + 2 * rim) * groups, (rows + 3) * groups
    tail = jnp.zeros((W - 8 - 2 * cols, 128), f32)
    r.raw_m[...] = jnp.zeros(r.raw_m.shape, f32)
    r.raw_c[...] = jnp.zeros(r.raw_c.shape, f32)
    for at in range(lines[0]):
        value = x(at % groups, at // groups)
        for k in range(r.raw_x.shape[0]):
            r.raw_x[k, at * W + 8 : at * W + 8 + 2 * cols, :] = value[:, k * 128 : (k + 1) * 128]
            r.raw_x[k, at * W + 8 + 2 * cols : (at + 1) * W, :] = tail
    for strip, x0, m0, c0 in ((r.lft, 8 - over, 8 - rim, 6), (r.rgt, 8 + 2 * cols, 8 + cols, 8 + cols)):
        r.flat[...] = strip[...].astype(f32)
        at = 0
        for c in range(over):
            for k in range(2):
                r.raw_x[k, pl.ds(x0 + c, lines[0], stride=W), :] = r.flat[at : at + lines[0], k * 128 : (k + 1) * 128]
            at += lines[0]
        for c in range(0, rim + 1, 2):
            for k in range(2):
                if c + k < rim:
                    r.raw_m[0, pl.ds(m0 + c + k, lines[1], stride=V), :] = r.flat[
                        at : at + lines[1], k * 128 : (k + 1) * 128
                    ]
            at += lines[1]
        for c in range(2):
            for h in range(0, width // 128, 2):
                for k in range(2):
                    r.raw_c[h + k, pl.ds(c0 + c, lines[2], stride=V), :] = r.flat[
                        at : at + lines[2], k * 128 : (k + 1) * 128
                    ]
                at += lines[2]
    for out, n_rows, start in ((r.xe, rows + 5, 2), (r.xo, rows + 6, 1)):
        for n in range(n_rows):
            for b in range(3):
                for k in range(r.raw_x.shape[0]):
                    parts = [
                        strided(r.raw_x, k, ((2 * n + start) * groups + g) * W + 3 + b, S, 2) for g in range(groups)
                    ]
                    at = b * cin + k * 128
                    out[n * L : (n + 1) * L, at : at + 128] = jnp.concatenate(parts, axis=0).astype(bf16)
    copies.start(N.xe, N.xo)
    for at in range(lines[1]):
        r.raw_m[0, at * V + 8 : at * V + 8 + cols, :] = mask(at % groups, at // groups)
    for n in range(1, rows + 6):
        for g in range(groups):
            to, at = (n - 1) * L + g * S, (n * groups + g) * V
            r.maskp[to : to + S, :] = r.raw_m[0, at + 6 : at + 6 + S, :]
    for at in range(lines[2]):
        value = cot(at % groups, at // groups + 2)
        for k in range(r.raw_c.shape[0]):
            lanes = slice(k * 128, (k + 1) * 128)
            r.raw_c[k, at * V + 8 : at * V + 8 + cols, :] = value[:, lanes]
            r.cotq[at * S : (at + 1) * S, lanes] = r.raw_c[k, at * V + 7 : at * V + 7 + S, :]
    copies.start(N.cotq)
    r.ownp[...] = jnp.zeros(r.ownp.shape, f32)
    for i in range(rows):
        for g in range(groups):
            at = (i + 2) * L + g * S + 2
            r.ownp[at : at + cols, :] = r.own[g, i].astype(f32)
    copies.wait(N.w1, N.wp)
    for k, (m0, m) in enumerate(chunks(r.pre1.shape[0], r.pre1.shape[0] // 3)):
        z = matmul(r.xo[m0 : m0 + m, :], r.w1[0])
        z += matmul(r.xe[m0 : m0 + m, :], r.w1[1])
        z += matmul(r.xo[L + m0 : L + m0 + m, :], r.w1[2])
        r.pre1[m0 : m0 + m, :] = z
        copies.start((N.pre1, k))
        r.prep[m0 : m0 + m, :] = matmul(r.xe[m0 : m0 + m, cin : 2 * cin], r.wp[...])
        copies.start((N.prep, k))
    copies.wait(N.xe, N.xo, N.pre1, N.prep, N.cotq)


def second_kernel(r, copies):
    width = r.gain.shape[1]
    t = jnp.sum(r.tot1[...], axis=0)
    n = wide(t[:, 4 * width :], width)
    center, inv = moments(t[:, :width], t[:, width : 2 * width], n)
    proj = moments(t[:, 2 * width : 3 * width], t[:, 3 * width : 4 * width], n)
    r.mom1[...] = jnp.concatenate([center, inv, n, *proj, jnp.zeros((3, width), f32)], axis=0)
    scale = inv * r.gain[...]
    M, Q = r.pre1.shape[0], r.pre2.shape[0]
    L = (M - Q) // 2
    copies.wait(N.pre1)
    for m0, m in chunks(M, 104):
        v = (r.pre1[m0 : m0 + m, :] - center) * scale + r.shift[...]
        mask = wide(r.maskp[m0 : m0 + m, :], width)
        r.hid[m0 : m0 + m, :] = 0.5 * v * (1.0 + gelu_parts(v)) * mask
    r.hid[M:, :] = jnp.zeros((r.hid.shape[0] - M, width), f32)
    for m0, m in chunks(M, 208):
        for b in range(3):
            r.h3[m0 : m0 + m, b * width : (b + 1) * width] = r.hid[m0 + b : m0 + b + m, :].astype(bf16)
    copies.start(N.h3)
    copies.wait(N.w2)
    sums = [jnp.zeros((1, width), f32)] * 2
    for k, (m0, m) in enumerate(chunks(Q, Q // 3)):
        z = matmul(r.h3[m0 : m0 + m, :], r.w2[0])
        z += matmul(r.h3[L + m0 : L + m0 + m, :], r.w2[1])
        z += matmul(r.h3[2 * L + m0 : 2 * L + m0 + m, :], r.w2[2])
        r.pre2[m0 : m0 + m, :] = z
        copies.start((N.pre2, k))
        zm = z * wide(r.ownp[L + 1 + m0 : L + 1 + m0 + m, :], width)
        sums = [sums[0] + column_sum(zm), sums[1] + column_sum(zm * z)]
    row = jnp.concatenate(sums, axis=1)
    r.spread[...] = jnp.broadcast_to(row[None], r.spread.shape)
    copies.start(N.spread)
    copies.wait(N.h3, N.pre2, N.spread)


def part(r, at, *fields, first=0):
    bit = r.bits[0] == 1
    for k, field in enumerate(fields, first):
        half = field.shape[1] // 2
        low, high = field[:, :half], field[:, half:]
        r.mine[k, at : at + field.shape[0], :] = jnp.where(bit, high, low)
        r.theirs[k, at : at + field.shape[0], :] = jnp.where(bit, low, high)


def mine_of(r, row):
    half = row.shape[1] // 2
    return jnp.where(r.bits[0] == 1, row[:, half:], row[:, :half])


def third_kernel(r, copies):
    groups, rows, cols, width = r.out.shape
    S = cols + 8
    L = groups * S
    n = r.mom1[2:3, :]
    t = jnp.sum(r.tot2[...], axis=0)
    c2, i2 = moments(t[:, :width], t[:, width:], n)
    cp, ip = r.mom1[3:4, :], r.mom1[4:5, :]
    r.mom2[...] = jnp.concatenate([c2, i2, cp, ip, jnp.zeros((4, width), f32)], axis=0)
    sums = [jnp.zeros((1, width), f32)] * 3
    both_shift = r.shift2[...] + r.shiftp[...]
    total = r.grad.shape[0] // S
    for line in range(total):
        if line % (total // 2) == 0:
            k = line // (total // 2)
            copies.wait((N.pre2, k), (N.prep, k), (N.cotq, k))
        at = line * S
        shifted = slice(L + 1 + at, L + 1 + at + S)
        n2 = (r.pre2[at : at + S, :] - c2) * i2
        np_ = (r.prep[shifted, :] - cp) * ip
        v = n2 * r.gain2[...] + np_ * r.gainp[...] + both_shift
        mask = wide(r.maskp[shifted, :], width)
        own = wide(r.ownp[shifted, :], width)
        t = gelu_parts(v)
        r.field[at : at + S, :] = 0.5 * v * (1.0 + t) * mask
        g = gelu_slope(v, t) * mask * r.cotq[at : at + S, :]
        r.grad[at : at + S, :] = g
        g = g * own
        if L <= at < L + r.mine.shape[1]:
            part(r, at - L, g, n2 * own, np_ * own)
            if at - L + S == r.mine.shape[1] // 2:
                copies.start((N.mine, 0), (N.theirs, 0))
        new = [column_sum(g * n2), column_sum(g), column_sum(g * np_)]
        sums = [a + b for a, b in zip(sums, new)]
        if (line + 1) % (total // 2) == 0:
            copies.start((N.grad, (line + 1) // (total // 2) - 1))
    row = jnp.concatenate(sums, axis=1)
    r.spread[...] = jnp.broadcast_to(row[None], r.spread.shape)
    copies.start(N.spread, (N.mine, 1), (N.theirs, 1))
    for i in range(rows):
        for g in range(groups):
            at = (i + 1) * L + g * S + 1
            r.out[g, i, :, :] = r.field[at : at + cols, :].astype(bf16)
    copies.start(N.out)
    copies.wait(N.grad, N.out, N.spread, N.mine, N.theirs)


def fourth_kernel(r, copies):
    width = r.gain.shape[1]
    Q, U, rows_w = r.pre2.shape[0], r.act.shape[0], r.gpu.shape[0]
    L = U - rows_w
    center, inv, n = (r.mom1[k : k + 1, :] for k in range(3))
    c2, i2, cp, ip = (r.mom2[k : k + 1, :] for k in range(4))
    t3 = jnp.sum(r.tot3[...], axis=0)
    gg2, gs, ggp = (t3[:, k * width : (k + 1) * width] for k in range(3))
    r.gain_second[...], r.shift_second[...], r.gain_proj[...], r.shift_proj[...] = gg2, gs, ggp, gs
    tiny = N.gain_second, N.shift_second, N.gain_proj, N.shift_proj
    copies.start(*tiny)
    for m0, m in chunks(Q, L):
        if m0 in (0, 6 * L):
            copies.wait((N.grad, m0 // (6 * L)), (N.pre2, m0 // (6 * L)))
        mask = wide(r.maskp[L + 1 + m0 : L + 1 + m0 + m, :], width) / n
        n2 = (r.pre2[m0 : m0 + m, :] - c2) * i2
        back = mask * (gs + n2 * gg2)
        r.gq[m0 : m0 + m, :] = (r.gain2[...] * i2) * (r.grad[m0 : m0 + m, :] - back)
    r.gq[Q:, :] = jnp.zeros((r.gq.shape[0] - Q, width), f32)
    for m0, m in chunks(Q, 176):
        for b in range(3):
            r.g3[m0 : m0 + m, b * width : (b + 1) * width] = r.gq[m0 + b : m0 + b + m, :].astype(bf16)
    copies.wait(N.keep)
    for m0, m in chunks(U, L):
        frame = slice(2 * L + 2 + m0, 2 * L + 2 + m0 + m)
        n1 = (r.keep[frame, :] - center) * inv
        v = n1 * r.gain[...] + r.shift[...]
        mask = wide(r.maskp[frame, :], width)
        r.act[m0 : m0 + m, :] = gelu_slope(v, gelu_parts(v)) * mask
        r.normed[m0 : m0 + m, :] = n1 * mask
        if m0 < rows_w:
            part(r, m0, n1 * wide(r.ownp[frame, :], width), first=1)
    copies.start(N.normed, (N.mine, 1), (N.theirs, 1))
    for a in range(3):
        copies.wait((N.w2, a))
        gh = jnp.zeros((U, width), f32)
        for b in range(3):
            gh += matmul_nt(
                r.g3[L * a : L * a + U, b * width : (b + 1) * width],
                r.w2[2 - a, (2 - b) * width : (3 - b) * width, :],
            )
        r.gh[...] = gh if a == 0 else r.gh[...] + gh
    sums = [jnp.zeros((1, width), f32)] * 2
    for m0, m in chunks(U, L):
        g = r.act[m0 : m0 + m, :] * r.gh[m0 : m0 + m, :]
        r.act[m0 : m0 + m, :] = g
        g = g * wide(r.ownp[2 * L + 2 + m0 : 2 * L + 2 + m0 + m, :], width)
        if m0 < rows_w:
            part(r, m0, g)
        sums = [sums[0] + column_sum(g * r.normed[m0 : m0 + m, :]), sums[1] + column_sum(g)]
    row = jnp.concatenate(sums, axis=1)
    r.spread[...] = jnp.broadcast_to(row[None], r.spread.shape)
    copies.start(N.spread, (N.mine, 0), (N.theirs, 0), N.act)
    copies.wait(N.prep)
    for m0, m in chunks(rows_w, L):
        frame = slice(2 * L + 2 + m0, 2 * L + 2 + m0 + m)
        mask = wide(r.maskp[frame, :], width) / n
        back = mask * (gs + (r.prep[frame, :] - cp) * ip * ggp)
        r.gpu[m0 : m0 + m, :] = ((r.gainp[...] * ip) * (r.grad[L + 1 + m0 : L + 1 + m0 + m, :] - back)).astype(bf16)
    copies.start(N.gpu)
    copies.wait(N.normed, N.mine, N.theirs, N.spread, N.act, N.gpu, *tiny)


def split_store(r, rows, unit, first):
    quarter = unit // 4
    for k in range(rows // unit):
        for bit, base, sent, kept in ((1, 0, r.sent_a, r.kept_a), (2, 2 * quarter, r.sent_b, r.kept_b)):
            keep = pl.multiple_of(k * unit + base + r.bits[bit] * quarter, quarter)
            send = pl.multiple_of(k * unit + base + (1 - r.bits[bit]) * quarter, quarter)
            sent[first + k] = r.acc[pl.ds(send, quarter), :].astype(bf16)
            kept[first + k] = r.acc[pl.ds(keep, quarter), :]


def weights_second_kernel(r, copies):
    width = r.h3.shape[1] // 3
    cin = r.xe.shape[1] // 3
    rows_w = r.mine.shape[1]
    L = (r.h3.shape[0] - rows_w) // 5
    per = width // cin
    t3 = jnp.sum(r.tot3[...], axis=0)
    n = mine_of(r, r.mom1[2:3, :])
    gg2, gs, ggp = (mine_of(r, t3[:, k * width : (k + 1) * width]) / n for k in range(3))
    scale2, scalep = mine_of(r, r.gain2[...] * r.mom2[1:2, :]), mine_of(r, r.gainp[...] * r.mom2[3:4, :])
    half = scale2.shape[1]
    for source, name, own, out in ((r.mine, N.mine, r.ownp, r.near), (r.far3, N.far3, r.ownp_far, r.far)):
        copies.wait(name)
        r.pad[:, 0:8, :] = jnp.zeros((3, 8, half), f32)
        r.pad[:, 8:, :] = source[...]
        for m0, m in chunks(rows_w, 96):
            mask = wide(own[2 * L + 1 + m0 : 2 * L + 1 + m0 + m, :], half)
            rows = slice(8 + m0, 8 + m0 + m)
            back = mask * gs + r.pad[1, rows, :] * gg2
            out[m0 : m0 + m, :] = (scale2 * (r.pad[0, rows, :] - back)).astype(bf16)
            mask = wide(own[2 * L + m0 : 2 * L + m0 + m, :], half)
            rows = slice(7 + m0, 7 + m0 + m)
            back = mask * gs + r.pad[2, rows, :] * ggp
            out[rows_w + m0 : rows_w + m0 + m, :] = (scalep * (r.pad[0, rows, :] - back)).astype(bf16)
    for b in range(3):
        lanes = slice(b * width, (b + 1) * width)
        copies.wait((N.h3, b), (N.h3_far, b))
        for a in range(3):
            at = L * a + L
            r.acc[...] = matmul_tn(r.h3[at : at + rows_w, lanes], r.near[:rows_w, :]) + matmul_tn(
                r.h3_far[at : at + rows_w, lanes], r.far[:rows_w, :]
            )
            split_store(r, width, cin, (3 * b + a) * per)
        copies.start(*((name, b) for name in CHUNKS))
    at = 2 * L
    copies.wait(N.xe, N.xe_far)
    middle = slice(cin, 2 * cin)
    r.acc[0:cin, :] = matmul_tn(r.xe[at : at + rows_w, middle], r.near[rows_w:, :]) + matmul_tn(
        r.xe_far[at : at + rows_w, middle], r.far[rows_w:, :]
    )
    split_store(r, cin, cin, 9 * per)
    copies.start(*((name, 3) for name in CHUNKS))
    copies.wait(*CHUNKS)


def first_back(r, gg, gs, count):
    width = r.gain.shape[1]
    U = r.act.shape[0]
    L = U - r.rows_w
    inv, n = r.mom1[1:2, :], r.mom1[2:3, :]
    gg, gs = gg / n, gs / n
    scale = r.gain[...] * inv
    r.gf[0:8, :] = jnp.zeros((8, width), f32)
    r.gf[8 + count :, :] = jnp.zeros((r.gf.shape[0] - 8 - count, width), f32)
    for m0, m in chunks(count, L):
        mask = wide(r.maskp[2 * L + 2 + m0 : 2 * L + 2 + m0 + m, :], width)
        back = mask * gs + r.normed[m0 : m0 + m, :] * gg
        r.gf[8 + m0 : 8 + m0 + m, :] = scale * (r.act[m0 : m0 + m, :] - back)


def weights_first_kernel(r, copies):
    rows_w = r.mine.shape[1]
    cin = r.xe.shape[1] // 3
    L = (r.xe.shape[0] - rows_w) // 5
    width = r.gain.shape[1]
    t4 = jnp.sum(r.tot4[...], axis=0)
    r.gain_first[...], r.shift_first[...] = t4[:, :width], t4[:, width:]
    copies.start(N.gain_first, N.shift_first)
    n = mine_of(r, r.mom1[2:3, :])
    gg, gs = mine_of(r, t4[:, :width]) / n, mine_of(r, t4[:, width:]) / n
    scale = mine_of(r, r.gain[...] * r.mom1[1:2, :])
    half = scale.shape[1]
    for source, name, own, out in ((r.mine, N.mine, r.ownp, r.near), (r.far4, N.far4, r.ownp_far, r.far)):
        copies.wait(name)
        r.pad[:, 0:8, :] = jnp.zeros((2, 8, half), f32)
        r.pad[:, 8:, :] = source[...]
        for m0, m in chunks(rows_w, 96):
            mask = wide(own[2 * L + m0 : 2 * L + m0 + m, :], half)
            rows = slice(6 + m0, 6 + m0 + m)
            back = mask * gs + r.pad[1, rows, :] * gg
            out[m0 : m0 + m, :] = (scale * (r.pad[0, rows, :] - back)).astype(bf16)
    copies.wait(N.xe, N.xe_far)
    for k, a in enumerate((1, 0, 2)):
        if k == 1:
            copies.wait(N.xo, N.xo_far)
        source, source_far = (r.xe, r.xe_far) if a == 1 else (r.xo, r.xo_far)
        at = (3 if a == 2 else 2) * L
        for b in range(3):
            lanes = slice(b * cin, (b + 1) * cin)
            r.acc[lanes, :] = matmul_tn(source[at : at + rows_w, lanes], r.near[...]) + matmul_tn(
                source_far[at : at + rows_w, lanes], r.far[...]
            )
        split_store(r, 3 * cin, cin, a * 3)
        copies.start(*((name, a) for name in CHUNKS))
    copies.wait(N.gain_first, N.shift_first, *CHUNKS)


def inputs_kernel(r, copies):
    width = r.gpu.shape[1]
    groups, rows, cols = r.out.shape[0], r.out.shape[1] // 2, r.out.shape[2] // 2
    cin = r.out.shape[3]
    M = r.gpu.shape[0]
    S = cols + 8
    L = groups * S
    lines = r.lines
    U = r.act.shape[0]
    r.rows_w = M
    copies.wait(N.act, N.normed)
    first_back(r, r.gg[...], r.gs[...], U)
    for m0, m in chunks(U, 144):
        r.gu[m0 : m0 + m, :width] = r.gf[8 + m0 : 8 + m0 + m, :].astype(bf16)
        r.gu[m0 : m0 + m, width:] = r.gf[9 + m0 : 9 + m0 + m, :].astype(bf16)
    copies.wait(N.gpu, N.w1, N.wp)

    def tap(m0, m, a, b):
        di, dj = (1 if a == 0 else 0), (1 if b == 0 else 0)
        return matmul_nt(
            r.gu[di * L + m0 : di * L + m0 + m, dj * width : (dj + 1) * width],
            r.w1[a, b * cin : (b + 1) * cin, :],
        )

    for m0, m in chunks(M, 2 * L):
        pieces = {
            (0, 0): tap(m0, m, 1, 1) + matmul_nt(r.gpu[m0 : m0 + m, :], r.wp[...]),
            (0, 1): tap(m0, m, 1, 2) + tap(m0, m, 1, 0),
            (1, 0): tap(m0, m, 2, 1) + tap(m0, m, 0, 1),
            (1, 1): tap(m0, m, 2, 2) + tap(m0, m, 2, 0) + tap(m0, m, 0, 2) + tap(m0, m, 0, 0),
        }
        for (ro, co), v in pieces.items():
            for k in range(m // S):
                line = m0 // S + k
                i, g = line // groups, line % groups
                for h in range(lines.shape[0]):
                    lines[h, (2 * i + ro) * groups + g, pl.ds(co, cols, stride=2), :] = v[
                        k * S : k * S + cols, h * 128 : (h + 1) * 128
                    ]
    for n in range(2 * rows):
        for g in range(groups):
            for h in range(lines.shape[0]):
                r.out[g, n, :, h * 128 : (h + 1) * 128] = lines[h, n * groups + g].astype(bf16)
    copies.start(N.out)
    copies.wait(N.out)


def widen(half, spots, side, taps, per, swapped, into=None):
    total, n, m = half.shape
    extra = total - taps * per
    order = [(t % 3 * 3 + t // 3) if swapped else t for t in range(taps)]
    jobs = [(t * per, per, 0, order[t] * per) for t in range(taps)] + [(taps * per, 1, 1, 0)] * extra
    more = list(into or [])

    def body(spots_ref, half_ref, *refs):
        outs = refs[len(more) : len(more) + 1 + extra]
        narrow, full, sems = refs[len(more) + 1 + extra :]
        lanes = pl.ds(pl.multiple_of(spots_ref[4] * m, m), m)
        h = n // 4
        places = [pl.ds(pl.multiple_of(spots_ref[q] * h, h), h) for q in range(4)]
        reads = [
            pltpu.make_async_copy(half_ref.at[pl.ds(at, size)], narrow.at[pl.ds(at, size)], sems.at[0, k])
            for k, (at, size, _, _) in enumerate(jobs)
        ]
        writes = [
            [
                pltpu.make_async_copy(
                    full.at[pl.ds(at, size), pl.ds(q * h, h)],
                    outs[which].at[pl.ds(to, size), places[q], lanes],
                    sems.at[1 + q, k],
                )
                for q in range(4)
            ]
            for k, (at, size, which, to) in enumerate(jobs)
        ]
        for read in reads:
            read.start()
        for k, (at, size, _, _) in enumerate(jobs):
            reads[k].wait()
            full[at : at + size] = narrow[at : at + size].astype(f32)
            for write in writes[k]:
                write.start()
        for write in sum(writes, []):
            write.wait()

    hbm = pl.BlockSpec(memory_space=pltpu.HBM)
    return pl.pallas_call(
        body,
        out_shape=[shape((taps * per, n, 2 * m))] + [shape((1, n, 2 * m))] * extra,
        in_specs=[pl.BlockSpec(memory_space=pltpu.SMEM)] + [hbm] * (1 + len(more)),
        out_specs=[hbm] * (1 + extra),
        scratch_shapes=[
            pltpu.VMEM((total, n, m), bf16),
            pltpu.VMEM((total, n, m), f32),
            pltpu.SemaphoreType.DMA((5, len(jobs))),
        ],
        input_output_aliases={2 + k: k for k in range(len(more))},
        compiler_params=pltpu.CompilerParams(vmem_limit_bytes=20 * 1024 * 1024),
        cost_estimate=pl.CostEstimate(flops=0, bytes_accessed=0, transcendentals=0),
    )(jnp.concatenate([spots, side.reshape(1)]), half, *more)


def halve_kernel(r, copies):
    for p in range(r.count):
        kept, got = getattr(r, f"kept{p}"), getattr(r, f"got{p}")
        copies.wait(f"kept{p}", f"got{p}")
        to_send, to_keep = getattr(r, f"sent{p}"), getattr(r, f"left{p}")
        bit = r.bits[r.steps[p]] == 1
        h = kept.shape[1] // 2
        for t in range(kept.shape[0]):
            total = kept[t] + got[t].astype(f32)
            low, high = total[:h], total[h:]
            to_send[t] = jnp.where(bit, low, high).astype(bf16)
            to_keep[t] = jnp.where(bit, high, low)
        copies.start(f"sent{p}", f"left{p}")
    copies.wait(*(name for name in copies.jobs if name[:4] in (N.sent, N.left)))


def halve(bits, pairs, steps, cost):
    ins = dict(bits=bits)
    for p, (kept, got) in enumerate(pairs):
        ins[f"kept{p}"], ins[f"got{p}"] = kept, got
    taps, n, m = pairs[0][0].shape
    dims = (taps, n // 2, m)
    names = [str(p) for p in range(len(pairs))]
    outs = {}
    for name in names:
        outs[N.sent + name], outs[N.left + name] = shape(dims, bf16), shape(dims)

    def body(r, copies):
        r.count, r.steps = len(pairs), steps
        halve_kernel(r, copies)

    far_in = tuple(n for n in ins if n != N.bits)
    out = call(body, ins, outs, far_in=far_in, far_out=tuple(outs), smem=(N.bits,), cost=cost, limit=60, anywhere=(N.got0, N.got1))
    return [(out[N.sent + name], out[N.left + name]) for name in names]


def shifted(value, axis, steps):
    count = lax.axis_size(axis)
    first, last = (max(0, -steps), min(count, count - steps))
    return lax.ppermute(value, axis, [(source, source + steps) for source in range(first, last)])


def gather_sum(spread):
    return lax.all_to_all(spread, axes, 0, 0)


def bit_of(axis, step):
    return (lax.axis_index(axis) // step) % 2


def partner(value, axis, step):
    count = lax.axis_size(axis)
    return lax.ppermute(value, axis, [(i, i ^ step) for i in range(count)])


def steps_of(axis):
    count, step, out = lax.axis_size(axis), 1, []
    while step < count:
        out.append((axis, step))
        step *= 2
    return out


def split(total, axis, step):
    n = total.shape[1] // 2
    bit = bit_of(axis, step) == 1
    low, high = total[:, :n], total[:, n:]
    return jnp.where(bit, low, high).astype(bf16), jnp.where(bit, high, low)


def joined(value, other, axis, step, dim=1):
    bit = bit_of(axis, step) == 1
    return jnp.concatenate([jnp.where(bit, other, value), jnp.where(bit, value, other)], axis=dim)


class Tree:
    def __init__(self, parts, bits, plane, rest, core):
        self.bits, self.place = bits, {step: k for k, step in enumerate([core, *plane, *rest])}
        self.sent_a, self.kept_a, self.sent_b, self.kept_b = parts
        self.a, self.b, self.rest, self.core = plane, plane[::-1], rest, core
        p, n = len(plane), len(rest)
        self.stages = [(N.plane, k) for k in range(p)] + [(N.rest, k) for k in range(n)]
        self.stages += [(N.rest_join, k) for k in reversed(range(n))] + [(N.plane_join, k) for k in reversed(range(p))]
        self.stages += [(N.core, 0)]

    def next(self):
        return self.stages[0] if self.stages else None

    def start(self):
        kind, k = self.stages[0]
        if kind == N.plane:
            self.got = partner(self.sent_a, *self.a[k]), partner(self.sent_b, *self.b[k])
        elif kind == N.rest:
            self.got = (partner(self.sent, *self.rest[k]),)
        elif kind == N.rest_join:
            self.got = (partner(self.value, *self.rest[k]),)
        elif kind == N.plane_join:
            self.got = partner(self.value_a, *self.a[k]), partner(self.value_b, *self.b[k])
        else:
            self.got = (partner(self.value, *self.core),)

    def finish(self, cost=0):
        kind, k = self.stages.pop(0)
        if kind == N.plane:
            pairs = [(self.kept_a, self.got[0]), (self.kept_b, self.got[1])]
            nexts = [order[k + 1] for order in (self.a, self.b) if k + 1 < len(order)]
            if nexts and cost:
                pairs = halve(self.bits, pairs, [self.place[step] for step in nexts], cost)
                (self.sent_a, self.kept_a), (self.sent_b, self.kept_b) = pairs
                return
            total_a, total_b = (kept + got.astype(f32) for kept, got in pairs)
            if nexts:
                self.sent_a, self.kept_a = split(total_a, *nexts[0])
                self.sent_b, self.kept_b = split(total_b, *nexts[1])
            else:
                self.taps = total_a.shape[0]
                self.split_rest(jnp.concatenate([total_a, total_b], axis=0), 0)
        elif kind == N.rest:
            self.split_rest(self.kept + self.got[0].astype(f32), k + 1)
        elif kind == N.rest_join:
            self.value = joined(self.value, self.got[0], *self.rest[k])
            self.value_a, self.value_b = self.value[: self.taps], self.value[self.taps :]
        elif kind == N.plane_join and k > 0:
            self.value_a = joined(self.value_a, self.got[0], *self.a[k])
            self.value_b = joined(self.value_b, self.got[1], *self.b[k])
        elif kind == N.plane_join:
            pieces = self.value_a, self.got[0], self.value_b, self.got[1]
            self.value = jnp.concatenate(pieces, axis=1)

    def split_rest(self, total, k):
        if k < len(self.rest):
            self.sent, self.kept = split(total, *self.rest[k])
        else:
            self.value = total.astype(bf16)


def lockstep(*trees, beside=()):
    for t in trees:
        t.start()
    got, beside = lax.optimization_barrier(([t.got for t in trees], beside))
    for t, g in zip(trees, got):
        t.got = g
        t.finish()
    return beside


def on_device(inputs, w_first, gain_first, shift_first, w_second, gain_second, shift_second, w_proj, gain_proj, shift_proj, valid_mask, cotangent):
    groups, rows_in, cols_in, cin = inputs.shape
    rows, cols = rows_in // 2, cols_in // 2
    width = w_first.shape[3]
    half = width // 2
    S = cols + 8
    L = groups * S
    devices = lax.axis_size(N.rows) * lax.axis_size(N.cols) * lax.axis_size(N.grp)
    plane = steps_of(N.cols)
    core = steps_of(N.rows)[0]
    rest = steps_of(N.rows)[1:] + steps_of(N.grp)
    bits = jnp.stack([bit_of(*step) for step in (core, *plane, *rest)]).astype(jnp.int32)
    w1 = w_first.reshape(3, 3 * cin, width)
    w2 = w_second.reshape(3, 3 * width, width)
    as_row = lambda v: v.reshape(1, -1)
    own = jnp.broadcast_to(valid_mask.astype(bf16)[..., None], valid_mask.shape + (128,))
    MP, MQ, MU, MW = (rows + 5) * L, (rows + 3) * L, (rows + 1) * L, rows * L
    px = lambda m, k: 2 * m * k * width
    vec = lambda k: shape((1, k * width))
    all_devices = lambda k: shape((devices, 1, k))
    g1, b1, g2, b2, gp, bp = map(
        as_row, (gain_first, shift_first, gain_second, shift_second, gain_proj, shift_proj)
    )

    top1 = shifted(inputs[:, -1:], N.rows, 1)
    me, count = lax.axis_index(N.rows), lax.axis_size(N.rows)
    flags = jnp.stack([me > 0, me < count - 1]).astype(jnp.int32)
    flat_rows = shape((over * groups * cols_in + (width // 256 + 1) * rim * groups * cols, 256), bf16)
    packed = call(
        vertical_kernel,
        dict(flags=flags, x=inputs, cot=cotangent, own=own),
        dict(down=flat_rows) if count == 2 else dict(down=flat_rows, up=flat_rows),
        far_in=(N.x, N.cot),
        smem=(N.flags,),
        parts=dict(x=end_parts(rows_in, over), cot=end_parts(rows, rim)),
    )
    if count == 2:
        top = bot = lax.ppermute(packed["down"], "rows", [(0, 1), (1, 0)])
    else:
        top, bot = shifted(packed[N.down], N.rows, 1), shifted(packed[N.up], N.rows, -1)
    lft1 = shifted(jnp.concatenate([top1[:, :, -1:], inputs[:, :, -1:]], axis=1), N.cols, 1)
    (top, bot), lft1 = lax.optimization_barrier(((top, bot), lft1))
    lines = (rows_in + 2 * over) * groups, (rows + 2 * rim) * groups, (rows + 3) * groups
    n_strip = over * lines[0] + (rim + 1) // 2 * lines[1] + width // 128 * lines[2]
    n_strip = -(-n_strip // 16) * 16
    near = dict(flags=flags, x=inputs, cot=cotangent, own=own, top=top, bot=bot)
    strips = call(
        strips_kernel,
        near,
        dict(right=shape((n_strip, 256), bf16), left=shape((n_strip, 256), bf16)),
        dict(
            raw_x=pltpu.VMEM((cin // 128, lines[0] * cols_in, 128), f32),
            raw_m=pltpu.VMEM((1, lines[1] * cols, 128), f32),
            raw_c=pltpu.VMEM((width // 128, lines[2] * cols, 128), f32),
            flat=pltpu.VMEM((n_strip, 256), f32),
        ),
        smem=(N.flags,),
    )
    lft, rgt = shifted(strips[N.right], N.cols, 1), shifted(strips[N.left], N.cols, -1)
    lft1, _ = lax.optimization_barrier((lft1, strips[N.right]))
    stats = call(
        stats_kernel,
        dict(x=inputs, top=top1, lft=lft1, own=own, w1=w1, wp=w_proj),
        dict(spread=all_devices(4 * width + 128)),
        dict(
            raw=pltpu.VMEM((cin // 128, (rows_in + 1) * groups, cols_in + 8, 128), f32),
            xe=pltpu.VMEM((rows * groups * cols, 3 * cin), bf16),
            xo=pltpu.VMEM(((rows + 1) * groups * cols, 3 * cin), bf16),
        ),
        far_out=(N.spread,),
    )
    tot1 = gather_sum(stats[N.spread])

    first = call(
        first_kernel,
        dict(**near, lft=lft, rgt=rgt, w1=w1, wp=w_proj),
        dict(
            pre1=shape((MP, width)),
            prep=shape((MP, width)),
            xe=shape((MP, 3 * cin), bf16),
            xo=shape((MP + L, 3 * cin), bf16),
            ownp=shape((MP, 128)),
            maskp=shape((MP, 128)),
            cotq=shape((MQ, width)),
        ),
        dict(
            raw_x=pltpu.VMEM((cin // 128, lines[0] * (cols_in + 24), 128), f32),
            raw_m=pltpu.VMEM((1, lines[1] * (cols + 16), 128), f32),
            raw_c=pltpu.VMEM((width // 128, lines[2] * (cols + 16), 128), f32),
            flat=pltpu.VMEM((n_strip, 256), f32),
        ),
        far_in=(N.w1, N.wp),
        far_out=(N.xe, N.xo, N.pre1, N.prep, N.cotq),
        smem=(N.flags,),
        cost=20000000000,
        parts=dict(pre1=row_parts(MP, 3), prep=row_parts(MP, 3)),
    )
    xe, xo, ownp, maskp = first[N.xe], first[N.xo], first[N.ownp], first[N.maskp]
    far_xe, far_xo = partner(xe, *core), partner(xo, *core)

    second = call(
        second_kernel,
        dict(pre1=first[N.pre1], tot1=tot1, gain=g1, shift=b1, maskp=maskp, ownp=ownp, w2=w2),
        dict(h3=shape((MP, 3 * width), bf16), pre2=shape((MQ, width)), spread=all_devices(2 * width), mom1=shape((8, width))),
        dict(hid=pltpu.VMEM((MP + 8, width), f32)),
        far_in=(N.pre1, N.w2),
        far_out=(N.h3, N.pre2, N.spread),
        parts=dict(pre2=row_parts(MQ, 3)),
    )
    h3, pre2, mom1 = second[N.h3], second[N.pre2], second[N.mom1]
    tot2 = gather_sum(second[N.spread])
    tot2, far_h3 = lax.optimization_barrier((tot2, partner(h3, *core)))

    third = call(
        third_kernel,
        dict(
            bits=bits, pre2=pre2, prep=first[N.prep], mom1=mom1, tot2=tot2, gain2=g2, shift2=b2, gainp=gp, shiftp=bp,
            maskp=maskp, ownp=ownp, cotq=first[N.cotq],
        ),
        dict(
            out=shape((groups, rows, cols, width), bf16),
            grad=shape((MQ, width)),
            spread=all_devices(3 * width),
            mom2=shape((8, width)),
            mine=shape((3, MW, half)),
            theirs=shape((3, MW, half)),
        ),
        dict(field=pltpu.VMEM((MQ, width), f32)),
        far_in=(N.pre2, N.prep, N.cotq),
        far_out=(N.grad, N.spread, N.mine, N.theirs, N.out),
        smem=(N.bits,),
        parts=dict(
            mine=middle_parts(MW, 2), theirs=middle_parts(MW, 2),
            grad=row_parts(MQ, 2), pre2=row_parts(MQ, 2), cotq=row_parts(MQ, 2), prep=cuts(L, L + MQ // 2 + 8, L + MQ + 8)
        ),
    )
    mom2 = third[N.mom2]
    tot3 = gather_sum(third[N.spread])
    ownp_here, far3 = lax.optimization_barrier((ownp, partner(third[N.theirs], *core)))
    ownp_far = partner(ownp_here, *core)

    def chunk_shapes(taps):
        dims = (taps, cin // 4, half)
        return dict(sent_a=shape(dims, bf16), kept_a=shape(dims), sent_b=shape(dims, bf16), kept_b=shape(dims))

    per = width // cin
    taps2 = 9 * per + 1
    second_parts = call(
        weights_second_kernel,
        dict(
            bits=bits, mine=third[N.mine], far3=far3, h3=h3, h3_far=far_h3, xe=xe, xe_far=far_xe,
            tot3=tot3, mom1=mom1, mom2=mom2, gain2=g2, gainp=gp, ownp=ownp, ownp_far=ownp_far,
        ),
        chunk_shapes(taps2),
        dict(
            acc=pltpu.VMEM((width, half), f32),
            pad=pltpu.VMEM((3, MW + 8, half), f32),
            near=pltpu.VMEM((2 * MW, half), bf16),
            far=pltpu.VMEM((2 * MW, half), bf16),
        ),
        far_in=(N.mine, N.far3, N.h3, N.h3_far, N.xe, N.xe_far),
        anywhere=(N.far3,),
        far_out=CHUNKS,
        smem=(N.bits,),
        parts=dict(
            h3=lane_parts(3 * width, 3, pl.ds(L, MW + 2 * L)),
            h3_far=lane_parts(3 * width, 3, pl.ds(L, MW + 2 * L)),
            xe=[(0, (pl.ds(2 * L, MW), pl.ds(cin, cin)))],
            xe_far=[(0, (pl.ds(2 * L, MW), pl.ds(cin, cin)))],
            **{name: row_parts(taps2 - 1, 3) + [(3, (pl.ds(taps2 - 1, 1),))] for name in CHUNKS},
        ),
    ).values()
    grad, *second_parts = lax.optimization_barrier((third[N.grad], *second_parts))
    tree2 = Tree(second_parts, bits, plane, rest, core)
    tree2.start()
    hidden = call(
        fourth_kernel,
        dict(
            bits=bits, grad=grad, pre2=pre2, keep=first[N.pre1], w2=w2, prep=first[N.prep], mom1=mom1, mom2=mom2, tot3=tot3,
            gain=g1, shift=b1, gain2=g2, gainp=gp, maskp=maskp, ownp=ownp,
        ),
        dict(
            act=shape((MU, width)), normed=shape((MU, width)), spread=all_devices(2 * width),
            mine=shape((2, MW, half)), theirs=shape((2, MW, half)), gpu=shape((MW, width), bf16),
            gain_second=vec(1), shift_second=vec(1), gain_proj=vec(1), shift_proj=vec(1),
        ),
        dict(
            gq=pltpu.VMEM((MQ + 8, width), f32),
            g3=pltpu.VMEM((MQ, 3 * width), bf16),
            gh=pltpu.VMEM((MU, width), f32),
        ),
        far_in=(N.grad, N.pre2, N.keep, N.w2, N.prep),
        far_out=(
            N.act, N.normed, N.spread, N.mine, N.theirs, N.gpu, N.gain_second, N.shift_second, N.gain_proj, N.shift_proj
        ),
        smem=(N.bits,),
        limit=52,
        parts=dict(
            grad=cuts(0, 6 * L, MQ),
            pre2=cuts(0, 6 * L, MQ),
            keep=cuts(2 * L, 2 * L + MU + 8),
            w2=[(k, (pl.ds(2 - k, 1),)) for k in range(3)],
            prep=cuts(2 * L, 2 * L + MW + 8),
            mine=row_parts(2, 2),
            theirs=row_parts(2, 2),
        ),
    )
    tot4 = gather_sum(hidden[N.spread])
    tree2.finish(20000000000)
    near1, tree2.sent_a, tree2.sent_b = lax.optimization_barrier((hidden[N.mine], tree2.sent_a, tree2.sent_b))
    tree2.start()
    fifth = call(
        weights_first_kernel,
        dict(
            bits=bits, mine=near1, far4=partner(hidden[N.theirs], *core), xe=xe, xe_far=far_xe, xo=xo, xo_far=far_xo,
            tot4=tot4, mom1=mom1, gain=g1, ownp=ownp, ownp_far=ownp_far,
        ),
        dict(**chunk_shapes(9), gain_first=vec(1), shift_first=vec(1)),
        dict(
            acc=pltpu.VMEM((3 * cin, half), f32),
            pad=pltpu.VMEM((2, MW + 8, half), f32),
            near=pltpu.VMEM((MW, half), bf16),
            far=pltpu.VMEM((MW, half), bf16),
        ),
        far_in=(N.mine, N.far4, N.xe, N.xe_far, N.xo, N.xo_far),
        anywhere=(N.far4,),
        cost=20000000000,
        far_out=(*CHUNKS, N.gain_first, N.shift_first),
        smem=(N.bits,),
        parts=dict(
            xe=cuts(2 * L, 2 * L + MW),
            xe_far=cuts(2 * L, 2 * L + MW),
            xo=cuts(2 * L, 3 * L + MW),
            xo_far=cuts(2 * L, 3 * L + MW),
            **{name: row_parts(9, 3) for name in CHUNKS},
        ),
    )
    first_parts = [fifth[name] for name in CHUNKS]
    tree2.got, *first_parts = lax.optimization_barrier((tree2.got, *first_parts))
    tree2.finish()
    tree1 = Tree(first_parts, bits, plane, rest, core)

    grad_inputs = call(
        inputs_kernel,
        dict(
            act=hidden[N.act], normed=hidden[N.normed], gpu=hidden[N.gpu], w1=w1, wp=w_proj, mom1=mom1, gain=g1, maskp=maskp,
            gg=fifth[N.gain_first], gs=fifth[N.shift_first],
        ),
        dict(out=shape((groups, rows_in, cols_in, cin), bf16)),
        dict(
            lines=pltpu.VMEM((cin // 128, rows_in * groups, cols_in, 128), f32),
            gf=pltpu.VMEM((MU + 16, width), f32),
            gu=pltpu.VMEM((MU, 2 * width), bf16),
        ),
        far_in=(N.act, N.normed, N.gpu, N.w1, N.wp),
        far_out=(N.out,),
        cost=10000000000,
    )[N.out]
    side, low, high = (bits[tree2.place[step]] for step in (core, plane[0], plane[-1]))
    spots = jnp.stack([low, 1 - low, 2 + high, 3 - high])
    grad_inputs = lockstep(tree2, tree1, beside=grad_inputs)
    while tree2.next() != (N.plane_join, 0):
        lockstep(tree2, tree1)
    tree2.start()
    while tree1.next() != (N.plane_join, 0):
        tree1.start()
        if tree1.next() != (N.plane_join, 1):
            tree1.finish()
        else:
            tree1.got, tree2.got = lax.optimization_barrier((tree1.got, tree2.got))
            tree1.finish()
    tree2.finish()
    tree2.start()
    tree1.start()
    grad_second = widen(tree2.got[0], spots, 1 - side, 9, per, True, widen(tree2.value, spots, side, 9, per, True))
    tree1.got, grad_second = lax.optimization_barrier((tree1.got, grad_second))
    grad_w2, grad_wp = grad_second
    tree1.finish()
    tree1.start()
    (grad_w1,) = widen(tree1.got[0], spots, 1 - side, 3, 3, False, widen(tree1.value, spots, side, 3, 3, False))

    return (
        third[N.out],
        grad_inputs,
        grad_w1.reshape(w_first.shape),
        fifth[N.gain_first].reshape(width),
        fifth[N.shift_first].reshape(width),
        grad_w2.reshape(w_second.shape),
        hidden[N.gain_second].reshape(width),
        hidden[N.shift_second].reshape(width),
        grad_wp.reshape(w_proj.shape),
        hidden[N.gain_proj].reshape(width),
        hidden[N.shift_proj].reshape(width),
    )


def solution(mesh):
    spread = P("grp", "rows", "cols", None)
    return jax.shard_map(
        on_device,
        mesh=mesh,
        in_specs=(spread,) + (P(),) * 9 + (P("grp", "rows", "cols"), spread),
        out_specs=(spread, spread) + (P(),) * 9,
        check_vma=False,
    )
```

```python
import functools

import jax
import jax.numpy as jnp
from jax import lax
from jax.experimental import pallas as pl
from jax.experimental.pallas import tpu as pltpu
from jax.sharding import PartitionSpec as P

epsilon = 1e-05
axes = ("rows", "cols", "grp")
bf16 = jnp.bfloat16
f32 = jnp.float32
inner = 0.7978845608028654
cubic = 0.044715
over = 6
CHUNKS = "sent_a", "kept_a", "sent_b", "kept_b"
rim = 3


class Names:
    def __getattr__(self, name):
        return name


N = Names()


class Refs:
    def __init__(self, named):
        self.__dict__.update(named)


class Copies:
    def __init__(self, parts, pairs, sems):
        self.jobs = {}
        for k, (name, index) in enumerate(parts):
            source, target = pairs[name]
            if index:
                source, target = source.at[index[1]], target.at[index[1]]
            self.jobs.setdefault(name, []).append(pltpu.make_async_copy(source, target, sems.at[k]))

    def start(self, *names):
        for name, *which in map(named, names):
            for job in self.jobs[name][slice(*which) if which else slice(None)]:
                job.start()

    def start_all(self, names):
        for k in range(max((len(self.jobs[n]) for n in names), default=0)):
            for n in names:
                if k < len(self.jobs[n]):
                    self.jobs[n][k].start()

    def wait(self, *names):
        for name, *which in map(named, names):
            for job in self.jobs[name][slice(*which) if which else slice(None)]:
                job.wait()


def named(name):
    return (name,) if isinstance(name, str) else (name[0], name[1], name[1] + 1)


def row_parts(total, count):
    size = total // count
    return [(k, (pl.ds(k * size, size),)) for k in range(count)]


def middle_parts(total, count):
    size = total // count
    return [(k, (slice(None), pl.ds(k * size, size))) for k in range(count)]


def end_parts(total, size):
    return [(k, (slice(None), pl.ds(at, size))) for k, at in enumerate((0, total - size))]


def cuts(*at):
    return [(k, (pl.ds(a, b - a),)) for k, (a, b) in enumerate(zip(at, at[1:]))]


def lane_parts(total, count, rows=slice(None)):
    size = total // count
    return [(k, (rows, pl.ds(k * size, size))) for k in range(count)]


def call(body, ins, outs, scratch=None, far_in=(), far_out=(), smem=(), parts=None, limit=52, cost=0):
    scratch, parts = scratch or {}, parts or {}
    far = (*far_in, *far_out)
    jobs = [(name, index) for name in far for index in parts.get(name, [None])]

    def spec(name):
        if name in smem:
            return pl.BlockSpec(memory_space=pltpu.SMEM)
        return pl.BlockSpec(memory_space=pltpu.HBM if name in far else pltpu.VMEM)

    kinds = {**{n: shape(v.shape, v.dtype) for n, v in ins.items()}, **outs}

    def run(*refs):
        plain = dict(zip([*ins, *outs], refs))
        rest = refs[len(plain) :]
        buffers = dict(zip(far, rest))
        more = dict(zip(scratch, rest[len(far) :]))
        copies = None
        if far:
            pairs = {n: (plain[n], buffers[n]) if n in far_in else (buffers[n], plain[n]) for n in far}
            copies = Copies(jobs, pairs, rest[-1])
            copies.start_all(far_in)
        body(Refs({**plain, **buffers, **more}), copies)

    buffers = [pltpu.VMEM(kinds[n].shape, kinds[n].dtype) for n in far]
    sems = [pltpu.SemaphoreType.DMA((len(jobs),))] if far else []
    result = pl.pallas_call(
        run,
        out_shape=list(outs.values()),
        in_specs=[spec(n) for n in ins],
        out_specs=[spec(n) for n in outs],
        scratch_shapes=[*buffers, *scratch.values(), *sems],
        compiler_params=pltpu.CompilerParams(vmem_limit_bytes=limit * 1024 * 1024),
        cost_estimate=pl.CostEstimate(flops=cost, bytes_accessed=0, transcendentals=0),
    )(*ins.values())
    return dict(zip(outs, result))


def shape(dims, dtype=f32):
    return jax.ShapeDtypeStruct(dims, dtype)


def wide(mask, width):
    return jnp.concatenate([mask] * (width // mask.shape[1]), axis=1)


def matmul(a, b):
    return lax.dot_general(a, b, (((1,), (0,)), ((), ())), preferred_element_type=f32)


def matmul_nt(a, b):
    return lax.dot_general(a, b, (((1,), (1,)), ((), ())), preferred_element_type=f32)


def matmul_tn(a, b):
    return lax.dot_general(a, b, (((0,), (0,)), ((), ())), preferred_element_type=f32)


def gelu_parts(v):
    return jnp.tanh(inner * (v + cubic * v * v * v))


def gelu_slope(v, t):
    return 0.5 * (1.0 + t) + 0.5 * v * (1.0 - t * t) * (inner * (1.0 + 3.0 * cubic * v * v))


def column_sum(v):
    return jnp.sum(v, axis=0, keepdims=True)


def moments(total, squares, pixel_count):
    center = total / pixel_count
    spread = squares / pixel_count - center * center
    return center, lax.rsqrt(spread + epsilon)


def chunks(total, size):
    return [(at, min(size, total - at)) for at in range(0, total, size)]


def strided(ref, k, first, count, step):
    return ref[k, pl.ds(first, count, stride=step), :]


def vertical_kernel(r, copies):
    groups, width = r.x.shape[0], r.cot.shape[3]
    rows, cols = r.own.shape[1], r.own.shape[2]

    def pack(out, input_row, row, pick):
        at = 0
        for g in range(groups):
            for n in range(over):
                value = r.x[g, input_row(n)]
                out[at : at + 2 * cols, :] = pick(value, r.x[g, n])
                at += 2 * cols
        for k in range(0, width, 256):
            for g in range(groups):
                for n in range(rim):
                    lanes = slice(k, k + 256)
                    out[at : at + cols, :] = pick(r.cot[g, row(n), :, lanes], r.cot[g, n, :, lanes])
                    at += cols
        for g in range(groups):
            for n in range(rim):
                out[at : at + cols, :] = pick(wide(r.own[g, row(n)], 256), wide(r.own[g, n], 256))
                at += cols

    last = r.x.shape[1] - over
    copies.wait(N.x, N.cot)
    if hasattr(r, N.up):
        pack(r.down, lambda n: last + n, lambda n: rows - rim + n, lambda tail, head: tail)
        pack(r.up, lambda n: last + n, lambda n: rows - rim + n, lambda tail, head: head)
    else:
        bottom = r.flags[0] == 1
        pack(r.down, lambda n: last + n, lambda n: rows - rim + n, lambda tail, head: jnp.where(bottom, head, tail))


def rim_rows(r, own, n_own, n_rim, base, cols, split):
    groups = own.shape[0]
    size = groups * n_rim * cols

    def flat(ref, g, n):
        at = [base + k * size + (g * n_rim + n) * cols for k in range(split)]
        return jnp.concatenate([ref[p : p + cols, :] for p in at], axis=1).astype(f32)

    def read(g, n):
        if n < n_rim:
            return jnp.where(r.flags[0] == 1, flat(r.top, g, n), 0.0)
        if n < n_rim + n_own:
            return own[g, n - n_rim].astype(f32)
        return jnp.where(r.flags[1] == 1, flat(r.bot, g, n - n_rim - n_own), 0.0)

    return read


def fields(r):
    groups, width = r.x.shape[0], r.cot.shape[3]
    rows, cols = r.own.shape[1], r.own.shape[2]
    base = over * groups * 2 * cols
    piece = rim * groups * cols
    blocks = width // 256
    x = rim_rows(r, r.x, 2 * rows, over, 0, 2 * cols, 1)
    mask = rim_rows(r, r.own, rows, rim, base + blocks * piece, cols, 1)
    cot = rim_rows(r, r.cot, rows, rim, base, cols, blocks)
    return x, lambda g, n: mask(g, n)[:, :128], cot


def strips_kernel(r, copies):
    groups, width = r.x.shape[0], r.cot.shape[3]
    rows, cols = r.own.shape[1], r.own.shape[2]
    x, mask, cot = fields(r)
    lines = (2 * rows + 2 * over) * groups, (rows + 2 * rim) * groups, (rows + 3) * groups
    for raw, read, first, count, w in (
        (r.raw_x, x, 0, lines[0], 2 * cols),
        (r.raw_m, mask, 0, lines[1], cols),
        (r.raw_c, cot, 2, lines[2], cols),
    ):
        for at in range(count):
            value = read(at % groups, at // groups + first)
            for k in range(raw.shape[0]):
                raw[k, at * w : (at + 1) * w, :] = value[:, k * 128 : (k + 1) * 128]
    for out, x0, m0, c0 in ((r.right, 2 * cols - over, cols - rim, cols - 2), (r.left, 0, 0, 0)):
        pieces = []
        for c in range(over):
            pieces.append([strided(r.raw_x, k, x0 + c, lines[0], 2 * cols) for k in range(2)])
        for c in range(0, rim + 1, 2):
            pieces.append([strided(r.raw_m, 0, m0 + min(c + k, rim - 1), lines[1], cols) for k in range(2)])
        for c in range(2):
            for h in range(0, width // 128, 2):
                pieces.append([strided(r.raw_c, h + k, c0 + c, lines[2], cols) for k in range(2)])
        at = 0
        for low, high in pieces:
            r.flat[at : at + low.shape[0], :] = jnp.concatenate([low, high], axis=1)
            at += low.shape[0]
        if at < r.flat.shape[0]:
            r.flat[at:, :] = jnp.zeros((r.flat.shape[0] - at, 256), f32)
        out[...] = r.flat[...].astype(bf16)


def stats_kernel(r, copies):
    groups, cin = r.x.shape[0], r.x.shape[3]
    rows, S = r.own.shape[1], r.own.shape[2]
    L = groups * S
    width = r.w1.shape[2]
    raw = r.raw
    for n in range(2 * rows + 1):
        for g in range(groups):
            line = n * groups + g
            src = (r.top[g, 0] if n == 0 else r.x[g, n - 1]).astype(f32)
            side = r.lft[g, n].astype(f32)
            for k in range(raw.shape[0]):
                raw[k, line, 7:8, :] = side[:, k * 128 : (k + 1) * 128]
                raw[k, line, 8:, :] = src[:, k * 128 : (k + 1) * 128]
    for out, n_rows, start in ((r.xe, rows, 1), (r.xo, rows + 1, 0)):
        for n in range(n_rows):
            for b in range(3):
                for k in range(raw.shape[0]):
                    parts = [
                        raw[k, (2 * n + start) * groups + g, pl.ds(7 + b, S, stride=2), :]
                        for g in range(groups)
                    ]
                    at = b * cin + k * 128
                    out[n * L : (n + 1) * L, at : at + 128] = jnp.concatenate(
                        parts, axis=0
                    ).astype(bf16)
    mask = jnp.concatenate(
        [r.own[g, i].astype(f32) for i in range(rows) for g in range(groups)], axis=0
    )
    M = rows * L
    copies.wait(N.w1)
    z = matmul(r.xo[0:M, :], r.w1[0])
    z += matmul(r.xe[...], r.w1[1])
    z += matmul(r.xo[L : L + M, :], r.w1[2])
    zp = matmul(r.xe[:, cin : 2 * cin], r.wp[...])
    zm, zpm = z * wide(mask, width), zp * wide(mask, width)
    row = jnp.concatenate(
        [column_sum(zm), column_sum(zm * z), column_sum(zpm), column_sum(zpm * zp), column_sum(mask)], axis=1
    )
    r.spread[...] = jnp.broadcast_to(row[None], r.spread.shape)
    copies.start(N.spread)
    copies.wait(N.spread)


def first_kernel(r, copies):
    groups, cin, width = r.x.shape[0], r.x.shape[3], r.cot.shape[3]
    rows, cols = r.own.shape[1], r.own.shape[2]
    S = cols + 8
    L = groups * S
    W = 2 * cols + 24
    V = cols + 16
    x, mask, cot = fields(r)
    lines = (2 * rows + 2 * over) * groups, (rows + 2 * rim) * groups, (rows + 3) * groups
    tail = jnp.zeros((W - 8 - 2 * cols, 128), f32)
    r.raw_m[...] = jnp.zeros(r.raw_m.shape, f32)
    r.raw_c[...] = jnp.zeros(r.raw_c.shape, f32)
    for at in range(lines[0]):
        value = x(at % groups, at // groups)
        for k in range(r.raw_x.shape[0]):
            r.raw_x[k, at * W + 8 : at * W + 8 + 2 * cols, :] = value[:, k * 128 : (k + 1) * 128]
            r.raw_x[k, at * W + 8 + 2 * cols : (at + 1) * W, :] = tail
    for strip, x0, m0, c0 in ((r.lft, 8 - over, 8 - rim, 6), (r.rgt, 8 + 2 * cols, 8 + cols, 8 + cols)):
        r.flat[...] = strip[...].astype(f32)
        at = 0
        for c in range(over):
            for k in range(2):
                r.raw_x[k, pl.ds(x0 + c, lines[0], stride=W), :] = r.flat[at : at + lines[0], k * 128 : (k + 1) * 128]
            at += lines[0]
        for c in range(0, rim + 1, 2):
            for k in range(2):
                if c + k < rim:
                    r.raw_m[0, pl.ds(m0 + c + k, lines[1], stride=V), :] = r.flat[
                        at : at + lines[1], k * 128 : (k + 1) * 128
                    ]
            at += lines[1]
        for c in range(2):
            for h in range(0, width // 128, 2):
                for k in range(2):
                    r.raw_c[h + k, pl.ds(c0 + c, lines[2], stride=V), :] = r.flat[
                        at : at + lines[2], k * 128 : (k + 1) * 128
                    ]
                at += lines[2]
    for out, n_rows, start in ((r.xe, rows + 5, 2), (r.xo, rows + 6, 1)):
        for n in range(n_rows):
            for b in range(3):
                for k in range(r.raw_x.shape[0]):
                    parts = [
                        strided(r.raw_x, k, ((2 * n + start) * groups + g) * W + 3 + b, S, 2) for g in range(groups)
                    ]
                    at = b * cin + k * 128
                    out[n * L : (n + 1) * L, at : at + 128] = jnp.concatenate(parts, axis=0).astype(bf16)
    copies.start(N.xe, N.xo)
    for at in range(lines[1]):
        r.raw_m[0, at * V + 8 : at * V + 8 + cols, :] = mask(at % groups, at // groups)
    for n in range(1, rows + 6):
        for g in range(groups):
            to, at = (n - 1) * L + g * S, (n * groups + g) * V
            r.maskp[to : to + S, :] = r.raw_m[0, at + 6 : at + 6 + S, :]
    for at in range(lines[2]):
        value = cot(at % groups, at // groups + 2)
        for k in range(r.raw_c.shape[0]):
            lanes = slice(k * 128, (k + 1) * 128)
            r.raw_c[k, at * V + 8 : at * V + 8 + cols, :] = value[:, lanes]
            r.cotq[at * S : (at + 1) * S, lanes] = r.raw_c[k, at * V + 7 : at * V + 7 + S, :]
    copies.start(N.cotq)
    r.ownp[...] = jnp.zeros(r.ownp.shape, f32)
    for i in range(rows):
        for g in range(groups):
            at = (i + 2) * L + g * S + 2
            r.ownp[at : at + cols, :] = r.own[g, i].astype(f32)
    copies.wait(N.w1, N.wp)
    for k, (m0, m) in enumerate(chunks(r.pre1.shape[0], r.pre1.shape[0] // 3)):
        z = matmul(r.xo[m0 : m0 + m, :], r.w1[0])
        z += matmul(r.xe[m0 : m0 + m, :], r.w1[1])
        z += matmul(r.xo[L + m0 : L + m0 + m, :], r.w1[2])
        r.pre1[m0 : m0 + m, :] = z
        copies.start((N.pre1, k))
        r.prep[m0 : m0 + m, :] = matmul(r.xe[m0 : m0 + m, cin : 2 * cin], r.wp[...])
        copies.start((N.prep, k))
    copies.wait(N.xe, N.xo, N.pre1, N.prep, N.cotq)


def second_kernel(r, copies):
    width = r.gain.shape[1]
    t = jnp.sum(r.tot1[...], axis=0)
    n = wide(t[:, 4 * width :], width)
    center, inv = moments(t[:, :width], t[:, width : 2 * width], n)
    proj = moments(t[:, 2 * width : 3 * width], t[:, 3 * width : 4 * width], n)
    r.mom1[...] = jnp.concatenate([center, inv, n, *proj, jnp.zeros((3, width), f32)], axis=0)
    scale = inv * r.gain[...]
    M, Q = r.pre1.shape[0], r.pre2.shape[0]
    L = (M - Q) // 2
    copies.wait(N.pre1)
    for m0, m in chunks(M, 104):
        v = (r.pre1[m0 : m0 + m, :] - center) * scale + r.shift[...]
        mask = wide(r.maskp[m0 : m0 + m, :], width)
        r.hid[m0 : m0 + m, :] = 0.5 * v * (1.0 + gelu_parts(v)) * mask
    r.hid[M:, :] = jnp.zeros((r.hid.shape[0] - M, width), f32)
    for m0, m in chunks(M, 208):
        for b in range(3):
            r.h3[m0 : m0 + m, b * width : (b + 1) * width] = r.hid[m0 + b : m0 + b + m, :].astype(bf16)
    copies.start(N.h3)
    copies.wait(N.w2)
    sums = [jnp.zeros((1, width), f32)] * 2
    for k, (m0, m) in enumerate(chunks(Q, Q // 3)):
        z = matmul(r.h3[m0 : m0 + m, :], r.w2[0])
        z += matmul(r.h3[L + m0 : L + m0 + m, :], r.w2[1])
        z += matmul(r.h3[2 * L + m0 : 2 * L + m0 + m, :], r.w2[2])
        r.pre2[m0 : m0 + m, :] = z
        copies.start((N.pre2, k))
        zm = z * wide(r.ownp[L + 1 + m0 : L + 1 + m0 + m, :], width)
        sums = [sums[0] + column_sum(zm), sums[1] + column_sum(zm * z)]
    row = jnp.concatenate(sums, axis=1)
    r.spread[...] = jnp.broadcast_to(row[None], r.spread.shape)
    copies.start(N.spread)
    copies.wait(N.h3, N.pre2, N.spread)


def part(r, at, *fields, first=0):
    bit = r.bits[0] == 1
    for k, field in enumerate(fields, first):
        half = field.shape[1] // 2
        low, high = field[:, :half], field[:, half:]
        r.mine[k, at : at + field.shape[0], :] = jnp.where(bit, high, low)
        r.theirs[k, at : at + field.shape[0], :] = jnp.where(bit, low, high)


def mine_of(r, row):
    half = row.shape[1] // 2
    return jnp.where(r.bits[0] == 1, row[:, half:], row[:, :half])


def third_kernel(r, copies):
    groups, rows, cols, width = r.out.shape
    S = cols + 8
    L = groups * S
    n = r.mom1[2:3, :]
    t = jnp.sum(r.tot2[...], axis=0)
    c2, i2 = moments(t[:, :width], t[:, width:], n)
    cp, ip = r.mom1[3:4, :], r.mom1[4:5, :]
    r.mom2[...] = jnp.concatenate([c2, i2, cp, ip, jnp.zeros((4, width), f32)], axis=0)
    sums = [jnp.zeros((1, width), f32)] * 3
    both_shift = r.shift2[...] + r.shiftp[...]
    total = r.grad.shape[0] // S
    for line in range(total):
        if line % (total // 2) == 0:
            k = line // (total // 2)
            copies.wait((N.pre2, k), (N.prep, k), (N.cotq, k))
        at = line * S
        shifted = slice(L + 1 + at, L + 1 + at + S)
        n2 = (r.pre2[at : at + S, :] - c2) * i2
        np_ = (r.prep[shifted, :] - cp) * ip
        v = n2 * r.gain2[...] + np_ * r.gainp[...] + both_shift
        mask = wide(r.maskp[shifted, :], width)
        own = wide(r.ownp[shifted, :], width)
        t = gelu_parts(v)
        r.field[at : at + S, :] = 0.5 * v * (1.0 + t) * mask
        g = gelu_slope(v, t) * mask * r.cotq[at : at + S, :]
        r.grad[at : at + S, :] = g
        g = g * own
        if L <= at < L + r.mine.shape[1]:
            part(r, at - L, g, n2 * own, np_ * own)
            if at - L + S == r.mine.shape[1] // 2:
                copies.start((N.mine, 0), (N.theirs, 0))
        new = [column_sum(g * n2), column_sum(g), column_sum(g * np_)]
        sums = [a + b for a, b in zip(sums, new)]
        if (line + 1) % (total // 2) == 0:
            copies.start((N.grad, (line + 1) // (total // 2) - 1))
    row = jnp.concatenate(sums, axis=1)
    r.spread[...] = jnp.broadcast_to(row[None], r.spread.shape)
    copies.start(N.spread, (N.mine, 1), (N.theirs, 1))
    for i in range(rows):
        for g in range(groups):
            at = (i + 1) * L + g * S + 1
            r.out[g, i, :, :] = r.field[at : at + cols, :].astype(bf16)
    copies.start(N.out)
    copies.wait(N.grad, N.out, N.spread, N.mine, N.theirs)


def fourth_kernel(r, copies):
    width = r.gain.shape[1]
    Q, U, rows_w = r.pre2.shape[0], r.act.shape[0], r.gpu.shape[0]
    L = U - rows_w
    center, inv, n = (r.mom1[k : k + 1, :] for k in range(3))
    c2, i2, cp, ip = (r.mom2[k : k + 1, :] for k in range(4))
    t3 = jnp.sum(r.tot3[...], axis=0)
    gg2, gs, ggp = (t3[:, k * width : (k + 1) * width] for k in range(3))
    r.gain_second[...], r.shift_second[...], r.gain_proj[...], r.shift_proj[...] = gg2, gs, ggp, gs
    tiny = N.gain_second, N.shift_second, N.gain_proj, N.shift_proj
    copies.start(*tiny)
    for m0, m in chunks(Q, L):
        if m0 in (0, 6 * L):
            copies.wait((N.grad, m0 // (6 * L)), (N.pre2, m0 // (6 * L)))
        mask = wide(r.maskp[L + 1 + m0 : L + 1 + m0 + m, :], width) / n
        n2 = (r.pre2[m0 : m0 + m, :] - c2) * i2
        back = mask * (gs + n2 * gg2)
        r.gq[m0 : m0 + m, :] = (r.gain2[...] * i2) * (r.grad[m0 : m0 + m, :] - back)
    r.gq[Q:, :] = jnp.zeros((r.gq.shape[0] - Q, width), f32)
    for m0, m in chunks(Q, 176):
        for b in range(3):
            r.g3[m0 : m0 + m, b * width : (b + 1) * width] = r.gq[m0 + b : m0 + b + m, :].astype(bf16)
    copies.wait(N.keep)
    for m0, m in chunks(U, L):
        frame = slice(2 * L + 2 + m0, 2 * L + 2 + m0 + m)
        n1 = (r.keep[frame, :] - center) * inv
        v = n1 * r.gain[...] + r.shift[...]
        mask = wide(r.maskp[frame, :], width)
        r.act[m0 : m0 + m, :] = gelu_slope(v, gelu_parts(v)) * mask
        r.normed[m0 : m0 + m, :] = n1 * mask
        if m0 < rows_w:
            part(r, m0, n1 * wide(r.ownp[frame, :], width), first=1)
    copies.start(N.normed, (N.mine, 1), (N.theirs, 1))
    for a in range(3):
        copies.wait((N.w2, a))
        gh = jnp.zeros((U, width), f32)
        for b in range(3):
            gh += matmul_nt(
                r.g3[L * a : L * a + U, b * width : (b + 1) * width],
                r.w2[2 - a, (2 - b) * width : (3 - b) * width, :],
            )
        r.gh[...] = gh if a == 0 else r.gh[...] + gh
    sums = [jnp.zeros((1, width), f32)] * 2
    for m0, m in chunks(U, L):
        g = r.act[m0 : m0 + m, :] * r.gh[m0 : m0 + m, :]
        r.act[m0 : m0 + m, :] = g
        g = g * wide(r.ownp[2 * L + 2 + m0 : 2 * L + 2 + m0 + m, :], width)
        if m0 < rows_w:
            part(r, m0, g)
        sums = [sums[0] + column_sum(g * r.normed[m0 : m0 + m, :]), sums[1] + column_sum(g)]
    row = jnp.concatenate(sums, axis=1)
    r.spread[...] = jnp.broadcast_to(row[None], r.spread.shape)
    copies.start(N.spread, (N.mine, 0), (N.theirs, 0), N.act)
    copies.wait(N.prep)
    for m0, m in chunks(rows_w, L):
        frame = slice(2 * L + 2 + m0, 2 * L + 2 + m0 + m)
        mask = wide(r.maskp[frame, :], width) / n
        back = mask * (gs + (r.prep[frame, :] - cp) * ip * ggp)
        r.gpu[m0 : m0 + m, :] = ((r.gainp[...] * ip) * (r.grad[L + 1 + m0 : L + 1 + m0 + m, :] - back)).astype(bf16)
    copies.start(N.gpu)
    copies.wait(N.normed, N.mine, N.theirs, N.spread, N.act, N.gpu, *tiny)


def split_store(r, rows, unit, first):
    quarter = unit // 4
    for k in range(rows // unit):
        for bit, base, sent, kept in ((1, 0, r.sent_a, r.kept_a), (2, 2 * quarter, r.sent_b, r.kept_b)):
            keep = pl.multiple_of(k * unit + base + r.bits[bit] * quarter, quarter)
            send = pl.multiple_of(k * unit + base + (1 - r.bits[bit]) * quarter, quarter)
            sent[first + k] = r.acc[pl.ds(send, quarter), :].astype(bf16)
            kept[first + k] = r.acc[pl.ds(keep, quarter), :]


def weights_second_kernel(r, copies):
    width = r.h3.shape[1] // 3
    cin = r.xe.shape[1] // 3
    rows_w = r.mine.shape[1]
    L = (r.h3.shape[0] - rows_w) // 5
    per = width // cin
    t3 = jnp.sum(r.tot3[...], axis=0)
    n = mine_of(r, r.mom1[2:3, :])
    gg2, gs, ggp = (mine_of(r, t3[:, k * width : (k + 1) * width]) / n for k in range(3))
    scale2, scalep = mine_of(r, r.gain2[...] * r.mom2[1:2, :]), mine_of(r, r.gainp[...] * r.mom2[3:4, :])
    half = scale2.shape[1]
    for source, name, own, out in ((r.mine, N.mine, r.ownp, r.near), (r.far3, N.far3, r.ownp_far, r.far)):
        copies.wait(name)
        r.pad[:, 0:8, :] = jnp.zeros((3, 8, half), f32)
        r.pad[:, 8:, :] = source[...]
        for m0, m in chunks(rows_w, 96):
            mask = wide(own[2 * L + 1 + m0 : 2 * L + 1 + m0 + m, :], half)
            rows = slice(8 + m0, 8 + m0 + m)
            back = mask * gs + r.pad[1, rows, :] * gg2
            out[m0 : m0 + m, :] = (scale2 * (r.pad[0, rows, :] - back)).astype(bf16)
            mask = wide(own[2 * L + m0 : 2 * L + m0 + m, :], half)
            rows = slice(7 + m0, 7 + m0 + m)
            back = mask * gs + r.pad[2, rows, :] * ggp
            out[rows_w + m0 : rows_w + m0 + m, :] = (scalep * (r.pad[0, rows, :] - back)).astype(bf16)
    for b in range(3):
        lanes = slice(b * width, (b + 1) * width)
        copies.wait((N.h3, b), (N.h3_far, b))
        for a in range(3):
            at = L * a + L
            r.acc[...] = matmul_tn(r.h3[at : at + rows_w, lanes], r.near[:rows_w, :]) + matmul_tn(
                r.h3_far[at : at + rows_w, lanes], r.far[:rows_w, :]
            )
            split_store(r, width, cin, (3 * b + a) * per)
        copies.start(*((name, b) for name in CHUNKS))
    at = 2 * L
    copies.wait(N.xe, N.xe_far)
    middle = slice(cin, 2 * cin)
    r.acc[0:cin, :] = matmul_tn(r.xe[at : at + rows_w, middle], r.near[rows_w:, :]) + matmul_tn(
        r.xe_far[at : at + rows_w, middle], r.far[rows_w:, :]
    )
    split_store(r, cin, cin, 9 * per)
    copies.start(*((name, 3) for name in CHUNKS))
    copies.wait(*CHUNKS)


def first_back(r, gg, gs, count):
    width = r.gain.shape[1]
    U = r.act.shape[0]
    L = U - r.rows_w
    inv, n = r.mom1[1:2, :], r.mom1[2:3, :]
    gg, gs = gg / n, gs / n
    scale = r.gain[...] * inv
    r.gf[0:8, :] = jnp.zeros((8, width), f32)
    r.gf[8 + count :, :] = jnp.zeros((r.gf.shape[0] - 8 - count, width), f32)
    for m0, m in chunks(count, L):
        mask = wide(r.maskp[2 * L + 2 + m0 : 2 * L + 2 + m0 + m, :], width)
        back = mask * gs + r.normed[m0 : m0 + m, :] * gg
        r.gf[8 + m0 : 8 + m0 + m, :] = scale * (r.act[m0 : m0 + m, :] - back)


def weights_first_kernel(r, copies):
    rows_w = r.mine.shape[1]
    cin = r.xe.shape[1] // 3
    L = (r.xe.shape[0] - rows_w) // 5
    width = r.gain.shape[1]
    t4 = jnp.sum(r.tot4[...], axis=0)
    r.gain_first[...], r.shift_first[...] = t4[:, :width], t4[:, width:]
    copies.start(N.gain_first, N.shift_first)
    n = mine_of(r, r.mom1[2:3, :])
    gg, gs = mine_of(r, t4[:, :width]) / n, mine_of(r, t4[:, width:]) / n
    scale = mine_of(r, r.gain[...] * r.mom1[1:2, :])
    half = scale.shape[1]
    for source, name, own, out in ((r.mine, N.mine, r.ownp, r.near), (r.far4, N.far4, r.ownp_far, r.far)):
        copies.wait(name)
        r.pad[:, 0:8, :] = jnp.zeros((2, 8, half), f32)
        r.pad[:, 8:, :] = source[...]
        for m0, m in chunks(rows_w, 96):
            mask = wide(own[2 * L + m0 : 2 * L + m0 + m, :], half)
            rows = slice(6 + m0, 6 + m0 + m)
            back = mask * gs + r.pad[1, rows, :] * gg
            out[m0 : m0 + m, :] = (scale * (r.pad[0, rows, :] - back)).astype(bf16)
    copies.wait(N.xe, N.xe_far)
    for k, a in enumerate((1, 0, 2)):
        if k == 1:
            copies.wait(N.xo, N.xo_far)
        source, source_far = (r.xe, r.xe_far) if a == 1 else (r.xo, r.xo_far)
        at = (3 if a == 2 else 2) * L
        for b in range(3):
            lanes = slice(b * cin, (b + 1) * cin)
            r.acc[lanes, :] = matmul_tn(source[at : at + rows_w, lanes], r.near[...]) + matmul_tn(
                source_far[at : at + rows_w, lanes], r.far[...]
            )
        split_store(r, 3 * cin, cin, a * 3)
        copies.start(*((name, a) for name in CHUNKS))
    copies.wait(N.gain_first, N.shift_first, *CHUNKS)


def inputs_kernel(r, copies):
    width = r.gpu.shape[1]
    groups, rows, cols = r.out.shape[0], r.out.shape[1] // 2, r.out.shape[2] // 2
    cin = r.out.shape[3]
    M = r.gpu.shape[0]
    S = cols + 8
    L = groups * S
    lines = r.lines
    U = r.act.shape[0]
    r.rows_w = M
    copies.wait(N.act, N.normed)
    first_back(r, r.gg[...], r.gs[...], U)
    for m0, m in chunks(U, 144):
        r.gu[m0 : m0 + m, :width] = r.gf[8 + m0 : 8 + m0 + m, :].astype(bf16)
        r.gu[m0 : m0 + m, width:] = r.gf[9 + m0 : 9 + m0 + m, :].astype(bf16)
    copies.wait(N.gpu, N.w1, N.wp)

    def tap(m0, m, a, b):
        di, dj = (1 if a == 0 else 0), (1 if b == 0 else 0)
        return matmul_nt(
            r.gu[di * L + m0 : di * L + m0 + m, dj * width : (dj + 1) * width],
            r.w1[a, b * cin : (b + 1) * cin, :],
        )

    for m0, m in chunks(M, 2 * L):
        pieces = {
            (0, 0): tap(m0, m, 1, 1) + matmul_nt(r.gpu[m0 : m0 + m, :], r.wp[...]),
            (0, 1): tap(m0, m, 1, 2) + tap(m0, m, 1, 0),
            (1, 0): tap(m0, m, 2, 1) + tap(m0, m, 0, 1),
            (1, 1): tap(m0, m, 2, 2) + tap(m0, m, 2, 0) + tap(m0, m, 0, 2) + tap(m0, m, 0, 0),
        }
        for (ro, co), v in pieces.items():
            for k in range(m // S):
                line = m0 // S + k
                i, g = line // groups, line % groups
                for h in range(lines.shape[0]):
                    lines[h, (2 * i + ro) * groups + g, pl.ds(co, cols, stride=2), :] = v[
                        k * S : k * S + cols, h * 128 : (h + 1) * 128
                    ]
    for n in range(2 * rows):
        for g in range(groups):
            for h in range(lines.shape[0]):
                r.out[g, n, :, h * 128 : (h + 1) * 128] = lines[h, n * groups + g].astype(bf16)
    copies.start(N.out)
    copies.wait(N.out)


def widen(half, side, taps, per, swapped, into=None):
    total, n, m = half.shape
    extra = total - taps * per
    order = [(t % 3 * 3 + t // 3) if swapped else t for t in range(taps)]
    jobs = [(t * per, per, 0, order[t] * per) for t in range(taps)] + [(taps * per, 1, 1, 0)] * extra
    more = list(into or [])

    def body(side_ref, half_ref, *refs):
        outs = refs[len(more) : len(more) + 1 + extra]
        narrow, full, sems = refs[len(more) + 1 + extra :]
        lanes = pl.ds(pl.multiple_of(side_ref[0] * m, m), m)
        reads = [
            pltpu.make_async_copy(half_ref.at[pl.ds(at, size)], narrow.at[pl.ds(at, size)], sems.at[0, k])
            for k, (at, size, _, _) in enumerate(jobs)
        ]
        writes = [
            pltpu.make_async_copy(full.at[pl.ds(at, size)], outs[which].at[pl.ds(to, size), :, lanes], sems.at[1, k])
            for k, (at, size, which, to) in enumerate(jobs)
        ]
        for read in reads:
            read.start()
        for k, (at, size, _, _) in enumerate(jobs):
            reads[k].wait()
            full[at : at + size] = narrow[at : at + size].astype(f32)
            writes[k].start()
        for write in writes:
            write.wait()

    hbm = pl.BlockSpec(memory_space=pltpu.HBM)
    return pl.pallas_call(
        body,
        out_shape=[shape((taps * per, n, 2 * m))] + [shape((1, n, 2 * m))] * extra,
        in_specs=[pl.BlockSpec(memory_space=pltpu.SMEM)] + [hbm] * (1 + len(more)),
        out_specs=[hbm] * (1 + extra),
        scratch_shapes=[
            pltpu.VMEM((total, n, m), bf16),
            pltpu.VMEM((total, n, m), f32),
            pltpu.SemaphoreType.DMA((2, len(jobs))),
        ],
        input_output_aliases={2 + k: k for k in range(len(more))},
        compiler_params=pltpu.CompilerParams(vmem_limit_bytes=20 * 1024 * 1024),
        cost_estimate=pl.CostEstimate(flops=0, bytes_accessed=0, transcendentals=0),
    )(side.reshape(1), half, *more)


def halve_kernel(r, copies):
    for p in range(r.count):
        kept, got = getattr(r, f"kept{p}"), getattr(r, f"got{p}")
        copies.wait(f"kept{p}", f"got{p}")
        to_send, to_keep = getattr(r, f"sent{p}"), getattr(r, f"left{p}")
        bit = r.bits[r.steps[p]] == 1
        h = kept.shape[1] // 2
        for t in range(kept.shape[0]):
            total = kept[t] + got[t].astype(f32)
            low, high = total[:h], total[h:]
            to_send[t] = jnp.where(bit, low, high).astype(bf16)
            to_keep[t] = jnp.where(bit, high, low)
        copies.start(f"sent{p}", f"left{p}")
    copies.wait(*(name for name in copies.jobs if name[:4] in (N.sent, N.left)))


def halve(bits, pairs, steps, cost):
    ins = dict(bits=bits)
    for p, (kept, got) in enumerate(pairs):
        ins[f"kept{p}"], ins[f"got{p}"] = kept, got
    taps, n, m = pairs[0][0].shape
    dims = (taps, n // 2, m)
    names = [str(p) for p in range(len(pairs))]
    outs = {}
    for name in names:
        outs[N.sent + name], outs[N.left + name] = shape(dims, bf16), shape(dims)

    def body(r, copies):
        r.count, r.steps = len(pairs), steps
        halve_kernel(r, copies)

    far_in = tuple(n for n in ins if n != N.bits)
    out = call(body, ins, outs, far_in=far_in, far_out=tuple(outs), smem=(N.bits,), cost=cost, limit=60)
    return [(out[N.sent + name], out[N.left + name]) for name in names]


def shifted(value, axis, steps):
    count = lax.axis_size(axis)
    first, last = (max(0, -steps), min(count, count - steps))
    return lax.ppermute(value, axis, [(source, source + steps) for source in range(first, last)])


def gather_sum(spread):
    return lax.all_to_all(spread, axes, 0, 0)


def bit_of(axis, step):
    return (lax.axis_index(axis) // step) % 2


def partner(value, axis, step):
    count = lax.axis_size(axis)
    return lax.ppermute(value, axis, [(i, i ^ step) for i in range(count)])


def steps_of(axis):
    count, step, out = lax.axis_size(axis), 1, []
    while step < count:
        out.append((axis, step))
        step *= 2
    return out


def split(total, axis, step):
    n = total.shape[1] // 2
    bit = bit_of(axis, step) == 1
    low, high = total[:, :n], total[:, n:]
    return jnp.where(bit, low, high).astype(bf16), jnp.where(bit, high, low)


def joined(value, other, axis, step, dim=1):
    bit = bit_of(axis, step) == 1
    return jnp.concatenate([jnp.where(bit, other, value), jnp.where(bit, value, other)], axis=dim)


class Tree:
    def __init__(self, parts, bits, plane, rest, core):
        self.bits, self.place = bits, {step: k for k, step in enumerate([core, *plane, *rest])}
        self.sent_a, self.kept_a, self.sent_b, self.kept_b = parts
        self.a, self.b, self.rest, self.core = plane, plane[::-1], rest, core
        p, n = len(plane), len(rest)
        self.stages = [(N.plane, k) for k in range(p)] + [(N.rest, k) for k in range(n)]
        self.stages += [(N.rest_join, k) for k in reversed(range(n))] + [(N.plane_join, k) for k in reversed(range(p))]
        self.stages += [(N.core, 0)]

    def next(self):
        return self.stages[0] if self.stages else None

    def start(self):
        kind, k = self.stages[0]
        if kind == N.plane:
            self.got = partner(self.sent_a, *self.a[k]), partner(self.sent_b, *self.b[k])
        elif kind == N.rest:
            self.got = (partner(self.sent, *self.rest[k]),)
        elif kind == N.rest_join:
            self.got = (partner(self.value, *self.rest[k]),)
        elif kind == N.plane_join:
            self.got = partner(self.value_a, *self.a[k]), partner(self.value_b, *self.b[k])
        else:
            self.got = (partner(self.value, *self.core),)

    def finish(self, cost=0):
        kind, k = self.stages.pop(0)
        if kind == N.plane:
            pairs = [(self.kept_a, self.got[0]), (self.kept_b, self.got[1])]
            nexts = [order[k + 1] for order in (self.a, self.b) if k + 1 < len(order)]
            if nexts and cost:
                pairs = halve(self.bits, pairs, [self.place[step] for step in nexts], cost)
                (self.sent_a, self.kept_a), (self.sent_b, self.kept_b) = pairs
                return
            total_a, total_b = (kept + got.astype(f32) for kept, got in pairs)
            if nexts:
                self.sent_a, self.kept_a = split(total_a, *nexts[0])
                self.sent_b, self.kept_b = split(total_b, *nexts[1])
            else:
                self.taps = total_a.shape[0]
                self.split_rest(jnp.concatenate([total_a, total_b], axis=0), 0)
        elif kind == N.rest:
            self.split_rest(self.kept + self.got[0].astype(f32), k + 1)
        elif kind == N.rest_join:
            self.value = joined(self.value, self.got[0], *self.rest[k])
            self.value_a, self.value_b = self.value[: self.taps], self.value[self.taps :]
        elif kind == N.plane_join:
            self.value_a = joined(self.value_a, self.got[0], *self.a[k])
            self.value_b = joined(self.value_b, self.got[1], *self.b[k])
            self.value = jnp.concatenate([self.value_a, self.value_b], axis=1)

    def split_rest(self, total, k):
        if k < len(self.rest):
            self.sent, self.kept = split(total, *self.rest[k])
        else:
            self.value = total.astype(bf16)


def lockstep(*trees, beside=()):
    for t in trees:
        t.start()
    got, beside = lax.optimization_barrier(([t.got for t in trees], beside))
    for t, g in zip(trees, got):
        t.got = g
        t.finish()
    return beside


def on_device(inputs, w_first, gain_first, shift_first, w_second, gain_second, shift_second, w_proj, gain_proj, shift_proj, valid_mask, cotangent):
    groups, rows_in, cols_in, cin = inputs.shape
    rows, cols = rows_in // 2, cols_in // 2
    width = w_first.shape[3]
    half = width // 2
    S = cols + 8
    L = groups * S
    devices = lax.axis_size(N.rows) * lax.axis_size(N.cols) * lax.axis_size(N.grp)
    plane = steps_of(N.cols)
    core = steps_of(N.rows)[0]
    rest = steps_of(N.rows)[1:] + steps_of(N.grp)
    bits = jnp.stack([bit_of(*step) for step in (core, *plane, *rest)]).astype(jnp.int32)
    w1 = w_first.reshape(3, 3 * cin, width)
    w2 = w_second.reshape(3, 3 * width, width)
    as_row = lambda v: v.reshape(1, -1)
    own = jnp.broadcast_to(valid_mask.astype(bf16)[..., None], valid_mask.shape + (128,))
    MP, MQ, MU, MW = (rows + 5) * L, (rows + 3) * L, (rows + 1) * L, rows * L
    px = lambda m, k: 2 * m * k * width
    vec = lambda k: shape((1, k * width))
    all_devices = lambda k: shape((devices, 1, k))
    g1, b1, g2, b2, gp, bp = map(
        as_row, (gain_first, shift_first, gain_second, shift_second, gain_proj, shift_proj)
    )

    top1 = shifted(inputs[:, -1:], N.rows, 1)
    me, count = lax.axis_index(N.rows), lax.axis_size(N.rows)
    flags = jnp.stack([me > 0, me < count - 1]).astype(jnp.int32)
    flat_rows = shape((over * groups * cols_in + (width // 256 + 1) * rim * groups * cols, 256), bf16)
    packed = call(
        vertical_kernel,
        dict(flags=flags, x=inputs, cot=cotangent, own=own),
        dict(down=flat_rows) if count == 2 else dict(down=flat_rows, up=flat_rows),
        far_in=(N.x, N.cot),
        smem=(N.flags,),
        parts=dict(x=end_parts(rows_in, over), cot=end_parts(rows, rim)),
    )
    if count == 2:
        top = bot = lax.ppermute(packed["down"], "rows", [(0, 1), (1, 0)])
    else:
        top, bot = shifted(packed[N.down], N.rows, 1), shifted(packed[N.up], N.rows, -1)
    lft1 = shifted(jnp.concatenate([top1[:, :, -1:], inputs[:, :, -1:]], axis=1), N.cols, 1)
    (top, bot), lft1 = lax.optimization_barrier(((top, bot), lft1))
    lines = (rows_in + 2 * over) * groups, (rows + 2 * rim) * groups, (rows + 3) * groups
    n_strip = over * lines[0] + (rim + 1) // 2 * lines[1] + width // 128 * lines[2]
    n_strip = -(-n_strip // 16) * 16
    near = dict(flags=flags, x=inputs, cot=cotangent, own=own, top=top, bot=bot)
    strips = call(
        strips_kernel,
        near,
        dict(right=shape((n_strip, 256), bf16), left=shape((n_strip, 256), bf16)),
        dict(
            raw_x=pltpu.VMEM((cin // 128, lines[0] * cols_in, 128), f32),
            raw_m=pltpu.VMEM((1, lines[1] * cols, 128), f32),
            raw_c=pltpu.VMEM((width // 128, lines[2] * cols, 128), f32),
            flat=pltpu.VMEM((n_strip, 256), f32),
        ),
        smem=(N.flags,),
    )
    lft, rgt = shifted(strips[N.right], N.cols, 1), shifted(strips[N.left], N.cols, -1)
    lft1, _ = lax.optimization_barrier((lft1, strips[N.right]))
    stats = call(
        stats_kernel,
        dict(x=inputs, top=top1, lft=lft1, own=own, w1=w1, wp=w_proj),
        dict(spread=all_devices(4 * width + 128)),
        dict(
            raw=pltpu.VMEM((cin // 128, (rows_in + 1) * groups, cols_in + 8, 128), f32),
            xe=pltpu.VMEM((rows * groups * cols, 3 * cin), bf16),
            xo=pltpu.VMEM(((rows + 1) * groups * cols, 3 * cin), bf16),
        ),
        far_in=(N.w1,),
        far_out=(N.spread,),
    )
    tot1 = gather_sum(stats[N.spread])

    first = call(
        first_kernel,
        dict(**near, lft=lft, rgt=rgt, w1=w1, wp=w_proj),
        dict(
            pre1=shape((MP, width)),
            prep=shape((MP, width)),
            xe=shape((MP, 3 * cin), bf16),
            xo=shape((MP + L, 3 * cin), bf16),
            ownp=shape((MP, 128)),
            maskp=shape((MP, 128)),
            cotq=shape((MQ, width)),
        ),
        dict(
            raw_x=pltpu.VMEM((cin // 128, lines[0] * (cols_in + 24), 128), f32),
            raw_m=pltpu.VMEM((1, lines[1] * (cols + 16), 128), f32),
            raw_c=pltpu.VMEM((width // 128, lines[2] * (cols + 16), 128), f32),
            flat=pltpu.VMEM((n_strip, 256), f32),
        ),
        far_in=(N.w1, N.wp),
        far_out=(N.xe, N.xo, N.pre1, N.prep, N.cotq),
        smem=(N.flags,),
        cost=20000000000,
        parts=dict(pre1=row_parts(MP, 3), prep=row_parts(MP, 3)),
    )
    xe, xo, ownp, maskp = first[N.xe], first[N.xo], first[N.ownp], first[N.maskp]
    far_xe, far_xo = partner(xe, *core), partner(xo, *core)

    second = call(
        second_kernel,
        dict(pre1=first[N.pre1], tot1=tot1, gain=g1, shift=b1, maskp=maskp, ownp=ownp, w2=w2),
        dict(h3=shape((MP, 3 * width), bf16), pre2=shape((MQ, width)), spread=all_devices(2 * width), mom1=shape((8, width))),
        dict(hid=pltpu.VMEM((MP + 8, width), f32)),
        far_in=(N.pre1, N.w2),
        far_out=(N.h3, N.pre2, N.spread),
        parts=dict(pre2=row_parts(MQ, 3)),
    )
    h3, pre2, mom1 = second[N.h3], second[N.pre2], second[N.mom1]
    tot2 = gather_sum(second[N.spread])
    tot2, far_h3 = lax.optimization_barrier((tot2, partner(h3, *core)))

    third = call(
        third_kernel,
        dict(
            bits=bits, pre2=pre2, prep=first[N.prep], mom1=mom1, tot2=tot2, gain2=g2, shift2=b2, gainp=gp, shiftp=bp,
            maskp=maskp, ownp=ownp, cotq=first[N.cotq],
        ),
        dict(
            out=shape((groups, rows, cols, width), bf16),
            grad=shape((MQ, width)),
            spread=all_devices(3 * width),
            mom2=shape((8, width)),
            mine=shape((3, MW, half)),
            theirs=shape((3, MW, half)),
        ),
        dict(field=pltpu.VMEM((MQ, width), f32)),
        far_in=(N.pre2, N.prep, N.cotq),
        far_out=(N.grad, N.spread, N.mine, N.theirs, N.out),
        smem=(N.bits,),
        parts=dict(
            mine=middle_parts(MW, 2), theirs=middle_parts(MW, 2),
            grad=row_parts(MQ, 2), pre2=row_parts(MQ, 2), cotq=row_parts(MQ, 2), prep=cuts(L, L + MQ // 2 + 8, L + MQ + 8)
        ),
    )
    mom2 = third[N.mom2]
    tot3 = gather_sum(third[N.spread])
    ownp_here, far3 = lax.optimization_barrier((ownp, partner(third[N.theirs], *core)))
    ownp_far = partner(ownp_here, *core)

    def chunk_shapes(taps):
        dims = (taps, cin // 4, half)
        return dict(sent_a=shape(dims, bf16), kept_a=shape(dims), sent_b=shape(dims, bf16), kept_b=shape(dims))

    per = width // cin
    taps2 = 9 * per + 1
    second_parts = call(
        weights_second_kernel,
        dict(
            bits=bits, mine=third[N.mine], far3=far3, h3=h3, h3_far=far_h3, xe=xe, xe_far=far_xe,
            tot3=tot3, mom1=mom1, mom2=mom2, gain2=g2, gainp=gp, ownp=ownp, ownp_far=ownp_far,
        ),
        chunk_shapes(taps2),
        dict(
            acc=pltpu.VMEM((width, half), f32),
            pad=pltpu.VMEM((3, MW + 8, half), f32),
            near=pltpu.VMEM((2 * MW, half), bf16),
            far=pltpu.VMEM((2 * MW, half), bf16),
        ),
        far_in=(N.mine, N.far3, N.h3, N.h3_far, N.xe, N.xe_far),
        far_out=CHUNKS,
        smem=(N.bits,),
        parts=dict(
            h3=lane_parts(3 * width, 3, pl.ds(L, MW + 2 * L)),
            h3_far=lane_parts(3 * width, 3, pl.ds(L, MW + 2 * L)),
            xe=[(0, (pl.ds(2 * L, MW), pl.ds(cin, cin)))],
            xe_far=[(0, (pl.ds(2 * L, MW), pl.ds(cin, cin)))],
            **{name: row_parts(taps2 - 1, 3) + [(3, (pl.ds(taps2 - 1, 1),))] for name in CHUNKS},
        ),
    ).values()
    grad, *second_parts = lax.optimization_barrier((third[N.grad], *second_parts))
    tree2 = Tree(second_parts, bits, plane, rest, core)
    tree2.start()
    hidden = call(
        fourth_kernel,
        dict(
            bits=bits, grad=grad, pre2=pre2, keep=first[N.pre1], w2=w2, prep=first[N.prep], mom1=mom1, mom2=mom2, tot3=tot3,
            gain=g1, shift=b1, gain2=g2, gainp=gp, maskp=maskp, ownp=ownp,
        ),
        dict(
            act=shape((MU, width)), normed=shape((MU, width)), spread=all_devices(2 * width),
            mine=shape((2, MW, half)), theirs=shape((2, MW, half)), gpu=shape((MW, width), bf16),
            gain_second=vec(1), shift_second=vec(1), gain_proj=vec(1), shift_proj=vec(1),
        ),
        dict(
            gq=pltpu.VMEM((MQ + 8, width), f32),
            g3=pltpu.VMEM((MQ, 3 * width), bf16),
            gh=pltpu.VMEM((MU, width), f32),
        ),
        far_in=(N.grad, N.pre2, N.keep, N.w2, N.prep),
        far_out=(
            N.act, N.normed, N.spread, N.mine, N.theirs, N.gpu, N.gain_second, N.shift_second, N.gain_proj, N.shift_proj
        ),
        smem=(N.bits,),
        limit=52,
        parts=dict(
            grad=cuts(0, 6 * L, MQ),
            pre2=cuts(0, 6 * L, MQ),
            keep=cuts(2 * L, 2 * L + MU + 8),
            w2=[(k, (pl.ds(2 - k, 1),)) for k in range(3)],
            prep=cuts(2 * L, 2 * L + MW + 8),
            mine=row_parts(2, 2),
            theirs=row_parts(2, 2),
        ),
    )
    tot4 = gather_sum(hidden[N.spread])
    tree2.finish(20000000000)
    near1, tree2.sent_a, tree2.sent_b = lax.optimization_barrier((hidden[N.mine], tree2.sent_a, tree2.sent_b))
    tree2.start()
    fifth = call(
        weights_first_kernel,
        dict(
            bits=bits, mine=near1, far4=partner(hidden[N.theirs], *core), xe=xe, xe_far=far_xe, xo=xo, xo_far=far_xo,
            tot4=tot4, mom1=mom1, gain=g1, ownp=ownp, ownp_far=ownp_far,
        ),
        dict(**chunk_shapes(9), gain_first=vec(1), shift_first=vec(1)),
        dict(
            acc=pltpu.VMEM((3 * cin, half), f32),
            pad=pltpu.VMEM((2, MW + 8, half), f32),
            near=pltpu.VMEM((MW, half), bf16),
            far=pltpu.VMEM((MW, half), bf16),
        ),
        far_in=(N.mine, N.far4, N.xe, N.xe_far, N.xo, N.xo_far),
        cost=20000000000,
        far_out=(*CHUNKS, N.gain_first, N.shift_first),
        smem=(N.bits,),
        parts=dict(
            xe=cuts(2 * L, 2 * L + MW),
            xe_far=cuts(2 * L, 2 * L + MW),
            xo=cuts(2 * L, 3 * L + MW),
            xo_far=cuts(2 * L, 3 * L + MW),
            **{name: row_parts(9, 3) for name in CHUNKS},
        ),
    )
    first_parts = [fifth[name] for name in CHUNKS]
    tree2.got, *first_parts = lax.optimization_barrier((tree2.got, *first_parts))
    tree2.finish()
    tree1 = Tree(first_parts, bits, plane, rest, core)

    grad_inputs = call(
        inputs_kernel,
        dict(
            act=hidden[N.act], normed=hidden[N.normed], gpu=hidden[N.gpu], w1=w1, wp=w_proj, mom1=mom1, gain=g1, maskp=maskp,
            gg=fifth[N.gain_first], gs=fifth[N.shift_first],
        ),
        dict(out=shape((groups, rows_in, cols_in, cin), bf16)),
        dict(
            lines=pltpu.VMEM((cin // 128, rows_in * groups, cols_in, 128), f32),
            gf=pltpu.VMEM((MU + 16, width), f32),
            gu=pltpu.VMEM((MU, 2 * width), bf16),
        ),
        far_in=(N.act, N.normed, N.gpu, N.w1, N.wp),
        far_out=(N.out,),
        cost=10000000000,
    )[N.out]
    side = bit_of(*core).astype(jnp.int32)
    grad_inputs = lockstep(tree2, tree1, beside=grad_inputs)
    while tree2.next() != (N.plane_join, 0):
        lockstep(tree2, tree1)
    tree2.start()
    while tree1.next() != (N.plane_join, 0):
        tree1.start()
        if tree1.next() != (N.plane_join, 1):
            tree1.finish()
        else:
            tree1.got, tree2.got = lax.optimization_barrier((tree1.got, tree2.got))
            tree1.finish()
    tree2.finish()
    tree2.start()
    tree1.start()
    grad_second = widen(tree2.got[0], 1 - side, 9, per, True, widen(tree2.value, side, 9, per, True))
    tree1.got, grad_second = lax.optimization_barrier((tree1.got, grad_second))
    grad_w2, grad_wp = grad_second
    tree1.finish()
    tree1.start()
    (grad_w1,) = widen(tree1.got[0], 1 - side, 3, 3, False, widen(tree1.value, side, 3, 3, False))

    return (
        third[N.out],
        grad_inputs,
        grad_w1.reshape(w_first.shape),
        fifth[N.gain_first].reshape(width),
        fifth[N.shift_first].reshape(width),
        grad_w2.reshape(w_second.shape),
        hidden[N.gain_second].reshape(width),
        hidden[N.shift_second].reshape(width),
        grad_wp.reshape(w_proj.shape),
        hidden[N.gain_proj].reshape(width),
        hidden[N.shift_proj].reshape(width),
    )


def solution(mesh):
    spread = P("grp", "rows", "cols", None)
    return jax.shard_map(
        on_device,
        mesh=mesh,
        in_specs=(spread,) + (P(),) * 9 + (P("grp", "rows", "cols"), spread),
        out_specs=(spread, spread) + (P(),) * 9,
        check_vma=False,
    )
```

```python
import functools

import jax
import jax.numpy as jnp
from jax import lax
from jax.experimental import pallas as pl
from jax.experimental.pallas import tpu as pltpu
from jax.sharding import PartitionSpec as P

epsilon = 1e-05
axes = ("rows", "cols", "grp")
bf16 = jnp.bfloat16
f32 = jnp.float32
inner = 0.7978845608028654
cubic = 0.044715
over = 6
CHUNKS = "sent_a", "kept_a", "sent_b", "kept_b"
rim = 3


class Names:
    def __getattr__(self, name):
        return name


N = Names()


class Refs:
    def __init__(self, named):
        self.__dict__.update(named)


class Copies:
    def __init__(self, parts, pairs, sems):
        self.jobs = {}
        for k, (name, index) in enumerate(parts):
            source, target = pairs[name]
            if index:
                source, target = source.at[index[1]], target.at[index[1]]
            self.jobs.setdefault(name, []).append(pltpu.make_async_copy(source, target, sems.at[k]))

    def start(self, *names):
        for name, *which in map(named, names):
            for job in self.jobs[name][slice(*which) if which else slice(None)]:
                job.start()

    def start_all(self, names):
        for k in range(max((len(self.jobs[n]) for n in names), default=0)):
            for n in names:
                if k < len(self.jobs[n]):
                    self.jobs[n][k].start()

    def wait(self, *names):
        for name, *which in map(named, names):
            for job in self.jobs[name][slice(*which) if which else slice(None)]:
                job.wait()


def named(name):
    return (name,) if isinstance(name, str) else (name[0], name[1], name[1] + 1)


def row_parts(total, count):
    size = total // count
    return [(k, (pl.ds(k * size, size),)) for k in range(count)]


def middle_parts(total, count):
    size = total // count
    return [(k, (slice(None), pl.ds(k * size, size))) for k in range(count)]


def end_parts(total, size):
    return [(k, (slice(None), pl.ds(at, size))) for k, at in enumerate((0, total - size))]


def cuts(*at):
    return [(k, (pl.ds(a, b - a),)) for k, (a, b) in enumerate(zip(at, at[1:]))]


def lane_parts(total, count, rows=slice(None)):
    size = total // count
    return [(k, (rows, pl.ds(k * size, size))) for k in range(count)]


def call(body, ins, outs, scratch=None, far_in=(), far_out=(), smem=(), parts=None, limit=52, cost=0):
    scratch, parts = scratch or {}, parts or {}
    far = (*far_in, *far_out)
    jobs = [(name, index) for name in far for index in parts.get(name, [None])]

    def spec(name):
        if name in smem:
            return pl.BlockSpec(memory_space=pltpu.SMEM)
        return pl.BlockSpec(memory_space=pltpu.HBM if name in far else pltpu.VMEM)

    kinds = {**{n: shape(v.shape, v.dtype) for n, v in ins.items()}, **outs}

    def run(*refs):
        plain = dict(zip([*ins, *outs], refs))
        rest = refs[len(plain) :]
        buffers = dict(zip(far, rest))
        more = dict(zip(scratch, rest[len(far) :]))
        copies = None
        if far:
            pairs = {n: (plain[n], buffers[n]) if n in far_in else (buffers[n], plain[n]) for n in far}
            copies = Copies(jobs, pairs, rest[-1])
            copies.start_all(far_in)
        body(Refs({**plain, **buffers, **more}), copies)

    buffers = [pltpu.VMEM(kinds[n].shape, kinds[n].dtype) for n in far]
    sems = [pltpu.SemaphoreType.DMA((len(jobs),))] if far else []
    result = pl.pallas_call(
        run,
        out_shape=list(outs.values()),
        in_specs=[spec(n) for n in ins],
        out_specs=[spec(n) for n in outs],
        scratch_shapes=[*buffers, *scratch.values(), *sems],
        compiler_params=pltpu.CompilerParams(vmem_limit_bytes=limit * 1024 * 1024),
        cost_estimate=pl.CostEstimate(flops=cost, bytes_accessed=0, transcendentals=0),
    )(*ins.values())
    return dict(zip(outs, result))


def shape(dims, dtype=f32):
    return jax.ShapeDtypeStruct(dims, dtype)


def wide(mask, width):
    return jnp.concatenate([mask] * (width // mask.shape[1]), axis=1)


def matmul(a, b):
    return lax.dot_general(a, b, (((1,), (0,)), ((), ())), preferred_element_type=f32)


def matmul_nt(a, b):
    return lax.dot_general(a, b, (((1,), (1,)), ((), ())), preferred_element_type=f32)


def matmul_tn(a, b):
    return lax.dot_general(a, b, (((0,), (0,)), ((), ())), preferred_element_type=f32)


def gelu_parts(v):
    return jnp.tanh(inner * (v + cubic * v * v * v))


def gelu_slope(v, t):
    return 0.5 * (1.0 + t) + 0.5 * v * (1.0 - t * t) * (inner * (1.0 + 3.0 * cubic * v * v))


def column_sum(v):
    return jnp.sum(v, axis=0, keepdims=True)


def moments(total, squares, pixel_count):
    center = total / pixel_count
    spread = squares / pixel_count - center * center
    return center, lax.rsqrt(spread + epsilon)


def chunks(total, size):
    return [(at, min(size, total - at)) for at in range(0, total, size)]


def strided(ref, k, first, count, step):
    return ref[k, pl.ds(first, count, stride=step), :]


def vertical_kernel(r, copies):
    groups, width = r.x.shape[0], r.cot.shape[3]
    rows, cols = r.own.shape[1], r.own.shape[2]

    def pack(out, input_row, row, pick):
        at = 0
        for g in range(groups):
            for n in range(over):
                value = r.x[g, input_row(n)]
                out[at : at + 2 * cols, :] = pick(value, r.x[g, n])
                at += 2 * cols
        for k in range(0, width, 256):
            for g in range(groups):
                for n in range(rim):
                    lanes = slice(k, k + 256)
                    out[at : at + cols, :] = pick(r.cot[g, row(n), :, lanes], r.cot[g, n, :, lanes])
                    at += cols
        for g in range(groups):
            for n in range(rim):
                out[at : at + cols, :] = pick(wide(r.own[g, row(n)], 256), wide(r.own[g, n], 256))
                at += cols

    last = r.x.shape[1] - over
    copies.wait(N.x, N.cot)
    if hasattr(r, N.up):
        pack(r.down, lambda n: last + n, lambda n: rows - rim + n, lambda tail, head: tail)
        pack(r.up, lambda n: last + n, lambda n: rows - rim + n, lambda tail, head: head)
    else:
        bottom = r.flags[0] == 1
        pack(r.down, lambda n: last + n, lambda n: rows - rim + n, lambda tail, head: jnp.where(bottom, head, tail))


def rim_rows(r, own, n_own, n_rim, base, cols, split):
    groups = own.shape[0]
    size = groups * n_rim * cols

    def flat(ref, g, n):
        at = [base + k * size + (g * n_rim + n) * cols for k in range(split)]
        return jnp.concatenate([ref[p : p + cols, :] for p in at], axis=1).astype(f32)

    def read(g, n):
        if n < n_rim:
            return jnp.where(r.flags[0] == 1, flat(r.top, g, n), 0.0)
        if n < n_rim + n_own:
            return own[g, n - n_rim].astype(f32)
        return jnp.where(r.flags[1] == 1, flat(r.bot, g, n - n_rim - n_own), 0.0)

    return read


def fields(r):
    groups, width = r.x.shape[0], r.cot.shape[3]
    rows, cols = r.own.shape[1], r.own.shape[2]
    base = over * groups * 2 * cols
    piece = rim * groups * cols
    blocks = width // 256
    x = rim_rows(r, r.x, 2 * rows, over, 0, 2 * cols, 1)
    mask = rim_rows(r, r.own, rows, rim, base + blocks * piece, cols, 1)
    cot = rim_rows(r, r.cot, rows, rim, base, cols, blocks)
    return x, lambda g, n: mask(g, n)[:, :128], cot


def strips_kernel(r, copies):
    groups, width = r.x.shape[0], r.cot.shape[3]
    rows, cols = r.own.shape[1], r.own.shape[2]
    x, mask, cot = fields(r)
    lines = (2 * rows + 2 * over) * groups, (rows + 2 * rim) * groups, (rows + 3) * groups
    for raw, read, first, count, w in (
        (r.raw_x, x, 0, lines[0], 2 * cols),
        (r.raw_m, mask, 0, lines[1], cols),
        (r.raw_c, cot, 2, lines[2], cols),
    ):
        for at in range(count):
            value = read(at % groups, at // groups + first)
            for k in range(raw.shape[0]):
                raw[k, at * w : (at + 1) * w, :] = value[:, k * 128 : (k + 1) * 128]
    for out, x0, m0, c0 in ((r.right, 2 * cols - over, cols - rim, cols - 2), (r.left, 0, 0, 0)):
        pieces = []
        for c in range(over):
            pieces.append([strided(r.raw_x, k, x0 + c, lines[0], 2 * cols) for k in range(2)])
        for c in range(0, rim + 1, 2):
            pieces.append([strided(r.raw_m, 0, m0 + min(c + k, rim - 1), lines[1], cols) for k in range(2)])
        for c in range(2):
            for h in range(0, width // 128, 2):
                pieces.append([strided(r.raw_c, h + k, c0 + c, lines[2], cols) for k in range(2)])
        at = 0
        for low, high in pieces:
            r.flat[at : at + low.shape[0], :] = jnp.concatenate([low, high], axis=1)
            at += low.shape[0]
        if at < r.flat.shape[0]:
            r.flat[at:, :] = jnp.zeros((r.flat.shape[0] - at, 256), f32)
        out[...] = r.flat[...].astype(bf16)


def stats_kernel(r, copies):
    groups, cin = r.x.shape[0], r.x.shape[3]
    rows, S = r.own.shape[1], r.own.shape[2]
    L = groups * S
    width = r.w1.shape[2]
    raw = r.raw
    for n in range(2 * rows + 1):
        for g in range(groups):
            line = n * groups + g
            src = (r.top[g, 0] if n == 0 else r.x[g, n - 1]).astype(f32)
            side = r.lft[g, n].astype(f32)
            for k in range(raw.shape[0]):
                raw[k, line, 7:8, :] = side[:, k * 128 : (k + 1) * 128]
                raw[k, line, 8:, :] = src[:, k * 128 : (k + 1) * 128]
    for out, n_rows, start in ((r.xe, rows, 1), (r.xo, rows + 1, 0)):
        for n in range(n_rows):
            for b in range(3):
                for k in range(raw.shape[0]):
                    parts = [
                        raw[k, (2 * n + start) * groups + g, pl.ds(7 + b, S, stride=2), :]
                        for g in range(groups)
                    ]
                    at = b * cin + k * 128
                    out[n * L : (n + 1) * L, at : at + 128] = jnp.concatenate(
                        parts, axis=0
                    ).astype(bf16)
    mask = jnp.concatenate(
        [r.own[g, i].astype(f32) for i in range(rows) for g in range(groups)], axis=0
    )
    M = rows * L
    copies.wait(N.w1)
    z = matmul(r.xo[0:M, :], r.w1[0])
    z += matmul(r.xe[...], r.w1[1])
    z += matmul(r.xo[L : L + M, :], r.w1[2])
    zp = matmul(r.xe[:, cin : 2 * cin], r.wp[...])
    zm, zpm = z * wide(mask, width), zp * wide(mask, width)
    row = jnp.concatenate(
        [column_sum(zm), column_sum(zm * z), column_sum(zpm), column_sum(zpm * zp), column_sum(mask)], axis=1
    )
    r.spread[...] = jnp.broadcast_to(row[None], r.spread.shape)
    copies.start(N.spread)
    copies.wait(N.spread)


def first_kernel(r, copies):
    groups, cin, width = r.x.shape[0], r.x.shape[3], r.cot.shape[3]
    rows, cols = r.own.shape[1], r.own.shape[2]
    S = cols + 8
    L = groups * S
    W = 2 * cols + 24
    V = cols + 16
    x, mask, cot = fields(r)
    lines = (2 * rows + 2 * over) * groups, (rows + 2 * rim) * groups, (rows + 3) * groups
    tail = jnp.zeros((W - 8 - 2 * cols, 128), f32)
    r.raw_m[...] = jnp.zeros(r.raw_m.shape, f32)
    r.raw_c[...] = jnp.zeros(r.raw_c.shape, f32)
    for at in range(lines[0]):
        value = x(at % groups, at // groups)
        for k in range(r.raw_x.shape[0]):
            r.raw_x[k, at * W + 8 : at * W + 8 + 2 * cols, :] = value[:, k * 128 : (k + 1) * 128]
            r.raw_x[k, at * W + 8 + 2 * cols : (at + 1) * W, :] = tail
    for strip, x0, m0, c0 in ((r.lft, 8 - over, 8 - rim, 6), (r.rgt, 8 + 2 * cols, 8 + cols, 8 + cols)):
        r.flat[...] = strip[...].astype(f32)
        at = 0
        for c in range(over):
            for k in range(2):
                r.raw_x[k, pl.ds(x0 + c, lines[0], stride=W), :] = r.flat[at : at + lines[0], k * 128 : (k + 1) * 128]
            at += lines[0]
        for c in range(0, rim + 1, 2):
            for k in range(2):
                if c + k < rim:
                    r.raw_m[0, pl.ds(m0 + c + k, lines[1], stride=V), :] = r.flat[
                        at : at + lines[1], k * 128 : (k + 1) * 128
                    ]
            at += lines[1]
        for c in range(2):
            for h in range(0, width // 128, 2):
                for k in range(2):
                    r.raw_c[h + k, pl.ds(c0 + c, lines[2], stride=V), :] = r.flat[
                        at : at + lines[2], k * 128 : (k + 1) * 128
                    ]
                at += lines[2]
    for out, n_rows, start in ((r.xe, rows + 5, 2), (r.xo, rows + 6, 1)):
        for n in range(n_rows):
            for b in range(3):
                for k in range(r.raw_x.shape[0]):
                    parts = [
                        strided(r.raw_x, k, ((2 * n + start) * groups + g) * W + 3 + b, S, 2) for g in range(groups)
                    ]
                    at = b * cin + k * 128
                    out[n * L : (n + 1) * L, at : at + 128] = jnp.concatenate(parts, axis=0).astype(bf16)
    copies.start(N.xe, N.xo)
    for at in range(lines[1]):
        r.raw_m[0, at * V + 8 : at * V + 8 + cols, :] = mask(at % groups, at // groups)
    for n in range(1, rows + 6):
        for g in range(groups):
            to, at = (n - 1) * L + g * S, (n * groups + g) * V
            r.maskp[to : to + S, :] = r.raw_m[0, at + 6 : at + 6 + S, :]
    for at in range(lines[2]):
        value = cot(at % groups, at // groups + 2)
        for k in range(r.raw_c.shape[0]):
            lanes = slice(k * 128, (k + 1) * 128)
            r.raw_c[k, at * V + 8 : at * V + 8 + cols, :] = value[:, lanes]
            r.cotq[at * S : (at + 1) * S, lanes] = r.raw_c[k, at * V + 7 : at * V + 7 + S, :]
    copies.start(N.cotq)
    r.ownp[...] = jnp.zeros(r.ownp.shape, f32)
    for i in range(rows):
        for g in range(groups):
            at = (i + 2) * L + g * S + 2
            r.ownp[at : at + cols, :] = r.own[g, i].astype(f32)
    copies.wait(N.w1, N.wp)
    for k, (m0, m) in enumerate(chunks(r.pre1.shape[0], r.pre1.shape[0] // 3)):
        z = matmul(r.xo[m0 : m0 + m, :], r.w1[0])
        z += matmul(r.xe[m0 : m0 + m, :], r.w1[1])
        z += matmul(r.xo[L + m0 : L + m0 + m, :], r.w1[2])
        r.pre1[m0 : m0 + m, :] = z
        copies.start((N.pre1, k))
        r.prep[m0 : m0 + m, :] = matmul(r.xe[m0 : m0 + m, cin : 2 * cin], r.wp[...])
        copies.start((N.prep, k))
    copies.wait(N.xe, N.xo, N.pre1, N.prep, N.cotq)


def second_kernel(r, copies):
    width = r.gain.shape[1]
    t = jnp.sum(r.tot1[...], axis=0)
    n = wide(t[:, 4 * width :], width)
    center, inv = moments(t[:, :width], t[:, width : 2 * width], n)
    proj = moments(t[:, 2 * width : 3 * width], t[:, 3 * width : 4 * width], n)
    r.mom1[...] = jnp.concatenate([center, inv, n, *proj, jnp.zeros((3, width), f32)], axis=0)
    scale = inv * r.gain[...]
    M, Q = r.pre1.shape[0], r.pre2.shape[0]
    L = (M - Q) // 2
    copies.wait(N.pre1)
    for m0, m in chunks(M, 104):
        v = (r.pre1[m0 : m0 + m, :] - center) * scale + r.shift[...]
        mask = wide(r.maskp[m0 : m0 + m, :], width)
        r.hid[m0 : m0 + m, :] = 0.5 * v * (1.0 + gelu_parts(v)) * mask
    r.hid[M:, :] = jnp.zeros((r.hid.shape[0] - M, width), f32)
    for m0, m in chunks(M, 208):
        for b in range(3):
            r.h3[m0 : m0 + m, b * width : (b + 1) * width] = r.hid[m0 + b : m0 + b + m, :].astype(bf16)
    copies.start(N.h3)
    copies.wait(N.w2)
    sums = [jnp.zeros((1, width), f32)] * 2
    for k, (m0, m) in enumerate(chunks(Q, Q // 3)):
        z = matmul(r.h3[m0 : m0 + m, :], r.w2[0])
        z += matmul(r.h3[L + m0 : L + m0 + m, :], r.w2[1])
        z += matmul(r.h3[2 * L + m0 : 2 * L + m0 + m, :], r.w2[2])
        r.pre2[m0 : m0 + m, :] = z
        copies.start((N.pre2, k))
        zm = z * wide(r.ownp[L + 1 + m0 : L + 1 + m0 + m, :], width)
        sums = [sums[0] + column_sum(zm), sums[1] + column_sum(zm * z)]
    row = jnp.concatenate(sums, axis=1)
    r.spread[...] = jnp.broadcast_to(row[None], r.spread.shape)
    copies.start(N.spread)
    copies.wait(N.h3, N.pre2, N.spread)


def part(r, at, *fields, first=0):
    bit = r.bits[0] == 1
    for k, field in enumerate(fields, first):
        half = field.shape[1] // 2
        low, high = field[:, :half], field[:, half:]
        r.mine[k, at : at + field.shape[0], :] = jnp.where(bit, high, low)
        r.theirs[k, at : at + field.shape[0], :] = jnp.where(bit, low, high)


def mine_of(r, row):
    half = row.shape[1] // 2
    return jnp.where(r.bits[0] == 1, row[:, half:], row[:, :half])


def third_kernel(r, copies):
    groups, rows, cols, width = r.out.shape
    S = cols + 8
    L = groups * S
    n = r.mom1[2:3, :]
    t = jnp.sum(r.tot2[...], axis=0)
    c2, i2 = moments(t[:, :width], t[:, width:], n)
    cp, ip = r.mom1[3:4, :], r.mom1[4:5, :]
    r.mom2[...] = jnp.concatenate([c2, i2, cp, ip, jnp.zeros((4, width), f32)], axis=0)
    sums = [jnp.zeros((1, width), f32)] * 3
    both_shift = r.shift2[...] + r.shiftp[...]
    total = r.grad.shape[0] // S
    for line in range(total):
        if line % (total // 2) == 0:
            k = line // (total // 2)
            copies.wait((N.pre2, k), (N.prep, k), (N.cotq, k))
        at = line * S
        shifted = slice(L + 1 + at, L + 1 + at + S)
        n2 = (r.pre2[at : at + S, :] - c2) * i2
        np_ = (r.prep[shifted, :] - cp) * ip
        v = n2 * r.gain2[...] + np_ * r.gainp[...] + both_shift
        mask = wide(r.maskp[shifted, :], width)
        own = wide(r.ownp[shifted, :], width)
        t = gelu_parts(v)
        r.field[at : at + S, :] = 0.5 * v * (1.0 + t) * mask
        g = gelu_slope(v, t) * mask * r.cotq[at : at + S, :]
        r.grad[at : at + S, :] = g
        g = g * own
        if L <= at < L + r.mine.shape[1]:
            part(r, at - L, g, n2 * own, np_ * own)
            if at - L + S == r.mine.shape[1] // 2:
                copies.start((N.mine, 0), (N.theirs, 0))
        new = [column_sum(g * n2), column_sum(g), column_sum(g * np_)]
        sums = [a + b for a, b in zip(sums, new)]
        if (line + 1) % (total // 2) == 0:
            copies.start((N.grad, (line + 1) // (total // 2) - 1))
    row = jnp.concatenate(sums, axis=1)
    r.spread[...] = jnp.broadcast_to(row[None], r.spread.shape)
    copies.start(N.spread, (N.mine, 1), (N.theirs, 1))
    for i in range(rows):
        for g in range(groups):
            at = (i + 1) * L + g * S + 1
            r.out[g, i, :, :] = r.field[at : at + cols, :].astype(bf16)
    copies.start(N.out)
    copies.wait(N.grad, N.out, N.spread, N.mine, N.theirs)


def fourth_kernel(r, copies):
    width = r.gain.shape[1]
    Q, U, rows_w = r.pre2.shape[0], r.act.shape[0], r.gpu.shape[0]
    L = U - rows_w
    center, inv, n = (r.mom1[k : k + 1, :] for k in range(3))
    c2, i2, cp, ip = (r.mom2[k : k + 1, :] for k in range(4))
    t3 = jnp.sum(r.tot3[...], axis=0)
    gg2, gs, ggp = (t3[:, k * width : (k + 1) * width] for k in range(3))
    r.gain_second[...], r.shift_second[...], r.gain_proj[...], r.shift_proj[...] = gg2, gs, ggp, gs
    tiny = N.gain_second, N.shift_second, N.gain_proj, N.shift_proj
    copies.start(*tiny)
    for m0, m in chunks(Q, L):
        if m0 in (0, 6 * L):
            copies.wait((N.grad, m0 // (6 * L)), (N.pre2, m0 // (6 * L)))
        mask = wide(r.maskp[L + 1 + m0 : L + 1 + m0 + m, :], width) / n
        n2 = (r.pre2[m0 : m0 + m, :] - c2) * i2
        back = mask * (gs + n2 * gg2)
        r.gq[m0 : m0 + m, :] = (r.gain2[...] * i2) * (r.grad[m0 : m0 + m, :] - back)
    r.gq[Q:, :] = jnp.zeros((r.gq.shape[0] - Q, width), f32)
    for m0, m in chunks(Q, 176):
        for b in range(3):
            r.g3[m0 : m0 + m, b * width : (b + 1) * width] = r.gq[m0 + b : m0 + b + m, :].astype(bf16)
    copies.wait(N.keep)
    for m0, m in chunks(U, L):
        frame = slice(2 * L + 2 + m0, 2 * L + 2 + m0 + m)
        n1 = (r.keep[frame, :] - center) * inv
        v = n1 * r.gain[...] + r.shift[...]
        mask = wide(r.maskp[frame, :], width)
        r.act[m0 : m0 + m, :] = gelu_slope(v, gelu_parts(v)) * mask
        r.normed[m0 : m0 + m, :] = n1 * mask
        if m0 < rows_w:
            part(r, m0, n1 * wide(r.ownp[frame, :], width), first=1)
    copies.start(N.normed, (N.mine, 1), (N.theirs, 1))
    for a in range(3):
        copies.wait((N.w2, a))
        gh = jnp.zeros((U, width), f32)
        for b in range(3):
            gh += matmul_nt(
                r.g3[L * a : L * a + U, b * width : (b + 1) * width],
                r.w2[2 - a, (2 - b) * width : (3 - b) * width, :],
            )
        r.gh[...] = gh if a == 0 else r.gh[...] + gh
    sums = [jnp.zeros((1, width), f32)] * 2
    for m0, m in chunks(U, L):
        g = r.act[m0 : m0 + m, :] * r.gh[m0 : m0 + m, :]
        r.act[m0 : m0 + m, :] = g
        g = g * wide(r.ownp[2 * L + 2 + m0 : 2 * L + 2 + m0 + m, :], width)
        if m0 < rows_w:
            part(r, m0, g)
        sums = [sums[0] + column_sum(g * r.normed[m0 : m0 + m, :]), sums[1] + column_sum(g)]
    row = jnp.concatenate(sums, axis=1)
    r.spread[...] = jnp.broadcast_to(row[None], r.spread.shape)
    copies.start(N.spread, (N.mine, 0), (N.theirs, 0), N.act)
    copies.wait(N.prep)
    for m0, m in chunks(rows_w, L):
        frame = slice(2 * L + 2 + m0, 2 * L + 2 + m0 + m)
        mask = wide(r.maskp[frame, :], width) / n
        back = mask * (gs + (r.prep[frame, :] - cp) * ip * ggp)
        r.gpu[m0 : m0 + m, :] = ((r.gainp[...] * ip) * (r.grad[L + 1 + m0 : L + 1 + m0 + m, :] - back)).astype(bf16)
    copies.start(N.gpu)
    copies.wait(N.normed, N.mine, N.theirs, N.spread, N.act, N.gpu, *tiny)


def split_store(r, rows, unit, first):
    quarter = unit // 4
    for k in range(rows // unit):
        for bit, base, sent, kept in ((1, 0, r.sent_a, r.kept_a), (2, 2 * quarter, r.sent_b, r.kept_b)):
            keep = pl.multiple_of(k * unit + base + r.bits[bit] * quarter, quarter)
            send = pl.multiple_of(k * unit + base + (1 - r.bits[bit]) * quarter, quarter)
            sent[first + k] = r.acc[pl.ds(send, quarter), :].astype(bf16)
            kept[first + k] = r.acc[pl.ds(keep, quarter), :]


def weights_second_kernel(r, copies):
    width = r.h3.shape[1] // 3
    cin = r.xe.shape[1] // 3
    rows_w = r.mine.shape[1]
    L = (r.h3.shape[0] - rows_w) // 5
    per = width // cin
    t3 = jnp.sum(r.tot3[...], axis=0)
    n = mine_of(r, r.mom1[2:3, :])
    gg2, gs, ggp = (mine_of(r, t3[:, k * width : (k + 1) * width]) / n for k in range(3))
    scale2, scalep = mine_of(r, r.gain2[...] * r.mom2[1:2, :]), mine_of(r, r.gainp[...] * r.mom2[3:4, :])
    half = scale2.shape[1]
    for source, name, own, out in ((r.mine, N.mine, r.ownp, r.near), (r.far3, N.far3, r.ownp_far, r.far)):
        copies.wait(name)
        r.pad[:, 0:8, :] = jnp.zeros((3, 8, half), f32)
        r.pad[:, 8:, :] = source[...]
        for m0, m in chunks(rows_w, 96):
            mask = wide(own[2 * L + 1 + m0 : 2 * L + 1 + m0 + m, :], half)
            rows = slice(8 + m0, 8 + m0 + m)
            back = mask * gs + r.pad[1, rows, :] * gg2
            out[m0 : m0 + m, :] = (scale2 * (r.pad[0, rows, :] - back)).astype(bf16)
            mask = wide(own[2 * L + m0 : 2 * L + m0 + m, :], half)
            rows = slice(7 + m0, 7 + m0 + m)
            back = mask * gs + r.pad[2, rows, :] * ggp
            out[rows_w + m0 : rows_w + m0 + m, :] = (scalep * (r.pad[0, rows, :] - back)).astype(bf16)
    for b in range(3):
        lanes = slice(b * width, (b + 1) * width)
        copies.wait((N.h3, b), (N.h3_far, b))
        for a in range(3):
            at = L * a + L
            r.acc[...] = matmul_tn(r.h3[at : at + rows_w, lanes], r.near[:rows_w, :]) + matmul_tn(
                r.h3_far[at : at + rows_w, lanes], r.far[:rows_w, :]
            )
            split_store(r, width, cin, (3 * b + a) * per)
        copies.start(*((name, b) for name in CHUNKS))
    at = 2 * L
    copies.wait(N.xe, N.xe_far)
    middle = slice(cin, 2 * cin)
    r.acc[0:cin, :] = matmul_tn(r.xe[at : at + rows_w, middle], r.near[rows_w:, :]) + matmul_tn(
        r.xe_far[at : at + rows_w, middle], r.far[rows_w:, :]
    )
    split_store(r, cin, cin, 9 * per)
    copies.start(*((name, 3) for name in CHUNKS))
    copies.wait(*CHUNKS)


def first_back(r, gg, gs, count):
    width = r.gain.shape[1]
    U = r.act.shape[0]
    L = U - r.rows_w
    inv, n = r.mom1[1:2, :], r.mom1[2:3, :]
    gg, gs = gg / n, gs / n
    scale = r.gain[...] * inv
    r.gf[0:8, :] = jnp.zeros((8, width), f32)
    r.gf[8 + count :, :] = jnp.zeros((r.gf.shape[0] - 8 - count, width), f32)
    for m0, m in chunks(count, L):
        mask = wide(r.maskp[2 * L + 2 + m0 : 2 * L + 2 + m0 + m, :], width)
        back = mask * gs + r.normed[m0 : m0 + m, :] * gg
        r.gf[8 + m0 : 8 + m0 + m, :] = scale * (r.act[m0 : m0 + m, :] - back)


def weights_first_kernel(r, copies):
    rows_w = r.mine.shape[1]
    cin = r.xe.shape[1] // 3
    L = (r.xe.shape[0] - rows_w) // 5
    width = r.gain.shape[1]
    t4 = jnp.sum(r.tot4[...], axis=0)
    r.gain_first[...], r.shift_first[...] = t4[:, :width], t4[:, width:]
    copies.start(N.gain_first, N.shift_first)
    n = mine_of(r, r.mom1[2:3, :])
    gg, gs = mine_of(r, t4[:, :width]) / n, mine_of(r, t4[:, width:]) / n
    scale = mine_of(r, r.gain[...] * r.mom1[1:2, :])
    half = scale.shape[1]
    for source, name, own, out in ((r.mine, N.mine, r.ownp, r.near), (r.far4, N.far4, r.ownp_far, r.far)):
        copies.wait(name)
        r.pad[:, 0:8, :] = jnp.zeros((2, 8, half), f32)
        r.pad[:, 8:, :] = source[...]
        for m0, m in chunks(rows_w, 96):
            mask = wide(own[2 * L + m0 : 2 * L + m0 + m, :], half)
            rows = slice(6 + m0, 6 + m0 + m)
            back = mask * gs + r.pad[1, rows, :] * gg
            out[m0 : m0 + m, :] = (scale * (r.pad[0, rows, :] - back)).astype(bf16)
    copies.wait(N.xe, N.xe_far)
    for k, a in enumerate((1, 0, 2)):
        if k == 1:
            copies.wait(N.xo, N.xo_far)
        source, source_far = (r.xe, r.xe_far) if a == 1 else (r.xo, r.xo_far)
        at = (3 if a == 2 else 2) * L
        for b in range(3):
            lanes = slice(b * cin, (b + 1) * cin)
            r.acc[lanes, :] = matmul_tn(source[at : at + rows_w, lanes], r.near[...]) + matmul_tn(
                source_far[at : at + rows_w, lanes], r.far[...]
            )
        split_store(r, 3 * cin, cin, a * 3)
        copies.start(*((name, a) for name in CHUNKS))
    copies.wait(N.gain_first, N.shift_first, *CHUNKS)


def inputs_kernel(r, copies):
    width = r.gpu.shape[1]
    groups, rows, cols = r.out.shape[0], r.out.shape[1] // 2, r.out.shape[2] // 2
    cin = r.out.shape[3]
    M = r.gpu.shape[0]
    S = cols + 8
    L = groups * S
    lines = r.lines
    U = r.act.shape[0]
    r.rows_w = M
    copies.wait(N.act, N.normed)
    first_back(r, r.gg[...], r.gs[...], U)
    for m0, m in chunks(U, 144):
        r.gu[m0 : m0 + m, :width] = r.gf[8 + m0 : 8 + m0 + m, :].astype(bf16)
        r.gu[m0 : m0 + m, width:] = r.gf[9 + m0 : 9 + m0 + m, :].astype(bf16)
    copies.wait(N.gpu, N.w1, N.wp)

    def tap(m0, m, a, b):
        di, dj = (1 if a == 0 else 0), (1 if b == 0 else 0)
        return matmul_nt(
            r.gu[di * L + m0 : di * L + m0 + m, dj * width : (dj + 1) * width],
            r.w1[a, b * cin : (b + 1) * cin, :],
        )

    for m0, m in chunks(M, 2 * L):
        pieces = {
            (0, 0): tap(m0, m, 1, 1) + matmul_nt(r.gpu[m0 : m0 + m, :], r.wp[...]),
            (0, 1): tap(m0, m, 1, 2) + tap(m0, m, 1, 0),
            (1, 0): tap(m0, m, 2, 1) + tap(m0, m, 0, 1),
            (1, 1): tap(m0, m, 2, 2) + tap(m0, m, 2, 0) + tap(m0, m, 0, 2) + tap(m0, m, 0, 0),
        }
        for (ro, co), v in pieces.items():
            for k in range(m // S):
                line = m0 // S + k
                i, g = line // groups, line % groups
                for h in range(lines.shape[0]):
                    lines[h, (2 * i + ro) * groups + g, pl.ds(co, cols, stride=2), :] = v[
                        k * S : k * S + cols, h * 128 : (h + 1) * 128
                    ]
    for n in range(2 * rows):
        for g in range(groups):
            for h in range(lines.shape[0]):
                r.out[g, n, :, h * 128 : (h + 1) * 128] = lines[h, n * groups + g].astype(bf16)
    copies.start(N.out)
    copies.wait(N.out)


def widen(half, side, taps, per, swapped, into=None):
    total, n, m = half.shape
    extra = total - taps * per
    order = [(t % 3 * 3 + t // 3) if swapped else t for t in range(taps)]
    jobs = [(t * per, per, 0, order[t] * per) for t in range(taps)] + [(taps * per, 1, 1, 0)] * extra
    more = list(into or [])

    def body(side_ref, half_ref, *refs):
        outs = refs[len(more) : len(more) + 1 + extra]
        narrow, full, sems = refs[len(more) + 1 + extra :]
        lanes = pl.ds(pl.multiple_of(side_ref[0] * m, m), m)
        reads = [
            pltpu.make_async_copy(half_ref.at[pl.ds(at, size)], narrow.at[pl.ds(at, size)], sems.at[0, k])
            for k, (at, size, _, _) in enumerate(jobs)
        ]
        writes = [
            pltpu.make_async_copy(full.at[pl.ds(at, size)], outs[which].at[pl.ds(to, size), :, lanes], sems.at[1, k])
            for k, (at, size, which, to) in enumerate(jobs)
        ]
        for read in reads:
            read.start()
        for k, (at, size, _, _) in enumerate(jobs):
            reads[k].wait()
            full[at : at + size] = narrow[at : at + size].astype(f32)
            writes[k].start()
        for write in writes:
            write.wait()

    hbm = pl.BlockSpec(memory_space=pltpu.HBM)
    return pl.pallas_call(
        body,
        out_shape=[shape((taps * per, n, 2 * m))] + [shape((1, n, 2 * m))] * extra,
        in_specs=[pl.BlockSpec(memory_space=pltpu.SMEM)] + [hbm] * (1 + len(more)),
        out_specs=[hbm] * (1 + extra),
        scratch_shapes=[
            pltpu.VMEM((total, n, m), bf16),
            pltpu.VMEM((total, n, m), f32),
            pltpu.SemaphoreType.DMA((2, len(jobs))),
        ],
        input_output_aliases={2 + k: k for k in range(len(more))},
        compiler_params=pltpu.CompilerParams(vmem_limit_bytes=20 * 1024 * 1024),
        cost_estimate=pl.CostEstimate(flops=0, bytes_accessed=0, transcendentals=0),
    )(side.reshape(1), half, *more)


def halve_kernel(r, copies):
    for p in range(r.count):
        kept, got = getattr(r, f"kept{p}"), getattr(r, f"got{p}")
        copies.wait(f"kept{p}", f"got{p}")
        to_send, to_keep = getattr(r, f"sent{p}"), getattr(r, f"left{p}")
        bit = r.bits[r.steps[p]] == 1
        h = kept.shape[1] // 2
        for t in range(kept.shape[0]):
            total = kept[t] + got[t].astype(f32)
            low, high = total[:h], total[h:]
            to_send[t] = jnp.where(bit, low, high).astype(bf16)
            to_keep[t] = jnp.where(bit, high, low)
        copies.start(f"sent{p}", f"left{p}")
    copies.wait(*(name for name in copies.jobs if name[:4] in (N.sent, N.left)))


def halve(bits, pairs, steps, cost):
    ins = dict(bits=bits)
    for p, (kept, got) in enumerate(pairs):
        ins[f"kept{p}"], ins[f"got{p}"] = kept, got
    taps, n, m = pairs[0][0].shape
    dims = (taps, n // 2, m)
    names = [str(p) for p in range(len(pairs))]
    outs = {}
    for name in names:
        outs[N.sent + name], outs[N.left + name] = shape(dims, bf16), shape(dims)

    def body(r, copies):
        r.count, r.steps = len(pairs), steps
        halve_kernel(r, copies)

    far_in = tuple(n for n in ins if n != N.bits)
    out = call(body, ins, outs, far_in=far_in, far_out=tuple(outs), smem=(N.bits,), cost=cost, limit=60)
    return [(out[N.sent + name], out[N.left + name]) for name in names]


def shifted(value, axis, steps):
    count = lax.axis_size(axis)
    first, last = (max(0, -steps), min(count, count - steps))
    return lax.ppermute(value, axis, [(source, source + steps) for source in range(first, last)])


def gather_sum(spread):
    return lax.all_to_all(spread, axes, 0, 0)


def bit_of(axis, step):
    return (lax.axis_index(axis) // step) % 2


def partner(value, axis, step):
    count = lax.axis_size(axis)
    return lax.ppermute(value, axis, [(i, i ^ step) for i in range(count)])


def steps_of(axis):
    count, step, out = lax.axis_size(axis), 1, []
    while step < count:
        out.append((axis, step))
        step *= 2
    return out


def split(total, axis, step):
    n = total.shape[1] // 2
    bit = bit_of(axis, step) == 1
    low, high = total[:, :n], total[:, n:]
    return jnp.where(bit, low, high).astype(bf16), jnp.where(bit, high, low)


def joined(value, other, axis, step, dim=1):
    bit = bit_of(axis, step) == 1
    return jnp.concatenate([jnp.where(bit, other, value), jnp.where(bit, value, other)], axis=dim)


class Tree:
    def __init__(self, parts, bits, plane, rest, core):
        self.bits, self.place = bits, {step: k for k, step in enumerate([core, *plane, *rest])}
        self.sent_a, self.kept_a, self.sent_b, self.kept_b = parts
        self.a, self.b, self.rest, self.core = plane, plane[::-1], rest, core
        p, n = len(plane), len(rest)
        self.stages = [(N.plane, k) for k in range(p)] + [(N.rest, k) for k in range(n)]
        self.stages += [(N.rest_join, k) for k in reversed(range(n))] + [(N.plane_join, k) for k in reversed(range(p))]
        self.stages += [(N.core, 0)]

    def next(self):
        return self.stages[0] if self.stages else None

    def start(self):
        kind, k = self.stages[0]
        if kind == N.plane:
            self.got = partner(self.sent_a, *self.a[k]), partner(self.sent_b, *self.b[k])
        elif kind == N.rest:
            self.got = (partner(self.sent, *self.rest[k]),)
        elif kind == N.rest_join:
            self.got = (partner(self.value, *self.rest[k]),)
        elif kind == N.plane_join:
            self.got = partner(self.value_a, *self.a[k]), partner(self.value_b, *self.b[k])
        else:
            self.got = (partner(self.value, *self.core),)

    def finish(self, cost=0):
        kind, k = self.stages.pop(0)
        if kind == N.plane:
            pairs = [(self.kept_a, self.got[0]), (self.kept_b, self.got[1])]
            nexts = [order[k + 1] for order in (self.a, self.b) if k + 1 < len(order)]
            if nexts and cost:
                pairs = halve(self.bits, pairs, [self.place[step] for step in nexts], cost)
                (self.sent_a, self.kept_a), (self.sent_b, self.kept_b) = pairs
                return
            total_a, total_b = (kept + got.astype(f32) for kept, got in pairs)
            if nexts:
                self.sent_a, self.kept_a = split(total_a, *nexts[0])
                self.sent_b, self.kept_b = split(total_b, *nexts[1])
            else:
                self.taps = total_a.shape[0]
                self.split_rest(jnp.concatenate([total_a, total_b], axis=0), 0)
        elif kind == N.rest:
            self.split_rest(self.kept + self.got[0].astype(f32), k + 1)
        elif kind == N.rest_join:
            self.value = joined(self.value, self.got[0], *self.rest[k])
            self.value_a, self.value_b = self.value[: self.taps], self.value[self.taps :]
        elif kind == N.plane_join:
            self.value_a = joined(self.value_a, self.got[0], *self.a[k])
            self.value_b = joined(self.value_b, self.got[1], *self.b[k])
            self.value = jnp.concatenate([self.value_a, self.value_b], axis=1)

    def split_rest(self, total, k):
        if k < len(self.rest):
            self.sent, self.kept = split(total, *self.rest[k])
        else:
            self.value = total.astype(bf16)


def lockstep(*trees, beside=()):
    for t in trees:
        t.start()
    got, beside = lax.optimization_barrier(([t.got for t in trees], beside))
    for t, g in zip(trees, got):
        t.got = g
        t.finish()
    return beside


def on_device(inputs, w_first, gain_first, shift_first, w_second, gain_second, shift_second, w_proj, gain_proj, shift_proj, valid_mask, cotangent):
    groups, rows_in, cols_in, cin = inputs.shape
    rows, cols = rows_in // 2, cols_in // 2
    width = w_first.shape[3]
    half = width // 2
    S = cols + 8
    L = groups * S
    devices = lax.axis_size(N.rows) * lax.axis_size(N.cols) * lax.axis_size(N.grp)
    plane = steps_of(N.cols)
    core = steps_of(N.rows)[0]
    rest = steps_of(N.rows)[1:] + steps_of(N.grp)
    bits = jnp.stack([bit_of(*step) for step in (core, *plane, *rest)]).astype(jnp.int32)
    w1 = w_first.reshape(3, 3 * cin, width)
    w2 = w_second.reshape(3, 3 * width, width)
    as_row = lambda v: v.reshape(1, -1)
    own = jnp.broadcast_to(valid_mask.astype(bf16)[..., None], valid_mask.shape + (128,))
    MP, MQ, MU, MW = (rows + 5) * L, (rows + 3) * L, (rows + 1) * L, rows * L
    px = lambda m, k: 2 * m * k * width
    vec = lambda k: shape((1, k * width))
    all_devices = lambda k: shape((devices, 1, k))
    g1, b1, g2, b2, gp, bp = map(
        as_row, (gain_first, shift_first, gain_second, shift_second, gain_proj, shift_proj)
    )

    top1 = shifted(inputs[:, -1:], N.rows, 1)
    me, count = lax.axis_index(N.rows), lax.axis_size(N.rows)
    flags = jnp.stack([me > 0, me < count - 1]).astype(jnp.int32)
    flat_rows = shape((over * groups * cols_in + (width // 256 + 1) * rim * groups * cols, 256), bf16)
    packed = call(
        vertical_kernel,
        dict(flags=flags, x=inputs, cot=cotangent, own=own),
        dict(down=flat_rows) if count == 2 else dict(down=flat_rows, up=flat_rows),
        far_in=(N.x, N.cot),
        smem=(N.flags,),
        parts=dict(x=end_parts(rows_in, over), cot=end_parts(rows, rim)),
    )
    if count == 2:
        top = bot = lax.ppermute(packed["down"], "rows", [(0, 1), (1, 0)])
    else:
        top, bot = shifted(packed[N.down], N.rows, 1), shifted(packed[N.up], N.rows, -1)
    (top, bot), top1 = lax.optimization_barrier(((top, bot), top1))
    lines = (rows_in + 2 * over) * groups, (rows + 2 * rim) * groups, (rows + 3) * groups
    n_strip = over * lines[0] + (rim + 1) // 2 * lines[1] + width // 128 * lines[2]
    n_strip = -(-n_strip // 16) * 16
    near = dict(flags=flags, x=inputs, cot=cotangent, own=own, top=top, bot=bot)
    strips = call(
        strips_kernel,
        near,
        dict(right=shape((n_strip, 256), bf16), left=shape((n_strip, 256), bf16)),
        dict(
            raw_x=pltpu.VMEM((cin // 128, lines[0] * cols_in, 128), f32),
            raw_m=pltpu.VMEM((1, lines[1] * cols, 128), f32),
            raw_c=pltpu.VMEM((width // 128, lines[2] * cols, 128), f32),
            flat=pltpu.VMEM((n_strip, 256), f32),
        ),
        smem=(N.flags,),
    )
    edge = jnp.concatenate([top1[:, :, -1:], inputs[:, :, -1:]], axis=1)
    edge, right, left = lax.optimization_barrier((edge, strips[N.right], strips[N.left]))
    lft1, right, left = lax.optimization_barrier((shifted(edge, N.cols, 1), right, left))
    lft, rgt = shifted(right, N.cols, 1), shifted(left, N.cols, -1)
    stats = call(
        stats_kernel,
        dict(x=inputs, top=top1, lft=lft1, own=own, w1=w1, wp=w_proj),
        dict(spread=all_devices(4 * width + 128)),
        dict(
            raw=pltpu.VMEM((cin // 128, (rows_in + 1) * groups, cols_in + 8, 128), f32),
            xe=pltpu.VMEM((rows * groups * cols, 3 * cin), bf16),
            xo=pltpu.VMEM(((rows + 1) * groups * cols, 3 * cin), bf16),
        ),
        far_in=(N.w1,),
        far_out=(N.spread,),
    )
    tot1 = gather_sum(stats[N.spread])

    first = call(
        first_kernel,
        dict(**near, lft=lft, rgt=rgt, w1=w1, wp=w_proj),
        dict(
            pre1=shape((MP, width)),
            prep=shape((MP, width)),
            xe=shape((MP, 3 * cin), bf16),
            xo=shape((MP + L, 3 * cin), bf16),
            ownp=shape((MP, 128)),
            maskp=shape((MP, 128)),
            cotq=shape((MQ, width)),
        ),
        dict(
            raw_x=pltpu.VMEM((cin // 128, lines[0] * (cols_in + 24), 128), f32),
            raw_m=pltpu.VMEM((1, lines[1] * (cols + 16), 128), f32),
            raw_c=pltpu.VMEM((width // 128, lines[2] * (cols + 16), 128), f32),
            flat=pltpu.VMEM((n_strip, 256), f32),
        ),
        far_in=(N.w1, N.wp),
        far_out=(N.xe, N.xo, N.pre1, N.prep, N.cotq),
        smem=(N.flags,),
        cost=20000000000,
        parts=dict(pre1=row_parts(MP, 3), prep=row_parts(MP, 3)),
    )
    xe, xo, ownp, maskp = first[N.xe], first[N.xo], first[N.ownp], first[N.maskp]
    far_xe, far_xo = partner(xe, *core), partner(xo, *core)

    second = call(
        second_kernel,
        dict(pre1=first[N.pre1], tot1=tot1, gain=g1, shift=b1, maskp=maskp, ownp=ownp, w2=w2),
        dict(h3=shape((MP, 3 * width), bf16), pre2=shape((MQ, width)), spread=all_devices(2 * width), mom1=shape((8, width))),
        dict(hid=pltpu.VMEM((MP + 8, width), f32)),
        far_in=(N.pre1, N.w2),
        far_out=(N.h3, N.pre2, N.spread),
        parts=dict(pre2=row_parts(MQ, 3)),
    )
    h3, pre2, mom1 = second[N.h3], second[N.pre2], second[N.mom1]
    tot2 = gather_sum(second[N.spread])
    tot2, far_h3 = lax.optimization_barrier((tot2, partner(h3, *core)))

    third = call(
        third_kernel,
        dict(
            bits=bits, pre2=pre2, prep=first[N.prep], mom1=mom1, tot2=tot2, gain2=g2, shift2=b2, gainp=gp, shiftp=bp,
            maskp=maskp, ownp=ownp, cotq=first[N.cotq],
        ),
        dict(
            out=shape((groups, rows, cols, width), bf16),
            grad=shape((MQ, width)),
            spread=all_devices(3 * width),
            mom2=shape((8, width)),
            mine=shape((3, MW, half)),
            theirs=shape((3, MW, half)),
        ),
        dict(field=pltpu.VMEM((MQ, width), f32)),
        far_in=(N.pre2, N.prep, N.cotq),
        far_out=(N.grad, N.spread, N.mine, N.theirs, N.out),
        smem=(N.bits,),
        parts=dict(
            mine=middle_parts(MW, 2), theirs=middle_parts(MW, 2),
            grad=row_parts(MQ, 2), pre2=row_parts(MQ, 2), cotq=row_parts(MQ, 2), prep=cuts(L, L + MQ // 2 + 8, L + MQ + 8)
        ),
    )
    mom2 = third[N.mom2]
    tot3 = gather_sum(third[N.spread])
    ownp_here, far3 = lax.optimization_barrier((ownp, partner(third[N.theirs], *core)))
    ownp_far = partner(ownp_here, *core)

    def chunk_shapes(taps):
        dims = (taps, cin // 4, half)
        return dict(sent_a=shape(dims, bf16), kept_a=shape(dims), sent_b=shape(dims, bf16), kept_b=shape(dims))

    per = width // cin
    taps2 = 9 * per + 1
    second_parts = call(
        weights_second_kernel,
        dict(
            bits=bits, mine=third[N.mine], far3=far3, h3=h3, h3_far=far_h3, xe=xe, xe_far=far_xe,
            tot3=tot3, mom1=mom1, mom2=mom2, gain2=g2, gainp=gp, ownp=ownp, ownp_far=ownp_far,
        ),
        chunk_shapes(taps2),
        dict(
            acc=pltpu.VMEM((width, half), f32),
            pad=pltpu.VMEM((3, MW + 8, half), f32),
            near=pltpu.VMEM((2 * MW, half), bf16),
            far=pltpu.VMEM((2 * MW, half), bf16),
        ),
        far_in=(N.mine, N.far3, N.h3, N.h3_far, N.xe, N.xe_far),
        far_out=CHUNKS,
        smem=(N.bits,),
        parts=dict(
            h3=lane_parts(3 * width, 3, pl.ds(L, MW + 2 * L)),
            h3_far=lane_parts(3 * width, 3, pl.ds(L, MW + 2 * L)),
            xe=[(0, (pl.ds(2 * L, MW), pl.ds(cin, cin)))],
            xe_far=[(0, (pl.ds(2 * L, MW), pl.ds(cin, cin)))],
            **{name: row_parts(taps2 - 1, 3) + [(3, (pl.ds(taps2 - 1, 1),))] for name in CHUNKS},
        ),
    ).values()
    grad, *second_parts = lax.optimization_barrier((third[N.grad], *second_parts))
    tree2 = Tree(second_parts, bits, plane, rest, core)
    tree2.start()
    hidden = call(
        fourth_kernel,
        dict(
            bits=bits, grad=grad, pre2=pre2, keep=first[N.pre1], w2=w2, prep=first[N.prep], mom1=mom1, mom2=mom2, tot3=tot3,
            gain=g1, shift=b1, gain2=g2, gainp=gp, maskp=maskp, ownp=ownp,
        ),
        dict(
            act=shape((MU, width)), normed=shape((MU, width)), spread=all_devices(2 * width),
            mine=shape((2, MW, half)), theirs=shape((2, MW, half)), gpu=shape((MW, width), bf16),
            gain_second=vec(1), shift_second=vec(1), gain_proj=vec(1), shift_proj=vec(1),
        ),
        dict(
            gq=pltpu.VMEM((MQ + 8, width), f32),
            g3=pltpu.VMEM((MQ, 3 * width), bf16),
            gh=pltpu.VMEM((MU, width), f32),
        ),
        far_in=(N.grad, N.pre2, N.keep, N.w2, N.prep),
        far_out=(
            N.act, N.normed, N.spread, N.mine, N.theirs, N.gpu, N.gain_second, N.shift_second, N.gain_proj, N.shift_proj
        ),
        smem=(N.bits,),
        limit=52,
        parts=dict(
            grad=cuts(0, 6 * L, MQ),
            pre2=cuts(0, 6 * L, MQ),
            keep=cuts(2 * L, 2 * L + MU + 8),
            w2=[(k, (pl.ds(2 - k, 1),)) for k in range(3)],
            prep=cuts(2 * L, 2 * L + MW + 8),
            mine=row_parts(2, 2),
            theirs=row_parts(2, 2),
        ),
    )
    tot4 = gather_sum(hidden[N.spread])
    tree2.finish(20000000000)
    near1, tree2.sent_a, tree2.sent_b = lax.optimization_barrier((hidden[N.mine], tree2.sent_a, tree2.sent_b))
    tree2.start()
    fifth = call(
        weights_first_kernel,
        dict(
            bits=bits, mine=near1, far4=partner(hidden[N.theirs], *core), xe=xe, xe_far=far_xe, xo=xo, xo_far=far_xo,
            tot4=tot4, mom1=mom1, gain=g1, ownp=ownp, ownp_far=ownp_far,
        ),
        dict(**chunk_shapes(9), gain_first=vec(1), shift_first=vec(1)),
        dict(
            acc=pltpu.VMEM((3 * cin, half), f32),
            pad=pltpu.VMEM((2, MW + 8, half), f32),
            near=pltpu.VMEM((MW, half), bf16),
            far=pltpu.VMEM((MW, half), bf16),
        ),
        far_in=(N.mine, N.far4, N.xe, N.xe_far, N.xo, N.xo_far),
        cost=20000000000,
        far_out=(*CHUNKS, N.gain_first, N.shift_first),
        smem=(N.bits,),
        parts=dict(
            xe=cuts(2 * L, 2 * L + MW),
            xe_far=cuts(2 * L, 2 * L + MW),
            xo=cuts(2 * L, 3 * L + MW),
            xo_far=cuts(2 * L, 3 * L + MW),
            **{name: row_parts(9, 3) for name in CHUNKS},
        ),
    )
    first_parts = [fifth[name] for name in CHUNKS]
    tree2.got, *first_parts = lax.optimization_barrier((tree2.got, *first_parts))
    tree2.finish()
    tree1 = Tree(first_parts, bits, plane, rest, core)

    grad_inputs = call(
        inputs_kernel,
        dict(
            act=hidden[N.act], normed=hidden[N.normed], gpu=hidden[N.gpu], w1=w1, wp=w_proj, mom1=mom1, gain=g1, maskp=maskp,
            gg=fifth[N.gain_first], gs=fifth[N.shift_first],
        ),
        dict(out=shape((groups, rows_in, cols_in, cin), bf16)),
        dict(
            lines=pltpu.VMEM((cin // 128, rows_in * groups, cols_in, 128), f32),
            gf=pltpu.VMEM((MU + 16, width), f32),
            gu=pltpu.VMEM((MU, 2 * width), bf16),
        ),
        far_in=(N.act, N.normed, N.gpu, N.w1, N.wp),
        far_out=(N.out,),
        cost=10000000000,
    )[N.out]
    side = bit_of(*core).astype(jnp.int32)
    grad_inputs = lockstep(tree2, tree1, beside=grad_inputs)
    while tree2.next() != (N.plane_join, 0):
        lockstep(tree2, tree1)
    tree2.start()
    while tree1.next() != (N.plane_join, 0):
        tree1.start()
        if tree1.next() != (N.plane_join, 1):
            tree1.finish()
        else:
            tree1.got, tree2.got = lax.optimization_barrier((tree1.got, tree2.got))
            tree1.finish()
    tree2.finish()
    tree2.start()
    tree1.start()
    grad_second = widen(tree2.got[0], 1 - side, 9, per, True, widen(tree2.value, side, 9, per, True))
    tree1.got, grad_second = lax.optimization_barrier((tree1.got, grad_second))
    grad_w2, grad_wp = grad_second
    tree1.finish()
    tree1.start()
    (grad_w1,) = widen(tree1.got[0], 1 - side, 3, 3, False, widen(tree1.value, side, 3, 3, False))

    return (
        third[N.out],
        grad_inputs,
        grad_w1.reshape(w_first.shape),
        fifth[N.gain_first].reshape(width),
        fifth[N.shift_first].reshape(width),
        grad_w2.reshape(w_second.shape),
        hidden[N.gain_second].reshape(width),
        hidden[N.shift_second].reshape(width),
        grad_wp.reshape(w_proj.shape),
        hidden[N.gain_proj].reshape(width),
        hidden[N.shift_proj].reshape(width),
    )


def solution(mesh):
    spread = P("grp", "rows", "cols", None)
    return jax.shard_map(
        on_device,
        mesh=mesh,
        in_specs=(spread,) + (P(),) * 9 + (P("grp", "rows", "cols"), spread),
        out_specs=(spread, spread) + (P(),) * 9,
        check_vma=False,
    )
```

```python
import functools

import jax
import jax.numpy as jnp
from jax import lax
from jax.experimental import pallas as pl
from jax.experimental.pallas import tpu as pltpu
from jax.sharding import PartitionSpec as P

epsilon = 1e-05
axes = ("rows", "cols", "grp")
bf16 = jnp.bfloat16
f32 = jnp.float32
inner = 0.7978845608028654
cubic = 0.044715
over = 6
CHUNKS = "sent_a", "kept_a", "sent_b", "kept_b"
rim = 3


class Names:
    def __getattr__(self, name):
        return name


N = Names()


class Refs:
    def __init__(self, named):
        self.__dict__.update(named)


class Copies:
    def __init__(self, parts, pairs, sems):
        self.jobs = {}
        for k, (name, index) in enumerate(parts):
            source, target = pairs[name]
            if index:
                source, target = source.at[index[1]], target.at[index[1]]
            self.jobs.setdefault(name, []).append(pltpu.make_async_copy(source, target, sems.at[k]))

    def start(self, *names):
        for name, *which in map(named, names):
            for job in self.jobs[name][slice(*which) if which else slice(None)]:
                job.start()

    def start_all(self, names):
        for k in range(max((len(self.jobs[n]) for n in names), default=0)):
            for n in names:
                if k < len(self.jobs[n]):
                    self.jobs[n][k].start()

    def wait(self, *names):
        for name, *which in map(named, names):
            for job in self.jobs[name][slice(*which) if which else slice(None)]:
                job.wait()


def named(name):
    return (name,) if isinstance(name, str) else (name[0], name[1], name[1] + 1)


def row_parts(total, count):
    size = total // count
    return [(k, (pl.ds(k * size, size),)) for k in range(count)]


def middle_parts(total, count):
    size = total // count
    return [(k, (slice(None), pl.ds(k * size, size))) for k in range(count)]


def end_parts(total, size):
    return [(k, (slice(None), pl.ds(at, size))) for k, at in enumerate((0, total - size))]


def cuts(*at):
    return [(k, (pl.ds(a, b - a),)) for k, (a, b) in enumerate(zip(at, at[1:]))]


def lane_parts(total, count, rows=slice(None)):
    size = total // count
    return [(k, (rows, pl.ds(k * size, size))) for k in range(count)]


def call(body, ins, outs, scratch=None, far_in=(), far_out=(), smem=(), parts=None, limit=52, cost=0):
    scratch, parts = scratch or {}, parts or {}
    far = (*far_in, *far_out)
    jobs = [(name, index) for name in far for index in parts.get(name, [None])]

    def spec(name):
        if name in smem:
            return pl.BlockSpec(memory_space=pltpu.SMEM)
        return pl.BlockSpec(memory_space=pltpu.HBM if name in far else pltpu.VMEM)

    kinds = {**{n: shape(v.shape, v.dtype) for n, v in ins.items()}, **outs}

    def run(*refs):
        plain = dict(zip([*ins, *outs], refs))
        rest = refs[len(plain) :]
        buffers = dict(zip(far, rest))
        more = dict(zip(scratch, rest[len(far) :]))
        copies = None
        if far:
            pairs = {n: (plain[n], buffers[n]) if n in far_in else (buffers[n], plain[n]) for n in far}
            copies = Copies(jobs, pairs, rest[-1])
            copies.start_all(far_in)
        body(Refs({**plain, **buffers, **more}), copies)

    buffers = [pltpu.VMEM(kinds[n].shape, kinds[n].dtype) for n in far]
    sems = [pltpu.SemaphoreType.DMA((len(jobs),))] if far else []
    result = pl.pallas_call(
        run,
        out_shape=list(outs.values()),
        in_specs=[spec(n) for n in ins],
        out_specs=[spec(n) for n in outs],
        scratch_shapes=[*buffers, *scratch.values(), *sems],
        compiler_params=pltpu.CompilerParams(vmem_limit_bytes=limit * 1024 * 1024),
        cost_estimate=pl.CostEstimate(flops=cost, bytes_accessed=0, transcendentals=0),
    )(*ins.values())
    return dict(zip(outs, result))


def shape(dims, dtype=f32):
    return jax.ShapeDtypeStruct(dims, dtype)


def wide(mask, width):
    return jnp.concatenate([mask] * (width // mask.shape[1]), axis=1)


def matmul(a, b):
    return lax.dot_general(a, b, (((1,), (0,)), ((), ())), preferred_element_type=f32)


def matmul_nt(a, b):
    return lax.dot_general(a, b, (((1,), (1,)), ((), ())), preferred_element_type=f32)


def matmul_tn(a, b):
    return lax.dot_general(a, b, (((0,), (0,)), ((), ())), preferred_element_type=f32)


def gelu_parts(v):
    return jnp.tanh(inner * (v + cubic * v * v * v))


def gelu_slope(v, t):
    return 0.5 * (1.0 + t) + 0.5 * v * (1.0 - t * t) * (inner * (1.0 + 3.0 * cubic * v * v))


def column_sum(v):
    return jnp.sum(v, axis=0, keepdims=True)


def moments(total, squares, pixel_count):
    center = total / pixel_count
    spread = squares / pixel_count - center * center
    return center, lax.rsqrt(spread + epsilon)


def chunks(total, size):
    return [(at, min(size, total - at)) for at in range(0, total, size)]


def strided(ref, k, first, count, step):
    return ref[k, pl.ds(first, count, stride=step), :]


def vertical_kernel(r, copies):
    groups, width = r.x.shape[0], r.cot.shape[3]
    rows, cols = r.own.shape[1], r.own.shape[2]

    def pack(out, input_row, row, pick):
        at = 0
        for g in range(groups):
            for n in range(over):
                value = r.x[g, input_row(n)]
                out[at : at + 2 * cols, :] = pick(value, r.x[g, n])
                at += 2 * cols
        for k in range(0, width, 256):
            for g in range(groups):
                for n in range(rim):
                    lanes = slice(k, k + 256)
                    out[at : at + cols, :] = pick(r.cot[g, row(n), :, lanes], r.cot[g, n, :, lanes])
                    at += cols
        for g in range(groups):
            for n in range(rim):
                out[at : at + cols, :] = pick(wide(r.own[g, row(n)], 256), wide(r.own[g, n], 256))
                at += cols

    last = r.x.shape[1] - over
    copies.wait(N.x, N.cot)
    if hasattr(r, N.up):
        pack(r.down, lambda n: last + n, lambda n: rows - rim + n, lambda tail, head: tail)
        pack(r.up, lambda n: last + n, lambda n: rows - rim + n, lambda tail, head: head)
    else:
        bottom = r.flags[0] == 1
        pack(r.down, lambda n: last + n, lambda n: rows - rim + n, lambda tail, head: jnp.where(bottom, head, tail))


def rim_rows(r, own, n_own, n_rim, base, cols, split):
    groups = own.shape[0]
    size = groups * n_rim * cols

    def flat(ref, g, n):
        at = [base + k * size + (g * n_rim + n) * cols for k in range(split)]
        return jnp.concatenate([ref[p : p + cols, :] for p in at], axis=1).astype(f32)

    def read(g, n):
        if n < n_rim:
            return jnp.where(r.flags[0] == 1, flat(r.top, g, n), 0.0)
        if n < n_rim + n_own:
            return own[g, n - n_rim].astype(f32)
        return jnp.where(r.flags[1] == 1, flat(r.bot, g, n - n_rim - n_own), 0.0)

    return read


def fields(r):
    groups, width = r.x.shape[0], r.cot.shape[3]
    rows, cols = r.own.shape[1], r.own.shape[2]
    base = over * groups * 2 * cols
    piece = rim * groups * cols
    blocks = width // 256
    x = rim_rows(r, r.x, 2 * rows, over, 0, 2 * cols, 1)
    mask = rim_rows(r, r.own, rows, rim, base + blocks * piece, cols, 1)
    cot = rim_rows(r, r.cot, rows, rim, base, cols, blocks)
    return x, lambda g, n: mask(g, n)[:, :128], cot


def strips_kernel(r, copies):
    groups, width = r.x.shape[0], r.cot.shape[3]
    rows, cols = r.own.shape[1], r.own.shape[2]
    x, mask, cot = fields(r)
    lines = (2 * rows + 2 * over) * groups, (rows + 2 * rim) * groups, (rows + 3) * groups
    for raw, read, first, count, w in (
        (r.raw_x, x, 0, lines[0], 2 * cols),
        (r.raw_m, mask, 0, lines[1], cols),
        (r.raw_c, cot, 2, lines[2], cols),
    ):
        for at in range(count):
            value = read(at % groups, at // groups + first)
            for k in range(raw.shape[0]):
                raw[k, at * w : (at + 1) * w, :] = value[:, k * 128 : (k + 1) * 128]
    for out, x0, m0, c0 in ((r.right, 2 * cols - over, cols - rim, cols - 2), (r.left, 0, 0, 0)):
        pieces = []
        for c in range(over):
            pieces.append([strided(r.raw_x, k, x0 + c, lines[0], 2 * cols) for k in range(2)])
        for c in range(0, rim + 1, 2):
            pieces.append([strided(r.raw_m, 0, m0 + min(c + k, rim - 1), lines[1], cols) for k in range(2)])
        for c in range(2):
            for h in range(0, width // 128, 2):
                pieces.append([strided(r.raw_c, h + k, c0 + c, lines[2], cols) for k in range(2)])
        at = 0
        for low, high in pieces:
            r.flat[at : at + low.shape[0], :] = jnp.concatenate([low, high], axis=1)
            at += low.shape[0]
        if at < r.flat.shape[0]:
            r.flat[at:, :] = jnp.zeros((r.flat.shape[0] - at, 256), f32)
        out[...] = r.flat[...].astype(bf16)


def stats_kernel(r, copies):
    groups, cin = r.x.shape[0], r.x.shape[3]
    rows, S = r.own.shape[1], r.own.shape[2]
    L = groups * S
    width = r.w1.shape[2]
    raw = r.raw
    for n in range(2 * rows + 1):
        for g in range(groups):
            line = n * groups + g
            src = (r.top[g, 0] if n == 0 else r.x[g, n - 1]).astype(f32)
            side = r.lft[g, n].astype(f32)
            for k in range(raw.shape[0]):
                raw[k, line, 7:8, :] = side[:, k * 128 : (k + 1) * 128]
                raw[k, line, 8:, :] = src[:, k * 128 : (k + 1) * 128]
    for out, n_rows, start in ((r.xe, rows, 1), (r.xo, rows + 1, 0)):
        for n in range(n_rows):
            for b in range(3):
                for k in range(raw.shape[0]):
                    parts = [
                        raw[k, (2 * n + start) * groups + g, pl.ds(7 + b, S, stride=2), :]
                        for g in range(groups)
                    ]
                    at = b * cin + k * 128
                    out[n * L : (n + 1) * L, at : at + 128] = jnp.concatenate(
                        parts, axis=0
                    ).astype(bf16)
    mask = jnp.concatenate(
        [r.own[g, i].astype(f32) for i in range(rows) for g in range(groups)], axis=0
    )
    M = rows * L
    copies.wait(N.w1)
    z = matmul(r.xo[0:M, :], r.w1[0])
    z += matmul(r.xe[...], r.w1[1])
    z += matmul(r.xo[L : L + M, :], r.w1[2])
    zp = matmul(r.xe[:, cin : 2 * cin], r.wp[...])
    zm, zpm = z * wide(mask, width), zp * wide(mask, width)
    row = jnp.concatenate(
        [column_sum(zm), column_sum(zm * z), column_sum(zpm), column_sum(zpm * zp), column_sum(mask)], axis=1
    )
    r.spread[...] = jnp.broadcast_to(row[None], r.spread.shape)
    copies.start(N.spread)
    copies.wait(N.spread)


def first_kernel(r, copies):
    groups, cin, width = r.x.shape[0], r.x.shape[3], r.cot.shape[3]
    rows, cols = r.own.shape[1], r.own.shape[2]
    S = cols + 8
    L = groups * S
    W = 2 * cols + 24
    V = cols + 16
    x, mask, cot = fields(r)
    lines = (2 * rows + 2 * over) * groups, (rows + 2 * rim) * groups, (rows + 3) * groups
    tail = jnp.zeros((W - 8 - 2 * cols, 128), f32)
    r.raw_m[...] = jnp.zeros(r.raw_m.shape, f32)
    r.raw_c[...] = jnp.zeros(r.raw_c.shape, f32)
    for at in range(lines[0]):
        value = x(at % groups, at // groups)
        for k in range(r.raw_x.shape[0]):
            r.raw_x[k, at * W + 8 : at * W + 8 + 2 * cols, :] = value[:, k * 128 : (k + 1) * 128]
            r.raw_x[k, at * W + 8 + 2 * cols : (at + 1) * W, :] = tail
    for strip, x0, m0, c0 in ((r.lft, 8 - over, 8 - rim, 6), (r.rgt, 8 + 2 * cols, 8 + cols, 8 + cols)):
        r.flat[...] = strip[...].astype(f32)
        at = 0
        for c in range(over):
            for k in range(2):
                r.raw_x[k, pl.ds(x0 + c, lines[0], stride=W), :] = r.flat[at : at + lines[0], k * 128 : (k + 1) * 128]
            at += lines[0]
        for c in range(0, rim + 1, 2):
            for k in range(2):
                if c + k < rim:
                    r.raw_m[0, pl.ds(m0 + c + k, lines[1], stride=V), :] = r.flat[
                        at : at + lines[1], k * 128 : (k + 1) * 128
                    ]
            at += lines[1]
        for c in range(2):
            for h in range(0, width // 128, 2):
                for k in range(2):
                    r.raw_c[h + k, pl.ds(c0 + c, lines[2], stride=V), :] = r.flat[
                        at : at + lines[2], k * 128 : (k + 1) * 128
                    ]
                at += lines[2]
    for out, n_rows, start in ((r.xe, rows + 5, 2), (r.xo, rows + 6, 1)):
        for n in range(n_rows):
            for b in range(3):
                for k in range(r.raw_x.shape[0]):
                    parts = [
                        strided(r.raw_x, k, ((2 * n + start) * groups + g) * W + 3 + b, S, 2) for g in range(groups)
                    ]
                    at = b * cin + k * 128
                    out[n * L : (n + 1) * L, at : at + 128] = jnp.concatenate(parts, axis=0).astype(bf16)
    copies.start(N.xe, N.xo)
    for at in range(lines[1]):
        r.raw_m[0, at * V + 8 : at * V + 8 + cols, :] = mask(at % groups, at // groups)
    for n in range(1, rows + 6):
        for g in range(groups):
            to, at = (n - 1) * L + g * S, (n * groups + g) * V
            r.maskp[to : to + S, :] = r.raw_m[0, at + 6 : at + 6 + S, :]
    for at in range(lines[2]):
        value = cot(at % groups, at // groups + 2)
        for k in range(r.raw_c.shape[0]):
            lanes = slice(k * 128, (k + 1) * 128)
            r.raw_c[k, at * V + 8 : at * V + 8 + cols, :] = value[:, lanes]
            r.cotq[at * S : (at + 1) * S, lanes] = r.raw_c[k, at * V + 7 : at * V + 7 + S, :]
    copies.start(N.cotq)
    r.ownp[...] = jnp.zeros(r.ownp.shape, f32)
    for i in range(rows):
        for g in range(groups):
            at = (i + 2) * L + g * S + 2
            r.ownp[at : at + cols, :] = r.own[g, i].astype(f32)
    copies.wait(N.w1, N.wp)
    for k, (m0, m) in enumerate(chunks(r.pre1.shape[0], r.pre1.shape[0] // 3)):
        z = matmul(r.xo[m0 : m0 + m, :], r.w1[0])
        z += matmul(r.xe[m0 : m0 + m, :], r.w1[1])
        z += matmul(r.xo[L + m0 : L + m0 + m, :], r.w1[2])
        r.pre1[m0 : m0 + m, :] = z
        copies.start((N.pre1, k))
        r.prep[m0 : m0 + m, :] = matmul(r.xe[m0 : m0 + m, cin : 2 * cin], r.wp[...])
        copies.start((N.prep, k))
    copies.wait(N.xe, N.xo, N.pre1, N.prep, N.cotq)


def second_kernel(r, copies):
    width = r.gain.shape[1]
    t = jnp.sum(r.tot1[...], axis=0)
    n = wide(t[:, 4 * width :], width)
    center, inv = moments(t[:, :width], t[:, width : 2 * width], n)
    proj = moments(t[:, 2 * width : 3 * width], t[:, 3 * width : 4 * width], n)
    r.mom1[...] = jnp.concatenate([center, inv, n, *proj, jnp.zeros((3, width), f32)], axis=0)
    scale = inv * r.gain[...]
    M, Q = r.pre1.shape[0], r.pre2.shape[0]
    L = (M - Q) // 2
    copies.wait(N.pre1)
    for m0, m in chunks(M, 104):
        v = (r.pre1[m0 : m0 + m, :] - center) * scale + r.shift[...]
        mask = wide(r.maskp[m0 : m0 + m, :], width)
        r.hid[m0 : m0 + m, :] = 0.5 * v * (1.0 + gelu_parts(v)) * mask
    r.hid[M:, :] = jnp.zeros((r.hid.shape[0] - M, width), f32)
    for m0, m in chunks(M, 208):
        for b in range(3):
            r.h3[m0 : m0 + m, b * width : (b + 1) * width] = r.hid[m0 + b : m0 + b + m, :].astype(bf16)
    copies.start(N.h3)
    copies.wait(N.w2)
    sums = [jnp.zeros((1, width), f32)] * 2
    for k, (m0, m) in enumerate(chunks(Q, Q // 3)):
        z = matmul(r.h3[m0 : m0 + m, :], r.w2[0])
        z += matmul(r.h3[L + m0 : L + m0 + m, :], r.w2[1])
        z += matmul(r.h3[2 * L + m0 : 2 * L + m0 + m, :], r.w2[2])
        r.pre2[m0 : m0 + m, :] = z
        copies.start((N.pre2, k))
        zm = z * wide(r.ownp[L + 1 + m0 : L + 1 + m0 + m, :], width)
        sums = [sums[0] + column_sum(zm), sums[1] + column_sum(zm * z)]
    row = jnp.concatenate(sums, axis=1)
    r.spread[...] = jnp.broadcast_to(row[None], r.spread.shape)
    copies.start(N.spread)
    copies.wait(N.h3, N.pre2, N.spread)


def part(r, at, *fields, first=0):
    bit = r.bits[0] == 1
    for k, field in enumerate(fields, first):
        half = field.shape[1] // 2
        low, high = field[:, :half], field[:, half:]
        r.mine[k, at : at + field.shape[0], :] = jnp.where(bit, high, low)
        r.theirs[k, at : at + field.shape[0], :] = jnp.where(bit, low, high)


def mine_of(r, row):
    half = row.shape[1] // 2
    return jnp.where(r.bits[0] == 1, row[:, half:], row[:, :half])


def third_kernel(r, copies):
    groups, rows, cols, width = r.out.shape
    S = cols + 8
    L = groups * S
    n = r.mom1[2:3, :]
    t = jnp.sum(r.tot2[...], axis=0)
    c2, i2 = moments(t[:, :width], t[:, width:], n)
    cp, ip = r.mom1[3:4, :], r.mom1[4:5, :]
    r.mom2[...] = jnp.concatenate([c2, i2, cp, ip, jnp.zeros((4, width), f32)], axis=0)
    sums = [jnp.zeros((1, width), f32)] * 3
    both_shift = r.shift2[...] + r.shiftp[...]
    total = r.grad.shape[0] // S
    for line in range(total):
        if line % (total // 2) == 0:
            k = line // (total // 2)
            copies.wait((N.pre2, k), (N.prep, k), (N.cotq, k))
        at = line * S
        shifted = slice(L + 1 + at, L + 1 + at + S)
        n2 = (r.pre2[at : at + S, :] - c2) * i2
        np_ = (r.prep[shifted, :] - cp) * ip
        v = n2 * r.gain2[...] + np_ * r.gainp[...] + both_shift
        mask = wide(r.maskp[shifted, :], width)
        own = wide(r.ownp[shifted, :], width)
        t = gelu_parts(v)
        r.field[at : at + S, :] = 0.5 * v * (1.0 + t) * mask
        g = gelu_slope(v, t) * mask * r.cotq[at : at + S, :]
        r.grad[at : at + S, :] = g
        g = g * own
        if L <= at < L + r.mine.shape[1]:
            part(r, at - L, g, n2 * own, np_ * own)
            if at - L + S == r.mine.shape[1] // 2:
                copies.start((N.mine, 0), (N.theirs, 0))
        new = [column_sum(g * n2), column_sum(g), column_sum(g * np_)]
        sums = [a + b for a, b in zip(sums, new)]
        if (line + 1) % (total // 2) == 0:
            copies.start((N.grad, (line + 1) // (total // 2) - 1))
    row = jnp.concatenate(sums, axis=1)
    r.spread[...] = jnp.broadcast_to(row[None], r.spread.shape)
    copies.start(N.spread, (N.mine, 1), (N.theirs, 1))
    for i in range(rows):
        for g in range(groups):
            at = (i + 1) * L + g * S + 1
            r.out[g, i, :, :] = r.field[at : at + cols, :].astype(bf16)
    copies.start(N.out)
    copies.wait(N.grad, N.out, N.spread, N.mine, N.theirs)


def fourth_kernel(r, copies):
    width = r.gain.shape[1]
    Q, U, rows_w = r.pre2.shape[0], r.act.shape[0], r.gpu.shape[0]
    L = U - rows_w
    center, inv, n = (r.mom1[k : k + 1, :] for k in range(3))
    c2, i2, cp, ip = (r.mom2[k : k + 1, :] for k in range(4))
    t3 = jnp.sum(r.tot3[...], axis=0)
    gg2, gs, ggp = (t3[:, k * width : (k + 1) * width] for k in range(3))
    r.gain_second[...], r.shift_second[...], r.gain_proj[...], r.shift_proj[...] = gg2, gs, ggp, gs
    tiny = N.gain_second, N.shift_second, N.gain_proj, N.shift_proj
    copies.start(*tiny)
    for m0, m in chunks(Q, L):
        if m0 in (0, 6 * L):
            copies.wait((N.grad, m0 // (6 * L)), (N.pre2, m0 // (6 * L)))
        mask = wide(r.maskp[L + 1 + m0 : L + 1 + m0 + m, :], width) / n
        n2 = (r.pre2[m0 : m0 + m, :] - c2) * i2
        back = mask * (gs + n2 * gg2)
        r.gq[m0 : m0 + m, :] = (r.gain2[...] * i2) * (r.grad[m0 : m0 + m, :] - back)
    r.gq[Q:, :] = jnp.zeros((r.gq.shape[0] - Q, width), f32)
    for m0, m in chunks(Q, 176):
        for b in range(3):
            r.g3[m0 : m0 + m, b * width : (b + 1) * width] = r.gq[m0 + b : m0 + b + m, :].astype(bf16)
    copies.wait(N.keep)
    for m0, m in chunks(U, L):
        frame = slice(2 * L + 2 + m0, 2 * L + 2 + m0 + m)
        n1 = (r.keep[frame, :] - center) * inv
        v = n1 * r.gain[...] + r.shift[...]
        mask = wide(r.maskp[frame, :], width)
        r.act[m0 : m0 + m, :] = gelu_slope(v, gelu_parts(v)) * mask
        r.normed[m0 : m0 + m, :] = n1 * mask
        if m0 < rows_w:
            part(r, m0, n1 * wide(r.ownp[frame, :], width), first=1)
    copies.start(N.normed, (N.mine, 1), (N.theirs, 1))
    for a in range(3):
        copies.wait((N.w2, a))
        gh = jnp.zeros((U, width), f32)
        for b in range(3):
            gh += matmul_nt(
                r.g3[L * a : L * a + U, b * width : (b + 1) * width],
                r.w2[2 - a, (2 - b) * width : (3 - b) * width, :],
            )
        r.gh[...] = gh if a == 0 else r.gh[...] + gh
    sums = [jnp.zeros((1, width), f32)] * 2
    for m0, m in chunks(U, L):
        g = r.act[m0 : m0 + m, :] * r.gh[m0 : m0 + m, :]
        r.act[m0 : m0 + m, :] = g
        g = g * wide(r.ownp[2 * L + 2 + m0 : 2 * L + 2 + m0 + m, :], width)
        if m0 < rows_w:
            part(r, m0, g)
        sums = [sums[0] + column_sum(g * r.normed[m0 : m0 + m, :]), sums[1] + column_sum(g)]
    row = jnp.concatenate(sums, axis=1)
    r.spread[...] = jnp.broadcast_to(row[None], r.spread.shape)
    copies.start(N.spread, (N.mine, 0), (N.theirs, 0), N.act)
    copies.wait(N.prep)
    for m0, m in chunks(rows_w, L):
        frame = slice(2 * L + 2 + m0, 2 * L + 2 + m0 + m)
        mask = wide(r.maskp[frame, :], width) / n
        back = mask * (gs + (r.prep[frame, :] - cp) * ip * ggp)
        r.gpu[m0 : m0 + m, :] = ((r.gainp[...] * ip) * (r.grad[L + 1 + m0 : L + 1 + m0 + m, :] - back)).astype(bf16)
    copies.start(N.gpu)
    copies.wait(N.normed, N.mine, N.theirs, N.spread, N.act, N.gpu, *tiny)


def split_store(r, rows, unit, first):
    quarter = unit // 4
    for k in range(rows // unit):
        for bit, base, sent, kept in ((1, 0, r.sent_a, r.kept_a), (2, 2 * quarter, r.sent_b, r.kept_b)):
            keep = pl.multiple_of(k * unit + base + r.bits[bit] * quarter, quarter)
            send = pl.multiple_of(k * unit + base + (1 - r.bits[bit]) * quarter, quarter)
            sent[first + k] = r.acc[pl.ds(send, quarter), :].astype(bf16)
            kept[first + k] = r.acc[pl.ds(keep, quarter), :]


def weights_second_kernel(r, copies):
    width = r.h3.shape[1] // 3
    cin = r.xe.shape[1] // 3
    rows_w = r.mine.shape[1]
    L = (r.h3.shape[0] - rows_w) // 5
    per = width // cin
    t3 = jnp.sum(r.tot3[...], axis=0)
    n = mine_of(r, r.mom1[2:3, :])
    gg2, gs, ggp = (mine_of(r, t3[:, k * width : (k + 1) * width]) / n for k in range(3))
    scale2, scalep = mine_of(r, r.gain2[...] * r.mom2[1:2, :]), mine_of(r, r.gainp[...] * r.mom2[3:4, :])
    half = scale2.shape[1]
    for source, name, own, out in ((r.mine, N.mine, r.ownp, r.near), (r.far3, N.far3, r.ownp_far, r.far)):
        copies.wait(name)
        r.pad[:, 0:8, :] = jnp.zeros((3, 8, half), f32)
        r.pad[:, 8:, :] = source[...]
        for m0, m in chunks(rows_w, 96):
            mask = wide(own[2 * L + 1 + m0 : 2 * L + 1 + m0 + m, :], half)
            rows = slice(8 + m0, 8 + m0 + m)
            back = mask * gs + r.pad[1, rows, :] * gg2
            out[m0 : m0 + m, :] = (scale2 * (r.pad[0, rows, :] - back)).astype(bf16)
            mask = wide(own[2 * L + m0 : 2 * L + m0 + m, :], half)
            rows = slice(7 + m0, 7 + m0 + m)
            back = mask * gs + r.pad[2, rows, :] * ggp
            out[rows_w + m0 : rows_w + m0 + m, :] = (scalep * (r.pad[0, rows, :] - back)).astype(bf16)
    for b in range(3):
        lanes = slice(b * width, (b + 1) * width)
        copies.wait((N.h3, b), (N.h3_far, b))
        for a in range(3):
            at = L * a + L
            r.acc[...] = matmul_tn(r.h3[at : at + rows_w, lanes], r.near[:rows_w, :]) + matmul_tn(
                r.h3_far[at : at + rows_w, lanes], r.far[:rows_w, :]
            )
            split_store(r, width, cin, (3 * b + a) * per)
        copies.start(*((name, b) for name in CHUNKS))
    at = 2 * L
    copies.wait(N.xe, N.xe_far)
    middle = slice(cin, 2 * cin)
    r.acc[0:cin, :] = matmul_tn(r.xe[at : at + rows_w, middle], r.near[rows_w:, :]) + matmul_tn(
        r.xe_far[at : at + rows_w, middle], r.far[rows_w:, :]
    )
    split_store(r, cin, cin, 9 * per)
    copies.start(*((name, 3) for name in CHUNKS))
    copies.wait(*CHUNKS)


def first_back(r, gg, gs, count):
    width = r.gain.shape[1]
    U = r.act.shape[0]
    L = U - r.rows_w
    inv, n = r.mom1[1:2, :], r.mom1[2:3, :]
    gg, gs = gg / n, gs / n
    scale = r.gain[...] * inv
    r.gf[0:8, :] = jnp.zeros((8, width), f32)
    r.gf[8 + count :, :] = jnp.zeros((r.gf.shape[0] - 8 - count, width), f32)
    for m0, m in chunks(count, L):
        mask = wide(r.maskp[2 * L + 2 + m0 : 2 * L + 2 + m0 + m, :], width)
        back = mask * gs + r.normed[m0 : m0 + m, :] * gg
        r.gf[8 + m0 : 8 + m0 + m, :] = scale * (r.act[m0 : m0 + m, :] - back)


def weights_first_kernel(r, copies):
    rows_w = r.mine.shape[1]
    cin = r.xe.shape[1] // 3
    L = (r.xe.shape[0] - rows_w) // 5
    width = r.gain.shape[1]
    t4 = jnp.sum(r.tot4[...], axis=0)
    r.gain_first[...], r.shift_first[...] = t4[:, :width], t4[:, width:]
    copies.start(N.gain_first, N.shift_first)
    n = mine_of(r, r.mom1[2:3, :])
    gg, gs = mine_of(r, t4[:, :width]) / n, mine_of(r, t4[:, width:]) / n
    scale = mine_of(r, r.gain[...] * r.mom1[1:2, :])
    half = scale.shape[1]
    for source, name, own, out in ((r.mine, N.mine, r.ownp, r.near), (r.far4, N.far4, r.ownp_far, r.far)):
        copies.wait(name)
        r.pad[:, 0:8, :] = jnp.zeros((2, 8, half), f32)
        r.pad[:, 8:, :] = source[...]
        for m0, m in chunks(rows_w, 96):
            mask = wide(own[2 * L + m0 : 2 * L + m0 + m, :], half)
            rows = slice(6 + m0, 6 + m0 + m)
            back = mask * gs + r.pad[1, rows, :] * gg
            out[m0 : m0 + m, :] = (scale * (r.pad[0, rows, :] - back)).astype(bf16)
    copies.wait(N.xe, N.xe_far)
    for k, a in enumerate((1, 0, 2)):
        if k == 1:
            copies.wait(N.xo, N.xo_far)
        source, source_far = (r.xe, r.xe_far) if a == 1 else (r.xo, r.xo_far)
        at = (3 if a == 2 else 2) * L
        for b in range(3):
            lanes = slice(b * cin, (b + 1) * cin)
            r.acc[lanes, :] = matmul_tn(source[at : at + rows_w, lanes], r.near[...]) + matmul_tn(
                source_far[at : at + rows_w, lanes], r.far[...]
            )
        split_store(r, 3 * cin, cin, a * 3)
        copies.start(*((name, a) for name in CHUNKS))
    copies.wait(N.gain_first, N.shift_first, *CHUNKS)


def inputs_kernel(r, copies):
    width = r.gpu.shape[1]
    groups, rows, cols = r.out.shape[0], r.out.shape[1] // 2, r.out.shape[2] // 2
    cin = r.out.shape[3]
    M = r.gpu.shape[0]
    S = cols + 8
    L = groups * S
    lines = r.lines
    U = r.act.shape[0]
    r.rows_w = M
    copies.wait(N.act, N.normed)
    first_back(r, r.gg[...], r.gs[...], U)
    for m0, m in chunks(U, 144):
        r.gu[m0 : m0 + m, :width] = r.gf[8 + m0 : 8 + m0 + m, :].astype(bf16)
        r.gu[m0 : m0 + m, width:] = r.gf[9 + m0 : 9 + m0 + m, :].astype(bf16)
    copies.wait(N.gpu, N.w1, N.wp)

    def tap(m0, m, a, b):
        di, dj = (1 if a == 0 else 0), (1 if b == 0 else 0)
        return matmul_nt(
            r.gu[di * L + m0 : di * L + m0 + m, dj * width : (dj + 1) * width],
            r.w1[a, b * cin : (b + 1) * cin, :],
        )

    for m0, m in chunks(M, 2 * L):
        pieces = {
            (0, 0): tap(m0, m, 1, 1) + matmul_nt(r.gpu[m0 : m0 + m, :], r.wp[...]),
            (0, 1): tap(m0, m, 1, 2) + tap(m0, m, 1, 0),
            (1, 0): tap(m0, m, 2, 1) + tap(m0, m, 0, 1),
            (1, 1): tap(m0, m, 2, 2) + tap(m0, m, 2, 0) + tap(m0, m, 0, 2) + tap(m0, m, 0, 0),
        }
        for (ro, co), v in pieces.items():
            for k in range(m // S):
                line = m0 // S + k
                i, g = line // groups, line % groups
                for h in range(lines.shape[0]):
                    lines[h, (2 * i + ro) * groups + g, pl.ds(co, cols, stride=2), :] = v[
                        k * S : k * S + cols, h * 128 : (h + 1) * 128
                    ]
    for n in range(2 * rows):
        for g in range(groups):
            for h in range(lines.shape[0]):
                r.out[g, n, :, h * 128 : (h + 1) * 128] = lines[h, n * groups + g].astype(bf16)
    copies.start(N.out)
    copies.wait(N.out)


def widen(half, side, taps, per, swapped, into=None):
    total, n, m = half.shape
    extra = total - taps * per
    order = [(t % 3 * 3 + t // 3) if swapped else t for t in range(taps)]
    jobs = [(t * per, per, 0, order[t] * per) for t in range(taps)] + [(taps * per, 1, 1, 0)] * extra
    more = list(into or [])

    def body(side_ref, half_ref, *refs):
        outs = refs[len(more) : len(more) + 1 + extra]
        narrow, full, sems = refs[len(more) + 1 + extra :]
        lanes = pl.ds(pl.multiple_of(side_ref[0] * m, m), m)
        reads = [
            pltpu.make_async_copy(half_ref.at[pl.ds(at, size)], narrow.at[pl.ds(at, size)], sems.at[0, k])
            for k, (at, size, _, _) in enumerate(jobs)
        ]
        writes = [
            pltpu.make_async_copy(full.at[pl.ds(at, size)], outs[which].at[pl.ds(to, size), :, lanes], sems.at[1, k])
            for k, (at, size, which, to) in enumerate(jobs)
        ]
        for read in reads:
            read.start()
        for k, (at, size, _, _) in enumerate(jobs):
            reads[k].wait()
            full[at : at + size] = narrow[at : at + size].astype(f32)
            writes[k].start()
        for write in writes:
            write.wait()

    hbm = pl.BlockSpec(memory_space=pltpu.HBM)
    return pl.pallas_call(
        body,
        out_shape=[shape((taps * per, n, 2 * m))] + [shape((1, n, 2 * m))] * extra,
        in_specs=[pl.BlockSpec(memory_space=pltpu.SMEM)] + [hbm] * (1 + len(more)),
        out_specs=[hbm] * (1 + extra),
        scratch_shapes=[
            pltpu.VMEM((total, n, m), bf16),
            pltpu.VMEM((total, n, m), f32),
            pltpu.SemaphoreType.DMA((2, len(jobs))),
        ],
        input_output_aliases={2 + k: k for k in range(len(more))},
        compiler_params=pltpu.CompilerParams(vmem_limit_bytes=20 * 1024 * 1024),
        cost_estimate=pl.CostEstimate(flops=0, bytes_accessed=0, transcendentals=0),
    )(side.reshape(1), half, *more)


def halve_kernel(r, copies):
    for p in range(r.count):
        kept, got = getattr(r, f"kept{p}"), getattr(r, f"got{p}")
        copies.wait(f"kept{p}", f"got{p}")
        to_send, to_keep = getattr(r, f"sent{p}"), getattr(r, f"left{p}")
        bit = r.bits[r.steps[p]] == 1
        h = kept.shape[1] // 2
        for t in range(kept.shape[0]):
            total = kept[t] + got[t].astype(f32)
            low, high = total[:h], total[h:]
            to_send[t] = jnp.where(bit, low, high).astype(bf16)
            to_keep[t] = jnp.where(bit, high, low)
        copies.start(f"sent{p}", f"left{p}")
    copies.wait(*(name for name in copies.jobs if name[:4] in (N.sent, N.left)))


def halve(bits, pairs, steps, cost):
    ins = dict(bits=bits)
    for p, (kept, got) in enumerate(pairs):
        ins[f"kept{p}"], ins[f"got{p}"] = kept, got
    taps, n, m = pairs[0][0].shape
    dims = (taps, n // 2, m)
    names = [str(p) for p in range(len(pairs))]
    outs = {}
    for name in names:
        outs[N.sent + name], outs[N.left + name] = shape(dims, bf16), shape(dims)

    def body(r, copies):
        r.count, r.steps = len(pairs), steps
        halve_kernel(r, copies)

    far_in = tuple(n for n in ins if n != N.bits)
    out = call(body, ins, outs, far_in=far_in, far_out=tuple(outs), smem=(N.bits,), cost=cost, limit=60)
    return [(out[N.sent + name], out[N.left + name]) for name in names]


def shifted(value, axis, steps):
    count = lax.axis_size(axis)
    first, last = (max(0, -steps), min(count, count - steps))
    return lax.ppermute(value, axis, [(source, source + steps) for source in range(first, last)])


def gather_sum(spread):
    return lax.all_to_all(spread, axes, 0, 0)


def bit_of(axis, step):
    return (lax.axis_index(axis) // step) % 2


def partner(value, axis, step):
    count = lax.axis_size(axis)
    return lax.ppermute(value, axis, [(i, i ^ step) for i in range(count)])


def steps_of(axis):
    count, step, out = lax.axis_size(axis), 1, []
    while step < count:
        out.append((axis, step))
        step *= 2
    return out


def split(total, axis, step):
    n = total.shape[1] // 2
    bit = bit_of(axis, step) == 1
    low, high = total[:, :n], total[:, n:]
    return jnp.where(bit, low, high).astype(bf16), jnp.where(bit, high, low)


def joined(value, other, axis, step, dim=1):
    bit = bit_of(axis, step) == 1
    return jnp.concatenate([jnp.where(bit, other, value), jnp.where(bit, value, other)], axis=dim)


def gathered(pieces, spots, cost=0):
    taps, h, m = pieces[0].shape
    count = len(pieces)

    def body(spots_ref, *refs):
        out, sems = refs[count:]
        copies = []
        for q in range(count):
            rows = pl.ds(pl.multiple_of(spots_ref[q] * h, h), h)
            copies.append(pltpu.make_async_copy(refs[q], out.at[:, rows], sems.at[q]))
        for copy in copies:
            copy.start()
        for copy in copies:
            copy.wait()

    anywhere = pl.BlockSpec(memory_space=pl.ANY)
    return pl.pallas_call(
        body,
        out_shape=shape((taps, count * h, m), pieces[0].dtype),
        in_specs=[pl.BlockSpec(memory_space=pltpu.SMEM)] + [anywhere] * count,
        out_specs=anywhere,
        scratch_shapes=[pltpu.SemaphoreType.DMA((count,))],
        compiler_params=pltpu.CompilerParams(vmem_limit_bytes=16 * 1024 * 1024),
        cost_estimate=pl.CostEstimate(flops=cost, bytes_accessed=0, transcendentals=0),
    )(spots, *pieces)


class Tree:
    def __init__(self, parts, bits, plane, rest, core):
        self.bits, self.place = bits, {step: k for k, step in enumerate([core, *plane, *rest])}
        self.sent_a, self.kept_a, self.sent_b, self.kept_b = parts
        self.a, self.b, self.rest, self.core = plane, plane[::-1], rest, core
        p, n = len(plane), len(rest)
        self.stages = [(N.plane, k) for k in range(p)] + [(N.rest, k) for k in range(n)]
        self.stages += [(N.rest_join, k) for k in reversed(range(n))] + [(N.plane_join, k) for k in reversed(range(p))]
        self.stages += [(N.core, 0)]

    def next(self):
        return self.stages[0] if self.stages else None

    def start(self):
        kind, k = self.stages[0]
        if kind == N.plane:
            self.got = partner(self.sent_a, *self.a[k]), partner(self.sent_b, *self.b[k])
        elif kind == N.rest:
            self.got = (partner(self.sent, *self.rest[k]),)
        elif kind == N.rest_join:
            self.got = (partner(self.value, *self.rest[k]),)
        elif kind == N.plane_join:
            self.got = partner(self.value_a, *self.a[k]), partner(self.value_b, *self.b[k])
        else:
            self.got = (partner(self.value, *self.core),)

    def finish(self, cost=0):
        kind, k = self.stages.pop(0)
        if kind == N.plane:
            pairs = [(self.kept_a, self.got[0]), (self.kept_b, self.got[1])]
            nexts = [order[k + 1] for order in (self.a, self.b) if k + 1 < len(order)]
            if nexts and cost:
                pairs = halve(self.bits, pairs, [self.place[step] for step in nexts], cost)
                (self.sent_a, self.kept_a), (self.sent_b, self.kept_b) = pairs
                return
            total_a, total_b = (kept + got.astype(f32) for kept, got in pairs)
            if nexts:
                self.sent_a, self.kept_a = split(total_a, *nexts[0])
                self.sent_b, self.kept_b = split(total_b, *nexts[1])
            else:
                self.taps = total_a.shape[0]
                self.split_rest(jnp.concatenate([total_a, total_b], axis=0), 0)
        elif kind == N.rest:
            self.split_rest(self.kept + self.got[0].astype(f32), k + 1)
        elif kind == N.rest_join:
            self.value = joined(self.value, self.got[0], *self.rest[k])
            self.value_a, self.value_b = self.value[: self.taps], self.value[self.taps :]
        elif kind == N.plane_join:
            if k == 0 and cost:
                low, high = (self.bits[self.place[step]] for step in (self.a[0], self.b[0]))
                spots = jnp.stack([low, 1 - low, 2 + high, 3 - high])
                self.value = gathered([self.value_a, self.got[0], self.value_b, self.got[1]], spots, cost)
            else:
                self.value_a = joined(self.value_a, self.got[0], *self.a[k])
                self.value_b = joined(self.value_b, self.got[1], *self.b[k])
                self.value = jnp.concatenate([self.value_a, self.value_b], axis=1)

    def split_rest(self, total, k):
        if k < len(self.rest):
            self.sent, self.kept = split(total, *self.rest[k])
        else:
            self.value = total.astype(bf16)


def lockstep(*trees, beside=()):
    for t in trees:
        t.start()
    got, beside = lax.optimization_barrier(([t.got for t in trees], beside))
    for t, g in zip(trees, got):
        t.got = g
        t.finish()
    return beside


def on_device(inputs, w_first, gain_first, shift_first, w_second, gain_second, shift_second, w_proj, gain_proj, shift_proj, valid_mask, cotangent):
    groups, rows_in, cols_in, cin = inputs.shape
    rows, cols = rows_in // 2, cols_in // 2
    width = w_first.shape[3]
    half = width // 2
    S = cols + 8
    L = groups * S
    devices = lax.axis_size(N.rows) * lax.axis_size(N.cols) * lax.axis_size(N.grp)
    plane = steps_of(N.cols)
    core = steps_of(N.rows)[0]
    rest = steps_of(N.rows)[1:] + steps_of(N.grp)
    bits = jnp.stack([bit_of(*step) for step in (core, *plane, *rest)]).astype(jnp.int32)
    w1 = w_first.reshape(3, 3 * cin, width)
    w2 = w_second.reshape(3, 3 * width, width)
    as_row = lambda v: v.reshape(1, -1)
    own = jnp.broadcast_to(valid_mask.astype(bf16)[..., None], valid_mask.shape + (128,))
    MP, MQ, MU, MW = (rows + 5) * L, (rows + 3) * L, (rows + 1) * L, rows * L
    px = lambda m, k: 2 * m * k * width
    vec = lambda k: shape((1, k * width))
    all_devices = lambda k: shape((devices, 1, k))
    g1, b1, g2, b2, gp, bp = map(
        as_row, (gain_first, shift_first, gain_second, shift_second, gain_proj, shift_proj)
    )

    top1 = shifted(inputs[:, -1:], N.rows, 1)
    me, count = lax.axis_index(N.rows), lax.axis_size(N.rows)
    flags = jnp.stack([me > 0, me < count - 1]).astype(jnp.int32)
    flat_rows = shape((over * groups * cols_in + (width // 256 + 1) * rim * groups * cols, 256), bf16)
    packed = call(
        vertical_kernel,
        dict(flags=flags, x=inputs, cot=cotangent, own=own),
        dict(down=flat_rows) if count == 2 else dict(down=flat_rows, up=flat_rows),
        far_in=(N.x, N.cot),
        smem=(N.flags,),
        parts=dict(x=end_parts(rows_in, over), cot=end_parts(rows, rim)),
    )
    if count == 2:
        top = bot = lax.ppermute(packed["down"], "rows", [(0, 1), (1, 0)])
    else:
        top, bot = shifted(packed[N.down], N.rows, 1), shifted(packed[N.up], N.rows, -1)
    (top, bot), top1 = lax.optimization_barrier(((top, bot), top1))
    lines = (rows_in + 2 * over) * groups, (rows + 2 * rim) * groups, (rows + 3) * groups
    n_strip = over * lines[0] + (rim + 1) // 2 * lines[1] + width // 128 * lines[2]
    n_strip = -(-n_strip // 16) * 16
    near = dict(flags=flags, x=inputs, cot=cotangent, own=own, top=top, bot=bot)
    strips = call(
        strips_kernel,
        near,
        dict(right=shape((n_strip, 256), bf16), left=shape((n_strip, 256), bf16)),
        dict(
            raw_x=pltpu.VMEM((cin // 128, lines[0] * cols_in, 128), f32),
            raw_m=pltpu.VMEM((1, lines[1] * cols, 128), f32),
            raw_c=pltpu.VMEM((width // 128, lines[2] * cols, 128), f32),
            flat=pltpu.VMEM((n_strip, 256), f32),
        ),
        smem=(N.flags,),
    )
    edge = jnp.concatenate([top1[:, :, -1:], inputs[:, :, -1:]], axis=1)
    edge, right, left = lax.optimization_barrier((edge, strips[N.right], strips[N.left]))
    lft1, right, left = lax.optimization_barrier((shifted(edge, N.cols, 1), right, left))
    lft, rgt = shifted(right, N.cols, 1), shifted(left, N.cols, -1)
    stats = call(
        stats_kernel,
        dict(x=inputs, top=top1, lft=lft1, own=own, w1=w1, wp=w_proj),
        dict(spread=all_devices(4 * width + 128)),
        dict(
            raw=pltpu.VMEM((cin // 128, (rows_in + 1) * groups, cols_in + 8, 128), f32),
            xe=pltpu.VMEM((rows * groups * cols, 3 * cin), bf16),
            xo=pltpu.VMEM(((rows + 1) * groups * cols, 3 * cin), bf16),
        ),
        far_in=(N.w1,),
        far_out=(N.spread,),
    )
    tot1 = gather_sum(stats[N.spread])

    first = call(
        first_kernel,
        dict(**near, lft=lft, rgt=rgt, w1=w1, wp=w_proj),
        dict(
            pre1=shape((MP, width)),
            prep=shape((MP, width)),
            xe=shape((MP, 3 * cin), bf16),
            xo=shape((MP + L, 3 * cin), bf16),
            ownp=shape((MP, 128)),
            maskp=shape((MP, 128)),
            cotq=shape((MQ, width)),
        ),
        dict(
            raw_x=pltpu.VMEM((cin // 128, lines[0] * (cols_in + 24), 128), f32),
            raw_m=pltpu.VMEM((1, lines[1] * (cols + 16), 128), f32),
            raw_c=pltpu.VMEM((width // 128, lines[2] * (cols + 16), 128), f32),
            flat=pltpu.VMEM((n_strip, 256), f32),
        ),
        far_in=(N.w1, N.wp),
        far_out=(N.xe, N.xo, N.pre1, N.prep, N.cotq),
        smem=(N.flags,),
        cost=20000000000,
        parts=dict(pre1=row_parts(MP, 3), prep=row_parts(MP, 3)),
    )
    xe, xo, ownp, maskp = first[N.xe], first[N.xo], first[N.ownp], first[N.maskp]
    far_xe, far_xo = partner(xe, *core), partner(xo, *core)

    second = call(
        second_kernel,
        dict(pre1=first[N.pre1], tot1=tot1, gain=g1, shift=b1, maskp=maskp, ownp=ownp, w2=w2),
        dict(h3=shape((MP, 3 * width), bf16), pre2=shape((MQ, width)), spread=all_devices(2 * width), mom1=shape((8, width))),
        dict(hid=pltpu.VMEM((MP + 8, width), f32)),
        far_in=(N.pre1, N.w2),
        far_out=(N.h3, N.pre2, N.spread),
        parts=dict(pre2=row_parts(MQ, 3)),
    )
    h3, pre2, mom1 = second[N.h3], second[N.pre2], second[N.mom1]
    tot2 = gather_sum(second[N.spread])
    tot2, far_h3 = lax.optimization_barrier((tot2, partner(h3, *core)))

    third = call(
        third_kernel,
        dict(
            bits=bits, pre2=pre2, prep=first[N.prep], mom1=mom1, tot2=tot2, gain2=g2, shift2=b2, gainp=gp, shiftp=bp,
            maskp=maskp, ownp=ownp, cotq=first[N.cotq],
        ),
        dict(
            out=shape((groups, rows, cols, width), bf16),
            grad=shape((MQ, width)),
            spread=all_devices(3 * width),
            mom2=shape((8, width)),
            mine=shape((3, MW, half)),
            theirs=shape((3, MW, half)),
        ),
        dict(field=pltpu.VMEM((MQ, width), f32)),
        far_in=(N.pre2, N.prep, N.cotq),
        far_out=(N.grad, N.spread, N.mine, N.theirs, N.out),
        smem=(N.bits,),
        parts=dict(
            mine=middle_parts(MW, 2), theirs=middle_parts(MW, 2),
            grad=row_parts(MQ, 2), pre2=row_parts(MQ, 2), cotq=row_parts(MQ, 2), prep=cuts(L, L + MQ // 2 + 8, L + MQ + 8)
        ),
    )
    mom2 = third[N.mom2]
    tot3 = gather_sum(third[N.spread])
    ownp_here, far3 = lax.optimization_barrier((ownp, partner(third[N.theirs], *core)))
    ownp_far = partner(ownp_here, *core)

    def chunk_shapes(taps):
        dims = (taps, cin // 4, half)
        return dict(sent_a=shape(dims, bf16), kept_a=shape(dims), sent_b=shape(dims, bf16), kept_b=shape(dims))

    per = width // cin
    taps2 = 9 * per + 1
    second_parts = call(
        weights_second_kernel,
        dict(
            bits=bits, mine=third[N.mine], far3=far3, h3=h3, h3_far=far_h3, xe=xe, xe_far=far_xe,
            tot3=tot3, mom1=mom1, mom2=mom2, gain2=g2, gainp=gp, ownp=ownp, ownp_far=ownp_far,
        ),
        chunk_shapes(taps2),
        dict(
            acc=pltpu.VMEM((width, half), f32),
            pad=pltpu.VMEM((3, MW + 8, half), f32),
            near=pltpu.VMEM((2 * MW, half), bf16),
            far=pltpu.VMEM((2 * MW, half), bf16),
        ),
        far_in=(N.mine, N.far3, N.h3, N.h3_far, N.xe, N.xe_far),
        far_out=CHUNKS,
        smem=(N.bits,),
        parts=dict(
            h3=lane_parts(3 * width, 3, pl.ds(L, MW + 2 * L)),
            h3_far=lane_parts(3 * width, 3, pl.ds(L, MW + 2 * L)),
            xe=[(0, (pl.ds(2 * L, MW), pl.ds(cin, cin)))],
            xe_far=[(0, (pl.ds(2 * L, MW), pl.ds(cin, cin)))],
            **{name: row_parts(taps2 - 1, 3) + [(3, (pl.ds(taps2 - 1, 1),))] for name in CHUNKS},
        ),
    ).values()
    grad, *second_parts = lax.optimization_barrier((third[N.grad], *second_parts))
    tree2 = Tree(second_parts, bits, plane, rest, core)
    tree2.start()
    hidden = call(
        fourth_kernel,
        dict(
            bits=bits, grad=grad, pre2=pre2, keep=first[N.pre1], w2=w2, prep=first[N.prep], mom1=mom1, mom2=mom2, tot3=tot3,
            gain=g1, shift=b1, gain2=g2, gainp=gp, maskp=maskp, ownp=ownp,
        ),
        dict(
            act=shape((MU, width)), normed=shape((MU, width)), spread=all_devices(2 * width),
            mine=shape((2, MW, half)), theirs=shape((2, MW, half)), gpu=shape((MW, width), bf16),
            gain_second=vec(1), shift_second=vec(1), gain_proj=vec(1), shift_proj=vec(1),
        ),
        dict(
            gq=pltpu.VMEM((MQ + 8, width), f32),
            g3=pltpu.VMEM((MQ, 3 * width), bf16),
            gh=pltpu.VMEM((MU, width), f32),
        ),
        far_in=(N.grad, N.pre2, N.keep, N.w2, N.prep),
        far_out=(
            N.act, N.normed, N.spread, N.mine, N.theirs, N.gpu, N.gain_second, N.shift_second, N.gain_proj, N.shift_proj
        ),
        smem=(N.bits,),
        limit=52,
        parts=dict(
            grad=cuts(0, 6 * L, MQ),
            pre2=cuts(0, 6 * L, MQ),
            keep=cuts(2 * L, 2 * L + MU + 8),
            w2=[(k, (pl.ds(2 - k, 1),)) for k in range(3)],
            prep=cuts(2 * L, 2 * L + MW + 8),
            mine=row_parts(2, 2),
            theirs=row_parts(2, 2),
        ),
    )
    tot4 = gather_sum(hidden[N.spread])
    tree2.finish(20000000000)
    near1, tree2.sent_a, tree2.sent_b = lax.optimization_barrier((hidden[N.mine], tree2.sent_a, tree2.sent_b))
    tree2.start()
    fifth = call(
        weights_first_kernel,
        dict(
            bits=bits, mine=near1, far4=partner(hidden[N.theirs], *core), xe=xe, xe_far=far_xe, xo=xo, xo_far=far_xo,
            tot4=tot4, mom1=mom1, gain=g1, ownp=ownp, ownp_far=ownp_far,
        ),
        dict(**chunk_shapes(9), gain_first=vec(1), shift_first=vec(1)),
        dict(
            acc=pltpu.VMEM((3 * cin, half), f32),
            pad=pltpu.VMEM((2, MW + 8, half), f32),
            near=pltpu.VMEM((MW, half), bf16),
            far=pltpu.VMEM((MW, half), bf16),
        ),
        far_in=(N.mine, N.far4, N.xe, N.xe_far, N.xo, N.xo_far),
        cost=20000000000,
        far_out=(*CHUNKS, N.gain_first, N.shift_first),
        smem=(N.bits,),
        parts=dict(
            xe=cuts(2 * L, 2 * L + MW),
            xe_far=cuts(2 * L, 2 * L + MW),
            xo=cuts(2 * L, 3 * L + MW),
            xo_far=cuts(2 * L, 3 * L + MW),
            **{name: row_parts(9, 3) for name in CHUNKS},
        ),
    )
    first_parts = [fifth[name] for name in CHUNKS]
    tree2.got, *first_parts = lax.optimization_barrier((tree2.got, *first_parts))
    tree2.finish()
    tree1 = Tree(first_parts, bits, plane, rest, core)

    grad_inputs = call(
        inputs_kernel,
        dict(
            act=hidden[N.act], normed=hidden[N.normed], gpu=hidden[N.gpu], w1=w1, wp=w_proj, mom1=mom1, gain=g1, maskp=maskp,
            gg=fifth[N.gain_first], gs=fifth[N.shift_first],
        ),
        dict(out=shape((groups, rows_in, cols_in, cin), bf16)),
        dict(
            lines=pltpu.VMEM((cin // 128, rows_in * groups, cols_in, 128), f32),
            gf=pltpu.VMEM((MU + 16, width), f32),
            gu=pltpu.VMEM((MU, 2 * width), bf16),
        ),
        far_in=(N.act, N.normed, N.gpu, N.w1, N.wp),
        far_out=(N.out,),
        cost=10000000000,
    )[N.out]
    side = bit_of(*core).astype(jnp.int32)
    grad_inputs = lockstep(tree2, tree1, beside=grad_inputs)
    while tree2.next() != (N.plane_join, 0):
        lockstep(tree2, tree1)
    tree2.start()
    while tree1.next() != (N.plane_join, 0):
        tree1.start()
        if tree1.next() != (N.plane_join, 1):
            tree1.finish()
        else:
            tree1.got, tree2.got = lax.optimization_barrier((tree1.got, tree2.got))
            tree1.finish()
    tree2.finish()
    tree2.start()
    tree1.start()
    grad_second = widen(tree2.got[0], 1 - side, 9, per, True, widen(tree2.value, side, 9, per, True))
    tree1.got, grad_second = lax.optimization_barrier((tree1.got, grad_second))
    grad_w2, grad_wp = grad_second
    tree1.finish(1)
    tree1.start()
    (grad_w1,) = widen(tree1.got[0], 1 - side, 3, 3, False, widen(tree1.value, side, 3, 3, False))

    return (
        third[N.out],
        grad_inputs,
        grad_w1.reshape(w_first.shape),
        fifth[N.gain_first].reshape(width),
        fifth[N.shift_first].reshape(width),
        grad_w2.reshape(w_second.shape),
        hidden[N.gain_second].reshape(width),
        hidden[N.shift_second].reshape(width),
        grad_wp.reshape(w_proj.shape),
        hidden[N.gain_proj].reshape(width),
        hidden[N.shift_proj].reshape(width),
    )


def solution(mesh):
    spread = P("grp", "rows", "cols", None)
    return jax.shard_map(
        on_device,
        mesh=mesh,
        in_specs=(spread,) + (P(),) * 9 + (P("grp", "rows", "cols"), spread),
        out_specs=(spread, spread) + (P(),) * 9,
        check_vma=False,
    )
```

```python
import functools

import jax
import jax.numpy as jnp
from jax import lax
from jax.experimental import pallas as pl
from jax.experimental.pallas import tpu as pltpu
from jax.sharding import PartitionSpec as P

epsilon = 1e-05
axes = ("rows", "cols", "grp")
bf16 = jnp.bfloat16
f32 = jnp.float32
inner = 0.7978845608028654
cubic = 0.044715
over = 6
CHUNKS = "sent_a", "kept_a", "sent_b", "kept_b"
rim = 3


class Names:
    def __getattr__(self, name):
        return name


N = Names()


class Refs:
    def __init__(self, named):
        self.__dict__.update(named)


class Copies:
    def __init__(self, parts, pairs, sems):
        self.jobs = {}
        for k, (name, index) in enumerate(parts):
            source, target = pairs[name]
            if index:
                source, target = source.at[index[1]], target.at[index[1]]
            self.jobs.setdefault(name, []).append(pltpu.make_async_copy(source, target, sems.at[k]))

    def start(self, *names):
        for name, *which in map(named, names):
            for job in self.jobs[name][slice(*which) if which else slice(None)]:
                job.start()

    def start_all(self, names):
        for k in range(max((len(self.jobs[n]) for n in names), default=0)):
            for n in names:
                if k < len(self.jobs[n]):
                    self.jobs[n][k].start()

    def wait(self, *names):
        for name, *which in map(named, names):
            for job in self.jobs[name][slice(*which) if which else slice(None)]:
                job.wait()


def named(name):
    return (name,) if isinstance(name, str) else (name[0], name[1], name[1] + 1)


def row_parts(total, count):
    size = total // count
    return [(k, (pl.ds(k * size, size),)) for k in range(count)]


def middle_parts(total, count):
    size = total // count
    return [(k, (slice(None), pl.ds(k * size, size))) for k in range(count)]


def end_parts(total, size):
    return [(k, (slice(None), pl.ds(at, size))) for k, at in enumerate((0, total - size))]


def cuts(*at):
    return [(k, (pl.ds(a, b - a),)) for k, (a, b) in enumerate(zip(at, at[1:]))]


def lane_parts(total, count, rows=slice(None)):
    size = total // count
    return [(k, (rows, pl.ds(k * size, size))) for k in range(count)]


def call(body, ins, outs, scratch=None, far_in=(), far_out=(), smem=(), parts=None, limit=52, cost=0):
    scratch, parts = scratch or {}, parts or {}
    far = (*far_in, *far_out)
    jobs = [(name, index) for name in far for index in parts.get(name, [None])]

    def spec(name):
        if name in smem:
            return pl.BlockSpec(memory_space=pltpu.SMEM)
        return pl.BlockSpec(memory_space=pltpu.HBM if name in far else pltpu.VMEM)

    kinds = {**{n: shape(v.shape, v.dtype) for n, v in ins.items()}, **outs}

    def run(*refs):
        plain = dict(zip([*ins, *outs], refs))
        rest = refs[len(plain) :]
        buffers = dict(zip(far, rest))
        more = dict(zip(scratch, rest[len(far) :]))
        copies = None
        if far:
            pairs = {n: (plain[n], buffers[n]) if n in far_in else (buffers[n], plain[n]) for n in far}
            copies = Copies(jobs, pairs, rest[-1])
            copies.start_all(far_in)
        body(Refs({**plain, **buffers, **more}), copies)

    buffers = [pltpu.VMEM(kinds[n].shape, kinds[n].dtype) for n in far]
    sems = [pltpu.SemaphoreType.DMA((len(jobs),))] if far else []
    result = pl.pallas_call(
        run,
        out_shape=list(outs.values()),
        in_specs=[spec(n) for n in ins],
        out_specs=[spec(n) for n in outs],
        scratch_shapes=[*buffers, *scratch.values(), *sems],
        compiler_params=pltpu.CompilerParams(vmem_limit_bytes=limit * 1024 * 1024),
        cost_estimate=pl.CostEstimate(flops=cost, bytes_accessed=0, transcendentals=0),
    )(*ins.values())
    return dict(zip(outs, result))


def shape(dims, dtype=f32):
    return jax.ShapeDtypeStruct(dims, dtype)


def wide(mask, width):
    return jnp.concatenate([mask] * (width // mask.shape[1]), axis=1)


def matmul(a, b):
    return lax.dot_general(a, b, (((1,), (0,)), ((), ())), preferred_element_type=f32)


def matmul_nt(a, b):
    return lax.dot_general(a, b, (((1,), (1,)), ((), ())), preferred_element_type=f32)


def matmul_tn(a, b):
    return lax.dot_general(a, b, (((0,), (0,)), ((), ())), preferred_element_type=f32)


def gelu_parts(v):
    return jnp.tanh(inner * (v + cubic * v * v * v))


def gelu_slope(v, t):
    return 0.5 * (1.0 + t) + 0.5 * v * (1.0 - t * t) * (inner * (1.0 + 3.0 * cubic * v * v))


def column_sum(v):
    return jnp.sum(v, axis=0, keepdims=True)


def moments(total, squares, pixel_count):
    center = total / pixel_count
    spread = squares / pixel_count - center * center
    return center, lax.rsqrt(spread + epsilon)


def chunks(total, size):
    return [(at, min(size, total - at)) for at in range(0, total, size)]


def strided(ref, k, first, count, step):
    return ref[k, pl.ds(first, count, stride=step), :]


def vertical_kernel(r, copies):
    groups, width = r.x.shape[0], r.cot.shape[3]
    rows, cols = r.own.shape[1], r.own.shape[2]

    def pack(out, input_row, row, pick):
        at = 0
        for g in range(groups):
            for n in range(over):
                value = r.x[g, input_row(n)]
                out[at : at + 2 * cols, :] = pick(value, r.x[g, n])
                at += 2 * cols
        for k in range(0, width, 256):
            for g in range(groups):
                for n in range(rim):
                    lanes = slice(k, k + 256)
                    out[at : at + cols, :] = pick(r.cot[g, row(n), :, lanes], r.cot[g, n, :, lanes])
                    at += cols
        for g in range(groups):
            for n in range(rim):
                out[at : at + cols, :] = pick(wide(r.own[g, row(n)], 256), wide(r.own[g, n], 256))
                at += cols

    last = r.x.shape[1] - over
    copies.wait(N.x, N.cot)
    if hasattr(r, N.up):
        pack(r.down, lambda n: last + n, lambda n: rows - rim + n, lambda tail, head: tail)
        pack(r.up, lambda n: last + n, lambda n: rows - rim + n, lambda tail, head: head)
    else:
        bottom = r.flags[0] == 1
        pack(r.down, lambda n: last + n, lambda n: rows - rim + n, lambda tail, head: jnp.where(bottom, head, tail))


def rim_rows(r, own, n_own, n_rim, base, cols, split):
    groups = own.shape[0]
    size = groups * n_rim * cols

    def flat(ref, g, n):
        at = [base + k * size + (g * n_rim + n) * cols for k in range(split)]
        return jnp.concatenate([ref[p : p + cols, :] for p in at], axis=1).astype(f32)

    def read(g, n):
        if n < n_rim:
            return jnp.where(r.flags[0] == 1, flat(r.top, g, n), 0.0)
        if n < n_rim + n_own:
            return own[g, n - n_rim].astype(f32)
        return jnp.where(r.flags[1] == 1, flat(r.bot, g, n - n_rim - n_own), 0.0)

    return read


def fields(r):
    groups, width = r.x.shape[0], r.cot.shape[3]
    rows, cols = r.own.shape[1], r.own.shape[2]
    base = over * groups * 2 * cols
    piece = rim * groups * cols
    blocks = width // 256
    x = rim_rows(r, r.x, 2 * rows, over, 0, 2 * cols, 1)
    mask = rim_rows(r, r.own, rows, rim, base + blocks * piece, cols, 1)
    cot = rim_rows(r, r.cot, rows, rim, base, cols, blocks)
    return x, lambda g, n: mask(g, n)[:, :128], cot


def strips_kernel(r, copies):
    groups, width = r.x.shape[0], r.cot.shape[3]
    rows, cols = r.own.shape[1], r.own.shape[2]
    x, mask, cot = fields(r)
    lines = (2 * rows + 2 * over) * groups, (rows + 2 * rim) * groups, (rows + 3) * groups
    for raw, read, first, count, w in (
        (r.raw_x, x, 0, lines[0], 2 * cols),
        (r.raw_m, mask, 0, lines[1], cols),
        (r.raw_c, cot, 2, lines[2], cols),
    ):
        for at in range(count):
            value = read(at % groups, at // groups + first)
            for k in range(raw.shape[0]):
                raw[k, at * w : (at + 1) * w, :] = value[:, k * 128 : (k + 1) * 128]
    for out, x0, m0, c0 in ((r.right, 2 * cols - over, cols - rim, cols - 2), (r.left, 0, 0, 0)):
        pieces = []
        for c in range(over):
            pieces.append([strided(r.raw_x, k, x0 + c, lines[0], 2 * cols) for k in range(2)])
        for c in range(0, rim + 1, 2):
            pieces.append([strided(r.raw_m, 0, m0 + min(c + k, rim - 1), lines[1], cols) for k in range(2)])
        for c in range(2):
            for h in range(0, width // 128, 2):
                pieces.append([strided(r.raw_c, h + k, c0 + c, lines[2], cols) for k in range(2)])
        at = 0
        for low, high in pieces:
            r.flat[at : at + low.shape[0], :] = jnp.concatenate([low, high], axis=1)
            at += low.shape[0]
        if at < r.flat.shape[0]:
            r.flat[at:, :] = jnp.zeros((r.flat.shape[0] - at, 256), f32)
        out[...] = r.flat[...].astype(bf16)


def stats_kernel(r, copies):
    groups, cin = r.x.shape[0], r.x.shape[3]
    rows, S = r.own.shape[1], r.own.shape[2]
    L = groups * S
    width = r.w1.shape[2]
    raw = r.raw
    for n in range(2 * rows + 1):
        for g in range(groups):
            line = n * groups + g
            src = (r.top[g, 0] if n == 0 else r.x[g, n - 1]).astype(f32)
            side = r.lft[g, n].astype(f32)
            for k in range(raw.shape[0]):
                raw[k, line, 7:8, :] = side[:, k * 128 : (k + 1) * 128]
                raw[k, line, 8:, :] = src[:, k * 128 : (k + 1) * 128]
    for out, n_rows, start in ((r.xe, rows, 1), (r.xo, rows + 1, 0)):
        for n in range(n_rows):
            for b in range(3):
                for k in range(raw.shape[0]):
                    parts = [
                        raw[k, (2 * n + start) * groups + g, pl.ds(7 + b, S, stride=2), :]
                        for g in range(groups)
                    ]
                    at = b * cin + k * 128
                    out[n * L : (n + 1) * L, at : at + 128] = jnp.concatenate(
                        parts, axis=0
                    ).astype(bf16)
    mask = jnp.concatenate(
        [r.own[g, i].astype(f32) for i in range(rows) for g in range(groups)], axis=0
    )
    M = rows * L
    copies.wait(N.w1)
    z = matmul(r.xo[0:M, :], r.w1[0])
    z += matmul(r.xe[...], r.w1[1])
    z += matmul(r.xo[L : L + M, :], r.w1[2])
    zp = matmul(r.xe[:, cin : 2 * cin], r.wp[...])
    zm, zpm = z * wide(mask, width), zp * wide(mask, width)
    row = jnp.concatenate([column_sum(zm), column_sum(zm * z), column_sum(mask)], axis=1)
    r.spread[...] = jnp.broadcast_to(row[None], r.spread.shape)
    copies.start(N.spread)
    r.psum[...] = jnp.concatenate([column_sum(zpm), column_sum(zpm * zp)], axis=1)
    copies.start(N.psum)
    copies.wait(N.spread, N.psum)


def first_kernel(r, copies):
    groups, cin, width = r.x.shape[0], r.x.shape[3], r.cot.shape[3]
    rows, cols = r.own.shape[1], r.own.shape[2]
    S = cols + 8
    L = groups * S
    W = 2 * cols + 24
    V = cols + 16
    x, mask, cot = fields(r)
    lines = (2 * rows + 2 * over) * groups, (rows + 2 * rim) * groups, (rows + 3) * groups
    tail = jnp.zeros((W - 8 - 2 * cols, 128), f32)
    r.raw_m[...] = jnp.zeros(r.raw_m.shape, f32)
    r.raw_c[...] = jnp.zeros(r.raw_c.shape, f32)
    for at in range(lines[0]):
        value = x(at % groups, at // groups)
        for k in range(r.raw_x.shape[0]):
            r.raw_x[k, at * W + 8 : at * W + 8 + 2 * cols, :] = value[:, k * 128 : (k + 1) * 128]
            r.raw_x[k, at * W + 8 + 2 * cols : (at + 1) * W, :] = tail
    for strip, x0, m0, c0 in ((r.lft, 8 - over, 8 - rim, 6), (r.rgt, 8 + 2 * cols, 8 + cols, 8 + cols)):
        r.flat[...] = strip[...].astype(f32)
        at = 0
        for c in range(over):
            for k in range(2):
                r.raw_x[k, pl.ds(x0 + c, lines[0], stride=W), :] = r.flat[at : at + lines[0], k * 128 : (k + 1) * 128]
            at += lines[0]
        for c in range(0, rim + 1, 2):
            for k in range(2):
                if c + k < rim:
                    r.raw_m[0, pl.ds(m0 + c + k, lines[1], stride=V), :] = r.flat[
                        at : at + lines[1], k * 128 : (k + 1) * 128
                    ]
            at += lines[1]
        for c in range(2):
            for h in range(0, width // 128, 2):
                for k in range(2):
                    r.raw_c[h + k, pl.ds(c0 + c, lines[2], stride=V), :] = r.flat[
                        at : at + lines[2], k * 128 : (k + 1) * 128
                    ]
                at += lines[2]
    for out, n_rows, start in ((r.xe, rows + 5, 2), (r.xo, rows + 6, 1)):
        for n in range(n_rows):
            for b in range(3):
                for k in range(r.raw_x.shape[0]):
                    parts = [
                        strided(r.raw_x, k, ((2 * n + start) * groups + g) * W + 3 + b, S, 2) for g in range(groups)
                    ]
                    at = b * cin + k * 128
                    out[n * L : (n + 1) * L, at : at + 128] = jnp.concatenate(parts, axis=0).astype(bf16)
    copies.start(N.xe, N.xo)
    for at in range(lines[1]):
        r.raw_m[0, at * V + 8 : at * V + 8 + cols, :] = mask(at % groups, at // groups)
    for n in range(1, rows + 6):
        for g in range(groups):
            to, at = (n - 1) * L + g * S, (n * groups + g) * V
            r.maskp[to : to + S, :] = r.raw_m[0, at + 6 : at + 6 + S, :]
    for at in range(lines[2]):
        value = cot(at % groups, at // groups + 2)
        for k in range(r.raw_c.shape[0]):
            lanes = slice(k * 128, (k + 1) * 128)
            r.raw_c[k, at * V + 8 : at * V + 8 + cols, :] = value[:, lanes]
            r.cotq[at * S : (at + 1) * S, lanes] = r.raw_c[k, at * V + 7 : at * V + 7 + S, :]
    copies.start(N.cotq)
    r.ownp[...] = jnp.zeros(r.ownp.shape, f32)
    for i in range(rows):
        for g in range(groups):
            at = (i + 2) * L + g * S + 2
            r.ownp[at : at + cols, :] = r.own[g, i].astype(f32)
    copies.wait(N.w1, N.wp)
    for k, (m0, m) in enumerate(chunks(r.pre1.shape[0], r.pre1.shape[0] // 3)):
        z = matmul(r.xo[m0 : m0 + m, :], r.w1[0])
        z += matmul(r.xe[m0 : m0 + m, :], r.w1[1])
        z += matmul(r.xo[L + m0 : L + m0 + m, :], r.w1[2])
        r.pre1[m0 : m0 + m, :] = z
        copies.start((N.pre1, k))
        r.prep[m0 : m0 + m, :] = matmul(r.xe[m0 : m0 + m, cin : 2 * cin], r.wp[...])
        copies.start((N.prep, k))
    copies.wait(N.xe, N.xo, N.pre1, N.prep, N.cotq)


def second_kernel(r, copies):
    width = r.gain.shape[1]
    t = jnp.sum(r.tot1[...], axis=0)
    n = wide(t[:, 2 * width :], width)
    center, inv = moments(t[:, :width], t[:, width : 2 * width], n)
    r.mom1[...] = jnp.concatenate([center, inv, n, jnp.zeros((5, width), f32)], axis=0)
    scale = inv * r.gain[...]
    M, Q = r.pre1.shape[0], r.pre2.shape[0]
    L = (M - Q) // 2
    copies.wait(N.pre1)
    for m0, m in chunks(M, 104):
        v = (r.pre1[m0 : m0 + m, :] - center) * scale + r.shift[...]
        mask = wide(r.maskp[m0 : m0 + m, :], width)
        r.hid[m0 : m0 + m, :] = 0.5 * v * (1.0 + gelu_parts(v)) * mask
    r.hid[M:, :] = jnp.zeros((r.hid.shape[0] - M, width), f32)
    for m0, m in chunks(M, 208):
        for b in range(3):
            r.h3[m0 : m0 + m, b * width : (b + 1) * width] = r.hid[m0 + b : m0 + b + m, :].astype(bf16)
    copies.start(N.h3)
    copies.wait(N.w2)
    sums = [jnp.zeros((1, width), f32)] * 2
    for k, (m0, m) in enumerate(chunks(Q, Q // 3)):
        z = matmul(r.h3[m0 : m0 + m, :], r.w2[0])
        z += matmul(r.h3[L + m0 : L + m0 + m, :], r.w2[1])
        z += matmul(r.h3[2 * L + m0 : 2 * L + m0 + m, :], r.w2[2])
        r.pre2[m0 : m0 + m, :] = z
        copies.start((N.pre2, k))
        zm = z * wide(r.ownp[L + 1 + m0 : L + 1 + m0 + m, :], width)
        sums = [sums[0] + column_sum(zm), sums[1] + column_sum(zm * z)]
    row = jnp.concatenate([*sums, r.psum[...]], axis=1)
    r.spread[...] = jnp.broadcast_to(row[None], r.spread.shape)
    copies.start(N.spread)
    copies.wait(N.h3, N.pre2, N.spread)


def part(r, at, *fields, first=0):
    bit = r.bits[0] == 1
    for k, field in enumerate(fields, first):
        half = field.shape[1] // 2
        low, high = field[:, :half], field[:, half:]
        r.mine[k, at : at + field.shape[0], :] = jnp.where(bit, high, low)
        r.theirs[k, at : at + field.shape[0], :] = jnp.where(bit, low, high)


def mine_of(r, row):
    half = row.shape[1] // 2
    return jnp.where(r.bits[0] == 1, row[:, half:], row[:, :half])


def third_kernel(r, copies):
    groups, rows, cols, width = r.out.shape
    S = cols + 8
    L = groups * S
    n = r.mom1[2:3, :]
    t = jnp.sum(r.tot2[...], axis=0)
    parts = [t[:, k * width : (k + 1) * width] for k in range(4)]
    (c2, i2), (cp, ip) = moments(parts[0], parts[1], n), moments(parts[2], parts[3], n)
    r.mom2[...] = jnp.concatenate([c2, i2, cp, ip, jnp.zeros((4, width), f32)], axis=0)
    sums = [jnp.zeros((1, width), f32)] * 3
    both_shift = r.shift2[...] + r.shiftp[...]
    total = r.grad.shape[0] // S
    for line in range(total):
        if line % (total // 2) == 0:
            k = line // (total // 2)
            copies.wait((N.pre2, k), (N.prep, k), (N.cotq, k))
        at = line * S
        shifted = slice(L + 1 + at, L + 1 + at + S)
        n2 = (r.pre2[at : at + S, :] - c2) * i2
        np_ = (r.prep[shifted, :] - cp) * ip
        v = n2 * r.gain2[...] + np_ * r.gainp[...] + both_shift
        mask = wide(r.maskp[shifted, :], width)
        own = wide(r.ownp[shifted, :], width)
        t = gelu_parts(v)
        r.field[at : at + S, :] = 0.5 * v * (1.0 + t) * mask
        g = gelu_slope(v, t) * mask * r.cotq[at : at + S, :]
        r.grad[at : at + S, :] = g
        g = g * own
        if L <= at < L + r.mine.shape[1]:
            part(r, at - L, g, n2 * own, np_ * own)
            if at - L + S == r.mine.shape[1] // 2:
                copies.start((N.mine, 0), (N.theirs, 0))
        new = [column_sum(g * n2), column_sum(g), column_sum(g * np_)]
        sums = [a + b for a, b in zip(sums, new)]
        if (line + 1) % (total // 2) == 0:
            copies.start((N.grad, (line + 1) // (total // 2) - 1))
    row = jnp.concatenate(sums, axis=1)
    r.spread[...] = jnp.broadcast_to(row[None], r.spread.shape)
    copies.start(N.spread, (N.mine, 1), (N.theirs, 1))
    for i in range(rows):
        for g in range(groups):
            at = (i + 1) * L + g * S + 1
            r.out[g, i, :, :] = r.field[at : at + cols, :].astype(bf16)
    copies.start(N.out)
    copies.wait(N.grad, N.out, N.spread, N.mine, N.theirs)


def fourth_kernel(r, copies):
    width = r.gain.shape[1]
    Q, U, rows_w = r.pre2.shape[0], r.act.shape[0], r.gpu.shape[0]
    L = U - rows_w
    center, inv, n = (r.mom1[k : k + 1, :] for k in range(3))
    c2, i2, cp, ip = (r.mom2[k : k + 1, :] for k in range(4))
    t3 = jnp.sum(r.tot3[...], axis=0)
    gg2, gs, ggp = (t3[:, k * width : (k + 1) * width] for k in range(3))
    r.gain_second[...], r.shift_second[...], r.gain_proj[...], r.shift_proj[...] = gg2, gs, ggp, gs
    tiny = N.gain_second, N.shift_second, N.gain_proj, N.shift_proj
    copies.start(*tiny)
    for m0, m in chunks(Q, L):
        if m0 in (0, 6 * L):
            copies.wait((N.grad, m0 // (6 * L)), (N.pre2, m0 // (6 * L)))
        mask = wide(r.maskp[L + 1 + m0 : L + 1 + m0 + m, :], width) / n
        n2 = (r.pre2[m0 : m0 + m, :] - c2) * i2
        back = mask * (gs + n2 * gg2)
        r.gq[m0 : m0 + m, :] = (r.gain2[...] * i2) * (r.grad[m0 : m0 + m, :] - back)
    r.gq[Q:, :] = jnp.zeros((r.gq.shape[0] - Q, width), f32)
    for m0, m in chunks(Q, 176):
        for b in range(3):
            r.g3[m0 : m0 + m, b * width : (b + 1) * width] = r.gq[m0 + b : m0 + b + m, :].astype(bf16)
    copies.wait(N.keep)
    for m0, m in chunks(U, L):
        frame = slice(2 * L + 2 + m0, 2 * L + 2 + m0 + m)
        n1 = (r.keep[frame, :] - center) * inv
        v = n1 * r.gain[...] + r.shift[...]
        mask = wide(r.maskp[frame, :], width)
        r.act[m0 : m0 + m, :] = gelu_slope(v, gelu_parts(v)) * mask
        r.normed[m0 : m0 + m, :] = n1 * mask
        if m0 < rows_w:
            part(r, m0, n1 * wide(r.ownp[frame, :], width), first=1)
    copies.start(N.normed, (N.mine, 1), (N.theirs, 1))
    for a in range(3):
        copies.wait((N.w2, a))
        gh = jnp.zeros((U, width), f32)
        for b in range(3):
            gh += matmul_nt(
                r.g3[L * a : L * a + U, b * width : (b + 1) * width],
                r.w2[2 - a, (2 - b) * width : (3 - b) * width, :],
            )
        r.gh[...] = gh if a == 0 else r.gh[...] + gh
    sums = [jnp.zeros((1, width), f32)] * 2
    for m0, m in chunks(U, L):
        g = r.act[m0 : m0 + m, :] * r.gh[m0 : m0 + m, :]
        r.act[m0 : m0 + m, :] = g
        g = g * wide(r.ownp[2 * L + 2 + m0 : 2 * L + 2 + m0 + m, :], width)
        if m0 < rows_w:
            part(r, m0, g)
        sums = [sums[0] + column_sum(g * r.normed[m0 : m0 + m, :]), sums[1] + column_sum(g)]
    row = jnp.concatenate(sums, axis=1)
    r.spread[...] = jnp.broadcast_to(row[None], r.spread.shape)
    copies.start(N.spread, (N.mine, 0), (N.theirs, 0), N.act)
    copies.wait(N.prep)
    for m0, m in chunks(rows_w, L):
        frame = slice(2 * L + 2 + m0, 2 * L + 2 + m0 + m)
        mask = wide(r.maskp[frame, :], width) / n
        back = mask * (gs + (r.prep[frame, :] - cp) * ip * ggp)
        r.gpu[m0 : m0 + m, :] = ((r.gainp[...] * ip) * (r.grad[L + 1 + m0 : L + 1 + m0 + m, :] - back)).astype(bf16)
    copies.start(N.gpu)
    copies.wait(N.normed, N.mine, N.theirs, N.spread, N.act, N.gpu, *tiny)


def split_store(r, rows, unit, first):
    quarter = unit // 4
    for k in range(rows // unit):
        for bit, base, sent, kept in ((1, 0, r.sent_a, r.kept_a), (2, 2 * quarter, r.sent_b, r.kept_b)):
            keep = pl.multiple_of(k * unit + base + r.bits[bit] * quarter, quarter)
            send = pl.multiple_of(k * unit + base + (1 - r.bits[bit]) * quarter, quarter)
            sent[first + k] = r.acc[pl.ds(send, quarter), :].astype(bf16)
            kept[first + k] = r.acc[pl.ds(keep, quarter), :]


def weights_second_kernel(r, copies):
    width = r.h3.shape[1] // 3
    cin = r.xe.shape[1] // 3
    rows_w = r.mine.shape[1]
    L = (r.h3.shape[0] - rows_w) // 5
    per = width // cin
    t3 = jnp.sum(r.tot3[...], axis=0)
    n = mine_of(r, r.mom1[2:3, :])
    gg2, gs, ggp = (mine_of(r, t3[:, k * width : (k + 1) * width]) / n for k in range(3))
    scale2, scalep = mine_of(r, r.gain2[...] * r.mom2[1:2, :]), mine_of(r, r.gainp[...] * r.mom2[3:4, :])
    half = scale2.shape[1]
    for source, name, own, out in ((r.mine, N.mine, r.ownp, r.near), (r.far3, N.far3, r.ownp_far, r.far)):
        copies.wait(name)
        r.pad[:, 0:8, :] = jnp.zeros((3, 8, half), f32)
        r.pad[:, 8:, :] = source[...]
        for m0, m in chunks(rows_w, 96):
            mask = wide(own[2 * L + 1 + m0 : 2 * L + 1 + m0 + m, :], half)
            rows = slice(8 + m0, 8 + m0 + m)
            back = mask * gs + r.pad[1, rows, :] * gg2
            out[m0 : m0 + m, :] = (scale2 * (r.pad[0, rows, :] - back)).astype(bf16)
            mask = wide(own[2 * L + m0 : 2 * L + m0 + m, :], half)
            rows = slice(7 + m0, 7 + m0 + m)
            back = mask * gs + r.pad[2, rows, :] * ggp
            out[rows_w + m0 : rows_w + m0 + m, :] = (scalep * (r.pad[0, rows, :] - back)).astype(bf16)
    for b in range(3):
        lanes = slice(b * width, (b + 1) * width)
        copies.wait((N.h3, b), (N.h3_far, b))
        for a in range(3):
            at = L * a + L
            r.acc[...] = matmul_tn(r.h3[at : at + rows_w, lanes], r.near[:rows_w, :]) + matmul_tn(
                r.h3_far[at : at + rows_w, lanes], r.far[:rows_w, :]
            )
            split_store(r, width, cin, (3 * b + a) * per)
        copies.start(*((name, b) for name in CHUNKS))
    at = 2 * L
    copies.wait(N.xe, N.xe_far)
    middle = slice(cin, 2 * cin)
    r.acc[0:cin, :] = matmul_tn(r.xe[at : at + rows_w, middle], r.near[rows_w:, :]) + matmul_tn(
        r.xe_far[at : at + rows_w, middle], r.far[rows_w:, :]
    )
    split_store(r, cin, cin, 9 * per)
    copies.start(*((name, 3) for name in CHUNKS))
    copies.wait(*CHUNKS)


def first_back(r, gg, gs, count):
    width = r.gain.shape[1]
    U = r.act.shape[0]
    L = U - r.rows_w
    inv, n = r.mom1[1:2, :], r.mom1[2:3, :]
    gg, gs = gg / n, gs / n
    scale = r.gain[...] * inv
    r.gf[0:8, :] = jnp.zeros((8, width), f32)
    r.gf[8 + count :, :] = jnp.zeros((r.gf.shape[0] - 8 - count, width), f32)
    for m0, m in chunks(count, L):
        mask = wide(r.maskp[2 * L + 2 + m0 : 2 * L + 2 + m0 + m, :], width)
        back = mask * gs + r.normed[m0 : m0 + m, :] * gg
        r.gf[8 + m0 : 8 + m0 + m, :] = scale * (r.act[m0 : m0 + m, :] - back)


def weights_first_kernel(r, copies):
    rows_w = r.mine.shape[1]
    cin = r.xe.shape[1] // 3
    L = (r.xe.shape[0] - rows_w) // 5
    width = r.gain.shape[1]
    t4 = jnp.sum(r.tot4[...], axis=0)
    r.gain_first[...], r.shift_first[...] = t4[:, :width], t4[:, width:]
    copies.start(N.gain_first, N.shift_first)
    n = mine_of(r, r.mom1[2:3, :])
    gg, gs = mine_of(r, t4[:, :width]) / n, mine_of(r, t4[:, width:]) / n
    scale = mine_of(r, r.gain[...] * r.mom1[1:2, :])
    half = scale.shape[1]
    for source, name, own, out in ((r.mine, N.mine, r.ownp, r.near), (r.far4, N.far4, r.ownp_far, r.far)):
        copies.wait(name)
        r.pad[:, 0:8, :] = jnp.zeros((2, 8, half), f32)
        r.pad[:, 8:, :] = source[...]
        for m0, m in chunks(rows_w, 96):
            mask = wide(own[2 * L + m0 : 2 * L + m0 + m, :], half)
            rows = slice(6 + m0, 6 + m0 + m)
            back = mask * gs + r.pad[1, rows, :] * gg
            out[m0 : m0 + m, :] = (scale * (r.pad[0, rows, :] - back)).astype(bf16)
    copies.wait(N.xe, N.xe_far)
    for k, a in enumerate((1, 0, 2)):
        if k == 1:
            copies.wait(N.xo, N.xo_far)
        source, source_far = (r.xe, r.xe_far) if a == 1 else (r.xo, r.xo_far)
        at = (3 if a == 2 else 2) * L
        for b in range(3):
            lanes = slice(b * cin, (b + 1) * cin)
            r.acc[lanes, :] = matmul_tn(source[at : at + rows_w, lanes], r.near[...]) + matmul_tn(
                source_far[at : at + rows_w, lanes], r.far[...]
            )
        split_store(r, 3 * cin, cin, a * 3)
        copies.start(*((name, a) for name in CHUNKS))
    copies.wait(N.gain_first, N.shift_first, *CHUNKS)


def inputs_kernel(r, copies):
    width = r.gpu.shape[1]
    groups, rows, cols = r.out.shape[0], r.out.shape[1] // 2, r.out.shape[2] // 2
    cin = r.out.shape[3]
    M = r.gpu.shape[0]
    S = cols + 8
    L = groups * S
    lines = r.lines
    U = r.act.shape[0]
    r.rows_w = M
    copies.wait(N.act, N.normed)
    first_back(r, r.gg[...], r.gs[...], U)
    for m0, m in chunks(U, 144):
        r.gu[m0 : m0 + m, :width] = r.gf[8 + m0 : 8 + m0 + m, :].astype(bf16)
        r.gu[m0 : m0 + m, width:] = r.gf[9 + m0 : 9 + m0 + m, :].astype(bf16)
    copies.wait(N.gpu, N.w1, N.wp)

    def tap(m0, m, a, b):
        di, dj = (1 if a == 0 else 0), (1 if b == 0 else 0)
        return matmul_nt(
            r.gu[di * L + m0 : di * L + m0 + m, dj * width : (dj + 1) * width],
            r.w1[a, b * cin : (b + 1) * cin, :],
        )

    for m0, m in chunks(M, 2 * L):
        pieces = {
            (0, 0): tap(m0, m, 1, 1) + matmul_nt(r.gpu[m0 : m0 + m, :], r.wp[...]),
            (0, 1): tap(m0, m, 1, 2) + tap(m0, m, 1, 0),
            (1, 0): tap(m0, m, 2, 1) + tap(m0, m, 0, 1),
            (1, 1): tap(m0, m, 2, 2) + tap(m0, m, 2, 0) + tap(m0, m, 0, 2) + tap(m0, m, 0, 0),
        }
        for (ro, co), v in pieces.items():
            for k in range(m // S):
                line = m0 // S + k
                i, g = line // groups, line % groups
                for h in range(lines.shape[0]):
                    lines[h, (2 * i + ro) * groups + g, pl.ds(co, cols, stride=2), :] = v[
                        k * S : k * S + cols, h * 128 : (h + 1) * 128
                    ]
    for n in range(2 * rows):
        for g in range(groups):
            for h in range(lines.shape[0]):
                r.out[g, n, :, h * 128 : (h + 1) * 128] = lines[h, n * groups + g].astype(bf16)
    copies.start(N.out)
    copies.wait(N.out)


def widen(half, side, taps, per, swapped, into=None):
    total, n, m = half.shape
    extra = total - taps * per
    order = [(t % 3 * 3 + t // 3) if swapped else t for t in range(taps)]
    jobs = [(t * per, per, 0, order[t] * per) for t in range(taps)] + [(taps * per, 1, 1, 0)] * extra
    more = list(into or [])

    def body(side_ref, half_ref, *refs):
        outs = refs[len(more) : len(more) + 1 + extra]
        narrow, full, sems = refs[len(more) + 1 + extra :]
        lanes = pl.ds(pl.multiple_of(side_ref[0] * m, m), m)
        reads = [
            pltpu.make_async_copy(half_ref.at[pl.ds(at, size)], narrow.at[pl.ds(at, size)], sems.at[0, k])
            for k, (at, size, _, _) in enumerate(jobs)
        ]
        writes = [
            pltpu.make_async_copy(full.at[pl.ds(at, size)], outs[which].at[pl.ds(to, size), :, lanes], sems.at[1, k])
            for k, (at, size, which, to) in enumerate(jobs)
        ]
        for read in reads:
            read.start()
        for k, (at, size, _, _) in enumerate(jobs):
            reads[k].wait()
            full[at : at + size] = narrow[at : at + size].astype(f32)
            writes[k].start()
        for write in writes:
            write.wait()

    hbm = pl.BlockSpec(memory_space=pltpu.HBM)
    return pl.pallas_call(
        body,
        out_shape=[shape((taps * per, n, 2 * m))] + [shape((1, n, 2 * m))] * extra,
        in_specs=[pl.BlockSpec(memory_space=pltpu.SMEM)] + [hbm] * (1 + len(more)),
        out_specs=[hbm] * (1 + extra),
        scratch_shapes=[
            pltpu.VMEM((total, n, m), bf16),
            pltpu.VMEM((total, n, m), f32),
            pltpu.SemaphoreType.DMA((2, len(jobs))),
        ],
        input_output_aliases={2 + k: k for k in range(len(more))},
        compiler_params=pltpu.CompilerParams(vmem_limit_bytes=20 * 1024 * 1024),
        cost_estimate=pl.CostEstimate(flops=0, bytes_accessed=0, transcendentals=0),
    )(side.reshape(1), half, *more)


def halve_kernel(r, copies):
    for p in range(r.count):
        kept, got = getattr(r, f"kept{p}"), getattr(r, f"got{p}")
        copies.wait(f"kept{p}", f"got{p}")
        to_send, to_keep = getattr(r, f"sent{p}"), getattr(r, f"left{p}")
        bit = r.bits[r.steps[p]] == 1
        h = kept.shape[1] // 2
        for t in range(kept.shape[0]):
            total = kept[t] + got[t].astype(f32)
            low, high = total[:h], total[h:]
            to_send[t] = jnp.where(bit, low, high).astype(bf16)
            to_keep[t] = jnp.where(bit, high, low)
        copies.start(f"sent{p}", f"left{p}")
    copies.wait(*(name for name in copies.jobs if name[:4] in (N.sent, N.left)))


def halve(bits, pairs, steps, cost):
    ins = dict(bits=bits)
    for p, (kept, got) in enumerate(pairs):
        ins[f"kept{p}"], ins[f"got{p}"] = kept, got
    taps, n, m = pairs[0][0].shape
    dims = (taps, n // 2, m)
    names = [str(p) for p in range(len(pairs))]
    outs = {}
    for name in names:
        outs[N.sent + name], outs[N.left + name] = shape(dims, bf16), shape(dims)

    def body(r, copies):
        r.count, r.steps = len(pairs), steps
        halve_kernel(r, copies)

    far_in = tuple(n for n in ins if n != N.bits)
    out = call(body, ins, outs, far_in=far_in, far_out=tuple(outs), smem=(N.bits,), cost=cost, limit=60)
    return [(out[N.sent + name], out[N.left + name]) for name in names]


def shifted(value, axis, steps):
    count = lax.axis_size(axis)
    first, last = (max(0, -steps), min(count, count - steps))
    return lax.ppermute(value, axis, [(source, source + steps) for source in range(first, last)])


def gather_sum(spread):
    return lax.all_to_all(spread, axes, 0, 0)


def bit_of(axis, step):
    return (lax.axis_index(axis) // step) % 2


def partner(value, axis, step):
    count = lax.axis_size(axis)
    return lax.ppermute(value, axis, [(i, i ^ step) for i in range(count)])


def steps_of(axis):
    count, step, out = lax.axis_size(axis), 1, []
    while step < count:
        out.append((axis, step))
        step *= 2
    return out


def split(total, axis, step):
    n = total.shape[1] // 2
    bit = bit_of(axis, step) == 1
    low, high = total[:, :n], total[:, n:]
    return jnp.where(bit, low, high).astype(bf16), jnp.where(bit, high, low)


def joined(value, other, axis, step, dim=1):
    bit = bit_of(axis, step) == 1
    return jnp.concatenate([jnp.where(bit, other, value), jnp.where(bit, value, other)], axis=dim)


def gathered(pieces, spots, cost=0):
    taps, h, m = pieces[0].shape
    count = len(pieces)

    def body(spots_ref, *refs):
        out, sems = refs[count:]
        copies = []
        for q in range(count):
            rows = pl.ds(pl.multiple_of(spots_ref[q] * h, h), h)
            copies.append(pltpu.make_async_copy(refs[q], out.at[:, rows], sems.at[q]))
        for copy in copies:
            copy.start()
        for copy in copies:
            copy.wait()

    anywhere = pl.BlockSpec(memory_space=pl.ANY)
    return pl.pallas_call(
        body,
        out_shape=shape((taps, count * h, m), pieces[0].dtype),
        in_specs=[pl.BlockSpec(memory_space=pltpu.SMEM)] + [anywhere] * count,
        out_specs=anywhere,
        scratch_shapes=[pltpu.SemaphoreType.DMA((count,))],
        compiler_params=pltpu.CompilerParams(vmem_limit_bytes=16 * 1024 * 1024),
        cost_estimate=pl.CostEstimate(flops=cost, bytes_accessed=0, transcendentals=0),
    )(spots, *pieces)


class Tree:
    def __init__(self, parts, bits, plane, rest, core):
        self.bits, self.place = bits, {step: k for k, step in enumerate([core, *plane, *rest])}
        self.sent_a, self.kept_a, self.sent_b, self.kept_b = parts
        self.a, self.b, self.rest, self.core = plane, plane[::-1], rest, core
        p, n = len(plane), len(rest)
        self.stages = [(N.plane, k) for k in range(p)] + [(N.rest, k) for k in range(n)]
        self.stages += [(N.rest_join, k) for k in reversed(range(n))] + [(N.plane_join, k) for k in reversed(range(p))]
        self.stages += [(N.core, 0)]

    def next(self):
        return self.stages[0] if self.stages else None

    def start(self):
        kind, k = self.stages[0]
        if kind == N.plane:
            self.got = partner(self.sent_a, *self.a[k]), partner(self.sent_b, *self.b[k])
        elif kind == N.rest:
            self.got = (partner(self.sent, *self.rest[k]),)
        elif kind == N.rest_join:
            self.got = (partner(self.value, *self.rest[k]),)
        elif kind == N.plane_join:
            self.got = partner(self.value_a, *self.a[k]), partner(self.value_b, *self.b[k])
        else:
            self.got = (partner(self.value, *self.core),)

    def finish(self, cost=0):
        kind, k = self.stages.pop(0)
        if kind == N.plane:
            pairs = [(self.kept_a, self.got[0]), (self.kept_b, self.got[1])]
            nexts = [order[k + 1] for order in (self.a, self.b) if k + 1 < len(order)]
            if nexts and cost:
                pairs = halve(self.bits, pairs, [self.place[step] for step in nexts], cost)
                (self.sent_a, self.kept_a), (self.sent_b, self.kept_b) = pairs
                return
            total_a, total_b = (kept + got.astype(f32) for kept, got in pairs)
            if nexts:
                self.sent_a, self.kept_a = split(total_a, *nexts[0])
                self.sent_b, self.kept_b = split(total_b, *nexts[1])
            else:
                self.taps = total_a.shape[0]
                self.split_rest(jnp.concatenate([total_a, total_b], axis=0), 0)
        elif kind == N.rest:
            self.split_rest(self.kept + self.got[0].astype(f32), k + 1)
        elif kind == N.rest_join:
            self.value = joined(self.value, self.got[0], *self.rest[k])
            self.value_a, self.value_b = self.value[: self.taps], self.value[self.taps :]
        elif kind == N.plane_join:
            if k == 0 and cost:
                low, high = (self.bits[self.place[step]] for step in (self.a[0], self.b[0]))
                spots = jnp.stack([low, 1 - low, 2 + high, 3 - high])
                self.value = gathered([self.value_a, self.got[0], self.value_b, self.got[1]], spots, cost)
            else:
                self.value_a = joined(self.value_a, self.got[0], *self.a[k])
                self.value_b = joined(self.value_b, self.got[1], *self.b[k])
                self.value = jnp.concatenate([self.value_a, self.value_b], axis=1)

    def split_rest(self, total, k):
        if k < len(self.rest):
            self.sent, self.kept = split(total, *self.rest[k])
        else:
            self.value = total.astype(bf16)


def lockstep(*trees, beside=()):
    for t in trees:
        t.start()
    got, beside = lax.optimization_barrier(([t.got for t in trees], beside))
    for t, g in zip(trees, got):
        t.got = g
        t.finish()
    return beside


def on_device(inputs, w_first, gain_first, shift_first, w_second, gain_second, shift_second, w_proj, gain_proj, shift_proj, valid_mask, cotangent):
    groups, rows_in, cols_in, cin = inputs.shape
    rows, cols = rows_in // 2, cols_in // 2
    width = w_first.shape[3]
    half = width // 2
    S = cols + 8
    L = groups * S
    devices = lax.axis_size(N.rows) * lax.axis_size(N.cols) * lax.axis_size(N.grp)
    plane = steps_of(N.cols)
    core = steps_of(N.rows)[0]
    rest = steps_of(N.rows)[1:] + steps_of(N.grp)
    bits = jnp.stack([bit_of(*step) for step in (core, *plane, *rest)]).astype(jnp.int32)
    w1 = w_first.reshape(3, 3 * cin, width)
    w2 = w_second.reshape(3, 3 * width, width)
    as_row = lambda v: v.reshape(1, -1)
    own = jnp.broadcast_to(valid_mask.astype(bf16)[..., None], valid_mask.shape + (128,))
    MP, MQ, MU, MW = (rows + 5) * L, (rows + 3) * L, (rows + 1) * L, rows * L
    px = lambda m, k: 2 * m * k * width
    vec = lambda k: shape((1, k * width))
    all_devices = lambda k: shape((devices, 1, k))
    g1, b1, g2, b2, gp, bp = map(
        as_row, (gain_first, shift_first, gain_second, shift_second, gain_proj, shift_proj)
    )

    top1 = shifted(inputs[:, -1:], N.rows, 1)
    me, count = lax.axis_index(N.rows), lax.axis_size(N.rows)
    flags = jnp.stack([me > 0, me < count - 1]).astype(jnp.int32)
    flat_rows = shape((over * groups * cols_in + (width // 256 + 1) * rim * groups * cols, 256), bf16)
    packed = call(
        vertical_kernel,
        dict(flags=flags, x=inputs, cot=cotangent, own=own),
        dict(down=flat_rows) if count == 2 else dict(down=flat_rows, up=flat_rows),
        far_in=(N.x, N.cot),
        smem=(N.flags,),
        parts=dict(x=end_parts(rows_in, over), cot=end_parts(rows, rim)),
    )
    if count == 2:
        top = bot = lax.ppermute(packed["down"], "rows", [(0, 1), (1, 0)])
    else:
        top, bot = shifted(packed[N.down], N.rows, 1), shifted(packed[N.up], N.rows, -1)
    (top, bot), top1 = lax.optimization_barrier(((top, bot), top1))
    lines = (rows_in + 2 * over) * groups, (rows + 2 * rim) * groups, (rows + 3) * groups
    n_strip = over * lines[0] + (rim + 1) // 2 * lines[1] + width // 128 * lines[2]
    n_strip = -(-n_strip // 16) * 16
    near = dict(flags=flags, x=inputs, cot=cotangent, own=own, top=top, bot=bot)
    strips = call(
        strips_kernel,
        near,
        dict(right=shape((n_strip, 256), bf16), left=shape((n_strip, 256), bf16)),
        dict(
            raw_x=pltpu.VMEM((cin // 128, lines[0] * cols_in, 128), f32),
            raw_m=pltpu.VMEM((1, lines[1] * cols, 128), f32),
            raw_c=pltpu.VMEM((width // 128, lines[2] * cols, 128), f32),
            flat=pltpu.VMEM((n_strip, 256), f32),
        ),
        smem=(N.flags,),
    )
    edge = jnp.concatenate([top1[:, :, -1:], inputs[:, :, -1:]], axis=1)
    edge, right, left = lax.optimization_barrier((edge, strips[N.right], strips[N.left]))
    lft1, right, left = lax.optimization_barrier((shifted(edge, N.cols, 1), right, left))
    lft, rgt = shifted(right, N.cols, 1), shifted(left, N.cols, -1)
    stats = call(
        stats_kernel,
        dict(x=inputs, top=top1, lft=lft1, own=own, w1=w1, wp=w_proj),
        dict(spread=all_devices(2 * width + 128), psum=vec(2)),
        dict(
            raw=pltpu.VMEM((cin // 128, (rows_in + 1) * groups, cols_in + 8, 128), f32),
            xe=pltpu.VMEM((rows * groups * cols, 3 * cin), bf16),
            xo=pltpu.VMEM(((rows + 1) * groups * cols, 3 * cin), bf16),
        ),
        far_in=(N.w1,),
        far_out=(N.spread, N.psum),
    )
    tot1 = gather_sum(stats[N.spread])

    first = call(
        first_kernel,
        dict(**near, lft=lft, rgt=rgt, w1=w1, wp=w_proj),
        dict(
            pre1=shape((MP, width)),
            prep=shape((MP, width)),
            xe=shape((MP, 3 * cin), bf16),
            xo=shape((MP + L, 3 * cin), bf16),
            ownp=shape((MP, 128)),
            maskp=shape((MP, 128)),
            cotq=shape((MQ, width)),
        ),
        dict(
            raw_x=pltpu.VMEM((cin // 128, lines[0] * (cols_in + 24), 128), f32),
            raw_m=pltpu.VMEM((1, lines[1] * (cols + 16), 128), f32),
            raw_c=pltpu.VMEM((width // 128, lines[2] * (cols + 16), 128), f32),
            flat=pltpu.VMEM((n_strip, 256), f32),
        ),
        far_in=(N.w1, N.wp),
        far_out=(N.xe, N.xo, N.pre1, N.prep, N.cotq),
        smem=(N.flags,),
        cost=20000000000,
        parts=dict(pre1=row_parts(MP, 3), prep=row_parts(MP, 3)),
    )
    xe, xo, ownp, maskp = first[N.xe], first[N.xo], first[N.ownp], first[N.maskp]
    far_xe, far_xo = partner(xe, *core), partner(xo, *core)

    second = call(
        second_kernel,
        dict(pre1=first[N.pre1], tot1=tot1, gain=g1, shift=b1, maskp=maskp, ownp=ownp, w2=w2, psum=stats[N.psum]),
        dict(h3=shape((MP, 3 * width), bf16), pre2=shape((MQ, width)), spread=all_devices(4 * width), mom1=shape((8, width))),
        dict(hid=pltpu.VMEM((MP + 8, width), f32)),
        far_in=(N.pre1, N.w2),
        far_out=(N.h3, N.pre2, N.spread),
        parts=dict(pre2=row_parts(MQ, 3)),
    )
    h3, pre2, mom1 = second[N.h3], second[N.pre2], second[N.mom1]
    tot2 = gather_sum(second[N.spread])
    tot2, far_h3 = lax.optimization_barrier((tot2, partner(h3, *core)))

    third = call(
        third_kernel,
        dict(
            bits=bits, pre2=pre2, prep=first[N.prep], mom1=mom1, tot2=tot2, gain2=g2, shift2=b2, gainp=gp, shiftp=bp,
            maskp=maskp, ownp=ownp, cotq=first[N.cotq],
        ),
        dict(
            out=shape((groups, rows, cols, width), bf16),
            grad=shape((MQ, width)),
            spread=all_devices(3 * width),
            mom2=shape((8, width)),
            mine=shape((3, MW, half)),
            theirs=shape((3, MW, half)),
        ),
        dict(field=pltpu.VMEM((MQ, width), f32)),
        far_in=(N.pre2, N.prep, N.cotq),
        far_out=(N.grad, N.spread, N.mine, N.theirs, N.out),
        smem=(N.bits,),
        parts=dict(
            mine=middle_parts(MW, 2), theirs=middle_parts(MW, 2),
            grad=row_parts(MQ, 2), pre2=row_parts(MQ, 2), cotq=row_parts(MQ, 2), prep=cuts(L, L + MQ // 2 + 8, L + MQ + 8)
        ),
    )
    mom2 = third[N.mom2]
    tot3 = gather_sum(third[N.spread])
    ownp_here, far3 = lax.optimization_barrier((ownp, partner(third[N.theirs], *core)))
    ownp_far = partner(ownp_here, *core)

    def chunk_shapes(taps):
        dims = (taps, cin // 4, half)
        return dict(sent_a=shape(dims, bf16), kept_a=shape(dims), sent_b=shape(dims, bf16), kept_b=shape(dims))

    per = width // cin
    taps2 = 9 * per + 1
    second_parts = call(
        weights_second_kernel,
        dict(
            bits=bits, mine=third[N.mine], far3=far3, h3=h3, h3_far=far_h3, xe=xe, xe_far=far_xe,
            tot3=tot3, mom1=mom1, mom2=mom2, gain2=g2, gainp=gp, ownp=ownp, ownp_far=ownp_far,
        ),
        chunk_shapes(taps2),
        dict(
            acc=pltpu.VMEM((width, half), f32),
            pad=pltpu.VMEM((3, MW + 8, half), f32),
            near=pltpu.VMEM((2 * MW, half), bf16),
            far=pltpu.VMEM((2 * MW, half), bf16),
        ),
        far_in=(N.mine, N.far3, N.h3, N.h3_far, N.xe, N.xe_far),
        far_out=CHUNKS,
        smem=(N.bits,),
        parts=dict(
            h3=lane_parts(3 * width, 3, pl.ds(L, MW + 2 * L)),
            h3_far=lane_parts(3 * width, 3, pl.ds(L, MW + 2 * L)),
            xe=[(0, (pl.ds(2 * L, MW), pl.ds(cin, cin)))],
            xe_far=[(0, (pl.ds(2 * L, MW), pl.ds(cin, cin)))],
            **{name: row_parts(taps2 - 1, 3) + [(3, (pl.ds(taps2 - 1, 1),))] for name in CHUNKS},
        ),
    ).values()
    grad, *second_parts = lax.optimization_barrier((third[N.grad], *second_parts))
    tree2 = Tree(second_parts, bits, plane, rest, core)
    tree2.start()
    hidden = call(
        fourth_kernel,
        dict(
            bits=bits, grad=grad, pre2=pre2, keep=first[N.pre1], w2=w2, prep=first[N.prep], mom1=mom1, mom2=mom2, tot3=tot3,
            gain=g1, shift=b1, gain2=g2, gainp=gp, maskp=maskp, ownp=ownp,
        ),
        dict(
            act=shape((MU, width)), normed=shape((MU, width)), spread=all_devices(2 * width),
            mine=shape((2, MW, half)), theirs=shape((2, MW, half)), gpu=shape((MW, width), bf16),
            gain_second=vec(1), shift_second=vec(1), gain_proj=vec(1), shift_proj=vec(1),
        ),
        dict(
            gq=pltpu.VMEM((MQ + 8, width), f32),
            g3=pltpu.VMEM((MQ, 3 * width), bf16),
            gh=pltpu.VMEM((MU, width), f32),
        ),
        far_in=(N.grad, N.pre2, N.keep, N.w2, N.prep),
        far_out=(
            N.act, N.normed, N.spread, N.mine, N.theirs, N.gpu, N.gain_second, N.shift_second, N.gain_proj, N.shift_proj
        ),
        smem=(N.bits,),
        limit=52,
        parts=dict(
            grad=cuts(0, 6 * L, MQ),
            pre2=cuts(0, 6 * L, MQ),
            keep=cuts(2 * L, 2 * L + MU + 8),
            w2=[(k, (pl.ds(2 - k, 1),)) for k in range(3)],
            prep=cuts(2 * L, 2 * L + MW + 8),
            mine=row_parts(2, 2),
            theirs=row_parts(2, 2),
        ),
    )
    tot4 = gather_sum(hidden[N.spread])
    tree2.finish(20000000000)
    near1, tree2.sent_a, tree2.sent_b = lax.optimization_barrier((hidden[N.mine], tree2.sent_a, tree2.sent_b))
    tree2.start()
    fifth = call(
        weights_first_kernel,
        dict(
            bits=bits, mine=near1, far4=partner(hidden[N.theirs], *core), xe=xe, xe_far=far_xe, xo=xo, xo_far=far_xo,
            tot4=tot4, mom1=mom1, gain=g1, ownp=ownp, ownp_far=ownp_far,
        ),
        dict(**chunk_shapes(9), gain_first=vec(1), shift_first=vec(1)),
        dict(
            acc=pltpu.VMEM((3 * cin, half), f32),
            pad=pltpu.VMEM((2, MW + 8, half), f32),
            near=pltpu.VMEM((MW, half), bf16),
            far=pltpu.VMEM((MW, half), bf16),
        ),
        far_in=(N.mine, N.far4, N.xe, N.xe_far, N.xo, N.xo_far),
        cost=20000000000,
        far_out=(*CHUNKS, N.gain_first, N.shift_first),
        smem=(N.bits,),
        parts=dict(
            xe=cuts(2 * L, 2 * L + MW),
            xe_far=cuts(2 * L, 2 * L + MW),
            xo=cuts(2 * L, 3 * L + MW),
            xo_far=cuts(2 * L, 3 * L + MW),
            **{name: row_parts(9, 3) for name in CHUNKS},
        ),
    )
    first_parts = [fifth[name] for name in CHUNKS]
    tree2.got, *first_parts = lax.optimization_barrier((tree2.got, *first_parts))
    tree2.finish()
    tree1 = Tree(first_parts, bits, plane, rest, core)

    grad_inputs = call(
        inputs_kernel,
        dict(
            act=hidden[N.act], normed=hidden[N.normed], gpu=hidden[N.gpu], w1=w1, wp=w_proj, mom1=mom1, gain=g1, maskp=maskp,
            gg=fifth[N.gain_first], gs=fifth[N.shift_first],
        ),
        dict(out=shape((groups, rows_in, cols_in, cin), bf16)),
        dict(
            lines=pltpu.VMEM((cin // 128, rows_in * groups, cols_in, 128), f32),
            gf=pltpu.VMEM((MU + 16, width), f32),
            gu=pltpu.VMEM((MU, 2 * width), bf16),
        ),
        far_in=(N.act, N.normed, N.gpu, N.w1, N.wp),
        far_out=(N.out,),
        cost=10000000000,
    )[N.out]
    side = bit_of(*core).astype(jnp.int32)
    grad_inputs = lockstep(tree2, tree1, beside=grad_inputs)
    while tree2.next() != (N.plane_join, 0):
        lockstep(tree2, tree1)
    tree2.start()
    while tree1.next() != (N.plane_join, 0):
        tree1.start()
        if tree1.next() != (N.plane_join, 1):
            tree1.finish()
        else:
            tree1.got, tree2.got = lax.optimization_barrier((tree1.got, tree2.got))
            tree1.finish()
    tree2.finish()
    tree2.start()
    tree1.start()
    grad_second = widen(tree2.got[0], 1 - side, 9, per, True, widen(tree2.value, side, 9, per, True))
    tree1.got, grad_second = lax.optimization_barrier((tree1.got, grad_second))
    grad_w2, grad_wp = grad_second
    tree1.finish(1)
    tree1.start()
    (grad_w1,) = widen(tree1.got[0], 1 - side, 3, 3, False, widen(tree1.value, side, 3, 3, False))

    return (
        third[N.out],
        grad_inputs,
        grad_w1.reshape(w_first.shape),
        fifth[N.gain_first].reshape(width),
        fifth[N.shift_first].reshape(width),
        grad_w2.reshape(w_second.shape),
        hidden[N.gain_second].reshape(width),
        hidden[N.shift_second].reshape(width),
        grad_wp.reshape(w_proj.shape),
        hidden[N.gain_proj].reshape(width),
        hidden[N.shift_proj].reshape(width),
    )


def solution(mesh):
    spread = P("grp", "rows", "cols", None)
    return jax.shard_map(
        on_device,
        mesh=mesh,
        in_specs=(spread,) + (P(),) * 9 + (P("grp", "rows", "cols"), spread),
        out_specs=(spread, spread) + (P(),) * 9,
        check_vma=False,
    )
```

```python
import functools

import jax
import jax.numpy as jnp
from jax import lax
from jax.experimental import pallas as pl
from jax.experimental.pallas import tpu as pltpu
from jax.sharding import PartitionSpec as P

epsilon = 1e-05
axes = ("rows", "cols", "grp")
bf16 = jnp.bfloat16
f32 = jnp.float32
inner = 0.7978845608028654
cubic = 0.044715
over = 6
CHUNKS = "sent_a", "kept_a", "sent_b", "kept_b"
rim = 3


class Names:
    def __getattr__(self, name):
        return name


N = Names()


class Refs:
    def __init__(self, named):
        self.__dict__.update(named)


class Copies:
    def __init__(self, parts, pairs, sems):
        self.jobs = {}
        for k, (name, index) in enumerate(parts):
            source, target = pairs[name]
            if index:
                source, target = source.at[index[1]], target.at[index[1]]
            self.jobs.setdefault(name, []).append(pltpu.make_async_copy(source, target, sems.at[k]))

    def start(self, *names):
        for name, *which in map(named, names):
            for job in self.jobs[name][slice(*which) if which else slice(None)]:
                job.start()

    def start_all(self, names):
        for k in range(max((len(self.jobs[n]) for n in names), default=0)):
            for n in names:
                if k < len(self.jobs[n]):
                    self.jobs[n][k].start()

    def wait(self, *names):
        for name, *which in map(named, names):
            for job in self.jobs[name][slice(*which) if which else slice(None)]:
                job.wait()


def named(name):
    return (name,) if isinstance(name, str) else (name[0], name[1], name[1] + 1)


def row_parts(total, count):
    size = total // count
    return [(k, (pl.ds(k * size, size),)) for k in range(count)]


def middle_parts(total, count):
    size = total // count
    return [(k, (slice(None), pl.ds(k * size, size))) for k in range(count)]


def end_parts(total, size):
    return [(k, (slice(None), pl.ds(at, size))) for k, at in enumerate((0, total - size))]


def cuts(*at):
    return [(k, (pl.ds(a, b - a),)) for k, (a, b) in enumerate(zip(at, at[1:]))]


def lane_parts(total, count, rows=slice(None)):
    size = total // count
    return [(k, (rows, pl.ds(k * size, size))) for k in range(count)]


def call(body, ins, outs, scratch=None, far_in=(), far_out=(), smem=(), parts=None, limit=52, cost=0):
    scratch, parts = scratch or {}, parts or {}
    far = (*far_in, *far_out)
    jobs = [(name, index) for name in far for index in parts.get(name, [None])]

    def spec(name):
        if name in smem:
            return pl.BlockSpec(memory_space=pltpu.SMEM)
        return pl.BlockSpec(memory_space=pltpu.HBM if name in far else pltpu.VMEM)

    kinds = {**{n: shape(v.shape, v.dtype) for n, v in ins.items()}, **outs}

    def run(*refs):
        plain = dict(zip([*ins, *outs], refs))
        rest = refs[len(plain) :]
        buffers = dict(zip(far, rest))
        more = dict(zip(scratch, rest[len(far) :]))
        copies = None
        if far:
            pairs = {n: (plain[n], buffers[n]) if n in far_in else (buffers[n], plain[n]) for n in far}
            copies = Copies(jobs, pairs, rest[-1])
            copies.start_all(far_in)
        body(Refs({**plain, **buffers, **more}), copies)

    buffers = [pltpu.VMEM(kinds[n].shape, kinds[n].dtype) for n in far]
    sems = [pltpu.SemaphoreType.DMA((len(jobs),))] if far else []
    result = pl.pallas_call(
        run,
        out_shape=list(outs.values()),
        in_specs=[spec(n) for n in ins],
        out_specs=[spec(n) for n in outs],
        scratch_shapes=[*buffers, *scratch.values(), *sems],
        compiler_params=pltpu.CompilerParams(vmem_limit_bytes=limit * 1024 * 1024),
        cost_estimate=pl.CostEstimate(flops=cost, bytes_accessed=0, transcendentals=0),
    )(*ins.values())
    return dict(zip(outs, result))


def shape(dims, dtype=f32):
    return jax.ShapeDtypeStruct(dims, dtype)


def wide(mask, width):
    return jnp.concatenate([mask] * (width // mask.shape[1]), axis=1)


def matmul(a, b):
    return lax.dot_general(a, b, (((1,), (0,)), ((), ())), preferred_element_type=f32)


def matmul_nt(a, b):
    return lax.dot_general(a, b, (((1,), (1,)), ((), ())), preferred_element_type=f32)


def matmul_tn(a, b):
    return lax.dot_general(a, b, (((0,), (0,)), ((), ())), preferred_element_type=f32)


def gelu_parts(v):
    return jnp.tanh(inner * (v + cubic * v * v * v))


def gelu_slope(v, t):
    return 0.5 * (1.0 + t) + 0.5 * v * (1.0 - t * t) * (inner * (1.0 + 3.0 * cubic * v * v))


def column_sum(v):
    return jnp.sum(v, axis=0, keepdims=True)


def moments(total, squares, pixel_count):
    center = total / pixel_count
    spread = squares / pixel_count - center * center
    return center, lax.rsqrt(spread + epsilon)


def chunks(total, size):
    return [(at, min(size, total - at)) for at in range(0, total, size)]


def strided(ref, k, first, count, step):
    return ref[k, pl.ds(first, count, stride=step), :]


def vertical_kernel(r, copies):
    groups, width = r.x.shape[0], r.cot.shape[3]
    rows, cols = r.own.shape[1], r.own.shape[2]

    def pack(out, input_row, row, pick):
        at = 0
        for g in range(groups):
            for n in range(over):
                value = r.x[g, input_row(n)]
                out[at : at + 2 * cols, :] = pick(value, r.x[g, n])
                at += 2 * cols
        for k in range(0, width, 256):
            for g in range(groups):
                for n in range(rim):
                    lanes = slice(k, k + 256)
                    out[at : at + cols, :] = pick(r.cot[g, row(n), :, lanes], r.cot[g, n, :, lanes])
                    at += cols
        for g in range(groups):
            for n in range(rim):
                out[at : at + cols, :] = pick(wide(r.own[g, row(n)], 256), wide(r.own[g, n], 256))
                at += cols

    last = r.x.shape[1] - over
    copies.wait(N.x, N.cot)
    if hasattr(r, N.up):
        pack(r.down, lambda n: last + n, lambda n: rows - rim + n, lambda tail, head: tail)
        pack(r.up, lambda n: last + n, lambda n: rows - rim + n, lambda tail, head: head)
    else:
        bottom = r.flags[0] == 1
        pack(r.down, lambda n: last + n, lambda n: rows - rim + n, lambda tail, head: jnp.where(bottom, head, tail))


def rim_rows(r, own, n_own, n_rim, base, cols, split):
    groups = own.shape[0]
    size = groups * n_rim * cols

    def flat(ref, g, n):
        at = [base + k * size + (g * n_rim + n) * cols for k in range(split)]
        return jnp.concatenate([ref[p : p + cols, :] for p in at], axis=1).astype(f32)

    def read(g, n):
        if n < n_rim:
            return jnp.where(r.flags[0] == 1, flat(r.top, g, n), 0.0)
        if n < n_rim + n_own:
            return own[g, n - n_rim].astype(f32)
        return jnp.where(r.flags[1] == 1, flat(r.bot, g, n - n_rim - n_own), 0.0)

    return read


def fields(r):
    groups, width = r.x.shape[0], r.cot.shape[3]
    rows, cols = r.own.shape[1], r.own.shape[2]
    base = over * groups * 2 * cols
    piece = rim * groups * cols
    blocks = width // 256
    x = rim_rows(r, r.x, 2 * rows, over, 0, 2 * cols, 1)
    mask = rim_rows(r, r.own, rows, rim, base + blocks * piece, cols, 1)
    cot = rim_rows(r, r.cot, rows, rim, base, cols, blocks)
    return x, lambda g, n: mask(g, n)[:, :128], cot


def strips_kernel(r, copies):
    groups, width = r.x.shape[0], r.cot.shape[3]
    rows, cols = r.own.shape[1], r.own.shape[2]
    x, mask, cot = fields(r)
    lines = (2 * rows + 2 * over) * groups, (rows + 2 * rim) * groups, (rows + 3) * groups
    for raw, read, first, count, w in (
        (r.raw_x, x, 0, lines[0], 2 * cols),
        (r.raw_m, mask, 0, lines[1], cols),
        (r.raw_c, cot, 2, lines[2], cols),
    ):
        for at in range(count):
            value = read(at % groups, at // groups + first)
            for k in range(raw.shape[0]):
                raw[k, at * w : (at + 1) * w, :] = value[:, k * 128 : (k + 1) * 128]
    for out, x0, m0, c0 in ((r.right, 2 * cols - over, cols - rim, cols - 2), (r.left, 0, 0, 0)):
        pieces = []
        for c in range(over):
            pieces.append([strided(r.raw_x, k, x0 + c, lines[0], 2 * cols) for k in range(2)])
        for c in range(0, rim + 1, 2):
            pieces.append([strided(r.raw_m, 0, m0 + min(c + k, rim - 1), lines[1], cols) for k in range(2)])
        for c in range(2):
            for h in range(0, width // 128, 2):
                pieces.append([strided(r.raw_c, h + k, c0 + c, lines[2], cols) for k in range(2)])
        at = 0
        for low, high in pieces:
            r.flat[at : at + low.shape[0], :] = jnp.concatenate([low, high], axis=1)
            at += low.shape[0]
        if at < r.flat.shape[0]:
            r.flat[at:, :] = jnp.zeros((r.flat.shape[0] - at, 256), f32)
        out[...] = r.flat[...].astype(bf16)


def stats_kernel(r, copies):
    groups, cin = r.x.shape[0], r.x.shape[3]
    rows, S = r.own.shape[1], r.own.shape[2]
    L = groups * S
    width = r.w1.shape[2]
    raw = r.raw
    for n in range(2 * rows + 1):
        for g in range(groups):
            line = n * groups + g
            src = (r.top[g, 0] if n == 0 else r.x[g, n - 1]).astype(f32)
            side = r.lft[g, n].astype(f32)
            for k in range(raw.shape[0]):
                raw[k, line, 7:8, :] = side[:, k * 128 : (k + 1) * 128]
                raw[k, line, 8:, :] = src[:, k * 128 : (k + 1) * 128]
    for out, n_rows, start in ((r.xe, rows, 1), (r.xo, rows + 1, 0)):
        for n in range(n_rows):
            for b in range(3):
                for k in range(raw.shape[0]):
                    parts = [
                        raw[k, (2 * n + start) * groups + g, pl.ds(7 + b, S, stride=2), :]
                        for g in range(groups)
                    ]
                    at = b * cin + k * 128
                    out[n * L : (n + 1) * L, at : at + 128] = jnp.concatenate(
                        parts, axis=0
                    ).astype(bf16)
    mask = jnp.concatenate(
        [r.own[g, i].astype(f32) for i in range(rows) for g in range(groups)], axis=0
    )
    M = rows * L
    copies.wait(N.w1)
    z = matmul(r.xo[0:M, :], r.w1[0])
    z += matmul(r.xe[...], r.w1[1])
    z += matmul(r.xo[L : L + M, :], r.w1[2])
    zp = matmul(r.xe[:, cin : 2 * cin], r.wp[...])
    zm, zpm = z * wide(mask, width), zp * wide(mask, width)
    row = jnp.concatenate(
        [column_sum(zm), column_sum(zm * z), column_sum(zpm), column_sum(zpm * zp), column_sum(mask)], axis=1
    )
    r.spread[...] = jnp.broadcast_to(row[None], r.spread.shape)
    copies.start(N.spread)
    copies.wait(N.spread)


def first_kernel(r, copies):
    groups, cin, width = r.x.shape[0], r.x.shape[3], r.cot.shape[3]
    rows, cols = r.own.shape[1], r.own.shape[2]
    S = cols + 8
    L = groups * S
    W = 2 * cols + 24
    V = cols + 16
    x, mask, cot = fields(r)
    lines = (2 * rows + 2 * over) * groups, (rows + 2 * rim) * groups, (rows + 3) * groups
    tail = jnp.zeros((W - 8 - 2 * cols, 128), f32)
    r.raw_m[...] = jnp.zeros(r.raw_m.shape, f32)
    r.raw_c[...] = jnp.zeros(r.raw_c.shape, f32)
    for at in range(lines[0]):
        value = x(at % groups, at // groups)
        for k in range(r.raw_x.shape[0]):
            r.raw_x[k, at * W + 8 : at * W + 8 + 2 * cols, :] = value[:, k * 128 : (k + 1) * 128]
            r.raw_x[k, at * W + 8 + 2 * cols : (at + 1) * W, :] = tail
    for strip, x0, m0, c0 in ((r.lft, 8 - over, 8 - rim, 6), (r.rgt, 8 + 2 * cols, 8 + cols, 8 + cols)):
        r.flat[...] = strip[...].astype(f32)
        at = 0
        for c in range(over):
            for k in range(2):
                r.raw_x[k, pl.ds(x0 + c, lines[0], stride=W), :] = r.flat[at : at + lines[0], k * 128 : (k + 1) * 128]
            at += lines[0]
        for c in range(0, rim + 1, 2):
            for k in range(2):
                if c + k < rim:
                    r.raw_m[0, pl.ds(m0 + c + k, lines[1], stride=V), :] = r.flat[
                        at : at + lines[1], k * 128 : (k + 1) * 128
                    ]
            at += lines[1]
        for c in range(2):
            for h in range(0, width // 128, 2):
                for k in range(2):
                    r.raw_c[h + k, pl.ds(c0 + c, lines[2], stride=V), :] = r.flat[
                        at : at + lines[2], k * 128 : (k + 1) * 128
                    ]
                at += lines[2]
    for out, n_rows, start in ((r.xe, rows + 5, 2), (r.xo, rows + 6, 1)):
        for n in range(n_rows):
            for b in range(3):
                for k in range(r.raw_x.shape[0]):
                    parts = [
                        strided(r.raw_x, k, ((2 * n + start) * groups + g) * W + 3 + b, S, 2) for g in range(groups)
                    ]
                    at = b * cin + k * 128
                    out[n * L : (n + 1) * L, at : at + 128] = jnp.concatenate(parts, axis=0).astype(bf16)
    copies.start(N.xe, N.xo)
    for at in range(lines[1]):
        r.raw_m[0, at * V + 8 : at * V + 8 + cols, :] = mask(at % groups, at // groups)
    for n in range(1, rows + 6):
        for g in range(groups):
            to, at = (n - 1) * L + g * S, (n * groups + g) * V
            r.maskp[to : to + S, :] = r.raw_m[0, at + 6 : at + 6 + S, :]
    for at in range(lines[2]):
        value = cot(at % groups, at // groups + 2)
        for k in range(r.raw_c.shape[0]):
            lanes = slice(k * 128, (k + 1) * 128)
            r.raw_c[k, at * V + 8 : at * V + 8 + cols, :] = value[:, lanes]
            r.cotq[at * S : (at + 1) * S, lanes] = r.raw_c[k, at * V + 7 : at * V + 7 + S, :]
    copies.start(N.cotq)
    r.ownp[...] = jnp.zeros(r.ownp.shape, f32)
    for i in range(rows):
        for g in range(groups):
            at = (i + 2) * L + g * S + 2
            r.ownp[at : at + cols, :] = r.own[g, i].astype(f32)
    copies.wait(N.w1, N.wp)
    for k, (m0, m) in enumerate(chunks(r.pre1.shape[0], r.pre1.shape[0] // 3)):
        z = matmul(r.xo[m0 : m0 + m, :], r.w1[0])
        z += matmul(r.xe[m0 : m0 + m, :], r.w1[1])
        z += matmul(r.xo[L + m0 : L + m0 + m, :], r.w1[2])
        r.pre1[m0 : m0 + m, :] = z
        copies.start((N.pre1, k))
        r.prep[m0 : m0 + m, :] = matmul(r.xe[m0 : m0 + m, cin : 2 * cin], r.wp[...])
        copies.start((N.prep, k))
    copies.wait(N.xe, N.xo, N.pre1, N.prep, N.cotq)


def second_kernel(r, copies):
    width = r.gain.shape[1]
    t = jnp.sum(r.tot1[...], axis=0)
    n = wide(t[:, 4 * width :], width)
    center, inv = moments(t[:, :width], t[:, width : 2 * width], n)
    proj = moments(t[:, 2 * width : 3 * width], t[:, 3 * width : 4 * width], n)
    r.mom1[...] = jnp.concatenate([center, inv, n, *proj, jnp.zeros((3, width), f32)], axis=0)
    scale = inv * r.gain[...]
    M, Q = r.pre1.shape[0], r.pre2.shape[0]
    L = (M - Q) // 2
    copies.wait(N.pre1)
    for m0, m in chunks(M, 104):
        v = (r.pre1[m0 : m0 + m, :] - center) * scale + r.shift[...]
        mask = wide(r.maskp[m0 : m0 + m, :], width)
        r.hid[m0 : m0 + m, :] = 0.5 * v * (1.0 + gelu_parts(v)) * mask
    r.hid[M:, :] = jnp.zeros((r.hid.shape[0] - M, width), f32)
    for m0, m in chunks(M, 208):
        for b in range(3):
            r.h3[m0 : m0 + m, b * width : (b + 1) * width] = r.hid[m0 + b : m0 + b + m, :].astype(bf16)
    copies.start(N.h3)
    copies.wait(N.w2)
    sums = [jnp.zeros((1, width), f32)] * 2
    for k, (m0, m) in enumerate(chunks(Q, Q // 3)):
        z = matmul(r.h3[m0 : m0 + m, :], r.w2[0])
        z += matmul(r.h3[L + m0 : L + m0 + m, :], r.w2[1])
        z += matmul(r.h3[2 * L + m0 : 2 * L + m0 + m, :], r.w2[2])
        r.pre2[m0 : m0 + m, :] = z
        copies.start((N.pre2, k))
        zm = z * wide(r.ownp[L + 1 + m0 : L + 1 + m0 + m, :], width)
        sums = [sums[0] + column_sum(zm), sums[1] + column_sum(zm * z)]
    row = jnp.concatenate(sums, axis=1)
    r.spread[...] = jnp.broadcast_to(row[None], r.spread.shape)
    copies.start(N.spread)
    copies.wait(N.h3, N.pre2, N.spread)


def part(r, at, *fields, first=0):
    bit = r.bits[0] == 1
    for k, field in enumerate(fields, first):
        half = field.shape[1] // 2
        low, high = field[:, :half], field[:, half:]
        r.mine[k, at : at + field.shape[0], :] = jnp.where(bit, high, low)
        r.theirs[k, at : at + field.shape[0], :] = jnp.where(bit, low, high)


def mine_of(r, row):
    half = row.shape[1] // 2
    return jnp.where(r.bits[0] == 1, row[:, half:], row[:, :half])


def third_kernel(r, copies):
    groups, rows, cols, width = r.out.shape
    S = cols + 8
    L = groups * S
    n = r.mom1[2:3, :]
    t = jnp.sum(r.tot2[...], axis=0)
    c2, i2 = moments(t[:, :width], t[:, width:], n)
    cp, ip = r.mom1[3:4, :], r.mom1[4:5, :]
    r.mom2[...] = jnp.concatenate([c2, i2, cp, ip, jnp.zeros((4, width), f32)], axis=0)
    sums = [jnp.zeros((1, width), f32)] * 3
    both_shift = r.shift2[...] + r.shiftp[...]
    total = r.grad.shape[0] // S
    for line in range(total):
        if line % (total // 2) == 0:
            k = line // (total // 2)
            copies.wait((N.pre2, k), (N.prep, k), (N.cotq, k))
        at = line * S
        shifted = slice(L + 1 + at, L + 1 + at + S)
        n2 = (r.pre2[at : at + S, :] - c2) * i2
        np_ = (r.prep[shifted, :] - cp) * ip
        v = n2 * r.gain2[...] + np_ * r.gainp[...] + both_shift
        mask = wide(r.maskp[shifted, :], width)
        own = wide(r.ownp[shifted, :], width)
        t = gelu_parts(v)
        r.field[at : at + S, :] = 0.5 * v * (1.0 + t) * mask
        g = gelu_slope(v, t) * mask * r.cotq[at : at + S, :]
        r.grad[at : at + S, :] = g
        g = g * own
        if L <= at < L + r.mine.shape[1]:
            part(r, at - L, g, n2 * own, np_ * own)
            if at - L + S == r.mine.shape[1] // 2:
                copies.start((N.mine, 0), (N.theirs, 0))
        new = [column_sum(g * n2), column_sum(g), column_sum(g * np_)]
        sums = [a + b for a, b in zip(sums, new)]
        if (line + 1) % (total // 2) == 0:
            copies.start((N.grad, (line + 1) // (total // 2) - 1))
    row = jnp.concatenate(sums, axis=1)
    r.spread[...] = jnp.broadcast_to(row[None], r.spread.shape)
    copies.start(N.spread, (N.mine, 1), (N.theirs, 1))
    for i in range(rows):
        for g in range(groups):
            at = (i + 1) * L + g * S + 1
            r.out[g, i, :, :] = r.field[at : at + cols, :].astype(bf16)
    copies.start(N.out)
    copies.wait(N.grad, N.out, N.spread, N.mine, N.theirs)


def fourth_kernel(r, copies):
    width = r.gain.shape[1]
    Q, U, rows_w = r.pre2.shape[0], r.act.shape[0], r.gpu.shape[0]
    L = U - rows_w
    center, inv, n = (r.mom1[k : k + 1, :] for k in range(3))
    c2, i2, cp, ip = (r.mom2[k : k + 1, :] for k in range(4))
    t3 = jnp.sum(r.tot3[...], axis=0)
    gg2, gs, ggp = (t3[:, k * width : (k + 1) * width] for k in range(3))
    r.gain_second[...], r.shift_second[...], r.gain_proj[...], r.shift_proj[...] = gg2, gs, ggp, gs
    tiny = N.gain_second, N.shift_second, N.gain_proj, N.shift_proj
    copies.start(*tiny)
    for m0, m in chunks(Q, L):
        if m0 in (0, 6 * L):
            copies.wait((N.grad, m0 // (6 * L)), (N.pre2, m0 // (6 * L)))
        mask = wide(r.maskp[L + 1 + m0 : L + 1 + m0 + m, :], width) / n
        n2 = (r.pre2[m0 : m0 + m, :] - c2) * i2
        back = mask * (gs + n2 * gg2)
        r.gq[m0 : m0 + m, :] = (r.gain2[...] * i2) * (r.grad[m0 : m0 + m, :] - back)
    r.gq[Q:, :] = jnp.zeros((r.gq.shape[0] - Q, width), f32)
    for m0, m in chunks(Q, 176):
        for b in range(3):
            r.g3[m0 : m0 + m, b * width : (b + 1) * width] = r.gq[m0 + b : m0 + b + m, :].astype(bf16)
    copies.wait(N.keep)
    for m0, m in chunks(U, L):
        frame = slice(2 * L + 2 + m0, 2 * L + 2 + m0 + m)
        n1 = (r.keep[frame, :] - center) * inv
        v = n1 * r.gain[...] + r.shift[...]
        mask = wide(r.maskp[frame, :], width)
        r.act[m0 : m0 + m, :] = gelu_slope(v, gelu_parts(v)) * mask
        r.normed[m0 : m0 + m, :] = n1 * mask
        if m0 < rows_w:
            part(r, m0, n1 * wide(r.ownp[frame, :], width), first=1)
    copies.start(N.normed, (N.mine, 1), (N.theirs, 1))
    for a in range(3):
        copies.wait((N.w2, a))
        gh = jnp.zeros((U, width), f32)
        for b in range(3):
            gh += matmul_nt(
                r.g3[L * a : L * a + U, b * width : (b + 1) * width],
                r.w2[2 - a, (2 - b) * width : (3 - b) * width, :],
            )
        r.gh[...] = gh if a == 0 else r.gh[...] + gh
    sums = [jnp.zeros((1, width), f32)] * 2
    for m0, m in chunks(U, L):
        g = r.act[m0 : m0 + m, :] * r.gh[m0 : m0 + m, :]
        r.act[m0 : m0 + m, :] = g
        g = g * wide(r.ownp[2 * L + 2 + m0 : 2 * L + 2 + m0 + m, :], width)
        if m0 < rows_w:
            part(r, m0, g)
        sums = [sums[0] + column_sum(g * r.normed[m0 : m0 + m, :]), sums[1] + column_sum(g)]
    row = jnp.concatenate(sums, axis=1)
    r.spread[...] = jnp.broadcast_to(row[None], r.spread.shape)
    copies.start(N.spread, (N.mine, 0), (N.theirs, 0), N.act)
    copies.wait(N.prep)
    for m0, m in chunks(rows_w, L):
        frame = slice(2 * L + 2 + m0, 2 * L + 2 + m0 + m)
        mask = wide(r.maskp[frame, :], width) / n
        back = mask * (gs + (r.prep[frame, :] - cp) * ip * ggp)
        r.gpu[m0 : m0 + m, :] = ((r.gainp[...] * ip) * (r.grad[L + 1 + m0 : L + 1 + m0 + m, :] - back)).astype(bf16)
    copies.start(N.gpu)
    copies.wait(N.normed, N.mine, N.theirs, N.spread, N.act, N.gpu, *tiny)


def split_store(r, rows, unit, first):
    quarter = unit // 4
    for k in range(rows // unit):
        for bit, base, sent, kept in ((1, 0, r.sent_a, r.kept_a), (2, 2 * quarter, r.sent_b, r.kept_b)):
            keep = pl.multiple_of(k * unit + base + r.bits[bit] * quarter, quarter)
            send = pl.multiple_of(k * unit + base + (1 - r.bits[bit]) * quarter, quarter)
            sent[first + k] = r.acc[pl.ds(send, quarter), :].astype(bf16)
            kept[first + k] = r.acc[pl.ds(keep, quarter), :]


def weights_second_kernel(r, copies):
    width = r.h3.shape[1] // 3
    cin = r.xe.shape[1] // 3
    rows_w = r.mine.shape[1]
    L = (r.h3.shape[0] - rows_w) // 5
    per = width // cin
    t3 = jnp.sum(r.tot3[...], axis=0)
    n = mine_of(r, r.mom1[2:3, :])
    gg2, gs, ggp = (mine_of(r, t3[:, k * width : (k + 1) * width]) / n for k in range(3))
    scale2, scalep = mine_of(r, r.gain2[...] * r.mom2[1:2, :]), mine_of(r, r.gainp[...] * r.mom2[3:4, :])
    half = scale2.shape[1]
    for source, name, own, out in ((r.mine, N.mine, r.ownp, r.near), (r.far3, N.far3, r.ownp_far, r.far)):
        copies.wait(name)
        r.pad[:, 0:8, :] = jnp.zeros((3, 8, half), f32)
        r.pad[:, 8:, :] = source[...]
        for m0, m in chunks(rows_w, 96):
            mask = wide(own[2 * L + 1 + m0 : 2 * L + 1 + m0 + m, :], half)
            rows = slice(8 + m0, 8 + m0 + m)
            back = mask * gs + r.pad[1, rows, :] * gg2
            out[m0 : m0 + m, :] = (scale2 * (r.pad[0, rows, :] - back)).astype(bf16)
            mask = wide(own[2 * L + m0 : 2 * L + m0 + m, :], half)
            rows = slice(7 + m0, 7 + m0 + m)
            back = mask * gs + r.pad[2, rows, :] * ggp
            out[rows_w + m0 : rows_w + m0 + m, :] = (scalep * (r.pad[0, rows, :] - back)).astype(bf16)
    for b in range(3):
        lanes = slice(b * width, (b + 1) * width)
        copies.wait((N.h3, b), (N.h3_far, b))
        for a in range(3):
            at = L * a + L
            r.acc[...] = matmul_tn(r.h3[at : at + rows_w, lanes], r.near[:rows_w, :]) + matmul_tn(
                r.h3_far[at : at + rows_w, lanes], r.far[:rows_w, :]
            )
            split_store(r, width, cin, (3 * b + a) * per)
        copies.start(*((name, b) for name in CHUNKS))
    at = 2 * L
    copies.wait(N.xe, N.xe_far)
    middle = slice(cin, 2 * cin)
    r.acc[0:cin, :] = matmul_tn(r.xe[at : at + rows_w, middle], r.near[rows_w:, :]) + matmul_tn(
        r.xe_far[at : at + rows_w, middle], r.far[rows_w:, :]
    )
    split_store(r, cin, cin, 9 * per)
    copies.start(*((name, 3) for name in CHUNKS))
    copies.wait(*CHUNKS)


def first_back(r, gg, gs, count):
    width = r.gain.shape[1]
    U = r.act.shape[0]
    L = U - r.rows_w
    inv, n = r.mom1[1:2, :], r.mom1[2:3, :]
    gg, gs = gg / n, gs / n
    scale = r.gain[...] * inv
    r.gf[0:8, :] = jnp.zeros((8, width), f32)
    r.gf[8 + count :, :] = jnp.zeros((r.gf.shape[0] - 8 - count, width), f32)
    for m0, m in chunks(count, L):
        mask = wide(r.maskp[2 * L + 2 + m0 : 2 * L + 2 + m0 + m, :], width)
        back = mask * gs + r.normed[m0 : m0 + m, :] * gg
        r.gf[8 + m0 : 8 + m0 + m, :] = scale * (r.act[m0 : m0 + m, :] - back)


def weights_first_kernel(r, copies):
    rows_w = r.mine.shape[1]
    cin = r.xe.shape[1] // 3
    L = (r.xe.shape[0] - rows_w) // 5
    width = r.gain.shape[1]
    t4 = jnp.sum(r.tot4[...], axis=0)
    r.gain_first[...], r.shift_first[...] = t4[:, :width], t4[:, width:]
    copies.start(N.gain_first, N.shift_first)
    n = mine_of(r, r.mom1[2:3, :])
    gg, gs = mine_of(r, t4[:, :width]) / n, mine_of(r, t4[:, width:]) / n
    scale = mine_of(r, r.gain[...] * r.mom1[1:2, :])
    half = scale.shape[1]
    for source, name, own, out in ((r.mine, N.mine, r.ownp, r.near), (r.far4, N.far4, r.ownp_far, r.far)):
        copies.wait(name)
        r.pad[:, 0:8, :] = jnp.zeros((2, 8, half), f32)
        r.pad[:, 8:, :] = source[...]
        for m0, m in chunks(rows_w, 96):
            mask = wide(own[2 * L + m0 : 2 * L + m0 + m, :], half)
            rows = slice(6 + m0, 6 + m0 + m)
            back = mask * gs + r.pad[1, rows, :] * gg
            out[m0 : m0 + m, :] = (scale * (r.pad[0, rows, :] - back)).astype(bf16)
    copies.wait(N.xe, N.xe_far)
    for k, a in enumerate((1, 0, 2)):
        if k == 1:
            copies.wait(N.xo, N.xo_far)
        source, source_far = (r.xe, r.xe_far) if a == 1 else (r.xo, r.xo_far)
        at = (3 if a == 2 else 2) * L
        for b in range(3):
            lanes = slice(b * cin, (b + 1) * cin)
            r.acc[lanes, :] = matmul_tn(source[at : at + rows_w, lanes], r.near[...]) + matmul_tn(
                source_far[at : at + rows_w, lanes], r.far[...]
            )
        split_store(r, 3 * cin, cin, a * 3)
        copies.start(*((name, a) for name in CHUNKS))
    copies.wait(N.gain_first, N.shift_first, *CHUNKS)


def inputs_kernel(r, copies):
    width = r.gpu.shape[1]
    groups, rows, cols = r.out.shape[0], r.out.shape[1] // 2, r.out.shape[2] // 2
    cin = r.out.shape[3]
    M = r.gpu.shape[0]
    S = cols + 8
    L = groups * S
    lines = r.lines
    U = r.act.shape[0]
    r.rows_w = M
    copies.wait(N.act, N.normed)
    first_back(r, r.gg[...], r.gs[...], U)
    for m0, m in chunks(U, 144):
        r.gu[m0 : m0 + m, :width] = r.gf[8 + m0 : 8 + m0 + m, :].astype(bf16)
        r.gu[m0 : m0 + m, width:] = r.gf[9 + m0 : 9 + m0 + m, :].astype(bf16)
    copies.wait(N.gpu, N.w1, N.wp)

    def tap(m0, m, a, b):
        di, dj = (1 if a == 0 else 0), (1 if b == 0 else 0)
        return matmul_nt(
            r.gu[di * L + m0 : di * L + m0 + m, dj * width : (dj + 1) * width],
            r.w1[a, b * cin : (b + 1) * cin, :],
        )

    for m0, m in chunks(M, 2 * L):
        pieces = {
            (0, 0): tap(m0, m, 1, 1) + matmul_nt(r.gpu[m0 : m0 + m, :], r.wp[...]),
            (0, 1): tap(m0, m, 1, 2) + tap(m0, m, 1, 0),
            (1, 0): tap(m0, m, 2, 1) + tap(m0, m, 0, 1),
            (1, 1): tap(m0, m, 2, 2) + tap(m0, m, 2, 0) + tap(m0, m, 0, 2) + tap(m0, m, 0, 0),
        }
        for (ro, co), v in pieces.items():
            for k in range(m // S):
                line = m0 // S + k
                i, g = line // groups, line % groups
                for h in range(lines.shape[0]):
                    lines[h, (2 * i + ro) * groups + g, pl.ds(co, cols, stride=2), :] = v[
                        k * S : k * S + cols, h * 128 : (h + 1) * 128
                    ]
    for n in range(2 * rows):
        for g in range(groups):
            for h in range(lines.shape[0]):
                r.out[g, n, :, h * 128 : (h + 1) * 128] = lines[h, n * groups + g].astype(bf16)
    copies.start(N.out)
    copies.wait(N.out)


def widen(half, side, taps, per, swapped, into=None):
    total, n, m = half.shape
    extra = total - taps * per
    order = [(t % 3 * 3 + t // 3) if swapped else t for t in range(taps)]
    jobs = [(t * per, per, 0, order[t] * per) for t in range(taps)] + [(taps * per, 1, 1, 0)] * extra
    more = list(into or [])

    def body(side_ref, half_ref, *refs):
        outs = refs[len(more) : len(more) + 1 + extra]
        narrow, full, sems = refs[len(more) + 1 + extra :]
        lanes = pl.ds(pl.multiple_of(side_ref[0] * m, m), m)
        reads = [
            pltpu.make_async_copy(half_ref.at[pl.ds(at, size)], narrow.at[pl.ds(at, size)], sems.at[0, k])
            for k, (at, size, _, _) in enumerate(jobs)
        ]
        writes = [
            pltpu.make_async_copy(full.at[pl.ds(at, size)], outs[which].at[pl.ds(to, size), :, lanes], sems.at[1, k])
            for k, (at, size, which, to) in enumerate(jobs)
        ]
        for read in reads:
            read.start()
        for k, (at, size, _, _) in enumerate(jobs):
            reads[k].wait()
            full[at : at + size] = narrow[at : at + size].astype(f32)
            writes[k].start()
        for write in writes:
            write.wait()

    hbm = pl.BlockSpec(memory_space=pltpu.HBM)
    return pl.pallas_call(
        body,
        out_shape=[shape((taps * per, n, 2 * m))] + [shape((1, n, 2 * m))] * extra,
        in_specs=[pl.BlockSpec(memory_space=pltpu.SMEM)] + [hbm] * (1 + len(more)),
        out_specs=[hbm] * (1 + extra),
        scratch_shapes=[
            pltpu.VMEM((total, n, m), bf16),
            pltpu.VMEM((total, n, m), f32),
            pltpu.SemaphoreType.DMA((2, len(jobs))),
        ],
        input_output_aliases={2 + k: k for k in range(len(more))},
        compiler_params=pltpu.CompilerParams(vmem_limit_bytes=20 * 1024 * 1024),
        cost_estimate=pl.CostEstimate(flops=0, bytes_accessed=0, transcendentals=0),
    )(side.reshape(1), half, *more)


def halve_kernel(r, copies):
    for p in range(r.count):
        kept, got = getattr(r, f"kept{p}"), getattr(r, f"got{p}")
        copies.wait(f"kept{p}", f"got{p}")
        to_send, to_keep = getattr(r, f"sent{p}"), getattr(r, f"left{p}")
        bit = r.bits[r.steps[p]] == 1
        h = kept.shape[1] // 2
        for t in range(kept.shape[0]):
            total = kept[t] + got[t].astype(f32)
            low, high = total[:h], total[h:]
            to_send[t] = jnp.where(bit, low, high).astype(bf16)
            to_keep[t] = jnp.where(bit, high, low)
        copies.start(f"sent{p}", f"left{p}")
    copies.wait(*(name for name in copies.jobs if name[:4] in (N.sent, N.left)))


def halve(bits, pairs, steps, cost):
    ins = dict(bits=bits)
    for p, (kept, got) in enumerate(pairs):
        ins[f"kept{p}"], ins[f"got{p}"] = kept, got
    taps, n, m = pairs[0][0].shape
    dims = (taps, n // 2, m)
    names = [str(p) for p in range(len(pairs))]
    outs = {}
    for name in names:
        outs[N.sent + name], outs[N.left + name] = shape(dims, bf16), shape(dims)

    def body(r, copies):
        r.count, r.steps = len(pairs), steps
        halve_kernel(r, copies)

    far_in = tuple(n for n in ins if n != N.bits)
    out = call(body, ins, outs, far_in=far_in, far_out=tuple(outs), smem=(N.bits,), cost=cost, limit=60)
    return [(out[N.sent + name], out[N.left + name]) for name in names]


def shifted(value, axis, steps):
    count = lax.axis_size(axis)
    first, last = (max(0, -steps), min(count, count - steps))
    return lax.ppermute(value, axis, [(source, source + steps) for source in range(first, last)])


def gather_sum(spread):
    return lax.all_to_all(spread, axes, 0, 0)


def bit_of(axis, step):
    return (lax.axis_index(axis) // step) % 2


def partner(value, axis, step):
    count = lax.axis_size(axis)
    return lax.ppermute(value, axis, [(i, i ^ step) for i in range(count)])


def steps_of(axis):
    count, step, out = lax.axis_size(axis), 1, []
    while step < count:
        out.append((axis, step))
        step *= 2
    return out


def split(total, axis, step):
    n = total.shape[1] // 2
    bit = bit_of(axis, step) == 1
    low, high = total[:, :n], total[:, n:]
    return jnp.where(bit, low, high).astype(bf16), jnp.where(bit, high, low)


def joined(value, other, axis, step, dim=1):
    bit = bit_of(axis, step) == 1
    return jnp.concatenate([jnp.where(bit, other, value), jnp.where(bit, value, other)], axis=dim)


def gathered(pieces, spots, cost=0):
    taps, h, m = pieces[0].shape
    count = len(pieces)

    def body(spots_ref, *refs):
        out, sems = refs[count:]
        copies = []
        for q in range(count):
            rows = pl.ds(pl.multiple_of(spots_ref[q] * h, h), h)
            copies.append(pltpu.make_async_copy(refs[q], out.at[:, rows], sems.at[q]))
        for copy in copies:
            copy.start()
        for copy in copies:
            copy.wait()

    anywhere = pl.BlockSpec(memory_space=pl.ANY)
    return pl.pallas_call(
        body,
        out_shape=shape((taps, count * h, m), pieces[0].dtype),
        in_specs=[pl.BlockSpec(memory_space=pltpu.SMEM)] + [anywhere] * count,
        out_specs=anywhere,
        scratch_shapes=[pltpu.SemaphoreType.DMA((count,))],
        compiler_params=pltpu.CompilerParams(vmem_limit_bytes=16 * 1024 * 1024),
        cost_estimate=pl.CostEstimate(flops=cost, bytes_accessed=0, transcendentals=0),
    )(spots, *pieces)


class Tree:
    def __init__(self, parts, bits, plane, rest, core):
        self.bits, self.place = bits, {step: k for k, step in enumerate([core, *plane, *rest])}
        self.sent_a, self.kept_a, self.sent_b, self.kept_b = parts
        self.a, self.b, self.rest, self.core = plane, plane[::-1], rest, core
        p, n = len(plane), len(rest)
        self.stages = [(N.plane, k) for k in range(p)] + [(N.rest, k) for k in range(n)]
        self.stages += [(N.rest_join, k) for k in reversed(range(n))] + [(N.plane_join, k) for k in reversed(range(p))]
        self.stages += [(N.core, 0)]

    def next(self):
        return self.stages[0] if self.stages else None

    def start(self):
        kind, k = self.stages[0]
        if kind == N.plane:
            self.got = partner(self.sent_a, *self.a[k]), partner(self.sent_b, *self.b[k])
        elif kind == N.rest:
            self.got = (partner(self.sent, *self.rest[k]),)
        elif kind == N.rest_join:
            self.got = (partner(self.value, *self.rest[k]),)
        elif kind == N.plane_join:
            self.got = partner(self.value_a, *self.a[k]), partner(self.value_b, *self.b[k])
        else:
            self.got = (partner(self.value, *self.core),)

    def finish(self, cost=0):
        kind, k = self.stages.pop(0)
        if kind == N.plane:
            pairs = [(self.kept_a, self.got[0]), (self.kept_b, self.got[1])]
            nexts = [order[k + 1] for order in (self.a, self.b) if k + 1 < len(order)]
            if nexts and cost:
                pairs = halve(self.bits, pairs, [self.place[step] for step in nexts], cost)
                (self.sent_a, self.kept_a), (self.sent_b, self.kept_b) = pairs
                return
            total_a, total_b = (kept + got.astype(f32) for kept, got in pairs)
            if nexts:
                self.sent_a, self.kept_a = split(total_a, *nexts[0])
                self.sent_b, self.kept_b = split(total_b, *nexts[1])
            else:
                self.taps = total_a.shape[0]
                self.split_rest(jnp.concatenate([total_a, total_b], axis=0), 0)
        elif kind == N.rest:
            self.split_rest(self.kept + self.got[0].astype(f32), k + 1)
        elif kind == N.rest_join:
            self.value = joined(self.value, self.got[0], *self.rest[k])
            self.value_a, self.value_b = self.value[: self.taps], self.value[self.taps :]
        elif kind == N.plane_join:
            if k == 0 and cost:
                low, high = (self.bits[self.place[step]] for step in (self.a[0], self.b[0]))
                spots = jnp.stack([low, 1 - low, 2 + high, 3 - high])
                self.value = gathered([self.value_a, self.got[0], self.value_b, self.got[1]], spots, cost)
            else:
                self.value_a = joined(self.value_a, self.got[0], *self.a[k])
                self.value_b = joined(self.value_b, self.got[1], *self.b[k])
                self.value = jnp.concatenate([self.value_a, self.value_b], axis=1)

    def split_rest(self, total, k):
        if k < len(self.rest):
            self.sent, self.kept = split(total, *self.rest[k])
        else:
            self.value = total.astype(bf16)


def lockstep(*trees, beside=()):
    for t in trees:
        t.start()
    got, beside = lax.optimization_barrier(([t.got for t in trees], beside))
    for t, g in zip(trees, got):
        t.got = g
        t.finish()
    return beside


def on_device(inputs, w_first, gain_first, shift_first, w_second, gain_second, shift_second, w_proj, gain_proj, shift_proj, valid_mask, cotangent):
    groups, rows_in, cols_in, cin = inputs.shape
    rows, cols = rows_in // 2, cols_in // 2
    width = w_first.shape[3]
    half = width // 2
    S = cols + 8
    L = groups * S
    devices = lax.axis_size(N.rows) * lax.axis_size(N.cols) * lax.axis_size(N.grp)
    plane = steps_of(N.cols)
    core = steps_of(N.rows)[0]
    rest = steps_of(N.rows)[1:] + steps_of(N.grp)
    bits = jnp.stack([bit_of(*step) for step in (core, *plane, *rest)]).astype(jnp.int32)
    w1 = w_first.reshape(3, 3 * cin, width)
    w2 = w_second.reshape(3, 3 * width, width)
    as_row = lambda v: v.reshape(1, -1)
    own = jnp.broadcast_to(valid_mask.astype(bf16)[..., None], valid_mask.shape + (128,))
    MP, MQ, MU, MW = (rows + 5) * L, (rows + 3) * L, (rows + 1) * L, rows * L
    px = lambda m, k: 2 * m * k * width
    vec = lambda k: shape((1, k * width))
    all_devices = lambda k: shape((devices, 1, k))
    g1, b1, g2, b2, gp, bp = map(
        as_row, (gain_first, shift_first, gain_second, shift_second, gain_proj, shift_proj)
    )

    top1 = shifted(inputs[:, -1:], N.rows, 1)
    me, count = lax.axis_index(N.rows), lax.axis_size(N.rows)
    flags = jnp.stack([me > 0, me < count - 1]).astype(jnp.int32)
    flat_rows = shape((over * groups * cols_in + (width // 256 + 1) * rim * groups * cols, 256), bf16)
    packed = call(
        vertical_kernel,
        dict(flags=flags, x=inputs, cot=cotangent, own=own),
        dict(down=flat_rows) if count == 2 else dict(down=flat_rows, up=flat_rows),
        far_in=(N.x, N.cot),
        smem=(N.flags,),
        parts=dict(x=end_parts(rows_in, over), cot=end_parts(rows, rim)),
    )
    if count == 2:
        top = bot = lax.ppermute(packed["down"], "rows", [(0, 1), (1, 0)])
    else:
        top, bot = shifted(packed[N.down], N.rows, 1), shifted(packed[N.up], N.rows, -1)
    (top, bot), top1 = lax.optimization_barrier(((top, bot), top1))
    lines = (rows_in + 2 * over) * groups, (rows + 2 * rim) * groups, (rows + 3) * groups
    n_strip = over * lines[0] + (rim + 1) // 2 * lines[1] + width // 128 * lines[2]
    n_strip = -(-n_strip // 16) * 16
    near = dict(flags=flags, x=inputs, cot=cotangent, own=own, top=top, bot=bot)
    strips = call(
        strips_kernel,
        near,
        dict(right=shape((n_strip, 256), bf16), left=shape((n_strip, 256), bf16)),
        dict(
            raw_x=pltpu.VMEM((cin // 128, lines[0] * cols_in, 128), f32),
            raw_m=pltpu.VMEM((1, lines[1] * cols, 128), f32),
            raw_c=pltpu.VMEM((width // 128, lines[2] * cols, 128), f32),
            flat=pltpu.VMEM((n_strip, 256), f32),
        ),
        smem=(N.flags,),
    )
    edge = jnp.concatenate([top1[:, :, -1:], inputs[:, :, -1:]], axis=1)
    edge, right, left = lax.optimization_barrier((edge, strips[N.right], strips[N.left]))
    lft1, right, left = lax.optimization_barrier((shifted(edge, N.cols, 1), right, left))
    lft, rgt = shifted(right, N.cols, 1), shifted(left, N.cols, -1)
    stats = call(
        stats_kernel,
        dict(x=inputs, top=top1, lft=lft1, own=own, w1=w1, wp=w_proj),
        dict(spread=all_devices(4 * width + 128)),
        dict(
            raw=pltpu.VMEM((cin // 128, (rows_in + 1) * groups, cols_in + 8, 128), f32),
            xe=pltpu.VMEM((rows * groups * cols, 3 * cin), bf16),
            xo=pltpu.VMEM(((rows + 1) * groups * cols, 3 * cin), bf16),
        ),
        far_in=(N.w1,),
        far_out=(N.spread,),
    )
    tot1 = gather_sum(stats[N.spread])

    first = call(
        first_kernel,
        dict(**near, lft=lft, rgt=rgt, w1=w1, wp=w_proj),
        dict(
            pre1=shape((MP, width)),
            prep=shape((MP, width)),
            xe=shape((MP, 3 * cin), bf16),
            xo=shape((MP + L, 3 * cin), bf16),
            ownp=shape((MP, 128)),
            maskp=shape((MP, 128)),
            cotq=shape((MQ, width)),
        ),
        dict(
            raw_x=pltpu.VMEM((cin // 128, lines[0] * (cols_in + 24), 128), f32),
            raw_m=pltpu.VMEM((1, lines[1] * (cols + 16), 128), f32),
            raw_c=pltpu.VMEM((width // 128, lines[2] * (cols + 16), 128), f32),
            flat=pltpu.VMEM((n_strip, 256), f32),
        ),
        far_in=(N.w1, N.wp),
        far_out=(N.xe, N.xo, N.pre1, N.prep, N.cotq),
        smem=(N.flags,),
        cost=20000000000,
        parts=dict(pre1=row_parts(MP, 3), prep=row_parts(MP, 3)),
    )
    xe, xo, ownp, maskp = first[N.xe], first[N.xo], first[N.ownp], first[N.maskp]
    far_xe, far_xo = partner(xe, *core), partner(xo, *core)

    second = call(
        second_kernel,
        dict(pre1=first[N.pre1], tot1=tot1, gain=g1, shift=b1, maskp=maskp, ownp=ownp, w2=w2),
        dict(h3=shape((MP, 3 * width), bf16), pre2=shape((MQ, width)), spread=all_devices(2 * width), mom1=shape((8, width))),
        dict(hid=pltpu.VMEM((MP + 8, width), f32)),
        far_in=(N.pre1, N.w2),
        far_out=(N.h3, N.pre2, N.spread),
        parts=dict(pre2=row_parts(MQ, 3)),
    )
    h3, pre2, mom1 = second[N.h3], second[N.pre2], second[N.mom1]
    tot2 = gather_sum(second[N.spread])
    tot2, far_h3 = lax.optimization_barrier((tot2, partner(h3, *core)))

    third = call(
        third_kernel,
        dict(
            bits=bits, pre2=pre2, prep=first[N.prep], mom1=mom1, tot2=tot2, gain2=g2, shift2=b2, gainp=gp, shiftp=bp,
            maskp=maskp, ownp=ownp, cotq=first[N.cotq],
        ),
        dict(
            out=shape((groups, rows, cols, width), bf16),
            grad=shape((MQ, width)),
            spread=all_devices(3 * width),
            mom2=shape((8, width)),
            mine=shape((3, MW, half)),
            theirs=shape((3, MW, half)),
        ),
        dict(field=pltpu.VMEM((MQ, width), f32)),
        far_in=(N.pre2, N.prep, N.cotq),
        far_out=(N.grad, N.spread, N.mine, N.theirs, N.out),
        smem=(N.bits,),
        parts=dict(
            mine=middle_parts(MW, 2), theirs=middle_parts(MW, 2),
            grad=row_parts(MQ, 2), pre2=row_parts(MQ, 2), cotq=row_parts(MQ, 2), prep=cuts(L, L + MQ // 2 + 8, L + MQ + 8)
        ),
    )
    mom2 = third[N.mom2]
    tot3 = gather_sum(third[N.spread])
    ownp_here, far3 = lax.optimization_barrier((ownp, partner(third[N.theirs], *core)))
    ownp_far = partner(ownp_here, *core)

    def chunk_shapes(taps):
        dims = (taps, cin // 4, half)
        return dict(sent_a=shape(dims, bf16), kept_a=shape(dims), sent_b=shape(dims, bf16), kept_b=shape(dims))

    per = width // cin
    taps2 = 9 * per + 1
    second_parts = call(
        weights_second_kernel,
        dict(
            bits=bits, mine=third[N.mine], far3=far3, h3=h3, h3_far=far_h3, xe=xe, xe_far=far_xe,
            tot3=tot3, mom1=mom1, mom2=mom2, gain2=g2, gainp=gp, ownp=ownp, ownp_far=ownp_far,
        ),
        chunk_shapes(taps2),
        dict(
            acc=pltpu.VMEM((width, half), f32),
            pad=pltpu.VMEM((3, MW + 8, half), f32),
            near=pltpu.VMEM((2 * MW, half), bf16),
            far=pltpu.VMEM((2 * MW, half), bf16),
        ),
        far_in=(N.mine, N.far3, N.h3, N.h3_far, N.xe, N.xe_far),
        far_out=CHUNKS,
        smem=(N.bits,),
        parts=dict(
            h3=lane_parts(3 * width, 3, pl.ds(L, MW + 2 * L)),
            h3_far=lane_parts(3 * width, 3, pl.ds(L, MW + 2 * L)),
            xe=[(0, (pl.ds(2 * L, MW), pl.ds(cin, cin)))],
            xe_far=[(0, (pl.ds(2 * L, MW), pl.ds(cin, cin)))],
            **{name: row_parts(taps2 - 1, 3) + [(3, (pl.ds(taps2 - 1, 1),))] for name in CHUNKS},
        ),
    ).values()
    grad, *second_parts = lax.optimization_barrier((third[N.grad], *second_parts))
    tree2 = Tree(second_parts, bits, plane, rest, core)
    tree2.start()
    hidden = call(
        fourth_kernel,
        dict(
            bits=bits, grad=grad, pre2=pre2, keep=first[N.pre1], w2=w2, prep=first[N.prep], mom1=mom1, mom2=mom2, tot3=tot3,
            gain=g1, shift=b1, gain2=g2, gainp=gp, maskp=maskp, ownp=ownp,
        ),
        dict(
            act=shape((MU, width)), normed=shape((MU, width)), spread=all_devices(2 * width),
            mine=shape((2, MW, half)), theirs=shape((2, MW, half)), gpu=shape((MW, width), bf16),
            gain_second=vec(1), shift_second=vec(1), gain_proj=vec(1), shift_proj=vec(1),
        ),
        dict(
            gq=pltpu.VMEM((MQ + 8, width), f32),
            g3=pltpu.VMEM((MQ, 3 * width), bf16),
            gh=pltpu.VMEM((MU, width), f32),
        ),
        far_in=(N.grad, N.pre2, N.keep, N.w2, N.prep),
        far_out=(
            N.act, N.normed, N.spread, N.mine, N.theirs, N.gpu, N.gain_second, N.shift_second, N.gain_proj, N.shift_proj
        ),
        smem=(N.bits,),
        limit=52,
        parts=dict(
            grad=cuts(0, 6 * L, MQ),
            pre2=cuts(0, 6 * L, MQ),
            keep=cuts(2 * L, 2 * L + MU + 8),
            w2=[(k, (pl.ds(2 - k, 1),)) for k in range(3)],
            prep=cuts(2 * L, 2 * L + MW + 8),
            mine=row_parts(2, 2),
            theirs=row_parts(2, 2),
        ),
    )
    tot4 = gather_sum(hidden[N.spread])
    tree2.finish(20000000000)
    near1, tree2.sent_a, tree2.sent_b = lax.optimization_barrier((hidden[N.mine], tree2.sent_a, tree2.sent_b))
    tree2.start()
    fifth = call(
        weights_first_kernel,
        dict(
            bits=bits, mine=near1, far4=partner(hidden[N.theirs], *core), xe=xe, xe_far=far_xe, xo=xo, xo_far=far_xo,
            tot4=tot4, mom1=mom1, gain=g1, ownp=ownp, ownp_far=ownp_far,
        ),
        dict(**chunk_shapes(9), gain_first=vec(1), shift_first=vec(1)),
        dict(
            acc=pltpu.VMEM((3 * cin, half), f32),
            pad=pltpu.VMEM((2, MW + 8, half), f32),
            near=pltpu.VMEM((MW, half), bf16),
            far=pltpu.VMEM((MW, half), bf16),
        ),
        far_in=(N.mine, N.far4, N.xe, N.xe_far, N.xo, N.xo_far),
        cost=20000000000,
        far_out=(*CHUNKS, N.gain_first, N.shift_first),
        smem=(N.bits,),
        parts=dict(
            xe=cuts(2 * L, 2 * L + MW),
            xe_far=cuts(2 * L, 2 * L + MW),
            xo=cuts(2 * L, 3 * L + MW),
            xo_far=cuts(2 * L, 3 * L + MW),
            **{name: row_parts(9, 3) for name in CHUNKS},
        ),
    )
    first_parts = [fifth[name] for name in CHUNKS]
    tree2.got, *first_parts = lax.optimization_barrier((tree2.got, *first_parts))
    tree2.finish()
    tree1 = Tree(first_parts, bits, plane, rest, core)

    grad_inputs = call(
        inputs_kernel,
        dict(
            act=hidden[N.act], normed=hidden[N.normed], gpu=hidden[N.gpu], w1=w1, wp=w_proj, mom1=mom1, gain=g1, maskp=maskp,
            gg=fifth[N.gain_first], gs=fifth[N.shift_first],
        ),
        dict(out=shape((groups, rows_in, cols_in, cin), bf16)),
        dict(
            lines=pltpu.VMEM((cin // 128, rows_in * groups, cols_in, 128), f32),
            gf=pltpu.VMEM((MU + 16, width), f32),
            gu=pltpu.VMEM((MU, 2 * width), bf16),
        ),
        far_in=(N.act, N.normed, N.gpu, N.w1, N.wp),
        far_out=(N.out,),
        cost=10000000000,
    )[N.out]
    side = bit_of(*core).astype(jnp.int32)
    grad_inputs = lockstep(tree2, tree1, beside=grad_inputs)
    while tree2.next() != (N.plane_join, 0):
        lockstep(tree2, tree1)
    tree2.start()
    while tree1.next() != (N.plane_join, 0):
        tree1.start()
        if tree1.next() != (N.plane_join, 1):
            tree1.finish()
        else:
            tree1.got, tree2.got = lax.optimization_barrier((tree1.got, tree2.got))
            tree1.finish()
    tree2.finish()
    tree2.start()
    tree1.start()
    grad_second = widen(tree2.got[0], 1 - side, 9, per, True, widen(tree2.value, side, 9, per, True))
    tree1.got, grad_second = lax.optimization_barrier((tree1.got, grad_second))
    grad_w2, grad_wp = grad_second
    tree1.finish(1)
    tree1.start()
    (grad_w1,) = widen(tree1.got[0], 1 - side, 9, 1, False, widen(tree1.value, side, 9, 1, False))

    return (
        third[N.out],
        grad_inputs,
        grad_w1.reshape(w_first.shape),
        fifth[N.gain_first].reshape(width),
        fifth[N.shift_first].reshape(width),
        grad_w2.reshape(w_second.shape),
        hidden[N.gain_second].reshape(width),
        hidden[N.shift_second].reshape(width),
        grad_wp.reshape(w_proj.shape),
        hidden[N.gain_proj].reshape(width),
        hidden[N.shift_proj].reshape(width),
    )


def solution(mesh):
    spread = P("grp", "rows", "cols", None)
    return jax.shard_map(
        on_device,
        mesh=mesh,
        in_specs=(spread,) + (P(),) * 9 + (P("grp", "rows", "cols"), spread),
        out_specs=(spread, spread) + (P(),) * 9,
        check_vma=False,
    )
```

```python
import functools

import jax
import jax.numpy as jnp
from jax import lax
from jax.experimental import pallas as pl
from jax.experimental.pallas import tpu as pltpu
from jax.sharding import PartitionSpec as P

epsilon = 1e-05
axes = ("rows", "cols", "grp")
bf16 = jnp.bfloat16
f32 = jnp.float32
inner = 0.7978845608028654
cubic = 0.044715
over = 6
CHUNKS = "sent_a", "kept_a", "sent_b", "kept_b"
rim = 3


class Names:
    def __getattr__(self, name):
        return name


N = Names()


class Refs:
    def __init__(self, named):
        self.__dict__.update(named)


class Copies:
    def __init__(self, parts, pairs, sems):
        self.jobs = {}
        for k, (name, index) in enumerate(parts):
            source, target = pairs[name]
            if index:
                source, target = source.at[index[1]], target.at[index[1]]
            self.jobs.setdefault(name, []).append(pltpu.make_async_copy(source, target, sems.at[k]))

    def start(self, *names):
        for name, *which in map(named, names):
            for job in self.jobs[name][slice(*which) if which else slice(None)]:
                job.start()

    def start_all(self, names):
        for k in range(max((len(self.jobs[n]) for n in names), default=0)):
            for n in names:
                if k < len(self.jobs[n]):
                    self.jobs[n][k].start()

    def wait(self, *names):
        for name, *which in map(named, names):
            for job in self.jobs[name][slice(*which) if which else slice(None)]:
                job.wait()


def named(name):
    return (name,) if isinstance(name, str) else (name[0], name[1], name[1] + 1)


def row_parts(total, count):
    size = total // count
    return [(k, (pl.ds(k * size, size),)) for k in range(count)]


def middle_parts(total, count):
    size = total // count
    return [(k, (slice(None), pl.ds(k * size, size))) for k in range(count)]


def end_parts(total, size):
    return [(k, (slice(None), pl.ds(at, size))) for k, at in enumerate((0, total - size))]


def cuts(*at):
    return [(k, (pl.ds(a, b - a),)) for k, (a, b) in enumerate(zip(at, at[1:]))]


def lane_parts(total, count, rows=slice(None)):
    size = total // count
    return [(k, (rows, pl.ds(k * size, size))) for k in range(count)]


def call(body, ins, outs, scratch=None, far_in=(), far_out=(), smem=(), parts=None, limit=52, cost=0):
    scratch, parts = scratch or {}, parts or {}
    far = (*far_in, *far_out)
    jobs = [(name, index) for name in far for index in parts.get(name, [None])]

    def spec(name):
        if name in smem:
            return pl.BlockSpec(memory_space=pltpu.SMEM)
        return pl.BlockSpec(memory_space=pltpu.HBM if name in far else pltpu.VMEM)

    kinds = {**{n: shape(v.shape, v.dtype) for n, v in ins.items()}, **outs}

    def run(*refs):
        plain = dict(zip([*ins, *outs], refs))
        rest = refs[len(plain) :]
        buffers = dict(zip(far, rest))
        more = dict(zip(scratch, rest[len(far) :]))
        copies = None
        if far:
            pairs = {n: (plain[n], buffers[n]) if n in far_in else (buffers[n], plain[n]) for n in far}
            copies = Copies(jobs, pairs, rest[-1])
            copies.start_all(far_in)
        body(Refs({**plain, **buffers, **more}), copies)

    buffers = [pltpu.VMEM(kinds[n].shape, kinds[n].dtype) for n in far]
    sems = [pltpu.SemaphoreType.DMA((len(jobs),))] if far else []
    result = pl.pallas_call(
        run,
        out_shape=list(outs.values()),
        in_specs=[spec(n) for n in ins],
        out_specs=[spec(n) for n in outs],
        scratch_shapes=[*buffers, *scratch.values(), *sems],
        compiler_params=pltpu.CompilerParams(vmem_limit_bytes=limit * 1024 * 1024),
        cost_estimate=pl.CostEstimate(flops=cost, bytes_accessed=0, transcendentals=0),
    )(*ins.values())
    return dict(zip(outs, result))


def shape(dims, dtype=f32):
    return jax.ShapeDtypeStruct(dims, dtype)


def wide(mask, width):
    return jnp.concatenate([mask] * (width // mask.shape[1]), axis=1)


def matmul(a, b):
    return lax.dot_general(a, b, (((1,), (0,)), ((), ())), preferred_element_type=f32)


def matmul_nt(a, b):
    return lax.dot_general(a, b, (((1,), (1,)), ((), ())), preferred_element_type=f32)


def matmul_tn(a, b):
    return lax.dot_general(a, b, (((0,), (0,)), ((), ())), preferred_element_type=f32)


def gelu_parts(v):
    return jnp.tanh(inner * (v + cubic * v * v * v))


def gelu_slope(v, t):
    return 0.5 * (1.0 + t) + 0.5 * v * (1.0 - t * t) * (inner * (1.0 + 3.0 * cubic * v * v))


def column_sum(v):
    return jnp.sum(v, axis=0, keepdims=True)


def moments(total, squares, pixel_count):
    center = total / pixel_count
    spread = squares / pixel_count - center * center
    return center, lax.rsqrt(spread + epsilon)


def chunks(total, size):
    return [(at, min(size, total - at)) for at in range(0, total, size)]


def strided(ref, k, first, count, step):
    return ref[k, pl.ds(first, count, stride=step), :]


def vertical_kernel(r, copies):
    groups, width = r.x.shape[0], r.cot.shape[3]
    rows, cols = r.own.shape[1], r.own.shape[2]

    def pack(out, input_row, row, pick):
        at = 0
        for g in range(groups):
            for n in range(over):
                value = r.x[g, input_row(n)]
                out[at : at + 2 * cols, :] = pick(value, r.x[g, n])
                at += 2 * cols
        for k in range(0, width, 256):
            for g in range(groups):
                for n in range(rim):
                    lanes = slice(k, k + 256)
                    out[at : at + cols, :] = pick(r.cot[g, row(n), :, lanes], r.cot[g, n, :, lanes])
                    at += cols
        for g in range(groups):
            for n in range(rim):
                out[at : at + cols, :] = pick(wide(r.own[g, row(n)], 256), wide(r.own[g, n], 256))
                at += cols

    last = r.x.shape[1] - over
    copies.wait(N.x, N.cot)
    if hasattr(r, N.up):
        pack(r.down, lambda n: last + n, lambda n: rows - rim + n, lambda tail, head: tail)
        pack(r.up, lambda n: last + n, lambda n: rows - rim + n, lambda tail, head: head)
    else:
        bottom = r.flags[0] == 1
        pack(r.down, lambda n: last + n, lambda n: rows - rim + n, lambda tail, head: jnp.where(bottom, head, tail))


def rim_rows(r, own, n_own, n_rim, base, cols, split):
    groups = own.shape[0]
    size = groups * n_rim * cols

    def flat(ref, g, n):
        at = [base + k * size + (g * n_rim + n) * cols for k in range(split)]
        return jnp.concatenate([ref[p : p + cols, :] for p in at], axis=1).astype(f32)

    def read(g, n):
        if n < n_rim:
            return jnp.where(r.flags[0] == 1, flat(r.top, g, n), 0.0)
        if n < n_rim + n_own:
            return own[g, n - n_rim].astype(f32)
        return jnp.where(r.flags[1] == 1, flat(r.bot, g, n - n_rim - n_own), 0.0)

    return read


def fields(r):
    groups, width = r.x.shape[0], r.cot.shape[3]
    rows, cols = r.own.shape[1], r.own.shape[2]
    base = over * groups * 2 * cols
    piece = rim * groups * cols
    blocks = width // 256
    x = rim_rows(r, r.x, 2 * rows, over, 0, 2 * cols, 1)
    mask = rim_rows(r, r.own, rows, rim, base + blocks * piece, cols, 1)
    cot = rim_rows(r, r.cot, rows, rim, base, cols, blocks)
    return x, lambda g, n: mask(g, n)[:, :128], cot


def strips_kernel(r, copies):
    groups, width = r.x.shape[0], r.cot.shape[3]
    rows, cols = r.own.shape[1], r.own.shape[2]
    x, mask, cot = fields(r)
    lines = (2 * rows + 2 * over) * groups, (rows + 2 * rim) * groups, (rows + 3) * groups
    for raw, read, first, count, w in (
        (r.raw_x, x, 0, lines[0], 2 * cols),
        (r.raw_m, mask, 0, lines[1], cols),
        (r.raw_c, cot, 2, lines[2], cols),
    ):
        for at in range(count):
            value = read(at % groups, at // groups + first)
            for k in range(raw.shape[0]):
                raw[k, at * w : (at + 1) * w, :] = value[:, k * 128 : (k + 1) * 128]
    for out, x0, m0, c0 in ((r.right, 2 * cols - over, cols - rim, cols - 2), (r.left, 0, 0, 0)):
        pieces = []
        for c in range(over):
            pieces.append([strided(r.raw_x, k, x0 + c, lines[0], 2 * cols) for k in range(2)])
        for c in range(0, rim + 1, 2):
            pieces.append([strided(r.raw_m, 0, m0 + min(c + k, rim - 1), lines[1], cols) for k in range(2)])
        for c in range(2):
            for h in range(0, width // 128, 2):
                pieces.append([strided(r.raw_c, h + k, c0 + c, lines[2], cols) for k in range(2)])
        at = 0
        for low, high in pieces:
            r.flat[at : at + low.shape[0], :] = jnp.concatenate([low, high], axis=1)
            at += low.shape[0]
        if at < r.flat.shape[0]:
            r.flat[at:, :] = jnp.zeros((r.flat.shape[0] - at, 256), f32)
        out[...] = r.flat[...].astype(bf16)


def stats_kernel(r, copies):
    groups, cin = r.x.shape[0], r.x.shape[3]
    rows, S = r.own.shape[1], r.own.shape[2]
    L = groups * S
    width = r.w1.shape[2]
    raw = r.raw
    for n in range(2 * rows + 1):
        for g in range(groups):
            line = n * groups + g
            src = (r.top[g, 0] if n == 0 else r.x[g, n - 1]).astype(f32)
            side = r.lft[g, n].astype(f32)
            for k in range(raw.shape[0]):
                raw[k, line, 7:8, :] = side[:, k * 128 : (k + 1) * 128]
                raw[k, line, 8:, :] = src[:, k * 128 : (k + 1) * 128]
    for out, n_rows, start in ((r.xe, rows, 1), (r.xo, rows + 1, 0)):
        for n in range(n_rows):
            for b in range(3):
                for k in range(raw.shape[0]):
                    parts = [
                        raw[k, (2 * n + start) * groups + g, pl.ds(7 + b, S, stride=2), :]
                        for g in range(groups)
                    ]
                    at = b * cin + k * 128
                    out[n * L : (n + 1) * L, at : at + 128] = jnp.concatenate(
                        parts, axis=0
                    ).astype(bf16)
    mask = jnp.concatenate(
        [r.own[g, i].astype(f32) for i in range(rows) for g in range(groups)], axis=0
    )
    M = rows * L
    copies.wait(N.w1)
    z = matmul(r.xo[0:M, :], r.w1[0])
    z += matmul(r.xe[...], r.w1[1])
    z += matmul(r.xo[L : L + M, :], r.w1[2])
    zp = matmul(r.xe[:, cin : 2 * cin], r.wp[...])
    zm, zpm = z * wide(mask, width), zp * wide(mask, width)
    row = jnp.concatenate(
        [column_sum(zm), column_sum(zm * z), column_sum(zpm), column_sum(zpm * zp), column_sum(mask)], axis=1
    )
    r.spread[...] = jnp.broadcast_to(row[None], r.spread.shape)
    copies.start(N.spread)
    copies.wait(N.spread)


def first_kernel(r, copies):
    groups, cin, width = r.x.shape[0], r.x.shape[3], r.cot.shape[3]
    rows, cols = r.own.shape[1], r.own.shape[2]
    S = cols + 8
    L = groups * S
    W = 2 * cols + 24
    V = cols + 16
    x, mask, cot = fields(r)
    lines = (2 * rows + 2 * over) * groups, (rows + 2 * rim) * groups, (rows + 3) * groups
    tail = jnp.zeros((W - 8 - 2 * cols, 128), f32)
    r.raw_m[...] = jnp.zeros(r.raw_m.shape, f32)
    r.raw_c[...] = jnp.zeros(r.raw_c.shape, f32)
    for at in range(lines[0]):
        value = x(at % groups, at // groups)
        for k in range(r.raw_x.shape[0]):
            r.raw_x[k, at * W + 8 : at * W + 8 + 2 * cols, :] = value[:, k * 128 : (k + 1) * 128]
            r.raw_x[k, at * W + 8 + 2 * cols : (at + 1) * W, :] = tail
    for strip, x0, m0, c0 in ((r.lft, 8 - over, 8 - rim, 6), (r.rgt, 8 + 2 * cols, 8 + cols, 8 + cols)):
        r.flat[...] = strip[...].astype(f32)
        at = 0
        for c in range(over):
            for k in range(2):
                r.raw_x[k, pl.ds(x0 + c, lines[0], stride=W), :] = r.flat[at : at + lines[0], k * 128 : (k + 1) * 128]
            at += lines[0]
        for c in range(0, rim + 1, 2):
            for k in range(2):
                if c + k < rim:
                    r.raw_m[0, pl.ds(m0 + c + k, lines[1], stride=V), :] = r.flat[
                        at : at + lines[1], k * 128 : (k + 1) * 128
                    ]
            at += lines[1]
        for c in range(2):
            for h in range(0, width // 128, 2):
                for k in range(2):
                    r.raw_c[h + k, pl.ds(c0 + c, lines[2], stride=V), :] = r.flat[
                        at : at + lines[2], k * 128 : (k + 1) * 128
                    ]
                at += lines[2]
    for out, n_rows, start in ((r.xe, rows + 5, 2), (r.xo, rows + 6, 1)):
        for n in range(n_rows):
            for b in range(3):
                for k in range(r.raw_x.shape[0]):
                    parts = [
                        strided(r.raw_x, k, ((2 * n + start) * groups + g) * W + 3 + b, S, 2) for g in range(groups)
                    ]
                    at = b * cin + k * 128
                    out[n * L : (n + 1) * L, at : at + 128] = jnp.concatenate(parts, axis=0).astype(bf16)
    copies.start(N.xe, N.xo)
    for at in range(lines[1]):
        r.raw_m[0, at * V + 8 : at * V + 8 + cols, :] = mask(at % groups, at // groups)
    for n in range(1, rows + 6):
        for g in range(groups):
            to, at = (n - 1) * L + g * S, (n * groups + g) * V
            r.maskp[to : to + S, :] = r.raw_m[0, at + 6 : at + 6 + S, :]
    for at in range(lines[2]):
        value = cot(at % groups, at // groups + 2)
        for k in range(r.raw_c.shape[0]):
            lanes = slice(k * 128, (k + 1) * 128)
            r.raw_c[k, at * V + 8 : at * V + 8 + cols, :] = value[:, lanes]
            r.cotq[at * S : (at + 1) * S, lanes] = r.raw_c[k, at * V + 7 : at * V + 7 + S, :]
    copies.start(N.cotq)
    r.ownp[...] = jnp.zeros(r.ownp.shape, f32)
    for i in range(rows):
        for g in range(groups):
            at = (i + 2) * L + g * S + 2
            r.ownp[at : at + cols, :] = r.own[g, i].astype(f32)
    copies.wait(N.w1, N.wp)
    for k, (m0, m) in enumerate(chunks(r.pre1.shape[0], r.pre1.shape[0] // 3)):
        z = matmul(r.xo[m0 : m0 + m, :], r.w1[0])
        z += matmul(r.xe[m0 : m0 + m, :], r.w1[1])
        z += matmul(r.xo[L + m0 : L + m0 + m, :], r.w1[2])
        r.pre1[m0 : m0 + m, :] = z
        copies.start((N.pre1, k))
        r.prep[m0 : m0 + m, :] = matmul(r.xe[m0 : m0 + m, cin : 2 * cin], r.wp[...])
        copies.start((N.prep, k))
    copies.wait(N.xe, N.xo, N.pre1, N.prep, N.cotq)


def second_kernel(r, copies):
    width = r.gain.shape[1]
    t = jnp.sum(r.tot1[...], axis=0)
    n = wide(t[:, 4 * width :], width)
    center, inv = moments(t[:, :width], t[:, width : 2 * width], n)
    proj = moments(t[:, 2 * width : 3 * width], t[:, 3 * width : 4 * width], n)
    r.mom1[...] = jnp.concatenate([center, inv, n, *proj, jnp.zeros((3, width), f32)], axis=0)
    scale = inv * r.gain[...]
    M, Q = r.pre1.shape[0], r.pre2.shape[0]
    L = (M - Q) // 2
    copies.wait(N.pre1)
    for m0, m in chunks(M, 104):
        v = (r.pre1[m0 : m0 + m, :] - center) * scale + r.shift[...]
        mask = wide(r.maskp[m0 : m0 + m, :], width)
        r.hid[m0 : m0 + m, :] = 0.5 * v * (1.0 + gelu_parts(v)) * mask
    r.hid[M:, :] = jnp.zeros((r.hid.shape[0] - M, width), f32)
    for m0, m in chunks(M, 208):
        for b in range(3):
            r.h3[m0 : m0 + m, b * width : (b + 1) * width] = r.hid[m0 + b : m0 + b + m, :].astype(bf16)
    copies.start(N.h3)
    copies.wait(N.w2)
    sums = [jnp.zeros((1, width), f32)] * 2
    for k, (m0, m) in enumerate(chunks(Q, Q // 3)):
        z = matmul(r.h3[m0 : m0 + m, :], r.w2[0])
        z += matmul(r.h3[L + m0 : L + m0 + m, :], r.w2[1])
        z += matmul(r.h3[2 * L + m0 : 2 * L + m0 + m, :], r.w2[2])
        r.pre2[m0 : m0 + m, :] = z
        copies.start((N.pre2, k))
        zm = z * wide(r.ownp[L + 1 + m0 : L + 1 + m0 + m, :], width)
        sums = [sums[0] + column_sum(zm), sums[1] + column_sum(zm * z)]
    row = jnp.concatenate(sums, axis=1)
    r.spread[...] = jnp.broadcast_to(row[None], r.spread.shape)
    copies.start(N.spread)
    copies.wait(N.h3, N.pre2, N.spread)


def part(r, at, *fields, first=0):
    bit = r.bits[0] == 1
    for k, field in enumerate(fields, first):
        half = field.shape[1] // 2
        low, high = field[:, :half], field[:, half:]
        r.mine[k, at : at + field.shape[0], :] = jnp.where(bit, high, low)
        r.theirs[k, at : at + field.shape[0], :] = jnp.where(bit, low, high)


def mine_of(r, row):
    half = row.shape[1] // 2
    return jnp.where(r.bits[0] == 1, row[:, half:], row[:, :half])


def third_kernel(r, copies):
    groups, rows, cols, width = r.out.shape
    S = cols + 8
    L = groups * S
    n = r.mom1[2:3, :]
    t = jnp.sum(r.tot2[...], axis=0)
    c2, i2 = moments(t[:, :width], t[:, width:], n)
    cp, ip = r.mom1[3:4, :], r.mom1[4:5, :]
    r.mom2[...] = jnp.concatenate([c2, i2, cp, ip, jnp.zeros((4, width), f32)], axis=0)
    sums = [jnp.zeros((1, width), f32)] * 3
    both_shift = r.shift2[...] + r.shiftp[...]
    total = r.grad.shape[0] // S
    for line in range(total):
        if line % (total // 2) == 0:
            k = line // (total // 2)
            copies.wait((N.pre2, k), (N.prep, k), (N.cotq, k))
        at = line * S
        shifted = slice(L + 1 + at, L + 1 + at + S)
        n2 = (r.pre2[at : at + S, :] - c2) * i2
        np_ = (r.prep[shifted, :] - cp) * ip
        v = n2 * r.gain2[...] + np_ * r.gainp[...] + both_shift
        mask = wide(r.maskp[shifted, :], width)
        own = wide(r.ownp[shifted, :], width)
        t = gelu_parts(v)
        r.field[at : at + S, :] = 0.5 * v * (1.0 + t) * mask
        g = gelu_slope(v, t) * mask * r.cotq[at : at + S, :]
        r.grad[at : at + S, :] = g
        g = g * own
        if L <= at < L + r.mine.shape[1]:
            part(r, at - L, g, n2 * own, np_ * own)
            if at - L + S == r.mine.shape[1] // 2:
                copies.start((N.mine, 0), (N.theirs, 0))
        new = [column_sum(g * n2), column_sum(g), column_sum(g * np_)]
        sums = [a + b for a, b in zip(sums, new)]
        if (line + 1) % (total // 2) == 0:
            copies.start((N.grad, (line + 1) // (total // 2) - 1))
    row = jnp.concatenate(sums, axis=1)
    r.spread[...] = jnp.broadcast_to(row[None], r.spread.shape)
    copies.start(N.spread, (N.mine, 1), (N.theirs, 1))
    for i in range(rows):
        for g in range(groups):
            at = (i + 1) * L + g * S + 1
            r.out[g, i, :, :] = r.field[at : at + cols, :].astype(bf16)
    copies.start(N.out)
    copies.wait(N.grad, N.out, N.spread, N.mine, N.theirs)


def fourth_kernel(r, copies):
    width = r.gain.shape[1]
    Q, U, rows_w = r.pre2.shape[0], r.act.shape[0], r.gpu.shape[0]
    L = U - rows_w
    center, inv, n = (r.mom1[k : k + 1, :] for k in range(3))
    c2, i2, cp, ip = (r.mom2[k : k + 1, :] for k in range(4))
    t3 = jnp.sum(r.tot3[...], axis=0)
    gg2, gs, ggp = (t3[:, k * width : (k + 1) * width] for k in range(3))
    r.gain_second[...], r.shift_second[...], r.gain_proj[...], r.shift_proj[...] = gg2, gs, ggp, gs
    tiny = N.gain_second, N.shift_second, N.gain_proj, N.shift_proj
    copies.start(*tiny)
    for m0, m in chunks(Q, L):
        if m0 in (0, 6 * L):
            copies.wait((N.grad, m0 // (6 * L)), (N.pre2, m0 // (6 * L)))
        mask = wide(r.maskp[L + 1 + m0 : L + 1 + m0 + m, :], width) / n
        n2 = (r.pre2[m0 : m0 + m, :] - c2) * i2
        back = mask * (gs + n2 * gg2)
        r.gq[m0 : m0 + m, :] = (r.gain2[...] * i2) * (r.grad[m0 : m0 + m, :] - back)
    r.gq[Q:, :] = jnp.zeros((r.gq.shape[0] - Q, width), f32)
    for m0, m in chunks(Q, 176):
        for b in range(3):
            r.g3[m0 : m0 + m, b * width : (b + 1) * width] = r.gq[m0 + b : m0 + b + m, :].astype(bf16)
    copies.wait(N.keep)
    for m0, m in chunks(U, L):
        frame = slice(2 * L + 2 + m0, 2 * L + 2 + m0 + m)
        n1 = (r.keep[frame, :] - center) * inv
        v = n1 * r.gain[...] + r.shift[...]
        mask = wide(r.maskp[frame, :], width)
        r.act[m0 : m0 + m, :] = gelu_slope(v, gelu_parts(v)) * mask
        r.normed[m0 : m0 + m, :] = n1 * mask
        if m0 < rows_w:
            part(r, m0, n1 * wide(r.ownp[frame, :], width), first=1)
    copies.start(N.normed, (N.mine, 1), (N.theirs, 1))
    for a in range(3):
        copies.wait((N.w2, a))
        gh = jnp.zeros((U, width), f32)
        for b in range(3):
            gh += matmul_nt(
                r.g3[L * a : L * a + U, b * width : (b + 1) * width],
                r.w2[2 - a, (2 - b) * width : (3 - b) * width, :],
            )
        r.gh[...] = gh if a == 0 else r.gh[...] + gh
    sums = [jnp.zeros((1, width), f32)] * 2
    for m0, m in chunks(U, L):
        g = r.act[m0 : m0 + m, :] * r.gh[m0 : m0 + m, :]
        r.act[m0 : m0 + m, :] = g
        g = g * wide(r.ownp[2 * L + 2 + m0 : 2 * L + 2 + m0 + m, :], width)
        if m0 < rows_w:
            part(r, m0, g)
        sums = [sums[0] + column_sum(g * r.normed[m0 : m0 + m, :]), sums[1] + column_sum(g)]
    row = jnp.concatenate(sums, axis=1)
    r.spread[...] = jnp.broadcast_to(row[None], r.spread.shape)
    copies.start(N.spread, (N.mine, 0), (N.theirs, 0), N.act)
    copies.wait(N.prep)
    for m0, m in chunks(rows_w, L):
        frame = slice(2 * L + 2 + m0, 2 * L + 2 + m0 + m)
        mask = wide(r.maskp[frame, :], width) / n
        back = mask * (gs + (r.prep[frame, :] - cp) * ip * ggp)
        r.gpu[m0 : m0 + m, :] = ((r.gainp[...] * ip) * (r.grad[L + 1 + m0 : L + 1 + m0 + m, :] - back)).astype(bf16)
    copies.start(N.gpu)
    copies.wait(N.normed, N.mine, N.theirs, N.spread, N.act, N.gpu, *tiny)


def split_store(r, rows, unit, first):
    quarter = unit // 4
    for k in range(rows // unit):
        for bit, base, sent, kept in ((1, 0, r.sent_a, r.kept_a), (2, 2 * quarter, r.sent_b, r.kept_b)):
            keep = pl.multiple_of(k * unit + base + r.bits[bit] * quarter, quarter)
            send = pl.multiple_of(k * unit + base + (1 - r.bits[bit]) * quarter, quarter)
            sent[first + k] = r.acc[pl.ds(send, quarter), :].astype(bf16)
            kept[first + k] = r.acc[pl.ds(keep, quarter), :]


def weights_second_kernel(r, copies):
    width = r.h3.shape[1] // 3
    cin = r.xe.shape[1] // 3
    rows_w = r.mine.shape[1]
    L = (r.h3.shape[0] - rows_w) // 5
    per = width // cin
    t3 = jnp.sum(r.tot3[...], axis=0)
    n = mine_of(r, r.mom1[2:3, :])
    gg2, gs, ggp = (mine_of(r, t3[:, k * width : (k + 1) * width]) / n for k in range(3))
    scale2, scalep = mine_of(r, r.gain2[...] * r.mom2[1:2, :]), mine_of(r, r.gainp[...] * r.mom2[3:4, :])
    half = scale2.shape[1]
    for source, name, own, out in ((r.mine, N.mine, r.ownp, r.near), (r.far3, N.far3, r.ownp_far, r.far)):
        copies.wait(name)
        r.pad[:, 0:8, :] = jnp.zeros((3, 8, half), f32)
        r.pad[:, 8:, :] = source[...]
        for m0, m in chunks(rows_w, 96):
            mask = wide(own[2 * L + 1 + m0 : 2 * L + 1 + m0 + m, :], half)
            rows = slice(8 + m0, 8 + m0 + m)
            back = mask * gs + r.pad[1, rows, :] * gg2
            out[m0 : m0 + m, :] = (scale2 * (r.pad[0, rows, :] - back)).astype(bf16)
            mask = wide(own[2 * L + m0 : 2 * L + m0 + m, :], half)
            rows = slice(7 + m0, 7 + m0 + m)
            back = mask * gs + r.pad[2, rows, :] * ggp
            out[rows_w + m0 : rows_w + m0 + m, :] = (scalep * (r.pad[0, rows, :] - back)).astype(bf16)
    for b in range(3):
        lanes = slice(b * width, (b + 1) * width)
        copies.wait((N.h3, b), (N.h3_far, b))
        for a in range(3):
            at = L * a + L
            r.acc[...] = matmul_tn(r.h3[at : at + rows_w, lanes], r.near[:rows_w, :]) + matmul_tn(
                r.h3_far[at : at + rows_w, lanes], r.far[:rows_w, :]
            )
            split_store(r, width, cin, (3 * b + a) * per)
        copies.start(*((name, b) for name in CHUNKS))
    at = 2 * L
    copies.wait(N.xe, N.xe_far)
    middle = slice(cin, 2 * cin)
    r.acc[0:cin, :] = matmul_tn(r.xe[at : at + rows_w, middle], r.near[rows_w:, :]) + matmul_tn(
        r.xe_far[at : at + rows_w, middle], r.far[rows_w:, :]
    )
    split_store(r, cin, cin, 9 * per)
    copies.start(*((name, 3) for name in CHUNKS))
    copies.wait(*CHUNKS)


def first_back(r, gg, gs, count):
    width = r.gain.shape[1]
    U = r.act.shape[0]
    L = U - r.rows_w
    inv, n = r.mom1[1:2, :], r.mom1[2:3, :]
    gg, gs = gg / n, gs / n
    scale = r.gain[...] * inv
    r.gf[0:8, :] = jnp.zeros((8, width), f32)
    r.gf[8 + count :, :] = jnp.zeros((r.gf.shape[0] - 8 - count, width), f32)
    for m0, m in chunks(count, L):
        mask = wide(r.maskp[2 * L + 2 + m0 : 2 * L + 2 + m0 + m, :], width)
        back = mask * gs + r.normed[m0 : m0 + m, :] * gg
        r.gf[8 + m0 : 8 + m0 + m, :] = scale * (r.act[m0 : m0 + m, :] - back)


def weights_first_kernel(r, copies):
    rows_w = r.mine.shape[1]
    cin = r.xe.shape[1] // 3
    L = (r.xe.shape[0] - rows_w) // 5
    width = r.gain.shape[1]
    t4 = jnp.sum(r.tot4[...], axis=0)
    r.gain_first[...], r.shift_first[...] = t4[:, :width], t4[:, width:]
    copies.start(N.gain_first, N.shift_first)
    n = mine_of(r, r.mom1[2:3, :])
    gg, gs = mine_of(r, t4[:, :width]) / n, mine_of(r, t4[:, width:]) / n
    scale = mine_of(r, r.gain[...] * r.mom1[1:2, :])
    half = scale.shape[1]
    for source, name, own, out in ((r.mine, N.mine, r.ownp, r.near), (r.far4, N.far4, r.ownp_far, r.far)):
        copies.wait(name)
        r.pad[:, 0:8, :] = jnp.zeros((2, 8, half), f32)
        r.pad[:, 8:, :] = source[...]
        for m0, m in chunks(rows_w, 96):
            mask = wide(own[2 * L + m0 : 2 * L + m0 + m, :], half)
            rows = slice(6 + m0, 6 + m0 + m)
            back = mask * gs + r.pad[1, rows, :] * gg
            out[m0 : m0 + m, :] = (scale * (r.pad[0, rows, :] - back)).astype(bf16)
    copies.wait(N.xe, N.xe_far)
    for k, a in enumerate((1, 0, 2)):
        if k == 1:
            copies.wait(N.xo, N.xo_far)
        source, source_far = (r.xe, r.xe_far) if a == 1 else (r.xo, r.xo_far)
        at = (3 if a == 2 else 2) * L
        for b in range(3):
            lanes = slice(b * cin, (b + 1) * cin)
            r.acc[lanes, :] = matmul_tn(source[at : at + rows_w, lanes], r.near[...]) + matmul_tn(
                source_far[at : at + rows_w, lanes], r.far[...]
            )
        split_store(r, 3 * cin, cin, a * 3)
        copies.start(*((name, a) for name in CHUNKS))
    copies.wait(N.gain_first, N.shift_first, *CHUNKS)


def inputs_kernel(r, copies):
    width = r.gpu.shape[1]
    groups, rows, cols = r.out.shape[0], r.out.shape[1] // 2, r.out.shape[2] // 2
    cin = r.out.shape[3]
    M = r.gpu.shape[0]
    S = cols + 8
    L = groups * S
    lines = r.lines
    U = r.act.shape[0]
    r.rows_w = M
    copies.wait(N.act, N.normed)
    first_back(r, r.gg[...], r.gs[...], U)
    for m0, m in chunks(U, 144):
        r.gu[m0 : m0 + m, :width] = r.gf[8 + m0 : 8 + m0 + m, :].astype(bf16)
        r.gu[m0 : m0 + m, width:] = r.gf[9 + m0 : 9 + m0 + m, :].astype(bf16)
    copies.wait(N.gpu, N.w1, N.wp)

    def tap(m0, m, a, b):
        di, dj = (1 if a == 0 else 0), (1 if b == 0 else 0)
        return matmul_nt(
            r.gu[di * L + m0 : di * L + m0 + m, dj * width : (dj + 1) * width],
            r.w1[a, b * cin : (b + 1) * cin, :],
        )

    for m0, m in chunks(M, 2 * L):
        pieces = {
            (0, 0): tap(m0, m, 1, 1) + matmul_nt(r.gpu[m0 : m0 + m, :], r.wp[...]),
            (0, 1): tap(m0, m, 1, 2) + tap(m0, m, 1, 0),
            (1, 0): tap(m0, m, 2, 1) + tap(m0, m, 0, 1),
            (1, 1): tap(m0, m, 2, 2) + tap(m0, m, 2, 0) + tap(m0, m, 0, 2) + tap(m0, m, 0, 0),
        }
        for (ro, co), v in pieces.items():
            for k in range(m // S):
                line = m0 // S + k
                i, g = line // groups, line % groups
                for h in range(lines.shape[0]):
                    lines[h, (2 * i + ro) * groups + g, pl.ds(co, cols, stride=2), :] = v[
                        k * S : k * S + cols, h * 128 : (h + 1) * 128
                    ]
    for n in range(2 * rows):
        for g in range(groups):
            for h in range(lines.shape[0]):
                r.out[g, n, :, h * 128 : (h + 1) * 128] = lines[h, n * groups + g].astype(bf16)
    copies.start(N.out)
    copies.wait(N.out)


def widen(half, side, taps, per, swapped, into=None):
    total, n, m = half.shape
    extra = total - taps * per
    order = [(t % 3 * 3 + t // 3) if swapped else t for t in range(taps)]
    jobs = [(t * per, per, 0, order[t] * per) for t in range(taps)] + [(taps * per, 1, 1, 0)] * extra
    more = list(into or [])

    def body(side_ref, half_ref, *refs):
        outs = refs[len(more) : len(more) + 1 + extra]
        narrow, full, sems = refs[len(more) + 1 + extra :]
        lanes = pl.ds(pl.multiple_of(side_ref[0] * m, m), m)
        reads = [
            pltpu.make_async_copy(half_ref.at[pl.ds(at, size)], narrow.at[pl.ds(at, size)], sems.at[0, k])
            for k, (at, size, _, _) in enumerate(jobs)
        ]
        writes = [
            pltpu.make_async_copy(full.at[pl.ds(at, size)], outs[which].at[pl.ds(to, size), :, lanes], sems.at[1, k])
            for k, (at, size, which, to) in enumerate(jobs)
        ]
        for read in reads:
            read.start()
        for k, (at, size, _, _) in enumerate(jobs):
            reads[k].wait()
            full[at : at + size] = narrow[at : at + size].astype(f32)
            writes[k].start()
        for write in writes:
            write.wait()

    hbm = pl.BlockSpec(memory_space=pltpu.HBM)
    return pl.pallas_call(
        body,
        out_shape=[shape((taps * per, n, 2 * m))] + [shape((1, n, 2 * m))] * extra,
        in_specs=[pl.BlockSpec(memory_space=pltpu.SMEM)] + [hbm] * (1 + len(more)),
        out_specs=[hbm] * (1 + extra),
        scratch_shapes=[
            pltpu.VMEM((total, n, m), bf16),
            pltpu.VMEM((total, n, m), f32),
            pltpu.SemaphoreType.DMA((2, len(jobs))),
        ],
        input_output_aliases={2 + k: k for k in range(len(more))},
        compiler_params=pltpu.CompilerParams(vmem_limit_bytes=20 * 1024 * 1024),
        cost_estimate=pl.CostEstimate(flops=0, bytes_accessed=0, transcendentals=0),
    )(side.reshape(1), half, *more)


def halve_kernel(r, copies):
    for p in range(r.count):
        kept, got = getattr(r, f"kept{p}"), getattr(r, f"got{p}")
        copies.wait(f"kept{p}", f"got{p}")
        to_send, to_keep = getattr(r, f"sent{p}"), getattr(r, f"left{p}")
        bit = r.bits[r.steps[p]] == 1
        h = kept.shape[1] // 2
        for t in range(kept.shape[0]):
            total = kept[t] + got[t].astype(f32)
            low, high = total[:h], total[h:]
            to_send[t] = jnp.where(bit, low, high).astype(bf16)
            to_keep[t] = jnp.where(bit, high, low)
        copies.start(f"sent{p}", f"left{p}")
    copies.wait(*(name for name in copies.jobs if name[:4] in (N.sent, N.left)))


def halve(bits, pairs, steps, cost):
    ins = dict(bits=bits)
    for p, (kept, got) in enumerate(pairs):
        ins[f"kept{p}"], ins[f"got{p}"] = kept, got
    taps, n, m = pairs[0][0].shape
    dims = (taps, n // 2, m)
    names = [str(p) for p in range(len(pairs))]
    outs = {}
    for name in names:
        outs[N.sent + name], outs[N.left + name] = shape(dims, bf16), shape(dims)

    def body(r, copies):
        r.count, r.steps = len(pairs), steps
        halve_kernel(r, copies)

    far_in = tuple(n for n in ins if n != N.bits)
    out = call(body, ins, outs, far_in=far_in, far_out=tuple(outs), smem=(N.bits,), cost=cost, limit=60)
    return [(out[N.sent + name], out[N.left + name]) for name in names]


def shifted(value, axis, steps):
    count = lax.axis_size(axis)
    first, last = (max(0, -steps), min(count, count - steps))
    return lax.ppermute(value, axis, [(source, source + steps) for source in range(first, last)])


def gather_sum(spread):
    return lax.all_to_all(spread, axes, 0, 0)


def bit_of(axis, step):
    return (lax.axis_index(axis) // step) % 2


def partner(value, axis, step):
    count = lax.axis_size(axis)
    return lax.ppermute(value, axis, [(i, i ^ step) for i in range(count)])


def steps_of(axis):
    count, step, out = lax.axis_size(axis), 1, []
    while step < count:
        out.append((axis, step))
        step *= 2
    return out


def split(total, axis, step):
    n = total.shape[1] // 2
    bit = bit_of(axis, step) == 1
    low, high = total[:, :n], total[:, n:]
    return jnp.where(bit, low, high).astype(bf16), jnp.where(bit, high, low)


def joined(value, other, axis, step, dim=1):
    bit = bit_of(axis, step) == 1
    return jnp.concatenate([jnp.where(bit, other, value), jnp.where(bit, value, other)], axis=dim)


def gathered(pieces, spots, cost=0):
    taps, h, m = pieces[0].shape
    count = len(pieces)

    def body(spots_ref, *refs):
        out, sems = refs[count:]
        copies = []
        for q in range(count):
            rows = pl.ds(pl.multiple_of(spots_ref[q] * h, h), h)
            copies.append(pltpu.make_async_copy(refs[q], out.at[:, rows], sems.at[q]))
        for copy in copies:
            copy.start()
        for copy in copies:
            copy.wait()

    anywhere = pl.BlockSpec(memory_space=pl.ANY)
    return pl.pallas_call(
        body,
        out_shape=shape((taps, count * h, m), pieces[0].dtype),
        in_specs=[pl.BlockSpec(memory_space=pltpu.SMEM)] + [anywhere] * count,
        out_specs=anywhere,
        scratch_shapes=[pltpu.SemaphoreType.DMA((count,))],
        compiler_params=pltpu.CompilerParams(vmem_limit_bytes=16 * 1024 * 1024),
        cost_estimate=pl.CostEstimate(flops=cost, bytes_accessed=0, transcendentals=0),
    )(spots, *pieces)


class Tree:
    def __init__(self, parts, bits, plane, rest, core):
        self.bits, self.place = bits, {step: k for k, step in enumerate([core, *plane, *rest])}
        self.sent_a, self.kept_a, self.sent_b, self.kept_b = parts
        self.a, self.b, self.rest, self.core = plane, plane[::-1], rest, core
        p, n = len(plane), len(rest)
        self.stages = [(N.plane, k) for k in range(p)] + [(N.rest, k) for k in range(n)]
        self.stages += [(N.rest_join, k) for k in reversed(range(n))] + [(N.plane_join, k) for k in reversed(range(p))]
        self.stages += [(N.core, 0)]

    def next(self):
        return self.stages[0] if self.stages else None

    def start(self):
        kind, k = self.stages[0]
        if kind == N.plane:
            self.got = partner(self.sent_a, *self.a[k]), partner(self.sent_b, *self.b[k])
        elif kind == N.rest:
            self.got = (partner(self.sent, *self.rest[k]),)
        elif kind == N.rest_join:
            self.got = (partner(self.value, *self.rest[k]),)
        elif kind == N.plane_join:
            self.got = partner(self.value_a, *self.a[k]), partner(self.value_b, *self.b[k])
        else:
            self.got = (partner(self.value, *self.core),)

    def finish(self, cost=0):
        kind, k = self.stages.pop(0)
        if kind == N.plane:
            pairs = [(self.kept_a, self.got[0]), (self.kept_b, self.got[1])]
            nexts = [order[k + 1] for order in (self.a, self.b) if k + 1 < len(order)]
            if nexts and cost:
                pairs = halve(self.bits, pairs, [self.place[step] for step in nexts], cost)
                (self.sent_a, self.kept_a), (self.sent_b, self.kept_b) = pairs
                return
            total_a, total_b = (kept + got.astype(f32) for kept, got in pairs)
            if nexts:
                self.sent_a, self.kept_a = split(total_a, *nexts[0])
                self.sent_b, self.kept_b = split(total_b, *nexts[1])
            else:
                self.taps = total_a.shape[0]
                self.split_rest(jnp.concatenate([total_a, total_b], axis=0), 0)
        elif kind == N.rest:
            self.split_rest(self.kept + self.got[0].astype(f32), k + 1)
        elif kind == N.rest_join:
            self.value = joined(self.value, self.got[0], *self.rest[k])
            self.value_a, self.value_b = self.value[: self.taps], self.value[self.taps :]
        elif kind == N.plane_join:
            if k == 0 and cost:
                low, high = (self.bits[self.place[step]] for step in (self.a[0], self.b[0]))
                spots = jnp.stack([low, 1 - low, 2 + high, 3 - high])
                self.value = gathered([self.value_a, self.got[0], self.value_b, self.got[1]], spots, cost)
            else:
                self.value_a = joined(self.value_a, self.got[0], *self.a[k])
                self.value_b = joined(self.value_b, self.got[1], *self.b[k])
                self.value = jnp.concatenate([self.value_a, self.value_b], axis=1)

    def split_rest(self, total, k):
        if k < len(self.rest):
            self.sent, self.kept = split(total, *self.rest[k])
        else:
            self.value = total.astype(bf16)


def lockstep(*trees, beside=()):
    for t in trees:
        t.start()
    got, beside = lax.optimization_barrier(([t.got for t in trees], beside))
    for t, g in zip(trees, got):
        t.got = g
        t.finish()
    return beside


def on_device(inputs, w_first, gain_first, shift_first, w_second, gain_second, shift_second, w_proj, gain_proj, shift_proj, valid_mask, cotangent):
    groups, rows_in, cols_in, cin = inputs.shape
    rows, cols = rows_in // 2, cols_in // 2
    width = w_first.shape[3]
    half = width // 2
    S = cols + 8
    L = groups * S
    devices = lax.axis_size(N.rows) * lax.axis_size(N.cols) * lax.axis_size(N.grp)
    plane = steps_of(N.cols)
    core = steps_of(N.rows)[0]
    rest = steps_of(N.rows)[1:] + steps_of(N.grp)
    bits = jnp.stack([bit_of(*step) for step in (core, *plane, *rest)]).astype(jnp.int32)
    w1 = w_first.reshape(3, 3 * cin, width)
    w2 = w_second.reshape(3, 3 * width, width)
    as_row = lambda v: v.reshape(1, -1)
    own = jnp.broadcast_to(valid_mask.astype(bf16)[..., None], valid_mask.shape + (128,))
    MP, MQ, MU, MW = (rows + 5) * L, (rows + 3) * L, (rows + 1) * L, rows * L
    px = lambda m, k: 2 * m * k * width
    vec = lambda k: shape((1, k * width))
    all_devices = lambda k: shape((devices, 1, k))
    g1, b1, g2, b2, gp, bp = map(
        as_row, (gain_first, shift_first, gain_second, shift_second, gain_proj, shift_proj)
    )

    top1 = shifted(inputs[:, -1:], N.rows, 1)
    me, count = lax.axis_index(N.rows), lax.axis_size(N.rows)
    flags = jnp.stack([me > 0, me < count - 1]).astype(jnp.int32)
    flat_rows = shape((over * groups * cols_in + (width // 256 + 1) * rim * groups * cols, 256), bf16)
    packed = call(
        vertical_kernel,
        dict(flags=flags, x=inputs, cot=cotangent, own=own),
        dict(down=flat_rows) if count == 2 else dict(down=flat_rows, up=flat_rows),
        far_in=(N.x, N.cot),
        smem=(N.flags,),
        parts=dict(x=end_parts(rows_in, over), cot=end_parts(rows, rim)),
    )
    if count == 2:
        top = bot = lax.ppermute(packed["down"], "rows", [(0, 1), (1, 0)])
    else:
        top, bot = shifted(packed[N.down], N.rows, 1), shifted(packed[N.up], N.rows, -1)
    (top, bot), top1 = lax.optimization_barrier(((top, bot), top1))
    lines = (rows_in + 2 * over) * groups, (rows + 2 * rim) * groups, (rows + 3) * groups
    n_strip = over * lines[0] + (rim + 1) // 2 * lines[1] + width // 128 * lines[2]
    n_strip = -(-n_strip // 16) * 16
    near = dict(flags=flags, x=inputs, cot=cotangent, own=own, top=top, bot=bot)
    strips = call(
        strips_kernel,
        near,
        dict(right=shape((n_strip, 256), bf16), left=shape((n_strip, 256), bf16)),
        dict(
            raw_x=pltpu.VMEM((cin // 128, lines[0] * cols_in, 128), f32),
            raw_m=pltpu.VMEM((1, lines[1] * cols, 128), f32),
            raw_c=pltpu.VMEM((width // 128, lines[2] * cols, 128), f32),
            flat=pltpu.VMEM((n_strip, 256), f32),
        ),
        smem=(N.flags,),
    )
    edge = jnp.concatenate([top1[:, :, -1:], inputs[:, :, -1:]], axis=1)
    edge, right, left = lax.optimization_barrier((edge, strips[N.right], strips[N.left]))
    lft1, right, left = lax.optimization_barrier((shifted(edge, N.cols, 1), right, left))
    lft, rgt = shifted(right, N.cols, 1), shifted(left, N.cols, -1)
    stats = call(
        stats_kernel,
        dict(x=inputs, top=top1, lft=lft1, own=own, w1=w1, wp=w_proj),
        dict(spread=all_devices(4 * width + 128)),
        dict(
            raw=pltpu.VMEM((cin // 128, (rows_in + 1) * groups, cols_in + 8, 128), f32),
            xe=pltpu.VMEM((rows * groups * cols, 3 * cin), bf16),
            xo=pltpu.VMEM(((rows + 1) * groups * cols, 3 * cin), bf16),
        ),
        far_in=(N.w1,),
        far_out=(N.spread,),
    )
    tot1 = gather_sum(stats[N.spread])

    first = call(
        first_kernel,
        dict(**near, lft=lft, rgt=rgt, w1=w1, wp=w_proj),
        dict(
            pre1=shape((MP, width)),
            prep=shape((MP, width)),
            xe=shape((MP, 3 * cin), bf16),
            xo=shape((MP + L, 3 * cin), bf16),
            ownp=shape((MP, 128)),
            maskp=shape((MP, 128)),
            cotq=shape((MQ, width)),
        ),
        dict(
            raw_x=pltpu.VMEM((cin // 128, lines[0] * (cols_in + 24), 128), f32),
            raw_m=pltpu.VMEM((1, lines[1] * (cols + 16), 128), f32),
            raw_c=pltpu.VMEM((width // 128, lines[2] * (cols + 16), 128), f32),
            flat=pltpu.VMEM((n_strip, 256), f32),
        ),
        far_in=(N.w1, N.wp),
        far_out=(N.xe, N.xo, N.pre1, N.prep, N.cotq),
        smem=(N.flags,),
        cost=20000000000,
        parts=dict(pre1=row_parts(MP, 3), prep=row_parts(MP, 3)),
    )
    xe, xo, ownp, maskp = first[N.xe], first[N.xo], first[N.ownp], first[N.maskp]
    far_xe, far_xo = partner(xe, *core), partner(xo, *core)

    second = call(
        second_kernel,
        dict(pre1=first[N.pre1], tot1=tot1, gain=g1, shift=b1, maskp=maskp, ownp=ownp, w2=w2),
        dict(h3=shape((MP, 3 * width), bf16), pre2=shape((MQ, width)), spread=all_devices(2 * width), mom1=shape((8, width))),
        dict(hid=pltpu.VMEM((MP + 8, width), f32)),
        far_in=(N.pre1, N.w2),
        far_out=(N.h3, N.pre2, N.spread),
        parts=dict(pre2=row_parts(MQ, 3)),
    )
    h3, pre2, mom1 = second[N.h3], second[N.pre2], second[N.mom1]
    tot2 = gather_sum(second[N.spread])
    tot2, far_h3 = lax.optimization_barrier((tot2, partner(h3, *core)))

    third = call(
        third_kernel,
        dict(
            bits=bits, pre2=pre2, prep=first[N.prep], mom1=mom1, tot2=tot2, gain2=g2, shift2=b2, gainp=gp, shiftp=bp,
            maskp=maskp, ownp=ownp, cotq=first[N.cotq],
        ),
        dict(
            out=shape((groups, rows, cols, width), bf16),
            grad=shape((MQ, width)),
            spread=all_devices(3 * width),
            mom2=shape((8, width)),
            mine=shape((3, MW, half)),
            theirs=shape((3, MW, half)),
        ),
        dict(field=pltpu.VMEM((MQ, width), f32)),
        far_in=(N.pre2, N.prep, N.cotq),
        far_out=(N.grad, N.spread, N.mine, N.theirs, N.out),
        smem=(N.bits,),
        parts=dict(
            mine=middle_parts(MW, 2), theirs=middle_parts(MW, 2),
            grad=row_parts(MQ, 2), pre2=row_parts(MQ, 2), cotq=row_parts(MQ, 2), prep=cuts(L, L + MQ // 2 + 8, L + MQ + 8)
        ),
    )
    mom2 = third[N.mom2]
    tot3 = gather_sum(third[N.spread])
    ownp_here, far3 = lax.optimization_barrier((ownp, partner(third[N.theirs], *core)))
    ownp_far = partner(ownp_here, *core)

    def chunk_shapes(taps):
        dims = (taps, cin // 4, half)
        return dict(sent_a=shape(dims, bf16), kept_a=shape(dims), sent_b=shape(dims, bf16), kept_b=shape(dims))

    per = width // cin
    taps2 = 9 * per + 1
    second_parts = call(
        weights_second_kernel,
        dict(
            bits=bits, mine=third[N.mine], far3=far3, h3=h3, h3_far=far_h3, xe=xe, xe_far=far_xe,
            tot3=tot3, mom1=mom1, mom2=mom2, gain2=g2, gainp=gp, ownp=ownp, ownp_far=ownp_far,
        ),
        chunk_shapes(taps2),
        dict(
            acc=pltpu.VMEM((width, half), f32),
            pad=pltpu.VMEM((3, MW + 8, half), f32),
            near=pltpu.VMEM((2 * MW, half), bf16),
            far=pltpu.VMEM((2 * MW, half), bf16),
        ),
        far_in=(N.mine, N.far3, N.h3, N.h3_far, N.xe, N.xe_far),
        far_out=CHUNKS,
        smem=(N.bits,),
        parts=dict(
            h3=lane_parts(3 * width, 3, pl.ds(L, MW + 2 * L)),
            h3_far=lane_parts(3 * width, 3, pl.ds(L, MW + 2 * L)),
            xe=[(0, (pl.ds(2 * L, MW), pl.ds(cin, cin)))],
            xe_far=[(0, (pl.ds(2 * L, MW), pl.ds(cin, cin)))],
            **{name: row_parts(taps2 - 1, 3) + [(3, (pl.ds(taps2 - 1, 1),))] for name in CHUNKS},
        ),
    ).values()
    grad, *second_parts = lax.optimization_barrier((third[N.grad], *second_parts))
    tree2 = Tree(second_parts, bits, plane, rest, core)
    tree2.start()
    hidden = call(
        fourth_kernel,
        dict(
            bits=bits, grad=grad, pre2=pre2, keep=first[N.pre1], w2=w2, prep=first[N.prep], mom1=mom1, mom2=mom2, tot3=tot3,
            gain=g1, shift=b1, gain2=g2, gainp=gp, maskp=maskp, ownp=ownp,
        ),
        dict(
            act=shape((MU, width)), normed=shape((MU, width)), spread=all_devices(2 * width),
            mine=shape((2, MW, half)), theirs=shape((2, MW, half)), gpu=shape((MW, width), bf16),
            gain_second=vec(1), shift_second=vec(1), gain_proj=vec(1), shift_proj=vec(1),
        ),
        dict(
            gq=pltpu.VMEM((MQ + 8, width), f32),
            g3=pltpu.VMEM((MQ, 3 * width), bf16),
            gh=pltpu.VMEM((MU, width), f32),
        ),
        far_in=(N.grad, N.pre2, N.keep, N.w2, N.prep),
        far_out=(
            N.act, N.normed, N.spread, N.mine, N.theirs, N.gpu, N.gain_second, N.shift_second, N.gain_proj, N.shift_proj
        ),
        smem=(N.bits,),
        limit=52,
        parts=dict(
            grad=cuts(0, 6 * L, MQ),
            pre2=cuts(0, 6 * L, MQ),
            keep=cuts(2 * L, 2 * L + MU + 8),
            w2=[(k, (pl.ds(2 - k, 1),)) for k in range(3)],
            prep=cuts(2 * L, 2 * L + MW + 8),
            mine=row_parts(2, 2),
            theirs=row_parts(2, 2),
        ),
    )
    tot4 = gather_sum(hidden[N.spread])
    tree2.finish(20000000000)
    near1, tree2.sent_a, tree2.sent_b = lax.optimization_barrier((hidden[N.mine], tree2.sent_a, tree2.sent_b))
    tree2.start()
    fifth = call(
        weights_first_kernel,
        dict(
            bits=bits, mine=near1, far4=partner(hidden[N.theirs], *core), xe=xe, xe_far=far_xe, xo=xo, xo_far=far_xo,
            tot4=tot4, mom1=mom1, gain=g1, ownp=ownp, ownp_far=ownp_far,
        ),
        dict(**chunk_shapes(9), gain_first=vec(1), shift_first=vec(1)),
        dict(
            acc=pltpu.VMEM((3 * cin, half), f32),
            pad=pltpu.VMEM((2, MW + 8, half), f32),
            near=pltpu.VMEM((MW, half), bf16),
            far=pltpu.VMEM((MW, half), bf16),
        ),
        far_in=(N.mine, N.far4, N.xe, N.xe_far, N.xo, N.xo_far),
        cost=20000000000,
        far_out=(*CHUNKS, N.gain_first, N.shift_first),
        smem=(N.bits,),
        parts=dict(
            xe=cuts(2 * L, 2 * L + MW),
            xe_far=cuts(2 * L, 2 * L + MW),
            xo=cuts(2 * L, 3 * L + MW),
            xo_far=cuts(2 * L, 3 * L + MW),
            **{name: row_parts(9, 3) for name in CHUNKS},
        ),
    )
    first_parts = [fifth[name] for name in CHUNKS]
    tree2.got, *first_parts = lax.optimization_barrier((tree2.got, *first_parts))
    tree2.finish()
    tree1 = Tree(first_parts, bits, plane, rest, core)

    grad_inputs = call(
        inputs_kernel,
        dict(
            act=hidden[N.act], normed=hidden[N.normed], gpu=hidden[N.gpu], w1=w1, wp=w_proj, mom1=mom1, gain=g1, maskp=maskp,
            gg=fifth[N.gain_first], gs=fifth[N.shift_first],
        ),
        dict(out=shape((groups, rows_in, cols_in, cin), bf16)),
        dict(
            lines=pltpu.VMEM((cin // 128, rows_in * groups, cols_in, 128), f32),
            gf=pltpu.VMEM((MU + 16, width), f32),
            gu=pltpu.VMEM((MU, 2 * width), bf16),
        ),
        far_in=(N.act, N.normed, N.gpu, N.w1, N.wp),
        far_out=(N.out,),
        cost=10000000000,
    )[N.out]
    side = bit_of(*core).astype(jnp.int32)
    grad_inputs = lockstep(tree2, tree1, beside=grad_inputs)
    while tree2.next() != (N.plane_join, 0):
        lockstep(tree2, tree1)
    tree2.start()
    while tree1.next() != (N.plane_join, 0):
        tree1.start()
        if tree1.next() != (N.plane_join, 1):
            tree1.finish()
        else:
            tree1.got, tree2.got = lax.optimization_barrier((tree1.got, tree2.got))
            tree1.finish()
    tree2.finish()
    tree2.start()
    tree1.start()
    grad_second = widen(tree2.got[0], 1 - side, 9, per, True, widen(tree2.value, side, 9, per, True))
    tree1.got, grad_second = lax.optimization_barrier((tree1.got, grad_second))
    grad_w2, grad_wp = grad_second
    tree1.finish(1)
    tree1.start()
    (grad_w1,) = widen(tree1.got[0], 1 - side, 1, 9, False, widen(tree1.value, side, 1, 9, False))

    return (
        third[N.out],
        grad_inputs,
        grad_w1.reshape(w_first.shape),
        fifth[N.gain_first].reshape(width),
        fifth[N.shift_first].reshape(width),
        grad_w2.reshape(w_second.shape),
        hidden[N.gain_second].reshape(width),
        hidden[N.shift_second].reshape(width),
        grad_wp.reshape(w_proj.shape),
        hidden[N.gain_proj].reshape(width),
        hidden[N.shift_proj].reshape(width),
    )


def solution(mesh):
    spread = P("grp", "rows", "cols", None)
    return jax.shard_map(
        on_device,
        mesh=mesh,
        in_specs=(spread,) + (P(),) * 9 + (P("grp", "rows", "cols"), spread),
        out_specs=(spread, spread) + (P(),) * 9,
        check_vma=False,
    )
```
